32 devices in a mesh: cuts: 2 (over y), gx: 4 (over z), gy: 2 (over x), ma: 2 (over core).
Axes of the slice: x: 2, y: 2, z: 4, core: 2. Of those that a mesh axis runs over, the one named last changes fastest.
Arguments:
- eigen_modes: bfloat16 [4, 32, 32, 2, 3, 512], P('cuts', 'gx', 'gy', None, None, 'ma'), parts along dimension 0, may hold values from -0.25 to 0.25
- links_first: bfloat16 [4, 3, 3, 32, 32, 2], P('cuts', None, None, 'gx', 'gy'), parts along dimension 0, may hold values from -2.5 to 2.5
- links_second: bfloat16 [4, 3, 3, 32, 32, 2], P('cuts', None, None, 'gx', 'gy'), parts along dimension 0, may hold values from -2.5 to 2.5
Outputs:
- elementals: float32 [4, 2, 512, 512], P('cuts', None, ('gx', 'gy'), 'ma'), parts along dimension 0
The draws below stay inside these ranges and needn't reach their ends.
There are 2 independent parts, one for each index of `cuts`. The reference program is written for one: setup_inputs(seed, part) draws one part's arguments, and reference() takes and returns one part's arrays. A program takes and returns all parts, laid end to end along the dimension named above; each array names one. Nothing has to cross between parts.
All inputs are finite; a program needn't handle non-finite values.
Results may differ from the reference program's by a relative error of at most 0.0055.
Values may be sent and summed in bfloat16 or wider, within the bound.
No kernel may reach another device: no remote copies, remote signals or barrier semaphores. Data moves between devices by JAX's collectives and lax.ppermute only.
A program may use at most 64 MiB of HBM per device.

```python
import jax
import jax.numpy as jnp
from jax import lax

NEV = 512
NZ = 2
NX = 32
NY = 32


def spiked(drawn, stream_key, source, target, parts, factor):
    def block_of(position):
        return (jnp.arange(drawn.shape[position]) // (drawn.shape[position] // parts)).reshape((-1,) + (1,) * (drawn.ndim - 1 - position))

    near = jax.random.permutation(stream_key, parts)[block_of(target)]
    far = (block_of(target) + parts // 2) % parts
    return jnp.where((block_of(source) == near) | (block_of(source) == far), factor * drawn, drawn)


def block_levels(rng, extent, split, low, largest):
    factor_of, own = 1.0, jax.random.fold_in(rng, 6)
    for position, parts in split:
        heights = jnp.exp(jax.random.uniform(jax.random.fold_in(own, position), (parts,), jnp.float32, low / len(split), largest / len(split)))
        factor_of = factor_of * jnp.repeat(heights, extent[position] // parts).reshape([-1 if axis == position else 1 for axis in range(len(extent))])
    return factor_of


def scatter_about(stream_key, shape, scale, limit, cuts=(), dtype=jnp.bfloat16):
    values = scale * jax.random.normal(stream_key, shape, jnp.float32)
    if cuts:
        values = values * block_levels(stream_key, shape, cuts, -0.22, 0.18)
    return jnp.clip(values, -limit, limit).astype(dtype)


def gaussian_with(key, dims, scale, reach, split, heavy, dtype=jnp.bfloat16):
    drawn = scale * jax.random.normal(key, dims, jnp.float32)
    if split:
        drawn = drawn * block_levels(key, dims, split, -0.22, 0.18)
    return jnp.clip(spiked(drawn, jax.random.fold_in(key, 3), *heavy), -reach, reach).astype(dtype)


def setup_inputs(seed: int = 0, part: int = 0) -> dict:
    seeds = jax.random.split(jax.random.key(seed), 4)
    part_keys = jax.random.split(jax.random.fold_in(seeds[3], part), 4)
    eigen_modes = gaussian_with(part_keys[0], (2, NX, NY, NZ, 3, NEV), 0.03, 0.25, ((1, 4), (2, 2), (5, 2)), (1, 5, 4, 2.0))
    links_first = scatter_about(part_keys[1], (2, 3, 3, NX, NY, NZ), 0.41, 2.5, ((3, 4), (4, 2)))
    links_second = scatter_about(part_keys[2], (2, 3, 3, NX, NY, NZ), 0.41, 2.5, ((3, 4), (4, 2)))
    return {"eigen_modes": eigen_modes, "links_first": links_first, "links_second": links_second}


def split_links(linkage):
    real_part = jnp.transpose(linkage[0].astype(jnp.float32), (2, 3, 4, 0, 1))
    imag_part = jnp.transpose(linkage[1].astype(jnp.float32), (2, 3, 4, 0, 1))
    return real_part, imag_part


def apply_link(link_real, link_imag, field, dagger):
    if dagger:
        form = "xyzba,xyzbm->xyzam"
        factor = -1.0
    else:
        form = "xyzab,xyzbm->xyzam"
        factor = 1.0
    high = lax.Precision.HIGHEST
    real_out = jnp.einsum(form, link_real, field[0], precision=high) - factor * jnp.einsum(form, link_imag, field[1], precision=high)
    imag_out = jnp.einsum(form, link_real, field[1], precision=high) + factor * jnp.einsum(form, link_imag, field[0], precision=high)
    return jnp.stack([real_out, imag_out])


def covariant(link_real, link_imag, field, lattice_axis):
    forward = jnp.roll(field, -1, lattice_axis)
    backward = jnp.roll(apply_link(link_real, link_imag, field, True), 1, lattice_axis)
    return apply_link(link_real, link_imag, forward, False) - backward


def contract(left, right_side):
    return lax.dot_general(left, right_side, (((0,), (0,)), ((), ())), preferred_element_type=jnp.float32)


def reference(eigen_modes, links_first, links_second):
    first_real, first_imag = split_links(links_first)
    second_real, second_imag = split_links(links_second)
    block_width = 128
    nblocks = NEV // block_width
    vec_real = eigen_modes[0].reshape(-1, NEV)
    vec_imag = eigen_modes[1].reshape(-1, NEV)
    blocks = jnp.moveaxis(eigen_modes.reshape(2, NX, NY, NZ, 3, nblocks, block_width), 5, 0)

    def one_block(block_modes):
        field = block_modes.astype(jnp.float32)
        disp_x = covariant(first_real, first_imag, field, 1).astype(jnp.bfloat16)
        disp_xy = covariant(second_real, second_imag, disp_x.astype(jnp.float32), 2).astype(jnp.bfloat16)
        results = []
        for shifted in (disp_x, disp_xy):
            sh_real = shifted[0].reshape(-1, block_width)
            sh_imag = shifted[1].reshape(-1, block_width)
            real_out = contract(vec_real, sh_real) + contract(vec_imag, sh_imag)
            imag_out = contract(vec_real, sh_imag) - contract(vec_imag, sh_real)
            results.append(jnp.stack([real_out, imag_out]))
        return jnp.stack(results)

    stacked = lax.map(one_block, blocks)
    return jnp.moveaxis(stacked, 0, 3).reshape(2, 2, NEV, NEV)
```

```python
import jax
import jax.numpy as jnp
from jax import lax
from jax.sharding import PartitionSpec as P


def shifted(block, axis, distance):
    devices = range(lax.axis_size(axis))
    route = [((i - distance) % len(devices), i) for i in devices]
    return lax.ppermute(block, axis, route)


def apply_link(linkage, field, dagger):
    link_real = linkage[0].astype(jnp.float32)
    link_imag = linkage[1].astype(jnp.float32)
    factor = -1.0 if dagger else 1.0
    real_rows = []
    imag_rows = []
    for row in range(3):
        real_acc = None
        imag_acc = None
        for col in range(3):
            if dagger:
                coef_real = link_real[col, row][..., None]
                coef_imag = link_imag[col, row][..., None]
            else:
                coef_real = link_real[row, col][..., None]
                coef_imag = link_imag[row, col][..., None]
            field_real = field[0][:, :, :, col, :]
            field_imag = field[1][:, :, :, col, :]
            term_real = coef_real * field_real - factor * coef_imag * field_imag
            term_imag = coef_real * field_imag + factor * coef_imag * field_real
            real_acc = term_real if real_acc is None else real_acc + term_real
            imag_acc = term_imag if imag_acc is None else imag_acc + term_imag
        real_rows.append(real_acc)
        imag_rows.append(imag_acc)
    return jnp.stack([jnp.stack(real_rows, axis=3), jnp.stack(imag_rows, axis=3)])


def contract(left, right_side):
    return lax.dot_general(
        left, right_side, (((0,), (0,)), ((), ())), preferred_element_type=jnp.float32
    )


def sum_over(pieces, axis, dim):
    size = lax.axis_size(axis)
    me = lax.axis_index(axis)
    total = lax.dynamic_index_in_dim(pieces, me, dim)
    for step in range(1, size):
        outgoing = lax.dynamic_index_in_dim(pieces, (me + step) % size, dim)
        total = total + shifted(outgoing.astype(jnp.bfloat16), axis, step).astype(jnp.float32)
    return total


def sum_over_gx_at_once(pieces):
    narrow = lax.all_to_all(pieces.astype(jnp.bfloat16), "gx", 1, 1, tiled=True)
    return jnp.sum(narrow.astype(jnp.float32), axis=1, keepdims=True)


def local(eigen_modes, links_first, links_second):
    field = eigen_modes.astype(jnp.float32)
    upper_plane = shifted(eigen_modes[:, :1], "gx", -1)
    forward = jnp.concatenate([eigen_modes[:, 1:], upper_plane], axis=1).astype(jnp.float32)
    linked = apply_link(links_first, field, True)
    behind = shifted(linked[:, -1:], "gx", 1)
    backward = jnp.concatenate([behind, linked[:, :-1]], axis=1)
    disp_x = (apply_link(links_first, forward, False) - backward).astype(jnp.bfloat16)
    upper_row = shifted(disp_x[:, :, :1], "gy", -1)
    forward_y = jnp.concatenate([disp_x[:, :, 1:], upper_row], axis=2).astype(jnp.float32)
    linked_y = apply_link(links_second, disp_x.astype(jnp.float32), True)
    behind_y = shifted(linked_y[:, :, -1:], "gy", 1)
    backward_y = jnp.concatenate([behind_y, linked_y[:, :, :-1]], axis=2)
    disp_xy = (apply_link(links_second, forward_y, False) - backward_y).astype(jnp.bfloat16)
    width = eigen_modes.shape[5]
    xr_cols = disp_x[0].reshape(-1, width)
    xi_cols = disp_x[1].reshape(-1, width)
    yr_cols = disp_xy[0].reshape(-1, width)
    yi_cols = disp_xy[1].reshape(-1, width)
    shard_rows = lax.all_gather(eigen_modes, "ma", axis=5, tiled=True)
    count = shard_rows.shape[5]
    left_real = shard_rows[0].reshape(-1, count)
    left_imag = shard_rows[1].reshape(-1, count)
    outputs = []
    for col_real, col_imag in ((xr_cols, xi_cols), (yr_cols, yi_cols)):
        real_out = contract(left_real, col_real) + contract(left_imag, col_imag)
        imag_out = contract(left_real, col_imag) - contract(left_imag, col_real)
        parts = jnp.stack([real_out, imag_out])
        outputs.append(parts.reshape(2, lax.axis_size("gx"), lax.axis_size("gy"), -1, width))
    first = sum_over_gx_at_once(sum_over(outputs[0], "gy", 2))
    second = sum_over(sum_over(outputs[1], "gy", 2), "gx", 1)
    return jnp.stack([first[:, 0, 0], second[:, 0, 0]])


def solution(mesh):
    return jax.shard_map(
        local,
        mesh=mesh,
        in_specs=(
            P("cuts", "gx", "gy", None, None, "ma"),
            P("cuts", None, None, "gx", "gy", None),
            P("cuts", None, None, "gx", "gy", None),
        ),
        out_specs=P("cuts", None, ("gx", "gy"), "ma"),
        check_vma=False,
    )
```

```python
import jax
import jax.numpy as jnp
from jax import lax
from jax.experimental import pallas as pl
from jax.experimental.pallas import tpu as pltpu
from jax.sharding import PartitionSpec as P

VMEM_LIMIT = 48 * 1024 * 1024


def shifted(block, axis, distance):
    devices = range(lax.axis_size(axis))
    route = [((i - distance) % len(devices), i) for i in devices]
    return lax.ppermute(block, axis, route)


def call(body, out_shape, flops, operands, scratch=()):
    moved = sum(a.size * a.dtype.itemsize for a in operands)
    in_specs = [
        pl.BlockSpec(memory_space=pltpu.SMEM if a.dtype == jnp.int32 else pltpu.VMEM)
        for a in operands
    ]
    return pl.pallas_call(
        body,
        out_shape=out_shape,
        in_specs=in_specs,
        scratch_shapes=scratch,
        cost_estimate=pl.CostEstimate(flops=flops, bytes_accessed=moved, transcendentals=0),
        compiler_params=pltpu.CompilerParams(vmem_limit_bytes=VMEM_LIMIT),
    )(*operands)


def link_rows(linkage, dagger):
    order = (2, 1, 0, 3, 4) if dagger else (2, 0, 1, 3, 4)
    link_real = linkage[0].astype(jnp.float32).transpose(order)
    link_imag = linkage[1].astype(jnp.float32).transpose(order)
    link_real = link_real.reshape(link_real.shape[:2] + (-1,))
    link_imag = link_imag.reshape(link_imag.shape[:2] + (-1,))
    if dagger:
        top = jnp.concatenate([-link_real, -link_imag], axis=2)
        bottom = jnp.concatenate([link_imag, -link_real], axis=2)
    else:
        top = jnp.concatenate([link_real, -link_imag], axis=2)
        bottom = jnp.concatenate([link_imag, link_real], axis=2)
    return jnp.concatenate([top, bottom], axis=1)


def plane_rows(ref, x):
    parts, _, ys, colours, zs, width = ref.shape
    return jnp.concatenate(
        [ref[p, x, :, c].reshape(ys * zs, width) for p in range(parts) for c in range(colours)],
        axis=0,
    )


def prepare_kernel(raw_ref, rows_ref, turned_ref):
    for x in range(rows_ref.shape[0]):
        rows_ref[x] = plane_rows(raw_ref, x)
    planes, depth, width = rows_ref.shape
    turned_ref[...] = rows_ref[...].reshape(planes * depth, width).T


def turn_kernel(raw_ref, turned_ref, rows_ref):
    for x in range(rows_ref.shape[0]):
        rows_ref[x] = plane_rows(raw_ref, x)
    planes, depth, width = rows_ref.shape
    turned_ref[...] = rows_ref[...].reshape(planes * depth, width).T


def site_matrix(rows_and_masks):
    blocks = []
    for q in range(rows_and_masks[0][0].shape[0]):
        block = None
        for rows, mask in rows_and_masks:
            term = rows[q : q + 1] * mask
            block = term if block is None else block + term
        blocks.append(block.astype(jnp.bfloat16))
    return jnp.concatenate(blocks, axis=0)


def dot(a, b):
    return jnp.dot(a, b, preferred_element_type=jnp.float32)


def iotas(shape):
    return (
        lax.broadcasted_iota(jnp.int32, shape, 0),
        lax.broadcasted_iota(jnp.int32, shape, 1),
    )


def first_kernel(sites, zs, rows_ref, low_ref, high_ref, ahead_ref, back_ref, out_ref, first_ref, last_ref):
    planes, depth, _ = rows_ref.shape
    site, lane = iotas((sites, depth))
    same = (lane % sites == site).astype(jnp.float32)
    edge = first_ref.shape[1]
    row, lane = iotas((edge, depth))
    part_colour = (row // zs) * sites + row % zs
    used = row < (depth // sites) * zs
    pick_first = (used & (lane == part_colour)).astype(jnp.bfloat16)
    pick_last = (used & (lane == part_colour + sites - zs)).astype(jnp.bfloat16)
    low = plane_rows(low_ref, 0)
    high = plane_rows(high_ref, 0)
    for x in range(planes):
        below = low if x == 0 else rows_ref[x - 1]
        above = high if x == planes - 1 else rows_ref[x + 1]
        moved = dot(site_matrix([(ahead_ref[x], same)]), above)
        moved = moved + dot(site_matrix([(back_ref[x], same)]), below)
        moved = moved.astype(jnp.bfloat16)
        out_ref[x] = moved
        first_ref[x] = dot(pick_first, moved).astype(jnp.bfloat16)
        last_ref[x] = dot(pick_last, moved).astype(jnp.bfloat16)


def project(where_ref, field_ref, own_ref, others_ref, keep_ref, send_ref, right_ref, total_ref):
    planes, depth, width = field_ref.shape
    half = depth // 2
    for x in range(planes):
        top = pl.ds(x * depth, half)
        low = pl.ds(x * depth + half, half)
        real = field_ref[x, :half]
        imag = field_ref[x, half:]
        right_ref[top, :width] = real
        right_ref[top, width:] = imag
        right_ref[low, :width] = imag
        right_ref[low, width:] = -real
    right = right_ref[...]
    total_ref[0] = dot(own_ref[...], right)
    for k in range(others_ref.shape[0]):
        total_ref[k + 1] = dot(others_ref[k], right)
    groups, own_modes, _ = total_ref.shape
    across_x, rows = keep_ref.shape[1:3]
    across_y = send_ref.shape[0] + 1
    me_y, me_modes = where_ref[0], where_ref[1]
    for gx in range(across_x):
        for gy in range(across_y):
            start = (gx * across_y + gy) * rows
            group = lax.rem(start // own_modes + groups - me_modes, groups)
            begin = start % own_modes
            block = total_ref[group, begin : begin + rows]
            step = lax.rem(gy + across_y - me_y, across_y)

            @pl.when(step == 0)
            def _():
                for p in range(2):
                    keep_ref[p, gx] = block[:, p * width : (p + 1) * width]

            @pl.when(step != 0)
            def _():
                for p in range(2):
                    piece = block[:, p * width : (p + 1) * width]
                    send_ref[step - 1, p, gx] = piece.astype(send_ref.dtype)


def project_kernel(where_ref, field_ref, own_ref, others_ref, keep_ref, send_ref, right_ref, total_ref):
    project(where_ref, field_ref, own_ref, others_ref, keep_ref, send_ref, right_ref, total_ref)


def second_kernel(
    sites, zs, where_ref, rows_ref, low_ref, high_ref, ahead_ref, back_ref, edge_ref, own_ref, others_ref,
    keep_ref, send_ref, field_ref, right_ref, total_ref,
):
    planes, depth, _ = rows_ref.shape
    site, lane = iotas((sites, depth))
    to_next = (lane % sites == site + zs).astype(jnp.float32)
    to_last = (lane % sites == site - zs).astype(jnp.float32)
    edge = high_ref.shape[1]
    site, lane = iotas((sites, 2 * edge))
    wanted = lane % zs + jnp.where(lane < edge, sites - zs, 0)
    at_edge = (site == wanted).astype(jnp.float32)
    for x in range(planes):
        inner = site_matrix([(ahead_ref[x], to_next), (back_ref[x], to_last)])
        outer = site_matrix([(edge_ref[x], at_edge)])
        moved = dot(inner, rows_ref[x])
        moved = moved + dot(outer, jnp.concatenate([high_ref[x], low_ref[x]], axis=0))
        field_ref[x] = moved.astype(jnp.bfloat16)
    project(where_ref, field_ref, own_ref, others_ref, keep_ref, send_ref, right_ref, total_ref)


def sum_over_y(keep, send):
    total = keep
    for step in range(1, lax.axis_size("gy")):
        total = total + shifted(send[step - 1], "gy", step).astype(jnp.float32)
    return total


def sum_over_x(pieces):
    narrow = lax.all_to_all(pieces.astype(jnp.bfloat16), "gx", 1, 1, tiled=True)
    return jnp.sum(narrow.astype(jnp.float32), axis=1)


def local(eigen_modes, links_first, links_second):
    f32, bf16 = jnp.float32, jnp.bfloat16
    parts, planes, ys, zs, colours, width = eigen_modes.shape
    sites = ys * zs
    depth = parts * colours * sites
    edge = -(-parts * colours * zs // 16) * 16
    across_x, across_y, groups = (lax.axis_size(a) for a in ("gx", "gy", "ma"))
    rows = groups * width // (across_x * across_y)
    raw = eigen_modes.transpose(0, 1, 2, 4, 3, 5)

    high = shifted(raw[:, :1], "gx", -1)
    low = shifted(raw[:, -1:], "gx", 1)
    low_links = shifted(links_first[:, :, :, -1:], "gx", 1)
    others = [shifted(raw, "ma", -step) for step in range(1, groups)]
    low_links_y = shifted(links_second[:, :, :, :, -1:], "gy", 1)

    where = jnp.stack([lax.axis_index("gy"), lax.axis_index("ma")]).astype(jnp.int32)
    ahead_x = link_rows(links_first, False)
    back_x = link_rows(jnp.concatenate([low_links, links_first[:, :, :, :-1]], axis=3), True)
    ahead_y = link_rows(jnp.roll(links_second, 1, axis=4), False)
    back_y = link_rows(links_second, True)
    pad = ((0, 0), (0, 0), (0, edge - parts * colours * zs))
    edge_y = jnp.concatenate(
        [
            jnp.pad(link_rows(links_second[:, :, :, :, -1:], False), pad),
            jnp.pad(link_rows(low_links_y, True), pad),
        ],
        axis=2,
    )

    field_shape = jax.ShapeDtypeStruct((planes, depth, width), bf16)
    turned_shape = jax.ShapeDtypeStruct((width, planes * depth), bf16)
    edge_shape = jax.ShapeDtypeStruct((planes, edge, width), bf16)
    keep_shape = jax.ShapeDtypeStruct((parts, across_x, rows, width), f32)
    send_shape = jax.ShapeDtypeStruct((across_y - 1, parts, across_x, rows, width), bf16)
    right = pltpu.VMEM((planes * depth, parts * width), bf16)
    total = pltpu.VMEM((groups, width, parts * width), f32)
    step_flops = 2 * planes * depth * depth * width
    project_flops = 2 * groups * width * planes * depth * parts * width

    field, own = call(prepare_kernel, (field_shape, turned_shape), step_flops // 4, [raw])
    turned = [
        call(turn_kernel, turned_shape, step_flops // 4, [r], [pltpu.VMEM(field_shape.shape, bf16)])
        for r in others
    ]
    others = jnp.stack(turned)

    def first(*refs):
        first_kernel(sites, zs, *refs)

    moved, first_row, last_row = call(
        first, (field_shape, edge_shape, edge_shape), 2 * step_flops,
        [field, low, high, ahead_x, back_x],
    )
    high_y = shifted(first_row, "gy", -1)
    low_y = shifted(last_row, "gy", 1)
    keep_first, send_first = call(
        project_kernel, (keep_shape, send_shape), project_flops,
        [where, moved, own, others], [right, total],
    )

    def second(*refs):
        second_kernel(sites, zs, *refs)

    keep_second, send_second = call(
        second, (keep_shape, send_shape), step_flops + project_flops,
        [where, moved, low_y, high_y, ahead_y, back_y, edge_y, own, others],
        [pltpu.VMEM(field_shape.shape, bf16), right, total],
    )
    first_sum = sum_over_x(sum_over_y(keep_first, send_first))
    second_sum = sum_over_x(sum_over_y(keep_second, send_second))
    return jnp.stack([first_sum, second_sum])


def solution(mesh):
    return jax.shard_map(
        local,
        mesh=mesh,
        in_specs=(
            P("cuts", "gx", "gy", None, None, "ma"),
            P("cuts", None, None, "gx", "gy", None),
            P("cuts", None, None, "gx", "gy", None),
        ),
        out_specs=P("cuts", None, ("gx", "gy"), "ma"),
        check_vma=False,
    )
```

```python
import jax
import jax.numpy as jnp
from jax import lax
from jax.experimental import pallas as pl
from jax.experimental.pallas import tpu as pltpu
from jax.sharding import PartitionSpec as P

VMEM_LIMIT = 48 * 1024 * 1024


def shifted(block, axis, distance):
    devices = range(lax.axis_size(axis))
    route = [((i - distance) % len(devices), i) for i in devices]
    return lax.ppermute(block, axis, route)


def call(body, out_shape, flops, operands, scratch=()):
    moved = sum(a.size * a.dtype.itemsize for a in operands)
    in_specs = [
        pl.BlockSpec(memory_space=pltpu.SMEM if a.dtype == jnp.int32 else pltpu.VMEM)
        for a in operands
    ]
    return pl.pallas_call(
        body,
        out_shape=out_shape,
        in_specs=in_specs,
        scratch_shapes=scratch,
        cost_estimate=pl.CostEstimate(flops=flops, bytes_accessed=moved, transcendentals=0),
        compiler_params=pltpu.CompilerParams(vmem_limit_bytes=VMEM_LIMIT),
    )(*operands)


def dot(a, b):
    return jnp.dot(a, b, preferred_element_type=jnp.float32)


def pick(condition, value):
    return jnp.where(condition, value, 0.0).astype(jnp.bfloat16)


def coefficient_rows(ref, lanes, edge, ahead):
    parts, colours, _, planes, zs, ys = ref.shape
    sites = ys * zs
    depth = parts * colours * sites
    flat = ref[...].reshape(-1, ys)
    lane = lax.broadcasted_iota(jnp.int32, (1, lanes), 1)
    inner = lane < depth
    past = lax.rem(lane - depth + edge, edge)
    used = inner | (past < parts * colours * zs)
    lane_part = jnp.where(inner, lane // (colours * sites), past // (colours * zs))
    lane_colour = jnp.where(inner, lane // sites, past // zs) % colours
    lane_z = jnp.where(inner, lane, past) % zs
    shift = 1 if ahead and lanes > depth else 0
    lane_y = jnp.where(inner, (lane % sites) // zs, ys - 1 + shift)
    count = flat.shape[0]
    row = lax.broadcasted_iota(jnp.int32, (count, 1), 0)
    row_z = row % zs
    row_left = (row // (zs * planes * colours)) % colours
    row_right = (row // (zs * planes)) % colours
    y = lax.broadcasted_iota(jnp.int32, (ys, 1), 0)
    spread = dot(flat, pick(y + shift == lane_y, 1.0))
    match = (row_z == lane_z) & ((row_right if ahead else row_left) == lane_colour) & used
    spread = pick(match, spread)

    out = lax.broadcasted_iota(jnp.int32, (parts * planes * 8, 1), 0)
    field_part = out // (planes * 8)
    out_x = (out // 8) % planes
    out_part = (out % 8) // colours
    out_colour = (out % 8) % colours
    source = lax.broadcasted_iota(jnp.int32, (1, count), 1)
    source_x = (source // zs) % planes
    source_right = (source // (zs * planes)) % colours
    source_left = (source // (zs * planes * colours)) % colours
    source_part = source // (zs * planes * colours * colours)
    if ahead:
        sign = jnp.where((field_part == 1) & (out_part == 0), -1.0, 1.0)
    else:
        sign = jnp.where((field_part == 0) & (out_part == 1), 1.0, -1.0)
    chosen = (out_x == source_x) & (source_part == (out_part + field_part) % 2) & (out_part < parts)
    chosen = chosen & ((source_left if ahead else source_right) == out_colour)
    both = dot(pick(chosen, sign), spread)
    rows = jnp.where(lane_part == 0, both[: planes * 8], both[planes * 8 :])
    return rows.reshape(planes, 8, lanes)


def links_first_kernel(edge, links_ref, ahead_ref, back_ref, last_ref):
    lanes = ahead_ref.shape[2]
    ahead_ref[...] = coefficient_rows(links_ref, lanes, edge, True)
    back = coefficient_rows(links_ref, lanes, edge, False)
    back_ref[...] = back
    last_ref[...] = back[-1]


def links_second_kernel(edge, links_ref, ahead_ref, back_ref, last_ref):
    lanes = ahead_ref.shape[2]
    ahead_ref[...] = coefficient_rows(links_ref, lanes, edge, True)
    back = coefficient_rows(links_ref, lanes, edge, False)
    back_ref[...] = back
    last_ref[...] = back[:, :, lanes - last_ref.shape[2] :]


def plane_rows(ref, x):
    parts, _, ys, colours, zs, width = ref.shape
    return jnp.concatenate(
        [ref[p, x, :, c].reshape(ys * zs, width) for p in range(parts) for c in range(colours)],
        axis=0,
    )


def prepare_kernel(raw_ref, rows_ref, first_ref, last_ref):
    planes = rows_ref.shape[0]
    for x in range(planes):
        plane = plane_rows(raw_ref, x)
        rows_ref[x] = plane
        if x == 0:
            first_ref[...] = plane
        if x == planes - 1:
            last_ref[...] = plane


def turn_own_kernel(rows_ref, turned_ref):
    planes, depth, width = rows_ref.shape
    turned_ref[...] = rows_ref[...].reshape(planes * depth, width).T


def turn_kernel(raw_ref, turned_ref, rows_ref):
    for x in range(rows_ref.shape[0]):
        rows_ref[x] = plane_rows(raw_ref, x)
    planes, depth, width = rows_ref.shape
    turned_ref[...] = rows_ref[...].reshape(planes * depth, width).T


def site_matrix(rows_and_masks, count):
    blocks = []
    for q in range(count):
        block = None
        for rows, mask in rows_and_masks:
            term = rows[q : q + 1] * mask
            block = term if block is None else block + term
        blocks.append(block.astype(jnp.bfloat16))
    return jnp.concatenate(blocks, axis=0)


def iotas(shape):
    return (
        lax.broadcasted_iota(jnp.int32, shape, 0),
        lax.broadcasted_iota(jnp.int32, shape, 1),
    )


def first_kernel(
    sites, zs, rows_ref, low_ref, high_ref, ahead_ref, back_ref, past_ref, out_ref, first_ref, last_ref
):
    planes, depth, _ = rows_ref.shape
    site, lane = iotas((sites, depth))
    same = (lane % sites == site).astype(jnp.float32)
    edge = first_ref.shape[1]
    row, lane = iotas((edge, depth))
    part_colour = (row // zs) * sites + row % zs
    used = row < (depth // sites) * zs
    pick_first = (used & (lane == part_colour)).astype(jnp.bfloat16)
    pick_last = (used & (lane == part_colour + sites - zs)).astype(jnp.bfloat16)
    count = depth // sites
    for x in range(planes):
        below = low_ref[...] if x == 0 else rows_ref[x - 1]
        above = high_ref[...] if x == planes - 1 else rows_ref[x + 1]
        back = past_ref[...] if x == 0 else back_ref[x - 1]
        moved = dot(site_matrix([(ahead_ref[x], same)], count), above)
        moved = moved + dot(site_matrix([(back, same)], count), below)
        moved = moved.astype(jnp.bfloat16)
        out_ref[x] = moved
        first_ref[x] = dot(pick_first, moved).astype(jnp.bfloat16)
        last_ref[x] = dot(pick_last, moved).astype(jnp.bfloat16)


def project(where_ref, field_ref, own_ref, others_ref, keep_ref, send_ref, right_ref, total_ref):
    planes, depth, width = field_ref.shape
    half = depth // 2
    for x in range(planes):
        top = pl.ds(x * depth, half)
        low = pl.ds(x * depth + half, half)
        real = field_ref[x, :half]
        imag = field_ref[x, half:]
        right_ref[top, :width] = real
        right_ref[top, width:] = imag
        right_ref[low, :width] = imag
        right_ref[low, width:] = -real
    right = right_ref[...]
    total_ref[0] = dot(own_ref[...], right)
    for k in range(others_ref.shape[0]):
        total_ref[k + 1] = dot(others_ref[k], right)
    groups, own_modes, _ = total_ref.shape
    across_x, rows = keep_ref.shape[1:3]
    across_y = send_ref.shape[0] + 1
    me_y, me_modes = where_ref[0], where_ref[1]
    for gx in range(across_x):
        for gy in range(across_y):
            start = (gx * across_y + gy) * rows
            group = lax.rem(start // own_modes + groups - me_modes, groups)
            begin = start % own_modes
            block = total_ref[group, begin : begin + rows]
            step = lax.rem(gy + across_y - me_y, across_y)

            @pl.when(step == 0)
            def _():
                for p in range(2):
                    keep_ref[p, gx] = block[:, p * width : (p + 1) * width]

            @pl.when(step != 0)
            def _():
                for p in range(2):
                    piece = block[:, p * width : (p + 1) * width]
                    send_ref[step - 1, p, gx] = piece.astype(send_ref.dtype)


def project_kernel(where_ref, field_ref, own_ref, others_ref, keep_ref, send_ref, order_ref, right_ref, total_ref):
    order_ref[...] = jnp.zeros_like(order_ref)
    project(where_ref, field_ref, own_ref, others_ref, keep_ref, send_ref, right_ref, total_ref)


def second_kernel(
    sites, zs, where_ref, rows_ref, low_ref, high_ref, ahead_ref, back_ref, past_ref, own_ref, others_ref, order_ref,
    keep_ref, send_ref, field_ref, right_ref, total_ref,
):
    planes, depth, _ = rows_ref.shape
    edge = high_ref.shape[1]
    reach = depth + 2 * edge
    tail = past_ref.shape[2]
    head = back_ref.shape[2] - tail
    site, lane = iotas((sites, reach))
    inner = lane < depth
    upper = (lane >= depth) & (lane < depth + edge)
    lower = lane >= depth + edge
    edge_z = (lane - depth + edge) % edge % zs
    to_next = (inner & (lane % sites == site + zs)) | (upper & (site == sites - zs + edge_z))
    to_last = (inner & (lane % sites == site - zs)) | (lower & (site == edge_z))
    to_next = to_next.astype(jnp.float32)
    to_last = to_last.astype(jnp.float32)
    _, lane = iotas((8, tail))
    for x in range(planes):
        mixed = jnp.where(lane >= depth + edge - head, past_ref[x], back_ref[x, :, head:])
        back = jnp.concatenate([back_ref[x, :, :head], mixed], axis=1)[:, :reach]
        ahead = ahead_ref[x, :, :reach]
        matrix = site_matrix([(ahead, to_next), (back, to_last)], depth // sites)
        column = jnp.concatenate([rows_ref[x], high_ref[x], low_ref[x]], axis=0)
        field_ref[x] = dot(matrix, column).astype(jnp.bfloat16)
    project(where_ref, field_ref, own_ref, others_ref, keep_ref, send_ref, right_ref, total_ref)


def sum_over_y(keep, send):
    total = keep
    for step in range(1, lax.axis_size("gy")):
        total = total + shifted(send[step - 1], "gy", step).astype(jnp.float32)
    return total


def sum_over_x(pieces):
    narrow = lax.all_to_all(pieces.astype(jnp.bfloat16), "gx", 1, 1, tiled=True)
    return jnp.sum(narrow.astype(jnp.float32), axis=1)


def local(eigen_modes, links_first, links_second):
    f32, bf16 = jnp.float32, jnp.bfloat16
    parts, planes, ys, zs, colours, width = eigen_modes.shape
    sites = ys * zs
    depth = parts * colours * sites
    edge = -(-parts * colours * zs // 16) * 16
    across_x, across_y, groups = (lax.axis_size(a) for a in ("gx", "gy", "ma"))
    rows = groups * width // (across_x * across_y)
    raw = eigen_modes.transpose(0, 1, 2, 4, 3, 5)
    lanes = -(-(depth + 2 * edge) // 128) * 128
    where = jnp.stack([lax.axis_index("gy"), lax.axis_index("ma")]).astype(jnp.int32)
    field_shape = jax.ShapeDtypeStruct((planes, depth, width), bf16)
    turned_shape = jax.ShapeDtypeStruct((width, planes * depth), bf16)
    edge_shape = jax.ShapeDtypeStruct((planes, edge, width), bf16)
    keep_shape = jax.ShapeDtypeStruct((parts, across_x, rows, width), f32)
    send_shape = jax.ShapeDtypeStruct((across_y - 1, parts, across_x, rows, width), bf16)
    right = pltpu.VMEM((planes * depth, parts * width), bf16)
    total = pltpu.VMEM((groups, width, parts * width), f32)
    step_flops = 2 * planes * depth * depth * width
    project_flops = 2 * groups * width * planes * depth * parts * width

    plane_shape = jax.ShapeDtypeStruct((depth, width), bf16)
    link_shape = jax.ShapeDtypeStruct((planes, 8, depth), f32)
    link_y_shape = jax.ShapeDtypeStruct((planes, 8, lanes), f32)
    order_shape = jax.ShapeDtypeStruct((8, 128), f32)

    others = [shifted(raw, "ma", -step) for step in range(1, groups)]
    field, first_plane, last_plane = call(
        prepare_kernel, (field_shape, plane_shape, plane_shape), step_flops // 8, [raw]
    )
    high = shifted(first_plane, "gx", -1)
    low = shifted(last_plane, "gx", 1)

    def prepare_first(*refs):
        links_first_kernel(edge, *refs)

    def prepare_second(*refs):
        links_second_kernel(edge, *refs)

    ahead_x, back_x, back_x_last = call(
        prepare_first, (link_shape, link_shape, jax.ShapeDtypeStruct((8, depth), f32)),
        step_flops // 4, [links_first.transpose(0, 1, 2, 3, 5, 4)],
    )
    past_x = shifted(back_x_last, "gx", 1)
    ahead_y, back_y, back_y_last = call(
        prepare_second, (link_y_shape, link_y_shape, jax.ShapeDtypeStruct((planes, 8, 128), f32)),
        step_flops // 4, [links_second.transpose(0, 1, 2, 3, 5, 4)],
    )
    past_y = shifted(back_y_last, "gy", 1)
    own = call(turn_own_kernel, turned_shape, step_flops // 8, [field])
    turned = [
        call(turn_kernel, turned_shape, step_flops // 8, [r], [pltpu.VMEM(field_shape.shape, bf16)])
        for r in others
    ]
    others = jnp.stack(turned)

    def first(*refs):
        first_kernel(sites, zs, *refs)

    moved, first_row, last_row = call(
        first, (field_shape, edge_shape, edge_shape), 2 * step_flops,
        [field, low, high, ahead_x, back_x, past_x],
    )
    high_y = shifted(first_row, "gy", -1)
    low_y = shifted(last_row, "gy", 1)
    keep_first, send_first, order = call(
        project_kernel, (keep_shape, send_shape, order_shape), project_flops,
        [where, moved, own, others], [right, total],
    )

    def second(*refs):
        second_kernel(sites, zs, *refs)

    keep_second, send_second = call(
        second, (keep_shape, send_shape), step_flops + project_flops,
        [where, moved, low_y, high_y, ahead_y, back_y, past_y, own, others, order],
        [pltpu.VMEM(field_shape.shape, bf16), right, total],
    )
    first_sum = sum_over_x(sum_over_y(keep_first, send_first))
    second_sum = sum_over_x(sum_over_y(keep_second, send_second))
    return jnp.stack([first_sum, second_sum])


def solution(mesh):
    return jax.shard_map(
        local,
        mesh=mesh,
        in_specs=(
            P("cuts", "gx", "gy", None, None, "ma"),
            P("cuts", None, None, "gx", "gy", None),
            P("cuts", None, None, "gx", "gy", None),
        ),
        out_specs=P("cuts", None, ("gx", "gy"), "ma"),
        check_vma=False,
    )
```

```python
import jax
import jax.numpy as jnp
from jax import lax
from jax.experimental import pallas as pl
from jax.experimental.pallas import tpu as pltpu
from jax.sharding import PartitionSpec as P

VMEM_LIMIT = 48 * 1024 * 1024


def shifted(block, axis, distance):
    devices = range(lax.axis_size(axis))
    route = [((i - distance) % len(devices), i) for i in devices]
    return lax.ppermute(block, axis, route)


def across(block, axes, steps):
    sizes = [lax.axis_size(a) for a in axes]
    route = []
    for one in range(sizes[0]):
        for two in range(sizes[1]):
            source = ((one - steps[0]) % sizes[0]) * sizes[1] + (two - steps[1]) % sizes[1]
            route.append((source, one * sizes[1] + two))
    return lax.ppermute(block, axes, route)


def call(body, out_shape, flops, operands, scratch=()):
    moved = sum(a.size * a.dtype.itemsize for a in operands)
    in_specs = [
        pl.BlockSpec(memory_space=pltpu.SMEM if a.dtype == jnp.int32 else pltpu.VMEM)
        for a in operands
    ]
    return pl.pallas_call(
        body,
        out_shape=out_shape,
        in_specs=in_specs,
        scratch_shapes=scratch,
        cost_estimate=pl.CostEstimate(flops=flops, bytes_accessed=moved, transcendentals=0),
        compiler_params=pltpu.CompilerParams(vmem_limit_bytes=VMEM_LIMIT),
    )(*operands)


def dot(a, b):
    return jnp.dot(a, b, preferred_element_type=jnp.float32)


def pick(condition, value):
    return jnp.where(condition, value, 0.0).astype(jnp.bfloat16)


def coefficient_rows(ref, lanes, edge, ahead, scale=1.0):
    parts, colours, _, planes, zs, ys = ref.shape
    sites = ys * zs
    depth = parts * colours * sites
    flat = ref[...].reshape(-1, ys)
    lane = lax.broadcasted_iota(jnp.int32, (1, lanes), 1)
    inner = lane < depth
    past = lax.rem(lane - depth + edge, edge)
    used = inner | (past < parts * colours * zs)
    lane_part = jnp.where(inner, lane // (colours * sites), past // (colours * zs))
    lane_colour = jnp.where(inner, lane // sites, past // zs) % colours
    lane_z = jnp.where(inner, lane, past) % zs
    shift = 1 if ahead and lanes > depth else 0
    lane_y = jnp.where(inner, (lane % sites) // zs, ys - 1 + shift)
    count = flat.shape[0]
    row = lax.broadcasted_iota(jnp.int32, (count, 1), 0)
    row_z = row % zs
    row_left = (row // (zs * planes * colours)) % colours
    row_right = (row // (zs * planes)) % colours
    y = lax.broadcasted_iota(jnp.int32, (ys, 1), 0)
    spread = dot(flat, pick(y + shift == lane_y, 1.0))
    match = (row_z == lane_z) & ((row_right if ahead else row_left) == lane_colour) & used
    spread = pick(match, spread)

    out = lax.broadcasted_iota(jnp.int32, (parts * planes * 8, 1), 0)
    field_part = out // (planes * 8)
    out_x = (out // 8) % planes
    out_part = (out % 8) // colours
    out_colour = (out % 8) % colours
    source = lax.broadcasted_iota(jnp.int32, (1, count), 1)
    source_x = (source // zs) % planes
    source_right = (source // (zs * planes)) % colours
    source_left = (source // (zs * planes * colours)) % colours
    source_part = source // (zs * planes * colours * colours)
    if ahead:
        sign = jnp.where((field_part == 1) & (out_part == 0), -1.0, 1.0)
    else:
        sign = jnp.where((field_part == 0) & (out_part == 1), 1.0, -1.0)
    chosen = (out_x == source_x) & (source_part == (out_part + field_part) % 2) & (out_part < parts)
    chosen = chosen & ((source_left if ahead else source_right) == out_colour)
    both = dot(pick(chosen, scale * sign), spread)
    rows = jnp.where(lane_part == 0, both[: planes * 8], both[planes * 8 :])
    return rows.reshape(planes, 8, lanes)


def plane_rows(ref, x):
    parts, _, ys, colours, zs, width = ref.shape
    return jnp.concatenate(
        [ref[p, x, :, c].reshape(ys * zs, width) for p in range(parts) for c in range(colours)],
        axis=0,
    )


def site_matrix(rows_and_masks, count):
    blocks = []
    for q in range(count):
        block = None
        for rows, mask in rows_and_masks:
            term = rows[q : q + 1] * mask
            block = term if block is None else block + term
        blocks.append(block.astype(jnp.bfloat16))
    return jnp.concatenate(blocks, axis=0)


def iotas(shape):
    return (
        lax.broadcasted_iota(jnp.int32, shape, 0),
        lax.broadcasted_iota(jnp.int32, shape, 1),
    )


def prepare_kernel(
    raw_ref, links_x_ref, links_y_ref, rows_ref, first_ref, last_ref, edges_ref,
    ahead_x_ref, back_x_ref, ahead_y_ref, back_y_ref,
):
    planes, depth, width = rows_ref.shape
    zs = raw_ref.shape[4]
    sites = raw_ref.shape[2] * zs
    edge = last_ref.shape[0] - depth
    row, lane = iotas((2 * edge, depth))
    spot = row % edge
    wanted = (spot // zs) * sites + spot % zs + jnp.where(row < edge, 0, sites - zs)
    ends = ((spot < (depth // sites) * zs) & (lane == wanted)).astype(jnp.bfloat16)
    last_ref[depth:] = jnp.zeros((edge, width), last_ref.dtype)
    edges_ref[...] = jnp.zeros_like(edges_ref)
    for x in range(planes):
        plane = plane_rows(raw_ref, x)
        rows_ref[x] = plane
        edges_ref[x, : 2 * edge] = dot(ends, plane).astype(jnp.bfloat16)
        if x == 0:
            first_ref[...] = plane
        if x == planes - 1:
            last_ref[:depth] = plane
    ahead_x_ref[...] = coefficient_rows(links_x_ref, ahead_x_ref.shape[2], edge, True)
    back = coefficient_rows(links_x_ref, back_x_ref.shape[2], edge, False)
    back_x_ref[...] = back
    last_ref[depth : depth + 16, :depth] = jnp.concatenate([back[-1], back[-1]], axis=0).astype(jnp.bfloat16)
    lanes = ahead_y_ref.shape[2]
    ahead_y_ref[...] = coefficient_rows(links_y_ref, lanes, edge, True, -1.0)
    back = coefficient_rows(links_y_ref, lanes, edge, False, -1.0)
    back_y_ref[...] = back
    for x in range(planes):
        tail = back[x, :, lanes - 128 :]
        edges_ref[x, 2 * edge : 2 * edge + 16, :128] = jnp.concatenate([tail, tail], axis=0).astype(jnp.bfloat16)


def turn_kernel(raw_ref, rows_ref, turned_ref):
    planes, depth, width = rows_ref.shape
    for x in range(planes):
        rows_ref[x] = plane_rows(raw_ref, x)
    turned_ref[...] = rows_ref[...].reshape(planes * depth, width).T


def move_plane(same, count, ahead, back, above, below):
    moved = dot(site_matrix([(ahead, same)], count), above)
    return (moved + dot(site_matrix([(back, same)], count), below)).astype(jnp.bfloat16)


def same_site(sites, depth):
    site, lane = iotas((sites, depth))
    return (lane % sites == site).astype(jnp.float32)


def inner_kernel(sites, rows_ref, ahead_ref, back_ref, out_ref, turned_ref):
    planes, depth, width = rows_ref.shape
    same = same_site(sites, depth)
    for x in range(1, planes - 1):
        out_ref[x - 1] = move_plane(
            same, depth // sites, ahead_ref[x], back_ref[x - 1], rows_ref[x + 1], rows_ref[x - 1]
        )
    turned_ref[...] = rows_ref[...].reshape(planes * depth, width).T


def set_right(right_ref, x, moved):
    depth, width = moved.shape
    half = depth // 2
    real, imag = moved[:half], moved[half:]
    right_ref[x * depth : x * depth + half, :width] = real
    right_ref[x * depth : x * depth + half, width:] = imag
    right_ref[x * depth + half : (x + 1) * depth, :width] = imag
    right_ref[x * depth + half : (x + 1) * depth, width:] = -real


def project(lefts, right, my_bit, my_modes, halved, keep_ref, send_ref, total_ref):
    for k, left in enumerate(lefts):
        total_ref[k] = dot(left, right)
    groups, own_modes, _ = total_ref.shape
    parts, across_x, across_y, rows, width = keep_ref.shape

    def piece(index):
        start = index * rows
        group = lax.rem(start // own_modes + groups - my_modes, groups)
        begin = start % own_modes
        return total_ref[group, begin : begin + rows]

    for gx in range(across_x):
        for gy in range(across_y):
            if halved:
                base = gx * 2 * across_y + 2 * gy
                even, odd = piece(base), piece(base + 1)
            else:
                even, odd = piece(2 * gx * across_y + gy), piece((2 * gx + 1) * across_y + gy)
            keep = jnp.where(my_bit == 0, even, odd)
            send = jnp.where(my_bit == 0, odd, even).astype(send_ref.dtype)
            for p in range(parts):
                keep_ref[p, gx, gy] = keep[:, p * width : (p + 1) * width]
                send_ref[p, gx, gy] = send[:, p * width : (p + 1) * width]


def first_kernel(
    sites, where_ref, rows_ref, low_ref, high_ref, inner_ref, ahead_ref, back_ref, own_ref, others_ref,
    keep_ref, send_ref, right_ref, total_ref,
):
    planes, depth, _ = rows_ref.shape
    same = same_site(sites, depth)
    count = depth // sites
    past = low_ref[depth : depth + 8, :depth].astype(jnp.float32)
    moved = move_plane(same, count, ahead_ref[0], past, rows_ref[1], low_ref[:depth])
    set_right(right_ref, 0, moved)
    x = planes - 1
    moved = move_plane(same, count, ahead_ref[x], back_ref[x - 1], high_ref[...], rows_ref[x - 1])
    set_right(right_ref, x, moved)
    for x in range(1, planes - 1):
        set_right(right_ref, x, inner_ref[x - 1])
    lefts = [own_ref[...]] + [others_ref[k] for k in range(others_ref.shape[0])]
    project(lefts, right_ref[...], where_ref[1], where_ref[2], True, keep_ref, send_ref, total_ref)


def move_y_kernel(
    sites, zs, rows_ref, others_ref, ends_ref, other_ends_ref, ahead_ref, back_ref, turned_ref, field_ref
):
    planes, depth, width = rows_ref.shape
    groups = others_ref.shape[0] + 1
    edge = other_ends_ref.shape[2] // 2
    reach = depth + 2 * edge
    head = back_ref.shape[2] - 128
    site, lane = iotas((sites, reach))
    inner = lane < depth
    upper = (lane >= depth) & (lane < depth + edge)
    lower = lane >= depth + edge
    edge_z = (lane - depth + edge) % edge % zs
    to_next = (inner & (lane % sites == site + zs)) | (upper & (site == sites - zs + edge_z))
    to_last = (inner & (lane % sites == site - zs)) | (lower & (site == edge_z))
    to_next = to_next.astype(jnp.float32)
    to_last = to_last.astype(jnp.float32)
    _, lane = iotas((8, 128))
    for x in range(planes):
        past = ends_ref[x, 2 * edge : 2 * edge + 8, :128].astype(jnp.float32)
        mixed = jnp.where(lane >= depth + edge - head, past, back_ref[x, :, head:])
        back = jnp.concatenate([back_ref[x, :, :head], mixed], axis=1)[:, :reach]
        matrix = site_matrix([(ahead_ref[x, :, :reach], to_next), (back, to_last)], depth // sites)
        column = jnp.concatenate([rows_ref[x], ends_ref[x, : 2 * edge]], axis=0)
        field_ref[0, x] = dot(matrix, column).astype(jnp.bfloat16)
        for k in range(groups - 1):
            column = jnp.concatenate([others_ref[k, x], other_ends_ref[k, x]], axis=0)
            field_ref[k + 1, x] = dot(matrix, column).astype(jnp.bfloat16)
    for k in range(groups):
        turned_ref[k] = field_ref[k].reshape(planes * depth, width).T


def second_kernel(where_ref, lefts_ref, right_ref, keep_ref, send_ref, total_ref):
    lefts = [lefts_ref[k] for k in range(lefts_ref.shape[0])]
    project(lefts, right_ref[...], where_ref[0], where_ref[2], False, keep_ref, send_ref, total_ref)


def swap(block, axis, bit):
    return lax.ppermute(block, axis, [(i, i ^ (1 << bit)) for i in range(lax.axis_size(axis))])


def halve(total, dim, axis, bit):
    shape = total.shape
    split = total.reshape(shape[:dim] + (shape[dim] // 2, 2) + shape[dim + 1 :])
    mine = (lax.axis_index(axis) >> bit) & 1
    keep = lax.dynamic_index_in_dim(split, mine, dim + 1, keepdims=False)
    send = lax.dynamic_index_in_dim(split, 1 - mine, dim + 1, keepdims=False).astype(jnp.bfloat16)
    return keep + swap(send, axis, bit).astype(jnp.float32)


def bits(axis):
    return range(lax.axis_size(axis).bit_length() - 1)


def local(eigen_modes, links_first, links_second):
    f32, bf16 = jnp.float32, jnp.bfloat16
    parts, planes, ys, zs, colours, width = eigen_modes.shape
    sites = ys * zs
    depth = parts * colours * sites
    edge = -(-parts * colours * zs // 16) * 16
    lanes = -(-(depth + 2 * edge) // 128) * 128
    across_x, across_y, groups = (lax.axis_size(a) for a in ("gx", "gy", "ma"))
    rows = groups * width // (across_x * across_y)
    raw = eigen_modes.transpose(0, 1, 2, 4, 3, 5)
    where = jnp.stack([lax.axis_index("gx") % 2, lax.axis_index("gy") % 2, lax.axis_index("ma")])
    where = where.astype(jnp.int32)

    def shape(*dims, dtype=bf16):
        return jax.ShapeDtypeStruct(dims, dtype)

    field_shape = shape(planes, depth, width)
    turned_shape = shape(width, planes * depth)
    total = pltpu.VMEM((groups, width, parts * width), f32)
    step_flops = 2 * planes * depth * depth * width
    project_flops = 2 * groups * width * planes * depth * parts * width

    raw_others = [shifted(raw, "ma", -step) for step in range(1, groups)]
    field, first_plane, last_plane, ends, ahead_x, back_x, ahead_y, back_y = call(
        prepare_kernel,
        (
            field_shape, shape(depth, width), shape(depth + edge, width), shape(planes, 3 * edge, width),
            shape(planes, 8, depth, dtype=f32), shape(planes, 8, depth, dtype=f32),
            shape(planes, 8, lanes, dtype=f32), shape(planes, 8, lanes, dtype=f32),
        ),
        step_flops // 2,
        [raw, links_first.transpose(0, 1, 2, 3, 5, 4), links_second.transpose(0, 1, 2, 3, 5, 4)],
    )
    high = shifted(first_plane, "gx", -1)
    low = shifted(last_plane, "gx", 1)
    if across_y == 2:
        near = shifted(ends, "gy", 1)
        far = [across(ends[:, : 2 * edge], ("gy", "ma"), (1, -step)) for step in range(1, groups)]
    else:
        near = jnp.concatenate(
            [shifted(ends[:, :edge], "gy", -1), shifted(ends[:, edge:], "gy", 1)], axis=1
        )
        far = [
            jnp.concatenate(
                [
                    across(ends[:, :edge], ("gy", "ma"), (-1, -step)),
                    across(ends[:, edge : 2 * edge], ("gy", "ma"), (1, -step)),
                ],
                axis=1,
            )
            for step in range(1, groups)
        ]

    def inner(*refs):
        inner_kernel(sites, *refs)

    def first(*refs):
        first_kernel(sites, *refs)

    def move_y(*refs):
        move_y_kernel(sites, zs, *refs)

    moved, own = call(
        inner, (shape(planes - 2, depth, width), turned_shape), 2 * step_flops, [field, ahead_x, back_x]
    )
    turned = [call(turn_kernel, (field_shape, turned_shape), step_flops // 8, [r]) for r in raw_others]
    fields = jnp.stack([t[0] for t in turned])
    others = jnp.stack([t[1] for t in turned])
    keep_first, send_first, right = call(
        first,
        (
            shape(parts, across_x, across_y // 2, rows, width, dtype=f32),
            shape(parts, across_x, across_y // 2, rows, width),
            shape(planes * depth, parts * width),
        ),
        project_flops,
        [where, field, low, high, moved, ahead_x, back_x, own, others],
        [total],
    )
    lefts = call(
        move_y, shape(groups, width, planes * depth), 2 * step_flops,
        [field, fields, near, jnp.stack(far), ahead_y, back_y],
        [pltpu.VMEM((groups,) + field_shape.shape, bf16)],
    )
    keep_second, send_second = call(
        second_kernel,
        (
            shape(parts, across_x // 2, across_y, rows, width, dtype=f32),
            shape(parts, across_x // 2, across_y, rows, width),
        ),
        project_flops,
        [where, lefts, right],
        [total],
    )
    first_sum = keep_first + swap(send_first, "gy", 0).astype(f32)
    second_sum = keep_second + swap(send_second, "gx", 0).astype(f32)
    for bit in list(bits("gy"))[1:]:
        first_sum = halve(first_sum, 2, "gy", bit)
    for bit in bits("gy"):
        second_sum = halve(second_sum, 2, "gy", bit)
    for bit in bits("gx"):
        first_sum = halve(first_sum, 1, "gx", bit)
    for bit in list(bits("gx"))[1:]:
        second_sum = halve(second_sum, 1, "gx", bit)
    return jnp.stack([first_sum[:, 0, 0], second_sum[:, 0, 0]])


def solution(mesh):
    return jax.shard_map(
        local,
        mesh=mesh,
        in_specs=(
            P("cuts", "gx", "gy", None, None, "ma"),
            P("cuts", None, None, "gx", "gy", None),
            P("cuts", None, None, "gx", "gy", None),
        ),
        out_specs=P("cuts", None, ("gx", "gy"), "ma"),
        check_vma=False,
    )
```

```python
import jax
import jax.numpy as jnp
import numpy as np
from jax import lax
from jax.experimental import pallas as pl
from jax.experimental.pallas import tpu as pltpu
from jax.sharding import PartitionSpec as P

VMEM_LIMIT = 16 * 1024 * 1024


def shifted(block, axis, distance):
    devices = range(lax.axis_size(axis))
    route = [((i - distance) % len(devices), i) for i in devices]
    return lax.ppermute(block, axis, route)


def call(body, out_shape, flops, operands, scratch=(), place=pltpu.VMEM):
    moved = sum(a.size * a.dtype.itemsize for a in operands)
    in_specs = [
        pl.BlockSpec(memory_space=pltpu.SMEM if a.dtype == jnp.int32 else place) for a in operands
    ]
    return pl.pallas_call(
        body,
        out_shape=out_shape,
        in_specs=in_specs,
        scratch_shapes=scratch,
        cost_estimate=pl.CostEstimate(flops=flops, bytes_accessed=moved, transcendentals=0),
        compiler_params=pltpu.CompilerParams(vmem_limit_bytes=VMEM_LIMIT),
    )(*operands)


def dot(a, b):
    return jnp.dot(a, b, preferred_element_type=jnp.float32)


def iotas(shape):
    return (
        lax.broadcasted_iota(jnp.int32, shape, 0),
        lax.broadcasted_iota(jnp.int32, shape, 1),
    )


def place_of(x, planes):
    return planes - 2 if x == 0 else x if x == planes - 1 else x - 1


def lane_maps(parts, colours, planes, ys, zs, lanes):
    sites = ys * zs
    depth = parts * colours * sites
    row_size = parts * colours * zs
    lane = np.arange(lanes)
    inner = lane < depth
    past = (lane - depth) % row_size
    used = lane < depth + 2 * row_size
    part = np.where(inner, lane // (colours * sites), past // (colours * zs))
    colour = np.where(inner, lane // sites, past // zs) % colours
    z = np.where(inner, lane, past) % zs
    y = np.where(inner, lane % sites // zs, ys - 1)
    y_ahead = np.where(inner, lane % sites // zs, ys) - 1
    spread = y == np.arange(ys)[:, None]
    spread_ahead = y_ahead == np.arange(ys)[:, None]

    row = np.arange(parts * colours * colours * planes * zs)[:, None]
    row_z = row % zs
    row_x = row // zs % planes
    row_right = row // (zs * planes) % colours
    row_left = row // (zs * planes * colours) % colours
    row_part = row // (zs * planes * colours * colours)
    match_ahead = (row_z == z) & (row_right == colour) & used
    match_back = (row_z == z) & (row_left == colour) & used

    out = np.arange(parts * planes * 8)[:, None]
    field_part = out // (planes * 8)
    out_x = out // 8 % planes
    out_part = out % 8 // colours
    out_colour = out % 8 % colours
    source = (out_x == row_x.T) & (row_part.T == (out_part + field_part) % 2) & (out_part < parts)
    choose_ahead = source & (row_left.T == out_colour)
    choose_back = source & (row_right.T == out_colour)
    sign_ahead = np.where((field_part == 1) & (out_part == 0), -1.0, 1.0)
    sign_back = np.where((field_part == 0) & (out_part == 1), 1.0, -1.0)
    maps = (
        spread, spread_ahead, match_ahead, match_back, choose_ahead * sign_ahead, choose_back * sign_back,
        np.broadcast_to(part == 0, (8, lanes)),
    )
    return [m.astype(jnp.bfloat16) for m in maps]


def coefficients(flat, spread, match, choose, first_part, planes):
    both = dot(choose, (dot(flat, spread) * match).astype(jnp.bfloat16))
    half = both.shape[0] // 2
    rows = jnp.where(first_part, both[:half], both[half:])
    return rows.reshape(planes, 8, rows.shape[1])


def plane_rows(ref, x):
    parts, _, ys, colours, zs, width = ref.shape
    return jnp.concatenate(
        [ref[p, x, :, c].reshape(ys * zs, width) for p in range(parts) for c in range(colours)],
        axis=0,
    )


def site_matrix(rows_and_masks, count):
    blocks = []
    for q in range(count):
        block = None
        for rows, mask in rows_and_masks:
            term = rows[q : q + 1] * mask
            block = term if block is None else block + term
        blocks.append(block.astype(jnp.bfloat16))
    return jnp.concatenate(blocks, axis=0)


def prepare_kernel(
    raw_hbm, links_x_hbm, links_y_hbm, spread_hbm, spread_ahead_hbm, match_ahead_hbm, match_back_hbm,
    choose_ahead_hbm, choose_back_hbm, first_part_hbm,
    rows_ref, first_ref, last_ref, ends_ref, ahead_x_ref, back_x_ref, ahead_y_ref, back_y_ref,
    raw_ref, links_x_ref, links_y_ref, spread_ref, spread_ahead_ref, match_ahead_ref, match_back_ref,
    choose_ahead_ref, choose_back_ref, first_part_ref, arrived,
):
    sources = (
        raw_hbm, links_x_hbm, links_y_hbm, spread_hbm, spread_ahead_hbm, match_ahead_hbm, match_back_hbm,
        choose_ahead_hbm, choose_back_hbm, first_part_hbm,
    )
    targets = (
        raw_ref, links_x_ref, links_y_ref, spread_ref, spread_ahead_ref, match_ahead_ref, match_back_ref,
        choose_ahead_ref, choose_back_ref, first_part_ref,
    )
    copies = [
        pltpu.make_async_copy(source, target, arrived.at[i])
        for i, (source, target) in enumerate(zip(sources, targets))
    ]
    for copy in copies:
        copy.start()
    for copy in copies[1:]:
        copy.wait()

    planes, depth, width = rows_ref.shape
    zs = raw_ref.shape[4]
    sites = raw_ref.shape[2] * zs
    row_size = depth // sites * zs
    lanes = ahead_y_ref.shape[2]
    ys = raw_ref.shape[2]
    first_part = first_part_ref[:1].astype(jnp.float32) > 0.5
    match_ahead = match_ahead_ref[...].astype(jnp.float32)
    match_back = match_back_ref[...].astype(jnp.float32)
    flat = links_x_ref[...].reshape(-1, ys)
    ahead_x_ref[...] = coefficients(
        flat, spread_ref[...], match_ahead, choose_ahead_ref[...], first_part, planes
    )
    back_x = coefficients(flat, spread_ref[...], match_back, choose_back_ref[...], first_part, planes)
    back_x_ref[...] = back_x
    flat = links_y_ref[...].reshape(-1, ys)
    ahead_y_ref[...] = coefficients(
        flat, spread_ahead_ref[...], match_ahead, choose_ahead_ref[...], first_part, planes
    )
    back_y = coefficients(flat, spread_ref[...], match_back, choose_back_ref[...], first_part, planes)
    back_y_ref[...] = back_y

    row, lane = iotas((2 * row_size, depth))
    spot = row % row_size
    wanted = (spot // zs) * sites + spot % zs + jnp.where(row < row_size, 0, sites - zs)
    ends = (lane == wanted).astype(jnp.bfloat16)
    filler = jnp.zeros((8, width - 128), jnp.float32)
    spare = ends_ref.shape[1] - 2 * row_size - 8
    copies[0].wait()
    for x in range(planes):
        plane = plane_rows(raw_ref, x)
        rows_ref[place_of(x, planes)] = plane
        tail = jnp.concatenate([back_y[x, :, lanes - 128 :], filler], axis=1)
        pieces = [dot(ends, plane), tail]
        if spare:
            pieces.append(jnp.zeros((spare, width), jnp.float32))
        ends_ref[x] = jnp.concatenate(pieces, axis=0).astype(jnp.bfloat16)
        if x == 0:
            first_ref[...] = plane
        if x == planes - 1:
            last_ref[:depth] = plane
    end = back_x[planes - 1, :, :width]
    last_ref[depth:] = jnp.concatenate([end, end], axis=0).astype(jnp.bfloat16)


def turn_kernel(raw_ref, rows_ref, turned_ref):
    planes, depth, width = rows_ref.shape
    for x in range(planes):
        rows_ref[place_of(x, planes)] = plane_rows(raw_ref, x)
    turned_ref[...] = rows_ref[...].reshape(planes * depth, width).T


def move_plane(same, count, ahead, back, above, below):
    depth = same.shape[1]
    moved = dot(site_matrix([(ahead[:, :depth], same)], count), above)
    return (moved + dot(site_matrix([(back[:, :depth], same)], count), below)).astype(jnp.bfloat16)


def same_site(sites, depth):
    site, lane = iotas((sites, depth))
    return (lane % sites == site).astype(jnp.float32)


def set_right(right_ref, place, moved):
    depth, width = moved.shape
    half = depth // 2
    start = place * depth
    real, imag = moved[:half], moved[half:]
    right_ref[start : start + half, :width] = real
    right_ref[start : start + half, width:] = imag
    right_ref[start + half : start + depth, :width] = imag
    right_ref[start + half : start + depth, width:] = -real


def inner_kernel(sites, rows_ref, ahead_ref, back_ref, right_ref, turned_ref):
    planes, depth, width = rows_ref.shape
    same = same_site(sites, depth)
    for x in range(1, planes - 1):
        above = rows_ref[place_of(x + 1, planes)]
        below = rows_ref[place_of(x - 1, planes)]
        moved = move_plane(same, depth // sites, ahead_ref[x], back_ref[x - 1], above, below)
        set_right(right_ref, place_of(x, planes), moved)
    turned_ref[...] = rows_ref[...].reshape(planes * depth, width).T


def begin_first_kernel(own_ref, others_ref, right_ref, total_ref):
    inner = right_ref.shape[0]
    right = right_ref[...]
    total_ref[0] = dot(own_ref[:, :inner], right)
    for k in range(others_ref.shape[0]):
        total_ref[k + 1] = dot(others_ref[k, :, :inner], right)


def begin_second_kernel(lefts_ref, right_ref, total_ref):
    inner = right_ref.shape[0]
    right = right_ref[...]
    for k in range(lefts_ref.shape[0]):
        total_ref[k] = dot(lefts_ref[k, :, :inner], right)


def project(lefts, right, my_bit, my_modes, halved, begun_ref, keep_ref, send_ref, total_ref):
    for k, left in enumerate(lefts):
        total_ref[k] = begun_ref[k] + dot(left, right)
    groups, own_modes, _ = total_ref.shape
    parts, across_x, across_y, rows, width = keep_ref.shape

    def piece(index):
        start = index * rows
        group = lax.rem(start // own_modes + groups - my_modes, groups)
        begin = start % own_modes
        return total_ref[group, begin : begin + rows]

    for gx in range(across_x):
        for gy in range(across_y):
            if halved:
                base = gx * 2 * across_y + 2 * gy
                even, odd = piece(base), piece(base + 1)
            else:
                even, odd = piece(2 * gx * across_y + gy), piece((2 * gx + 1) * across_y + gy)
            keep = jnp.where(my_bit == 0, even, odd)
            send = jnp.where(my_bit == 0, odd, even).astype(send_ref.dtype)
            for p in range(parts):
                keep_ref[p, gx, gy] = keep[:, p * width : (p + 1) * width]
                send_ref[p, gx, gy] = send[:, p * width : (p + 1) * width]


def first_kernel(
    sites, where_ref, rows_ref, low_ref, high_ref, ahead_ref, back_ref, own_ref, others_ref, begun_ref,
    keep_ref, send_ref, right_ref, total_ref,
):
    planes, depth, _ = rows_ref.shape
    same = same_site(sites, depth)
    count = depth // sites
    past = low_ref[depth : depth + 8].astype(jnp.float32)
    above = rows_ref[place_of(1, planes)]
    set_right(right_ref, 0, move_plane(same, count, ahead_ref[0], past, above, low_ref[:depth]))
    x = planes - 1
    below = rows_ref[place_of(x - 1, planes)]
    moved = move_plane(same, count, ahead_ref[x], back_ref[x - 1], high_ref[...], below)
    set_right(right_ref, 1, moved)
    inner = (planes - 2) * depth
    lefts = [own_ref[:, inner:]] + [others_ref[k, :, inner:] for k in range(others_ref.shape[0])]
    my_bit, my_modes = where_ref[1], where_ref[2]
    project(lefts, right_ref[...], my_bit, my_modes, True, begun_ref, keep_ref, send_ref, total_ref)


def move_y_kernel(
    sites, zs, rows_ref, others_ref, near_ref, far_ref, ahead_ref, back_ref, turned_ref, field_ref
):
    planes, depth, width = rows_ref.shape
    groups = others_ref.shape[0] + 1
    row_size = depth // sites * zs
    reach = depth + near_ref.shape[1]
    head = back_ref.shape[2] - 128
    site, lane = iotas((sites, reach))
    inner = lane < depth
    upper = (lane >= depth) & (lane < depth + row_size)
    lower = (lane >= depth + row_size) & (lane < depth + 2 * row_size)
    lane_z = lane % zs
    to_next = (inner & (lane % sites == site + zs)) | (upper & (site == sites - zs + lane_z))
    to_last = (inner & (lane % sites == site - zs)) | (lower & (site == lane_z))
    to_next = jnp.where(to_next, -1.0, 0.0)
    to_last = jnp.where(to_last, -1.0, 0.0)
    _, lane = iotas((8, 128))
    for x in range(planes):
        past = near_ref[x, 2 * row_size : 2 * row_size + 8, :128].astype(jnp.float32)
        mixed = jnp.where(lane >= depth + row_size - head, past, back_ref[x, :, head:])
        back = jnp.concatenate([back_ref[x, :, :head], mixed], axis=1)[:, :reach]
        matrix = site_matrix([(ahead_ref[x, :, :reach], to_next), (back, to_last)], depth // sites)
        place = place_of(x, planes)
        column = jnp.concatenate([rows_ref[place], near_ref[x]], axis=0)
        field_ref[0, place] = dot(matrix, column).astype(jnp.bfloat16)
        for k in range(groups - 1):
            column = jnp.concatenate([others_ref[k, place], far_ref[k, x]], axis=0)
            field_ref[k + 1, place] = dot(matrix, column).astype(jnp.bfloat16)
    for k in range(groups):
        turned_ref[k] = field_ref[k].reshape(planes * depth, width).T


def second_kernel(where_ref, lefts_ref, right_ref, begun_ref, keep_ref, send_ref, total_ref):
    inner = lefts_ref.shape[2] - right_ref.shape[0]
    lefts = [lefts_ref[k, :, inner:] for k in range(lefts_ref.shape[0])]
    my_bit, my_modes = where_ref[0], where_ref[2]
    project(lefts, right_ref[...], my_bit, my_modes, False, begun_ref, keep_ref, send_ref, total_ref)


def swap(block, axis, bit):
    return lax.ppermute(block, axis, [(i, i ^ (1 << bit)) for i in range(lax.axis_size(axis))])


def halve(total, dim, axis, bit):
    shape = total.shape
    split = total.reshape(shape[:dim] + (shape[dim] // 2, 2) + shape[dim + 1 :])
    mine = (lax.axis_index(axis) >> bit) & 1
    keep = lax.dynamic_index_in_dim(split, mine, dim + 1, keepdims=False)
    send = lax.dynamic_index_in_dim(split, 1 - mine, dim + 1, keepdims=False).astype(jnp.bfloat16)
    return keep + swap(send, axis, bit).astype(jnp.float32)


def bits(axis):
    return range(lax.axis_size(axis).bit_length() - 1)


def local(eigen_modes, links_first, links_second):
    f32, bf16 = jnp.float32, jnp.bfloat16
    parts, planes, ys, zs, colours, width = eigen_modes.shape
    sites = ys * zs
    depth = parts * colours * sites
    row_size = parts * colours * zs
    edge = -(-(2 * row_size + 8) // 16) * 16
    lanes = -(-(depth + 2 * row_size) // 128) * 128
    across_x, across_y, groups = (lax.axis_size(a) for a in ("gx", "gy", "ma"))
    rows = groups * width // (across_x * across_y)
    inner_depth = (planes - 2) * depth
    raw = eigen_modes.transpose(0, 1, 2, 4, 3, 5)
    where = jnp.stack([lax.axis_index("gx") % 2, lax.axis_index("gy") % 2, lax.axis_index("ma")])
    where = where.astype(jnp.int32)

    def shape(*dims, dtype=bf16):
        return jax.ShapeDtypeStruct(dims, dtype)

    field_shape = shape(planes, depth, width)
    turned_shape = shape(width, planes * depth)
    total_shape = shape(groups, width, parts * width, dtype=f32)
    link_shape = shape(planes, 8, lanes, dtype=f32)
    total = pltpu.VMEM(total_shape.shape, f32)
    step_flops = 2 * planes * depth * depth * width
    project_flops = 2 * groups * width * planes * depth * parts * width

    raw_others = [shifted(raw, "ma", -step) for step in range(1, groups)]
    inputs = [raw, links_first.transpose(0, 1, 2, 3, 5, 4), links_second.transpose(0, 1, 2, 3, 5, 4)]
    inputs += [jnp.asarray(m) for m in lane_maps(parts, colours, planes, ys, zs, lanes)]
    field, first_plane, last_plane, ends, ahead_x, back_x, ahead_y, back_y = call(
        prepare_kernel,
        (
            field_shape, shape(depth, width), shape(depth + 16, width), shape(planes, edge, width),
            link_shape, link_shape, link_shape, link_shape,
        ),
        step_flops,
        inputs,
        [pltpu.VMEM(a.shape, a.dtype) for a in inputs] + [pltpu.SemaphoreType.DMA((len(inputs),))],
        pl.ANY,
    )
    high = shifted(first_plane, "gx", -1)
    low = shifted(last_plane, "gx", 1)
    near = shifted(ends, "gy", 1)
    if across_y != 2:
        ahead_row = lax.broadcasted_iota(jnp.int32, ends.shape, 1) < row_size
        near = jnp.where(ahead_row, shifted(ends, "gy", -1), near)
    far = jnp.stack([shifted(near, "ma", -step) for step in range(1, groups)])

    def inner(*refs):
        inner_kernel(sites, *refs)

    def first(*refs):
        first_kernel(sites, *refs)

    def move_y(*refs):
        move_y_kernel(sites, zs, *refs)

    right, own = call(
        inner, (shape(inner_depth, parts * width), turned_shape), 2 * step_flops, [field, ahead_x, back_x]
    )
    turned = [call(turn_kernel, (field_shape, turned_shape), step_flops // 4, [r]) for r in raw_others]
    fields = jnp.stack([t[0] for t in turned])
    others = jnp.stack([t[1] for t in turned])
    begun_first = call(begin_first_kernel, total_shape, project_flops, [own, others, right])
    keep_first, send_first, right_edge = call(
        first,
        (
            shape(parts, across_x, across_y // 2, rows, width, dtype=f32),
            shape(parts, across_x, across_y // 2, rows, width),
            shape(2 * depth, parts * width),
        ),
        project_flops,
        [where, field, low, high, ahead_x, back_x, own, others, begun_first],
        [total],
    )
    lefts = call(
        move_y, shape(groups, width, planes * depth), 2 * step_flops,
        [field, fields, near, far, ahead_y, back_y],
        [pltpu.VMEM((groups,) + field_shape.shape, bf16)],
    )
    begun_second = call(begin_second_kernel, total_shape, project_flops, [lefts, right])
    keep_second, send_second = call(
        second_kernel,
        (
            shape(parts, across_x // 2, across_y, rows, width, dtype=f32),
            shape(parts, across_x // 2, across_y, rows, width),
        ),
        project_flops,
        [where, lefts, right_edge, begun_second],
        [total],
    )
    first_sum = keep_first + swap(send_first, "gy", 0).astype(f32)
    second_sum = keep_second + swap(send_second, "gx", 0).astype(f32)
    for bit in list(bits("gy"))[1:]:
        first_sum = halve(first_sum, 2, "gy", bit)
    for bit in bits("gy"):
        second_sum = halve(second_sum, 2, "gy", bit)
    for bit in bits("gx"):
        first_sum = halve(first_sum, 1, "gx", bit)
    for bit in list(bits("gx"))[1:]:
        second_sum = halve(second_sum, 1, "gx", bit)
    return jnp.stack([first_sum[:, 0, 0], second_sum[:, 0, 0]])


def solution(mesh):
    return jax.shard_map(
        local,
        mesh=mesh,
        in_specs=(
            P("cuts", "gx", "gy", None, None, "ma"),
            P("cuts", None, None, "gx", "gy", None),
            P("cuts", None, None, "gx", "gy", None),
        ),
        out_specs=P("cuts", None, ("gx", "gy"), "ma"),
        check_vma=False,
    )
```

```python
import jax
import jax.numpy as jnp
import numpy as np
from jax import lax
from jax.experimental import pallas as pl
from jax.experimental.pallas import tpu as pltpu
from jax.sharding import PartitionSpec as P

VMEM_LIMIT = 16 * 1024 * 1024


def shifted(block, axis, distance):
    devices = range(lax.axis_size(axis))
    route = [((i - distance) % len(devices), i) for i in devices]
    return lax.ppermute(block, axis, route)


def call(body, out_shape, flops, operands, scratch=(), place=pltpu.VMEM):
    moved = sum(a.size * a.dtype.itemsize for a in operands)
    in_specs = [
        pl.BlockSpec(memory_space=pltpu.SMEM if a.dtype == jnp.int32 else place) for a in operands
    ]
    operands = [
        a if a.dtype == jnp.int32 else pltpu.with_memory_space_constraint(a, place) for a in operands
    ]
    return pl.pallas_call(
        body,
        out_shape=out_shape,
        in_specs=in_specs,
        scratch_shapes=scratch,
        cost_estimate=pl.CostEstimate(flops=flops, bytes_accessed=moved, transcendentals=0),
        compiler_params=pltpu.CompilerParams(vmem_limit_bytes=VMEM_LIMIT),
    )(*operands)


def dot(a, b):
    return jnp.dot(a, b, preferred_element_type=jnp.float32)


def iotas(shape):
    return (
        lax.broadcasted_iota(jnp.int32, shape, 0),
        lax.broadcasted_iota(jnp.int32, shape, 1),
    )


def place_of(x, planes):
    return planes - 2 if x == 0 else x if x == planes - 1 else x - 1


def lane_maps(parts, colours, planes, ys, zs, lanes):
    sites = ys * zs
    depth = parts * colours * sites
    row_size = parts * colours * zs
    lane = np.arange(lanes)
    inner = lane < depth
    past = (lane - depth) % row_size
    used = lane < depth + 2 * row_size
    part = np.where(inner, lane // (colours * sites), past // (colours * zs))
    colour = np.where(inner, lane // sites, past // zs) % colours
    z = np.where(inner, lane, past) % zs
    y = np.where(inner, lane % sites // zs, ys - 1)
    y_ahead = np.where(inner, lane % sites // zs, ys) - 1
    spread = y == np.arange(ys)[:, None]
    spread_ahead = y_ahead == np.arange(ys)[:, None]

    row = np.arange(parts * colours * colours * planes * zs)[:, None]
    row_z = row % zs
    row_x = row // zs % planes
    row_right = row // (zs * planes) % colours
    row_left = row // (zs * planes * colours) % colours
    row_part = row // (zs * planes * colours * colours)
    match_ahead = (row_z == z) & (row_right == colour) & used
    match_back = (row_z == z) & (row_left == colour) & used

    out = np.arange(parts * planes * 8)[:, None]
    field_part = out // (planes * 8)
    out_x = out // 8 % planes
    out_part = out % 8 // colours
    out_colour = out % 8 % colours
    source = (out_x == row_x.T) & (row_part.T == (out_part + field_part) % 2) & (out_part < parts)
    choose_ahead = source & (row_left.T == out_colour)
    choose_back = source & (row_right.T == out_colour)
    sign_ahead = np.where((field_part == 1) & (out_part == 0), -1.0, 1.0)
    sign_back = np.where((field_part == 0) & (out_part == 1), 1.0, -1.0)
    maps = (
        np.concatenate([spread, spread_ahead], axis=1), np.concatenate([match_ahead, match_back], axis=1),
        np.concatenate([choose_ahead * sign_ahead, choose_back * sign_back], axis=0),
        np.broadcast_to(part == 0, (8, lanes)),
    )
    return [m.astype(np.float32) for m in maps]


def coefficients(links_x, links_y, spread_ref, match_ref, choose_ref, first_part, planes):
    lanes = first_part.shape[1]
    wide = dot(jnp.concatenate([links_x, links_y], axis=0), spread_ref[...].astype(jnp.bfloat16))
    count = links_x.shape[0]
    match_ahead = match_ref[:, :lanes]
    match_back = match_ref[:, lanes:]
    ahead = jnp.concatenate([wide[:count, :lanes] * match_ahead, wide[count:, lanes:] * match_ahead], axis=1)
    back = jnp.concatenate([wide[:count, :lanes] * match_back, wide[count:, :lanes] * match_back], axis=1)
    half = choose_ref.shape[0] // 2
    out = []
    for chosen in (
        dot(choose_ref[:half].astype(jnp.bfloat16), ahead.astype(jnp.bfloat16)), dot(choose_ref[half:].astype(jnp.bfloat16), back.astype(jnp.bfloat16))
    ):
        for start in (0, lanes):
            part = chosen[:, start : start + lanes]
            rows = jnp.where(first_part, part[: half // 2], part[half // 2 :])
            out.append(rows.reshape(planes, 8, lanes))
    return out


def plane_rows(ref, x):
    parts, _, ys, colours, zs, width = ref.shape
    return jnp.concatenate(
        [ref[p, x, :, c].reshape(ys * zs, width) for p in range(parts) for c in range(colours)],
        axis=0,
    )


def site_matrix(rows_and_masks, count):
    blocks = []
    for q in range(count):
        block = None
        for rows, mask in rows_and_masks:
            term = rows[q : q + 1] * mask
            block = term if block is None else block + term
        blocks.append(block.astype(jnp.bfloat16))
    return jnp.concatenate(blocks, axis=0)


def prepare_kernel(
    raw_hbm, links_x_hbm, links_y_hbm, spread_hbm, match_hbm, choose_hbm, first_part_hbm,
    rows_ref, first_ref, last_ref, ends_ref, ahead_x_ref, back_x_ref, ahead_y_ref, back_y_ref,
    raw_ref, links_x_ref, links_y_ref, spread_ref, match_ref, choose_ref, first_part_ref, arrived,
):
    sources = (raw_hbm, links_x_hbm, links_y_hbm, spread_hbm, match_hbm, choose_hbm, first_part_hbm)
    targets = (raw_ref, links_x_ref, links_y_ref, spread_ref, match_ref, choose_ref, first_part_ref)
    copies = [
        pltpu.make_async_copy(source, target, arrived.at[i])
        for i, (source, target) in enumerate(zip(sources, targets))
    ]
    for copy in copies[1:] + copies[:1]:
        copy.start()
    for copy in copies[1:]:
        copy.wait()

    planes, depth, width = rows_ref.shape
    zs = raw_ref.shape[4]
    ys = raw_ref.shape[2]
    sites = ys * zs
    row_size = depth // sites * zs
    lanes = ahead_y_ref.shape[2]
    first_part = first_part_ref[:1] > 0.5
    ahead_x, ahead_y, back_x, back_y = coefficients(
        links_x_ref[...].reshape(-1, ys), links_y_ref[...].reshape(-1, ys),
        spread_ref, match_ref, choose_ref, first_part, planes,
    )
    ahead_x_ref[...] = ahead_x
    back_x_ref[...] = back_x
    ahead_y_ref[...] = ahead_y
    back_y_ref[...] = back_y

    row, lane = iotas((2 * row_size, depth))
    spot = row % row_size
    wanted = (spot // zs) * sites + spot % zs + jnp.where(row < row_size, 0, sites - zs)
    ends = (lane == wanted).astype(jnp.bfloat16)
    filler = jnp.zeros((8, width - 128), jnp.float32)
    spare = ends_ref.shape[1] - 2 * row_size - 8
    copies[0].wait()
    for x in range(planes):
        plane = plane_rows(raw_ref, x)
        rows_ref[place_of(x, planes)] = plane
        tail = jnp.concatenate([back_y[x, :, lanes - 128 :], filler], axis=1)
        pieces = [dot(ends, plane), tail]
        if spare:
            pieces.append(jnp.zeros((spare, width), jnp.float32))
        ends_ref[x] = jnp.concatenate(pieces, axis=0).astype(jnp.bfloat16)
        if x == 0:
            first_ref[...] = plane
        if x == planes - 1:
            last_ref[:depth] = plane
    end = back_x[planes - 1, :, :width]
    last_ref[depth:] = jnp.concatenate([end, end], axis=0).astype(jnp.bfloat16)


def turn_kernel(raw_ref, rows_ref, turned_ref):
    planes, depth, width = rows_ref.shape
    for x in range(planes):
        rows_ref[place_of(x, planes)] = plane_rows(raw_ref, x)
    turned_ref[...] = rows_ref[...].reshape(planes * depth, width).T


def move_plane(same, count, ahead, back, above, below):
    depth = same.shape[1]
    moved = dot(site_matrix([(ahead[:, :depth], same)], count), above)
    return (moved + dot(site_matrix([(back[:, :depth], same)], count), below)).astype(jnp.bfloat16)


def same_site(sites, depth):
    site, lane = iotas((sites, depth))
    return (lane % sites == site).astype(jnp.float32)


def set_right(right_ref, place, moved):
    depth, width = moved.shape
    half = depth // 2
    start = place * depth
    real, imag = moved[:half], moved[half:]
    right_ref[start : start + half, :width] = real
    right_ref[start : start + half, width:] = imag
    right_ref[start + half : start + depth, :width] = imag
    right_ref[start + half : start + depth, width:] = -real


def inner_kernel(sites, rows_ref, ahead_ref, back_ref, right_ref, turned_ref):
    planes, depth, width = rows_ref.shape
    same = same_site(sites, depth)
    for x in range(1, planes - 1):
        above = rows_ref[place_of(x + 1, planes)]
        below = rows_ref[place_of(x - 1, planes)]
        moved = move_plane(same, depth // sites, ahead_ref[x], back_ref[x - 1], above, below)
        set_right(right_ref, place_of(x, planes), moved)
    turned_ref[...] = rows_ref[...].reshape(planes * depth, width).T


def begin_first_kernel(own_ref, others_ref, right_ref, total_ref):
    inner = right_ref.shape[0]
    right = right_ref[...]
    total_ref[0] = dot(own_ref[:, :inner], right)
    for k in range(others_ref.shape[0]):
        total_ref[k + 1] = dot(others_ref[k, :, :inner], right)


def begin_second_kernel(lefts_ref, right_ref, total_ref):
    inner = right_ref.shape[0]
    right = right_ref[...]
    for k in range(lefts_ref.shape[0]):
        total_ref[k] = dot(lefts_ref[k, :, :inner], right)


def project(lefts, right, my_bit, my_modes, halved, begun_ref, keep_ref, send_ref, total_ref):
    for k, left in enumerate(lefts):
        total_ref[k] = begun_ref[k] + dot(left, right)
    groups, own_modes, _ = total_ref.shape
    parts, across_x, across_y, rows, width = keep_ref.shape

    def piece(index):
        start = index * rows
        group = lax.rem(start // own_modes + groups - my_modes, groups)
        begin = start % own_modes
        return total_ref[group, begin : begin + rows]

    for gx in range(across_x):
        for gy in range(across_y):
            if halved:
                base = gx * 2 * across_y + 2 * gy
                even, odd = piece(base), piece(base + 1)
            else:
                even, odd = piece(2 * gx * across_y + gy), piece((2 * gx + 1) * across_y + gy)
            keep = jnp.where(my_bit == 0, even, odd)
            send = jnp.where(my_bit == 0, odd, even).astype(send_ref.dtype)
            for p in range(parts):
                keep_ref[p, gx, gy] = keep[:, p * width : (p + 1) * width]
                send_ref[p, gx, gy] = send[:, p * width : (p + 1) * width]


def first_kernel(
    sites, where_ref, rows_ref, low_ref, high_ref, ahead_ref, back_ref, own_ref, others_ref, begun_ref,
    keep_ref, send_ref, right_ref, total_ref,
):
    planes, depth, _ = rows_ref.shape
    same = same_site(sites, depth)
    count = depth // sites
    past = low_ref[depth : depth + 8].astype(jnp.float32)
    above = rows_ref[place_of(1, planes)]
    set_right(right_ref, 0, move_plane(same, count, ahead_ref[0], past, above, low_ref[:depth]))
    x = planes - 1
    below = rows_ref[place_of(x - 1, planes)]
    moved = move_plane(same, count, ahead_ref[x], back_ref[x - 1], high_ref[...], below)
    set_right(right_ref, 1, moved)
    inner = (planes - 2) * depth
    lefts = [own_ref[:, inner:]] + [others_ref[k, :, inner:] for k in range(others_ref.shape[0])]
    my_bit, my_modes = where_ref[1], where_ref[2]
    project(lefts, right_ref[...], my_bit, my_modes, True, begun_ref, keep_ref, send_ref, total_ref)


def move_y_kernel(
    sites, zs, rows_ref, others_ref, near_ref, far_ref, ahead_ref, back_ref, turned_ref, field_ref
):
    planes, depth, width = rows_ref.shape
    groups = others_ref.shape[0] + 1
    row_size = depth // sites * zs
    reach = depth + near_ref.shape[1]
    head = back_ref.shape[2] - 128
    site, lane = iotas((sites, reach))
    inner = lane < depth
    upper = (lane >= depth) & (lane < depth + row_size)
    lower = (lane >= depth + row_size) & (lane < depth + 2 * row_size)
    lane_z = lane % zs
    to_next = (inner & (lane % sites == site + zs)) | (upper & (site == sites - zs + lane_z))
    to_last = (inner & (lane % sites == site - zs)) | (lower & (site == lane_z))
    to_next = jnp.where(to_next, -1.0, 0.0)
    to_last = jnp.where(to_last, -1.0, 0.0)
    _, lane = iotas((8, 128))
    for x in range(planes):
        past = near_ref[x, 2 * row_size : 2 * row_size + 8, :128].astype(jnp.float32)
        mixed = jnp.where(lane >= depth + row_size - head, past, back_ref[x, :, head:])
        back = jnp.concatenate([back_ref[x, :, :head], mixed], axis=1)[:, :reach]
        matrix = site_matrix([(ahead_ref[x, :, :reach], to_next), (back, to_last)], depth // sites)
        place = place_of(x, planes)
        column = jnp.concatenate([rows_ref[place], near_ref[x]], axis=0)
        field_ref[0, place] = dot(matrix, column).astype(jnp.bfloat16)
        for k in range(groups - 1):
            column = jnp.concatenate([others_ref[k, place], far_ref[k, x]], axis=0)
            field_ref[k + 1, place] = dot(matrix, column).astype(jnp.bfloat16)
    for k in range(groups):
        turned_ref[k] = field_ref[k].reshape(planes * depth, width).T


def second_kernel(where_ref, lefts_ref, right_ref, begun_ref, keep_ref, send_ref, total_ref):
    inner = lefts_ref.shape[2] - right_ref.shape[0]
    lefts = [lefts_ref[k, :, inner:] for k in range(lefts_ref.shape[0])]
    my_bit, my_modes = where_ref[0], where_ref[2]
    project(lefts, right_ref[...], my_bit, my_modes, False, begun_ref, keep_ref, send_ref, total_ref)


def swap(block, axis, bit):
    return lax.ppermute(block, axis, [(i, i ^ (1 << bit)) for i in range(lax.axis_size(axis))])


def halve(total, dim, axis, bit):
    shape = total.shape
    split = total.reshape(shape[:dim] + (shape[dim] // 2, 2) + shape[dim + 1 :])
    mine = (lax.axis_index(axis) >> bit) & 1
    keep = lax.dynamic_index_in_dim(split, mine, dim + 1, keepdims=False)
    send = lax.dynamic_index_in_dim(split, 1 - mine, dim + 1, keepdims=False).astype(jnp.bfloat16)
    return keep + swap(send, axis, bit).astype(jnp.float32)


def bits(axis):
    return range(lax.axis_size(axis).bit_length() - 1)


def local(eigen_modes, links_first, links_second):
    f32, bf16 = jnp.float32, jnp.bfloat16
    parts, planes, ys, zs, colours, width = eigen_modes.shape
    sites = ys * zs
    depth = parts * colours * sites
    row_size = parts * colours * zs
    edge = -(-(2 * row_size + 8) // 16) * 16
    lanes = -(-(depth + 2 * row_size) // 128) * 128
    across_x, across_y, groups = (lax.axis_size(a) for a in ("gx", "gy", "ma"))
    rows = groups * width // (across_x * across_y)
    inner_depth = (planes - 2) * depth
    raw = eigen_modes.transpose(0, 1, 2, 4, 3, 5)
    where = jnp.stack([lax.axis_index("gx") % 2, lax.axis_index("gy") % 2, lax.axis_index("ma")])
    where = where.astype(jnp.int32)

    def shape(*dims, dtype=bf16):
        return pltpu.VMEM(dims, dtype)

    field_shape = shape(planes, depth, width)
    turned_shape = shape(width, planes * depth)
    total_shape = shape(groups, width, parts * width, dtype=f32)
    link_shape = shape(planes, 8, lanes, dtype=f32)
    total = pltpu.VMEM(total_shape.shape, f32)
    step_flops = 2 * planes * depth * depth * width
    project_flops = 2 * groups * width * planes * depth * parts * width

    raw_others = [shifted(raw, "ma", -step) for step in range(1, groups)]
    inputs = [raw, links_first.transpose(0, 1, 2, 3, 5, 4), links_second.transpose(0, 1, 2, 3, 5, 4)]
    inputs += [jnp.asarray(m) for m in lane_maps(parts, colours, planes, ys, zs, lanes)]
    field, first_plane, last_plane, ends, ahead_x, back_x, ahead_y, back_y = call(
        prepare_kernel,
        (
            field_shape, shape(depth, width), shape(depth + 16, width), shape(planes, edge, width),
            link_shape, link_shape, link_shape, link_shape,
        ),
        step_flops,
        inputs,
        [pltpu.VMEM(a.shape, a.dtype) for a in inputs] + [pltpu.SemaphoreType.DMA((len(inputs),))],
        pltpu.HBM,
    )
    high = shifted(first_plane, "gx", -1)
    low = shifted(last_plane, "gx", 1)
    near = shifted(ends, "gy", 1)
    if across_y != 2:
        ahead_row = lax.broadcasted_iota(jnp.int32, ends.shape, 1) < row_size
        near = jnp.where(ahead_row, shifted(ends, "gy", -1), near)

    def inner(*refs):
        inner_kernel(sites, *refs)

    def first(*refs):
        first_kernel(sites, *refs)

    def move_y(*refs):
        move_y_kernel(sites, zs, *refs)

    right, own = call(
        inner, (shape(inner_depth, parts * width), turned_shape), 2 * step_flops, [field, ahead_x, back_x]
    )
    turned = [call(turn_kernel, (field_shape, turned_shape), step_flops // 4, [r]) for r in raw_others]
    fields = jnp.stack([t[0] for t in turned])
    others = jnp.stack([t[1] for t in turned])
    begun_first = call(begin_first_kernel, total_shape, project_flops, [own, others, right])
    near, begun_first = lax.optimization_barrier((near, begun_first))
    far = jnp.stack([shifted(near, "ma", -step) for step in range(1, groups)])
    keep_first, send_first, right_edge = call(
        first,
        (
            shape(parts, across_x, across_y // 2, rows, width, dtype=f32),
            shape(parts, across_x, across_y // 2, rows, width),
            shape(2 * depth, parts * width),
        ),
        project_flops,
        [where, field, low, high, ahead_x, back_x, own, others, begun_first],
        [total],
    )
    lefts = call(
        move_y, shape(groups, width, planes * depth), 2 * step_flops,
        [field, fields, near, far, ahead_y, back_y],
        [pltpu.VMEM((groups,) + field_shape.shape, bf16)],
    )
    begun_second = call(begin_second_kernel, total_shape, project_flops, [lefts, right])
    keep_second, send_second = call(
        second_kernel,
        (
            shape(parts, across_x // 2, across_y, rows, width, dtype=f32),
            shape(parts, across_x // 2, across_y, rows, width),
        ),
        project_flops,
        [where, lefts, right_edge, begun_second],
        [total],
    )
    first_sum = keep_first + swap(send_first, "gy", 0).astype(f32)
    second_sum = keep_second + swap(send_second, "gx", 0).astype(f32)
    for bit in list(bits("gy"))[1:]:
        first_sum = halve(first_sum, 2, "gy", bit)
    for bit in bits("gy"):
        second_sum = halve(second_sum, 2, "gy", bit)
    for bit in bits("gx"):
        first_sum = halve(first_sum, 1, "gx", bit)
    for bit in list(bits("gx"))[1:]:
        second_sum = halve(second_sum, 1, "gx", bit)
    return jnp.stack([first_sum[:, 0, 0], second_sum[:, 0, 0]])


def solution(mesh):
    return jax.shard_map(
        local,
        mesh=mesh,
        in_specs=(
            P("cuts", "gx", "gy", None, None, "ma"),
            P("cuts", None, None, "gx", "gy", None),
            P("cuts", None, None, "gx", "gy", None),
        ),
        out_specs=P("cuts", None, ("gx", "gy"), "ma"),
        check_vma=False,
    )
```

```python
import jax
import jax.numpy as jnp
import numpy as np
from jax import lax
from jax.experimental import pallas as pl
from jax.experimental.pallas import tpu as pltpu
from jax.sharding import PartitionSpec as P

VMEM_LIMIT = 16 * 1024 * 1024


def shifted(block, axis, distance):
    devices = range(lax.axis_size(axis))
    route = [((i - distance) % len(devices), i) for i in devices]
    return lax.ppermute(block, axis, route)


def call(body, out_shape, flops, operands, scratch=(), places=None):
    places = places or [pltpu.VMEM] * len(operands)
    places = [pltpu.SMEM if a.dtype == jnp.int32 else place for a, place in zip(operands, places)]
    return pl.pallas_call(
        body,
        out_shape=out_shape,
        in_specs=[pl.BlockSpec(memory_space=place) for place in places],
        scratch_shapes=scratch,
        cost_estimate=pl.CostEstimate(flops=4 * flops, bytes_accessed=0, transcendentals=0),
        compiler_params=pltpu.CompilerParams(vmem_limit_bytes=VMEM_LIMIT),
    )(
        *(
            a if place is pltpu.SMEM else pltpu.with_memory_space_constraint(a, place)
            for a, place in zip(operands, places)
        )
    )


def dot(a, b):
    return jnp.dot(a, b, preferred_element_type=jnp.float32)


def iotas(shape):
    return (
        lax.broadcasted_iota(jnp.int32, shape, 0),
        lax.broadcasted_iota(jnp.int32, shape, 1),
    )


def place_of(x, planes):
    return planes - 2 if x == 0 else x if x == planes - 1 else x - 1


def lane_maps(parts, colours, planes, ys, zs, lanes):
    sites = ys * zs
    depth = parts * colours * sites
    row_size = parts * colours * zs
    lane = np.arange(lanes)
    inner = lane < depth
    past = (lane - depth) % row_size
    used = lane < depth + 2 * row_size
    part = np.where(inner, lane // (colours * sites), past // (colours * zs))
    colour = np.where(inner, lane // sites, past // zs) % colours
    z = np.where(inner, lane, past) % zs
    y = np.where(inner, lane % sites // zs, ys - 1)
    y_ahead = np.where(inner, lane % sites // zs, ys) - 1
    spread = y == np.arange(ys)[:, None]
    spread_ahead = y_ahead == np.arange(ys)[:, None]

    row = np.arange(parts * colours * colours * planes * zs)[:, None]
    row_z = row % zs
    row_x = row // zs % planes
    row_right = row // (zs * planes) % colours
    row_left = row // (zs * planes * colours) % colours
    row_part = row // (zs * planes * colours * colours)
    match_ahead = (row_z == z) & (row_right == colour) & used
    match_back = (row_z == z) & (row_left == colour) & used

    out = np.arange(parts * planes * 8)[:, None]
    field_part = out // (planes * 8)
    out_x = out // 8 % planes
    out_part = out % 8 // colours
    out_colour = out % 8 % colours
    source = (out_x == row_x.T) & (row_part.T == (out_part + field_part) % 2) & (out_part < parts)
    choose_ahead = source & (row_left.T == out_colour)
    choose_back = source & (row_right.T == out_colour)
    sign_ahead = np.where((field_part == 1) & (out_part == 0), -1.0, 1.0)
    sign_back = np.where((field_part == 0) & (out_part == 1), 1.0, -1.0)
    maps = (
        np.concatenate([spread, spread_ahead], axis=1), np.concatenate([match_ahead, match_back], axis=1),
        np.concatenate([choose_ahead * sign_ahead, choose_back * sign_back], axis=0),
        np.broadcast_to(part == 0, (8, lanes)),
    )
    return [m.astype(np.float32) for m in maps]


def coefficients(links_x, links_y, spread_ref, match_ref, choose_ref, first_part, planes):
    lanes = first_part.shape[1]
    wide = dot(jnp.concatenate([links_x, links_y], axis=0), spread_ref[...].astype(jnp.bfloat16))
    count = links_x.shape[0]
    match_ahead = match_ref[:, :lanes]
    match_back = match_ref[:, lanes:]
    ahead = jnp.concatenate([wide[:count, :lanes] * match_ahead, wide[count:, lanes:] * match_ahead], axis=1)
    back = jnp.concatenate([wide[:count, :lanes] * match_back, wide[count:, :lanes] * match_back], axis=1)
    half = choose_ref.shape[0] // 2
    out = []
    for chosen in (
        dot(choose_ref[:half].astype(jnp.bfloat16), ahead.astype(jnp.bfloat16)), dot(choose_ref[half:].astype(jnp.bfloat16), back.astype(jnp.bfloat16))
    ):
        for start in (0, lanes):
            part = chosen[:, start : start + lanes]
            rows = jnp.where(first_part, part[: half // 2], part[half // 2 :])
            out.append(rows.reshape(planes, 8, lanes))
    return out


def plane_rows(ref, ys):
    parts, _, colours, zs, width = ref.shape
    return jnp.concatenate(
        [ref[p, :ys, c].reshape(ys * zs, width) for p in range(parts) for c in range(colours)],
        axis=0,
    )


def edges_kernel(where_ref, raw_hbm, links_hbm, first_ref, last_ref, order_ref, links_ref, arrived):
    parts, planes, ys, colours, zs, _ = raw_hbm.shape
    copies = [
        pltpu.make_async_copy(raw_hbm.at[:, planes - 1], last_ref.at[:, :ys], arrived.at[0]),
        pltpu.make_async_copy(raw_hbm.at[:, 0], first_ref, arrived.at[1]),
        pltpu.make_async_copy(links_hbm.at[:, :, :, planes - 1], links_ref, arrived.at[2]),
    ]
    for copy in copies:
        copy.start()
    order_ref[...] = jnp.zeros_like(order_ref)
    last_ref[:, ys:] = jnp.zeros((parts, colours) + last_ref.shape[2:], last_ref.dtype)
    copies[2].wait()
    last_ref[:, ys:, :, :, :ys] = links_ref[...]
    copies[0].wait()
    copies[1].wait()


def site_matrix(rows_and_masks, count):
    blocks = []
    for q in range(count):
        block = None
        for rows, mask in rows_and_masks:
            term = rows[q : q + 1] * mask
            block = term if block is None else block + term
        blocks.append(block.astype(jnp.bfloat16))
    return jnp.concatenate(blocks, axis=0)


def prepare_kernel(
    order_ref, raw_hbm, links_x_hbm, links_y_hbm, spread_hbm, match_hbm, choose_hbm, first_part_hbm, match_past_hbm, choose_past_hbm,
    rows_ref, ends_ref, ahead_x_ref, back_x_ref, ahead_y_ref, back_y_ref, past_maps_ref,
    raw_ref, links_x_ref, links_y_ref, spread_ref, match_ref, choose_ref, first_part_ref, match_past_ref, choose_past_ref,
    arrived,
):
    sources = (
        raw_hbm, links_x_hbm, links_y_hbm, spread_hbm, match_hbm, choose_hbm, first_part_hbm, match_past_hbm, choose_past_hbm
    )
    targets = (
        raw_ref, links_x_ref, links_y_ref, spread_ref, match_ref, choose_ref, first_part_ref, match_past_ref, choose_past_ref
    )
    copies = [
        pltpu.make_async_copy(source, target, arrived.at[i])
        for i, (source, target) in enumerate(zip(sources, targets))
    ]
    for copy in copies[1:] + copies[:1]:
        copy.start()
    for copy in copies[1:]:
        copy.wait()

    planes, depth, width = rows_ref.shape
    zs = raw_ref.shape[4]
    ys = raw_ref.shape[2]
    sites = ys * zs
    row_size = depth // sites * zs
    lanes = ahead_y_ref.shape[2]
    first_part = first_part_ref[:1] > 0.5
    ahead_x, ahead_y, back_x, back_y = coefficients(
        links_x_ref[...].reshape(-1, ys), links_y_ref[...].reshape(-1, ys),
        spread_ref, match_ref, choose_ref, first_part, planes,
    )
    ahead_x_ref[...] = ahead_x
    back_x_ref[...] = back_x
    ahead_y_ref[...] = ahead_y
    back_y_ref[...] = back_y

    row, lane = iotas((2 * row_size, depth))
    spot = row % row_size
    wanted = (spot // zs) * sites + spot % zs + jnp.where(row < row_size, 0, sites - zs)
    ends = (lane == wanted).astype(jnp.bfloat16)
    filler = jnp.zeros((8, width - 128), jnp.float32)
    spare = ends_ref.shape[1] - 2 * row_size - 8
    copies[0].wait()
    for x in range(planes):
        plane = plane_rows(raw_ref.at[:, x], ys)
        rows_ref[place_of(x, planes)] = plane
        tail = jnp.concatenate([back_y[x, :, lanes - 128 :], filler], axis=1)
        pieces = [dot(ends, plane), tail]
        if spare:
            pieces.append(jnp.zeros((spare, width), jnp.float32))
        ends_ref[x] = jnp.concatenate(pieces, axis=0).astype(jnp.bfloat16)
    lanes_past = past_maps_ref.shape[1]
    count, rows_past = match_past_ref.shape[0], choose_past_ref.shape[0]
    past_maps_ref[:ys] = spread_ref[:, :lanes_past]
    past_maps_ref[ys : ys + count] = match_past_ref[:, lanes_past:]
    past_maps_ref[ys + count :, : choose_past_ref.shape[1]] = choose_past_ref[rows_past // 2 :]


def turn_kernel(raw_ref, rows_ref, turned_ref):
    planes, depth, width = rows_ref.shape
    for x in range(planes):
        rows_ref[place_of(x, planes)] = plane_rows(raw_ref.at[:, x], raw_ref.shape[2])
    turned_ref[...] = rows_ref[...].reshape(planes * depth, width).T


def move_plane(same, count, ahead, back, above, below):
    depth = same.shape[1]
    moved = dot(site_matrix([(ahead[:, :depth], same)], count), above)
    return (moved + dot(site_matrix([(back[:, :depth], same)], count), below)).astype(jnp.bfloat16)


def same_site(sites, depth):
    site, lane = iotas((sites, depth))
    return (lane % sites == site).astype(jnp.float32)


def set_right(right_ref, place, moved):
    depth, width = moved.shape
    half = depth // 2
    start = place * depth
    real, imag = moved[:half], moved[half:]
    right_ref[start : start + half, :width] = real
    right_ref[start : start + half, width:] = imag
    right_ref[start + half : start + depth, :width] = imag
    right_ref[start + half : start + depth, width:] = -real


def inner_kernel(sites, rows_ref, ahead_ref, back_ref, right_ref, turned_ref):
    planes, depth, width = rows_ref.shape
    same = same_site(sites, depth)
    for x in range(1, planes - 1):
        above = rows_ref[place_of(x + 1, planes)]
        below = rows_ref[place_of(x - 1, planes)]
        moved = move_plane(same, depth // sites, ahead_ref[x], back_ref[x - 1], above, below)
        set_right(right_ref, place_of(x, planes), moved)
    turned_ref[...] = rows_ref[...].reshape(planes * depth, width).T


def begin_first_kernel(own_ref, others_ref, right_ref, total_ref):
    inner = right_ref.shape[0]
    right = right_ref[...]
    total_ref[0] = dot(own_ref[:, :inner], right)
    for k in range(others_ref.shape[0]):
        total_ref[k + 1] = dot(others_ref[k, :, :inner], right)


def begin_second_kernel(lefts_ref, right_ref, total_ref):
    inner = right_ref.shape[0]
    right = right_ref[...]
    for k in range(lefts_ref.shape[0]):
        total_ref[k] = dot(lefts_ref[k, :, :inner], right)


def project(lefts, right, my_bit, my_modes, halved, begun_ref, keep_ref, send_ref, total_ref):
    for k, left in enumerate(lefts):
        total_ref[k] = begun_ref[k] + dot(left, right)
    groups, own_modes, _ = total_ref.shape
    parts, across_x, across_y, rows, width = keep_ref.shape

    def piece(index):
        start = index * rows
        group = lax.rem(start // own_modes + groups - my_modes, groups)
        begin = start % own_modes
        return total_ref[group, begin : begin + rows]

    for gx in range(across_x):
        for gy in range(across_y):
            if halved:
                base = gx * 2 * across_y + 2 * gy
                even, odd = piece(base), piece(base + 1)
            else:
                even, odd = piece(2 * gx * across_y + gy), piece((2 * gx + 1) * across_y + gy)
            keep = jnp.where(my_bit == 0, even, odd)
            send = jnp.where(my_bit == 0, odd, even).astype(send_ref.dtype)
            for p in range(parts):
                keep_ref[p, gx, gy] = keep[:, p * width : (p + 1) * width]
                send_ref[p, gx, gy] = send[:, p * width : (p + 1) * width]


def first_kernel(
    sites, where_ref, rows_ref, low_ref, high_ref, ahead_ref, back_ref, past_maps_ref, own_ref, others_ref, begun_ref,
    keep_ref, send_ref, right_ref, total_ref,
):
    planes, depth, _ = rows_ref.shape
    same = same_site(sites, depth)
    count = depth // sites
    _, ys, colours, zs, _ = high_ref.shape
    links = low_ref[:, ys:, :, :, :ys].reshape(-1, ys)
    lanes = past_maps_ref.shape[1]
    spread = dot(links, past_maps_ref[:ys].astype(jnp.bfloat16)) * past_maps_ref[ys : ys + links.shape[0]]
    choose = past_maps_ref[ys + links.shape[0] :, : links.shape[0]]
    past = dot(choose.astype(jnp.bfloat16), spread.astype(jnp.bfloat16))
    _, lane = iotas((8, lanes))
    past = jnp.where(lane < depth // 2, past[:8], past[8:])
    above = rows_ref[place_of(1, planes)]
    set_right(right_ref, 0, move_plane(same, count, ahead_ref[0], past, above, plane_rows(low_ref, ys)))
    x = planes - 1
    below = rows_ref[place_of(x - 1, planes)]
    moved = move_plane(same, count, ahead_ref[x], back_ref[x - 1], plane_rows(high_ref, ys), below)
    set_right(right_ref, 1, moved)
    inner = (planes - 2) * depth
    lefts = [own_ref[:, inner:]] + [others_ref[k, :, inner:] for k in range(others_ref.shape[0])]
    my_bit, my_modes = lax.bitwise_and(where_ref[1], 1), where_ref[2]
    project(lefts, right_ref[...], my_bit, my_modes, True, begun_ref, keep_ref, send_ref, total_ref)


def move_y_kernel(
    sites, zs, rows_ref, others_ref, near_ref, far_ref, ahead_ref, back_ref, turned_ref, field_ref
):
    planes, depth, width = rows_ref.shape
    groups = others_ref.shape[0] + 1
    row_size = depth // sites * zs
    reach = depth + near_ref.shape[1]
    head = back_ref.shape[2] - 128
    site, lane = iotas((sites, reach))
    inner = lane < depth
    upper = (lane >= depth) & (lane < depth + row_size)
    lower = (lane >= depth + row_size) & (lane < depth + 2 * row_size)
    lane_z = lane % zs
    to_next = (inner & (lane % sites == site + zs)) | (upper & (site == sites - zs + lane_z))
    to_last = (inner & (lane % sites == site - zs)) | (lower & (site == lane_z))
    to_next = jnp.where(to_next, -1.0, 0.0)
    to_last = jnp.where(to_last, -1.0, 0.0)
    _, lane = iotas((8, 128))
    for x in range(planes):
        past = near_ref[x, 2 * row_size : 2 * row_size + 8, :128].astype(jnp.float32)
        mixed = jnp.where(lane >= depth + row_size - head, past, back_ref[x, :, head:])
        back = jnp.concatenate([back_ref[x, :, :head], mixed], axis=1)[:, :reach]
        matrix = site_matrix([(ahead_ref[x, :, :reach], to_next), (back, to_last)], depth // sites)
        place = place_of(x, planes)
        column = jnp.concatenate([rows_ref[place], near_ref[x]], axis=0)
        field_ref[0, place] = dot(matrix, column).astype(jnp.bfloat16)
        for k in range(groups - 1):
            column = jnp.concatenate([others_ref[k, place], far_ref[k, x]], axis=0)
            field_ref[k + 1, place] = dot(matrix, column).astype(jnp.bfloat16)
    for k in range(groups):
        turned_ref[k] = field_ref[k].reshape(planes * depth, width).T


def second_kernel(where_ref, lefts_ref, right_ref, begun_ref, keep_ref, send_ref, total_ref):
    inner = lefts_ref.shape[2] - right_ref.shape[0]
    lefts = [lefts_ref[k, :, inner:] for k in range(lefts_ref.shape[0])]
    my_bit, my_modes = lax.bitwise_and(where_ref[0], 1), where_ref[2]
    project(lefts, right_ref[...], my_bit, my_modes, False, begun_ref, keep_ref, send_ref, total_ref)


def swap(block, axis, bit):
    return lax.ppermute(block, axis, [(i, i ^ (1 << bit)) for i in range(lax.axis_size(axis))])


def merge_kernel(dim, bit, where_ref, kept_ref, came_ref, keep_ref, send_ref):
    mine = lax.bitwise_and(lax.shift_right_logical(where_ref[dim - 1], bit), 1)
    for gx in range(keep_ref.shape[1]):
        for gy in range(keep_ref.shape[2]):
            pair = []
            for odd in range(2):
                at = (slice(None), 2 * gx + odd, gy) if dim == 1 else (slice(None), gx, 2 * gy + odd)
                pair.append(kept_ref[at] + came_ref[at].astype(jnp.float32))
            keep_ref[:, gx, gy] = jnp.where(mine == 0, pair[0], pair[1])
            send_ref[:, gx, gy] = jnp.where(mine == 0, pair[1], pair[0]).astype(send_ref.dtype)


def halve(where, kept, came, axis, bit):
    dim = ("gx", "gy").index(axis) + 1
    dims = kept.shape[:dim] + (kept.shape[dim] // 2,) + kept.shape[dim + 1 :]

    def merge(*refs):
        merge_kernel(dim, bit, *refs)

    keep, send = call(
        merge, (pltpu.VMEM(dims, jnp.float32), pltpu.VMEM(dims, jnp.bfloat16)), kept.size, [where, kept, came]
    )
    return keep, swap(send, axis, bit)


def finish_kernel(*refs):
    out_ref = refs[-1]
    for d in range(out_ref.shape[0]):
        kept_ref, came_ref = refs[2 * d : 2 * d + 2]
        out_ref[d] = kept_ref[:, 0, 0] + came_ref[:, 0, 0].astype(jnp.float32)


def bits(axis):
    return range(lax.axis_size(axis).bit_length() - 1)


def local(eigen_modes, links_first, links_second):
    f32, bf16 = jnp.float32, jnp.bfloat16
    parts, planes, ys, zs, colours, width = eigen_modes.shape
    sites = ys * zs
    depth = parts * colours * sites
    row_size = parts * colours * zs
    edge = -(-(2 * row_size + 8) // 16) * 16
    lanes = -(-(depth + 2 * row_size) // 128) * 128
    across_x, across_y, groups = (lax.axis_size(a) for a in ("gx", "gy", "ma"))
    rows = groups * width // (across_x * across_y)
    inner_depth = (planes - 2) * depth
    raw = eigen_modes.transpose(0, 1, 2, 4, 3, 5)
    where = jnp.stack([lax.axis_index(a) for a in ("gx", "gy", "ma")]).astype(jnp.int32)

    def shape(*dims, dtype=bf16):
        return pltpu.VMEM(dims, dtype)

    field_shape = shape(planes, depth, width)
    turned_shape = shape(width, planes * depth)
    total_shape = shape(groups, width, parts * width, dtype=f32)
    link_shape = shape(planes, 8, lanes, dtype=f32)
    total = pltpu.VMEM(total_shape.shape, f32)
    step_flops = 2 * planes * depth * depth * width
    project_flops = 2 * groups * width * planes * depth * parts * width

    raw_others = [shifted(raw, "ma", -step) for step in range(1, groups)]
    raw_links_x, raw_links_y = (a.transpose(0, 1, 2, 3, 5, 4) for a in (links_first, links_second))
    first_plane, last_plane, order = call(
        edges_kernel,
        (
            shape(parts, ys, colours, zs, width), shape(parts, ys + colours, colours, zs, width),
            shape(8, 128, dtype=f32),
        ),
        0,
        [where, raw, raw_links_x],
        [pltpu.VMEM((parts, colours, colours, zs, ys), bf16), pltpu.SemaphoreType.DMA((3,))],
        [pltpu.SMEM, pltpu.HBM, pltpu.HBM],
    )
    high = shifted(first_plane, "gx", -1)
    low = shifted(last_plane, "gx", 1)
    maps = lane_maps(parts, colours, planes, ys, zs, lanes)
    past_maps = lane_maps(parts, colours, 1, ys, zs, lanes)
    inputs = [raw, raw_links_x, raw_links_y] + [jnp.asarray(m) for m in maps + past_maps[1:3]]
    past_rows = ys + past_maps[1].shape[0] + past_maps[2].shape[0] // 2
    field, ends, ahead_x, back_x, ahead_y, back_y, past_x = call(
        prepare_kernel,
        (
            field_shape, shape(planes, edge, width), link_shape, link_shape, link_shape, link_shape,
            shape(past_rows, lanes, dtype=f32),
        ),
        step_flops,
        [order] + inputs,
        [pltpu.VMEM(a.shape, a.dtype) for a in inputs] + [pltpu.SemaphoreType.DMA((len(inputs),))],
        [pltpu.VMEM] + [pltpu.HBM] * len(inputs),
    )
    near = shifted(ends, "gy", 1)
    if across_y != 2:
        ahead_row = lax.broadcasted_iota(jnp.int32, ends.shape, 1) < row_size
        near = jnp.where(ahead_row, shifted(ends, "gy", -1), near)

    def inner(*refs):
        inner_kernel(sites, *refs)

    def first(*refs):
        first_kernel(sites, *refs)

    def move_y(*refs):
        move_y_kernel(sites, zs, *refs)

    right, own = call(
        inner, (shape(inner_depth, parts * width), turned_shape), 2 * step_flops, [field, ahead_x, back_x]
    )
    turned = [call(turn_kernel, (field_shape, turned_shape), step_flops // 4, [r]) for r in raw_others]
    fields = jnp.stack([t[0] for t in turned])
    others = jnp.stack([t[1] for t in turned])
    begun_first = call(begin_first_kernel, total_shape, project_flops, [own, others, right])
    near, begun_first = lax.optimization_barrier((near, begun_first))
    far = jnp.stack([shifted(near, "ma", -step) for step in range(1, groups)])
    keep_first, send_first, right_edge = call(
        first,
        (
            shape(parts, across_x, across_y // 2, rows, width, dtype=f32),
            shape(parts, across_x, across_y // 2, rows, width),
            shape(2 * depth, parts * width),
        ),
        project_flops,
        [where, field, low, high, ahead_x, back_x, past_x, own, others, begun_first],
        [total],
    )
    lefts = call(
        move_y, shape(groups, width, planes * depth), 2 * step_flops,
        [field, fields, near, far, ahead_y, back_y],
        [pltpu.VMEM((groups,) + field_shape.shape, bf16)],
    )
    begun_second = call(begin_second_kernel, total_shape, project_flops, [lefts, right])
    keep_second, send_second = call(
        second_kernel,
        (
            shape(parts, across_x // 2, across_y, rows, width, dtype=f32),
            shape(parts, across_x // 2, across_y, rows, width),
        ),
        project_flops,
        [where, lefts, right_edge, begun_second],
        [total],
    )
    first_came = swap(send_first, "gy", 0)
    second_came = swap(send_second, "gx", 0)
    for bit in list(bits("gy"))[1:]:
        keep_first, first_came = halve(where, keep_first, first_came, "gy", bit)
    for bit in bits("gy"):
        keep_second, second_came = halve(where, keep_second, second_came, "gy", bit)
    for bit in bits("gx"):
        keep_first, first_came = halve(where, keep_first, first_came, "gx", bit)
    for bit in list(bits("gx"))[1:]:
        keep_second, second_came = halve(where, keep_second, second_came, "gx", bit)
    return call(
        finish_kernel, jax.ShapeDtypeStruct((2, parts, rows, width), f32), keep_first.size * 2,
        [keep_first, first_came, keep_second, second_came],
    )


def solution(mesh):
    return jax.shard_map(
        local,
        mesh=mesh,
        in_specs=(
            P("cuts", "gx", "gy", None, None, "ma"),
            P("cuts", None, None, "gx", "gy", None),
            P("cuts", None, None, "gx", "gy", None),
        ),
        out_specs=P("cuts", None, ("gx", "gy"), "ma"),
        check_vma=False,
    )
```

```python
import jax
import jax.numpy as jnp
import numpy as np
from jax import lax
from jax.experimental import pallas as pl
from jax.experimental.pallas import tpu as pltpu
from jax.sharding import PartitionSpec as P

VMEM_LIMIT = 16 * 1024 * 1024


def shifted(block, axis, distance):
    devices = range(lax.axis_size(axis))
    route = [((i - distance) % len(devices), i) for i in devices]
    return lax.ppermute(block, axis, route)


def call(body, out_shape, flops, operands, scratch=(), places=None):
    places = places or [pltpu.VMEM] * len(operands)
    return pl.pallas_call(
        body,
        out_shape=out_shape,
        in_specs=[pl.BlockSpec(memory_space=place) for place in places],
        scratch_shapes=scratch,
        cost_estimate=pl.CostEstimate(flops=4 * flops, bytes_accessed=0, transcendentals=0),
        compiler_params=pltpu.CompilerParams(vmem_limit_bytes=VMEM_LIMIT),
    )(*(pltpu.with_memory_space_constraint(a, place) for a, place in zip(operands, places)))


def dot(a, b):
    return jnp.dot(a, b, preferred_element_type=jnp.float32)


def iotas(shape):
    return (
        lax.broadcasted_iota(jnp.int32, shape, 0),
        lax.broadcasted_iota(jnp.int32, shape, 1),
    )


def place_of(x, planes):
    return planes - 2 if x == 0 else x if x == planes - 1 else x - 1


def lane_maps(parts, colours, planes, ys, zs, lanes):
    sites = ys * zs
    depth = parts * colours * sites
    row_size = parts * colours * zs
    lane = np.arange(lanes)
    inner = lane < depth
    past = (lane - depth) % row_size
    used = lane < depth + 2 * row_size
    part = np.where(inner, lane // (colours * sites), past // (colours * zs))
    colour = np.where(inner, lane // sites, past // zs) % colours
    z = np.where(inner, lane, past) % zs
    y = np.where(inner, lane % sites // zs, ys - 1)
    y_ahead = np.where(inner, lane % sites // zs, ys) - 1
    spread = y == np.arange(ys)[:, None]
    spread_ahead = y_ahead == np.arange(ys)[:, None]

    row = np.arange(parts * colours * colours * planes * zs)[:, None]
    row_z = row % zs
    row_x = row // zs % planes
    row_right = row // (zs * planes) % colours
    row_left = row // (zs * planes * colours) % colours
    row_part = row // (zs * planes * colours * colours)
    match_ahead = (row_z == z) & (row_right == colour) & used
    match_back = (row_z == z) & (row_left == colour) & used

    out = np.arange(parts * planes * 8)[:, None]
    field_part = out // (planes * 8)
    out_x = out // 8 % planes
    out_part = out % 8 // colours
    out_colour = out % 8 % colours
    source = (out_x == row_x.T) & (row_part.T == (out_part + field_part) % 2) & (out_part < parts)
    choose_ahead = source & (row_left.T == out_colour)
    choose_back = source & (row_right.T == out_colour)
    sign_ahead = np.where((field_part == 1) & (out_part == 0), -1.0, 1.0)
    sign_back = np.where((field_part == 0) & (out_part == 1), 1.0, -1.0)
    maps = (
        np.concatenate([spread, spread_ahead], axis=1), np.concatenate([match_ahead, match_back], axis=1),
        np.concatenate([choose_ahead * sign_ahead, choose_back * sign_back], axis=0),
        np.broadcast_to(part == 0, (8, lanes)),
    )
    return [np.pad(m, ((0, -len(m) % 8), (0, 2 * lanes - m.shape[1]))).astype(np.float32) for m in maps]


def coefficients(links_x, links_y, maps_ref, planes):
    lanes = maps_ref.shape[1] // 2
    ys = links_x.shape[1]
    count = links_x.shape[0]
    half = 2 * planes * 8
    wide = dot(jnp.concatenate([links_x, links_y], axis=0), maps_ref[:ys].astype(jnp.bfloat16))
    match = maps_ref[ys : ys + count]
    match_ahead, match_back = match[:, :lanes], match[:, lanes:]
    choose = maps_ref[ys + count : ys + count + 2 * half, :count].astype(jnp.bfloat16)
    first_part = maps_ref[ys + count + 2 * half : ys + count + 2 * half + 1, :lanes] > 0.5
    ahead = jnp.concatenate([wide[:count, :lanes] * match_ahead, wide[count:, lanes:] * match_ahead], axis=1)
    back = jnp.concatenate([wide[:count, :lanes] * match_back, wide[count:, :lanes] * match_back], axis=1)
    out = []
    for chosen in (
        dot(choose[:half], ahead.astype(jnp.bfloat16)), dot(choose[half:], back.astype(jnp.bfloat16))
    ):
        for start in (0, lanes):
            part = chosen[:, start : start + lanes]
            rows = jnp.where(first_part, part[: half // 2], part[half // 2 :])
            out.append(rows.reshape(planes, 8, lanes))
    return out


def plane_rows(ref, ys):
    parts, _, colours, zs, width = ref.shape
    return jnp.concatenate(
        [ref[p, :ys, c].reshape(ys * zs, width) for p in range(parts) for c in range(colours)],
        axis=0,
    )


def edges_kernel(raw_hbm, links_hbm, first_ref, last_ref, order_ref, links_ref, arrived):
    parts, planes, ys, colours, zs, _ = raw_hbm.shape
    copies = [
        pltpu.make_async_copy(raw_hbm.at[:, planes - 1], last_ref.at[:, :ys], arrived.at[0]),
        pltpu.make_async_copy(raw_hbm.at[:, 0], first_ref, arrived.at[1]),
        pltpu.make_async_copy(links_hbm.at[:, :, :, planes - 1], links_ref, arrived.at[2]),
    ]
    for copy in copies:
        copy.start()
    order_ref[...] = jnp.zeros_like(order_ref)
    last_ref[:, ys:] = jnp.zeros((parts, colours) + last_ref.shape[2:], last_ref.dtype)
    copies[2].wait()
    last_ref[:, ys:, :, :, :ys] = links_ref[...]
    copies[0].wait()
    copies[1].wait()


def site_matrix(rows_and_masks, count):
    blocks = []
    for q in range(count):
        block = None
        for rows, mask in rows_and_masks:
            term = rows[q : q + 1] * mask
            block = term if block is None else block + term
        blocks.append(block.astype(jnp.bfloat16))
    return jnp.concatenate(blocks, axis=0)


def prepare_kernel(
    order_ref, raw_hbm, links_x_hbm, links_y_hbm, maps_hbm,
    rows_ref, ends_ref, ahead_x_ref, back_x_ref, ahead_y_ref, back_y_ref,
    raw_ref, links_x_ref, links_y_ref, maps_ref, arrived,
):
    sources = (links_x_hbm, links_y_hbm, maps_hbm, raw_hbm)
    targets = (links_x_ref, links_y_ref, maps_ref, raw_ref)
    copies = [
        pltpu.make_async_copy(source, target, arrived.at[i])
        for i, (source, target) in enumerate(zip(sources, targets))
    ]
    for copy in copies:
        copy.start()
    for copy in copies[:3]:
        copy.wait()

    planes, depth, width = rows_ref.shape
    zs = raw_ref.shape[4]
    ys = raw_ref.shape[2]
    sites = ys * zs
    row_size = depth // sites * zs
    lanes = ahead_y_ref.shape[2]
    ahead_x, ahead_y, back_x, back_y = coefficients(
        links_x_ref[...].reshape(-1, ys), links_y_ref[...].reshape(-1, ys), maps_ref, planes
    )
    ahead_x_ref[...] = ahead_x
    back_x_ref[...] = back_x
    ahead_y_ref[...] = ahead_y
    back_y_ref[...] = back_y

    row, lane = iotas((2 * row_size, depth))
    spot = row % row_size
    wanted = (spot // zs) * sites + spot % zs + jnp.where(row < row_size, 0, sites - zs)
    ends = (lane == wanted).astype(jnp.bfloat16)
    filler = jnp.zeros((8, width - 128), jnp.float32)
    spare = ends_ref.shape[1] - 2 * row_size - 8
    copies[3].wait()
    for x in range(planes):
        plane = plane_rows(raw_ref.at[:, x], ys)
        rows_ref[place_of(x, planes)] = plane
        tail = jnp.concatenate([back_y[x, :, lanes - 128 :], filler], axis=1)
        pieces = [dot(ends, plane), tail]
        if spare:
            pieces.append(jnp.zeros((spare, width), jnp.float32))
        ends_ref[x] = jnp.concatenate(pieces, axis=0).astype(jnp.bfloat16)


def turn_kernel(raw_ref, rows_ref, turned_ref):
    planes, depth, width = rows_ref.shape
    for x in range(planes):
        rows_ref[place_of(x, planes)] = plane_rows(raw_ref.at[:, x], raw_ref.shape[2])
    turned_ref[...] = rows_ref[...].reshape(planes * depth, width).T


def move_plane(same, count, ahead, back, above, below):
    depth = same.shape[1]
    moved = dot(site_matrix([(ahead[:, :depth], same)], count), above)
    return (moved + dot(site_matrix([(back[:, :depth], same)], count), below)).astype(jnp.bfloat16)


def same_site(sites, depth):
    site, lane = iotas((sites, depth))
    return (lane % sites == site).astype(jnp.float32)


def set_right(right_ref, place, moved):
    depth, width = moved.shape
    half = depth // 2
    start = place * depth
    real, imag = moved[:half], moved[half:]
    right_ref[start : start + half, :width] = real
    right_ref[start : start + half, width:] = imag
    right_ref[start + half : start + depth, :width] = imag
    right_ref[start + half : start + depth, width:] = -real


def inner_kernel(sites, rows_ref, ahead_ref, back_ref, right_ref, turned_ref):
    planes, depth, width = rows_ref.shape
    same = same_site(sites, depth)
    for x in range(1, planes - 1):
        above = rows_ref[place_of(x + 1, planes)]
        below = rows_ref[place_of(x - 1, planes)]
        moved = move_plane(same, depth // sites, ahead_ref[x], back_ref[x - 1], above, below)
        set_right(right_ref, place_of(x, planes), moved)
    turned_ref[...] = rows_ref[...].reshape(planes * depth, width).T


def begin_first_kernel(own_ref, others_ref, right_ref, total_ref):
    inner = right_ref.shape[0]
    right = right_ref[...]
    total_ref[0] = dot(own_ref[:, :inner], right)
    for k in range(others_ref.shape[0]):
        total_ref[k + 1] = dot(others_ref[k, :, :inner], right)


def begin_second_kernel(lefts_ref, right_ref, total_ref):
    inner = right_ref.shape[0]
    right = right_ref[...]
    for k in range(lefts_ref.shape[0]):
        total_ref[k] = dot(lefts_ref[k, :, :inner], right)


def project(lefts, right, halved, begun_ref, keep_ref, send_ref, total_ref):
    my_bit = lax.bitwise_and(lax.axis_index("gy" if halved else "gx"), 1)
    my_modes = lax.axis_index("ma")
    for k, left in enumerate(lefts):
        total_ref[k] = begun_ref[k] + dot(left, right)
    groups, own_modes, _ = total_ref.shape
    parts, across_x, across_y, rows, width = keep_ref.shape

    def piece(index):
        start = index * rows
        group = lax.rem(start // own_modes + groups - my_modes, groups)
        begin = start % own_modes
        return total_ref[group, begin : begin + rows]

    for gx in range(across_x):
        for gy in range(across_y):
            if halved:
                base = gx * 2 * across_y + 2 * gy
                even, odd = piece(base), piece(base + 1)
            else:
                even, odd = piece(2 * gx * across_y + gy), piece((2 * gx + 1) * across_y + gy)
            keep = jnp.where(my_bit == 0, even, odd)
            send = jnp.where(my_bit == 0, odd, even).astype(send_ref.dtype)
            for p in range(parts):
                keep_ref[p, gx, gy] = keep[:, p * width : (p + 1) * width]
                send_ref[p, gx, gy] = send[:, p * width : (p + 1) * width]


def first_kernel(
    sites, rows_ref, low_ref, high_ref, ahead_ref, back_ref, past_maps_ref, own_ref, others_ref, begun_ref,
    keep_ref, send_ref, right_ref, total_ref,
):
    planes, depth, _ = rows_ref.shape
    same = same_site(sites, depth)
    count = depth // sites
    _, ys, colours, zs, _ = high_ref.shape
    links = low_ref[:, ys:, :, :, :ys].reshape(-1, ys)
    lanes = past_maps_ref.shape[1] // 2
    count = links.shape[0]
    spread = past_maps_ref[:ys, :lanes].astype(jnp.bfloat16)
    match = past_maps_ref[ys : ys + count, lanes:]
    start = past_maps_ref.shape[0] - 24
    choose = past_maps_ref[start : start + 16, :count].astype(jnp.bfloat16)
    past = dot(choose, (dot(links, spread) * match).astype(jnp.bfloat16))
    past = jnp.where(past_maps_ref[start + 16 : start + 17, :lanes] > 0.5, past[:8], past[8:])
    count = depth // sites
    above = rows_ref[place_of(1, planes)]
    set_right(right_ref, 0, move_plane(same, count, ahead_ref[0], past, above, plane_rows(low_ref, ys)))
    x = planes - 1
    below = rows_ref[place_of(x - 1, planes)]
    moved = move_plane(same, count, ahead_ref[x], back_ref[x - 1], plane_rows(high_ref, ys), below)
    set_right(right_ref, 1, moved)
    inner = (planes - 2) * depth
    lefts = [own_ref[:, inner:]] + [others_ref[k, :, inner:] for k in range(others_ref.shape[0])]
    project(lefts, right_ref[...], True, begun_ref, keep_ref, send_ref, total_ref)


def move_y_kernel(
    sites, zs, rows_ref, others_ref, near_ref, far_ref, ahead_ref, back_ref, turned_ref, field_ref
):
    planes, depth, width = rows_ref.shape
    groups = others_ref.shape[0] + 1
    row_size = depth // sites * zs
    reach = depth + near_ref.shape[1]
    head = back_ref.shape[2] - 128
    site, lane = iotas((sites, reach))
    inner = lane < depth
    upper = (lane >= depth) & (lane < depth + row_size)
    lower = (lane >= depth + row_size) & (lane < depth + 2 * row_size)
    lane_z = lane % zs
    to_next = (inner & (lane % sites == site + zs)) | (upper & (site == sites - zs + lane_z))
    to_last = (inner & (lane % sites == site - zs)) | (lower & (site == lane_z))
    to_next = jnp.where(to_next, -1.0, 0.0)
    to_last = jnp.where(to_last, -1.0, 0.0)
    _, lane = iotas((8, 128))
    for x in range(planes):
        past = near_ref[x, 2 * row_size : 2 * row_size + 8, :128].astype(jnp.float32)
        mixed = jnp.where(lane >= depth + row_size - head, past, back_ref[x, :, head:])
        back = jnp.concatenate([back_ref[x, :, :head], mixed], axis=1)[:, :reach]
        matrix = site_matrix([(ahead_ref[x, :, :reach], to_next), (back, to_last)], depth // sites)
        place = place_of(x, planes)
        column = jnp.concatenate([rows_ref[place], near_ref[x]], axis=0)
        field_ref[0, place] = dot(matrix, column).astype(jnp.bfloat16)
        for k in range(groups - 1):
            column = jnp.concatenate([others_ref[k, place], far_ref[k, x]], axis=0)
            field_ref[k + 1, place] = dot(matrix, column).astype(jnp.bfloat16)
    for k in range(groups):
        turned_ref[k] = field_ref[k].reshape(planes * depth, width).T


def second_kernel(lefts_ref, right_ref, begun_ref, keep_ref, send_ref, total_ref):
    inner = lefts_ref.shape[2] - right_ref.shape[0]
    lefts = [lefts_ref[k, :, inner:] for k in range(lefts_ref.shape[0])]
    project(lefts, right_ref[...], False, begun_ref, keep_ref, send_ref, total_ref)


def swap(block, axis, bit):
    return lax.ppermute(block, axis, [(i, i ^ (1 << bit)) for i in range(lax.axis_size(axis))])


def merge_kernel(dim, axis, bit, kept_ref, came_ref, keep_ref, send_ref):
    mine = lax.bitwise_and(lax.shift_right_logical(lax.axis_index(axis), bit), 1)
    for gx in range(keep_ref.shape[1]):
        for gy in range(keep_ref.shape[2]):
            pair = []
            for odd in range(2):
                at = (slice(None), 2 * gx + odd, gy) if dim == 1 else (slice(None), gx, 2 * gy + odd)
                pair.append(kept_ref[at] + came_ref[at].astype(jnp.float32))
            keep_ref[:, gx, gy] = jnp.where(mine == 0, pair[0], pair[1])
            send_ref[:, gx, gy] = jnp.where(mine == 0, pair[1], pair[0]).astype(send_ref.dtype)


def halve(kept, came, axis, bit):
    dim = ("gx", "gy").index(axis) + 1
    dims = kept.shape[:dim] + (kept.shape[dim] // 2,) + kept.shape[dim + 1 :]

    def merge(*refs):
        merge_kernel(dim, axis, bit, *refs)

    keep, send = call(
        merge, (pltpu.VMEM(dims, jnp.float32), pltpu.VMEM(dims, jnp.bfloat16)), kept.size, [kept, came]
    )
    return keep, swap(send, axis, bit)


def finish_kernel(*refs):
    out_ref = refs[-1]
    for d in range(out_ref.shape[0]):
        kept_ref, came_ref = refs[2 * d : 2 * d + 2]
        out_ref[d] = kept_ref[:, 0, 0] + came_ref[:, 0, 0].astype(jnp.float32)


def bits(axis):
    return range(lax.axis_size(axis).bit_length() - 1)


def local(eigen_modes, links_first, links_second):
    f32, bf16 = jnp.float32, jnp.bfloat16
    parts, planes, ys, zs, colours, width = eigen_modes.shape
    sites = ys * zs
    depth = parts * colours * sites
    row_size = parts * colours * zs
    edge = -(-(2 * row_size + 8) // 16) * 16
    lanes = -(-(depth + 2 * row_size) // 128) * 128
    across_x, across_y, groups = (lax.axis_size(a) for a in ("gx", "gy", "ma"))
    rows = groups * width // (across_x * across_y)
    inner_depth = (planes - 2) * depth
    raw = eigen_modes.transpose(0, 1, 2, 4, 3, 5)

    def shape(*dims, dtype=bf16):
        return pltpu.VMEM(dims, dtype)

    field_shape = shape(planes, depth, width)
    turned_shape = shape(width, planes * depth)
    total_shape = shape(groups, width, parts * width, dtype=f32)
    link_shape = shape(planes, 8, lanes, dtype=f32)
    total = pltpu.VMEM(total_shape.shape, f32)
    step_flops = 2 * planes * depth * depth * width
    project_flops = 2 * groups * width * planes * depth * parts * width

    raw_others = [shifted(raw, "ma", -step) for step in range(1, groups)]
    raw_links_x, raw_links_y = (a.transpose(0, 1, 2, 3, 5, 4) for a in (links_first, links_second))
    first_plane, last_plane, order = call(
        edges_kernel,
        (
            shape(parts, ys, colours, zs, width), shape(parts, ys + colours, colours, zs, width),
            shape(8, 128, dtype=f32),
        ),
        0,
        [raw, raw_links_x],
        [pltpu.VMEM((parts, colours, colours, zs, ys), bf16), pltpu.SemaphoreType.DMA((3,))],
        [pltpu.HBM, pltpu.HBM],
    )
    high = shifted(first_plane, "gx", -1)
    low = shifted(last_plane, "gx", 1)
    maps = jnp.asarray(np.concatenate(lane_maps(parts, colours, planes, ys, zs, lanes)))
    past_maps = jnp.asarray(np.concatenate(lane_maps(parts, colours, 1, ys, zs, lanes)))
    field, ends, ahead_x, back_x, ahead_y, back_y = call(
        prepare_kernel,
        (field_shape, shape(planes, edge, width), link_shape, link_shape, link_shape, link_shape),
        step_flops,
        [order, raw, raw_links_x, raw_links_y, maps],
        [pltpu.VMEM(a.shape, a.dtype) for a in (raw, raw_links_x, raw_links_y, maps)] + [pltpu.SemaphoreType.DMA((4,))],
        [pltpu.VMEM] + [pltpu.HBM] * 4,
    )
    near = shifted(ends, "gy", 1)
    if across_y != 2:
        ahead_row = lax.broadcasted_iota(jnp.int32, ends.shape, 1) < row_size
        near = jnp.where(ahead_row, shifted(ends, "gy", -1), near)

    def inner(*refs):
        inner_kernel(sites, *refs)

    def first(*refs):
        first_kernel(sites, *refs)

    def move_y(*refs):
        move_y_kernel(sites, zs, *refs)

    right, own = call(
        inner, (shape(inner_depth, parts * width), turned_shape), 2 * step_flops, [field, ahead_x, back_x]
    )
    turned = [call(turn_kernel, (field_shape, turned_shape), step_flops // 4, [r]) for r in raw_others]
    fields = jnp.stack([t[0] for t in turned])
    others = jnp.stack([t[1] for t in turned])
    begun_first = call(begin_first_kernel, total_shape, project_flops, [own, others, right])
    keep_first, send_first, right_edge = call(
        first,
        (
            shape(parts, across_x, across_y // 2, rows, width, dtype=f32),
            shape(parts, across_x, across_y // 2, rows, width),
            shape(2 * depth, parts * width),
        ),
        project_flops,
        [field, low, high, ahead_x, back_x, past_maps, own, others, begun_first],
        [total],
    )
    near, right_edge = lax.optimization_barrier((near, right_edge))
    far = jnp.stack([shifted(near, "ma", -step) for step in range(1, groups)])
    lefts = call(
        move_y, shape(groups, width, planes * depth), 2 * step_flops,
        [field, fields, near, far, ahead_y, back_y],
        [pltpu.VMEM((groups,) + field_shape.shape, bf16)],
    )
    begun_second = call(begin_second_kernel, total_shape, project_flops, [lefts, right])
    keep_second, send_second = call(
        second_kernel,
        (
            shape(parts, across_x // 2, across_y, rows, width, dtype=f32),
            shape(parts, across_x // 2, across_y, rows, width),
        ),
        project_flops,
        [lefts, right_edge, begun_second],
        [total],
    )
    first_came = swap(send_first, "gy", 0)
    second_came = swap(send_second, "gx", 0)
    for bit in list(bits("gy"))[1:]:
        keep_first, first_came = halve(keep_first, first_came, "gy", bit)
    for bit in bits("gy"):
        keep_second, second_came = halve(keep_second, second_came, "gy", bit)
    for bit in bits("gx"):
        keep_first, first_came = halve(keep_first, first_came, "gx", bit)
    for bit in list(bits("gx"))[1:]:
        keep_second, second_came = halve(keep_second, second_came, "gx", bit)
    return call(
        finish_kernel, jax.ShapeDtypeStruct((2, parts, rows, width), f32), keep_first.size * 2,
        [keep_first, first_came, keep_second, second_came],
    )


def solution(mesh):
    return jax.shard_map(
        local,
        mesh=mesh,
        in_specs=(
            P("cuts", "gx", "gy", None, None, "ma"),
            P("cuts", None, None, "gx", "gy", None),
            P("cuts", None, None, "gx", "gy", None),
        ),
        out_specs=P("cuts", None, ("gx", "gy"), "ma"),
        check_vma=False,
    )
```

```python
import jax
import jax.numpy as jnp
import numpy as np
from jax import lax
from jax.experimental import pallas as pl
from jax.experimental.pallas import tpu as pltpu
from jax.sharding import PartitionSpec as P

VMEM_LIMIT = 16 * 1024 * 1024


def shifted(block, axis, distance):
    devices = range(lax.axis_size(axis))
    route = [((i - distance) % len(devices), i) for i in devices]
    return lax.ppermute(block, axis, route)


def call(body, out_shape, flops, operands, scratch=(), places=None):
    places = places or [pltpu.VMEM] * len(operands)
    return pl.pallas_call(
        body,
        out_shape=out_shape,
        in_specs=[pl.BlockSpec(memory_space=place) for place in places],
        scratch_shapes=scratch,
        cost_estimate=pl.CostEstimate(flops=flops // 2, bytes_accessed=0, transcendentals=0),
        compiler_params=pltpu.CompilerParams(vmem_limit_bytes=VMEM_LIMIT),
    )(*(pltpu.with_memory_space_constraint(a, place) for a, place in zip(operands, places)))


def dot(a, b):
    return jnp.dot(a, b, preferred_element_type=jnp.float32)


def iotas(shape):
    return (
        lax.broadcasted_iota(jnp.int32, shape, 0),
        lax.broadcasted_iota(jnp.int32, shape, 1),
    )


def place_of(x, planes):
    return planes - 2 if x == 0 else x if x == planes - 1 else x - 1


def lane_maps(parts, colours, planes, ys, zs, lanes):
    sites = ys * zs
    depth = parts * colours * sites
    row_size = parts * colours * zs
    lane = np.arange(lanes)
    inner = lane < depth
    past = (lane - depth) % row_size
    used = lane < depth + 2 * row_size
    part = np.where(inner, lane // (colours * sites), past // (colours * zs))
    colour = np.where(inner, lane // sites, past // zs) % colours
    z = np.where(inner, lane, past) % zs
    y = np.where(inner, lane % sites // zs, ys - 1)
    y_ahead = np.where(inner, lane % sites // zs, ys) - 1
    spread = y == np.arange(ys)[:, None]
    spread_ahead = y_ahead == np.arange(ys)[:, None]

    row = np.arange(parts * colours * colours * planes * zs)[:, None]
    row_z = row % zs
    row_x = row // zs % planes
    row_right = row // (zs * planes) % colours
    row_left = row // (zs * planes * colours) % colours
    row_part = row // (zs * planes * colours * colours)
    match_ahead = (row_z == z) & (row_right == colour) & used
    match_back = (row_z == z) & (row_left == colour) & used

    out = np.arange(parts * planes * 8)[:, None]
    field_part = out // (planes * 8)
    out_x = out // 8 % planes
    out_part = out % 8 // colours
    out_colour = out % 8 % colours
    source = (out_x == row_x.T) & (row_part.T == (out_part + field_part) % 2) & (out_part < parts)
    choose_ahead = source & (row_left.T == out_colour)
    choose_back = source & (row_right.T == out_colour)
    sign_ahead = np.where((field_part == 1) & (out_part == 0), -1.0, 1.0)
    sign_back = np.where((field_part == 0) & (out_part == 1), 1.0, -1.0)
    maps = (
        np.concatenate([spread, spread_ahead], axis=1), np.concatenate([match_ahead, match_back], axis=1),
        np.concatenate([choose_ahead * sign_ahead, choose_back * sign_back], axis=0),
        np.broadcast_to(part == 0, (8, lanes)),
    )
    return [np.pad(m, ((0, -len(m) % 8), (0, 2 * lanes - m.shape[1]))).astype(np.float32) for m in maps]


def coefficients(links_x, links_y, maps_ref, planes):
    lanes = maps_ref.shape[1] // 2
    ys = links_x.shape[1]
    count = links_x.shape[0]
    half = 2 * planes * 8
    wide = dot(jnp.concatenate([links_x, links_y], axis=0), maps_ref[:ys].astype(jnp.bfloat16))
    match = maps_ref[ys : ys + count]
    match_ahead, match_back = match[:, :lanes], match[:, lanes:]
    choose = maps_ref[ys + count : ys + count + 2 * half, :count].astype(jnp.bfloat16)
    first_part = maps_ref[ys + count + 2 * half : ys + count + 2 * half + 1, :lanes] > 0.5
    ahead = jnp.concatenate([wide[:count, :lanes] * match_ahead, wide[count:, lanes:] * match_ahead], axis=1)
    back = jnp.concatenate([wide[:count, :lanes] * match_back, wide[count:, :lanes] * match_back], axis=1)
    out = []
    for chosen in (
        dot(choose[:half], ahead.astype(jnp.bfloat16)), dot(choose[half:], back.astype(jnp.bfloat16))
    ):
        for start in (0, lanes):
            part = chosen[:, start : start + lanes]
            rows = jnp.where(first_part, part[: half // 2], part[half // 2 :])
            out.append(rows.reshape(planes, 8, lanes))
    return out


def plane_rows(ref, ys):
    parts, _, colours, zs, width = ref.shape
    return jnp.concatenate(
        [ref[p, :ys, c].reshape(ys * zs, width) for p in range(parts) for c in range(colours)],
        axis=0,
    )


def edges_kernel(
    raw_hbm, links_x_hbm, links_y_hbm, maps_hbm,
    first_ref, last_ref, raw_ref, links_x_ref, links_y_ref, maps_ref, arrived,
):
    parts, planes, ys, colours, zs, _ = raw_hbm.shape
    sources = (
        raw_hbm.at[:, planes - 1], raw_hbm.at[:, 0], links_x_hbm, links_y_hbm, maps_hbm, raw_hbm
    )
    targets = (last_ref.at[:, :ys], first_ref, links_x_ref, links_y_ref, maps_ref, raw_ref)
    copies = [
        pltpu.make_async_copy(source, target, arrived.at[i])
        for i, (source, target) in enumerate(zip(sources, targets))
    ]
    for copy in copies:
        copy.start()
    last_ref[:, ys:] = jnp.zeros((parts, colours) + last_ref.shape[2:], last_ref.dtype)
    copies[2].wait()
    last_ref[:, ys:, :, :, :ys] = links_x_ref[:, :, :, planes - 1]
    for copy in copies[:2] + copies[3:]:
        copy.wait()


def site_matrix(rows_and_masks, count):
    blocks = []
    for q in range(count):
        block = None
        for rows, mask in rows_and_masks:
            term = rows[q : q + 1] * mask
            block = term if block is None else block + term
        blocks.append(block.astype(jnp.bfloat16))
    return jnp.concatenate(blocks, axis=0)


def prepare_kernel(
    raw_ref, links_x_ref, links_y_ref, maps_ref,
    rows_ref, ends_ref, ahead_x_ref, back_x_ref, ahead_y_ref, back_y_ref,
):
    planes, depth, width = rows_ref.shape
    zs = raw_ref.shape[4]
    ys = raw_ref.shape[2]
    sites = ys * zs
    row_size = depth // sites * zs
    lanes = ahead_y_ref.shape[2]
    ahead_x, ahead_y, back_x, back_y = coefficients(
        links_x_ref[...].reshape(-1, ys), links_y_ref[...].reshape(-1, ys), maps_ref, planes
    )
    ahead_x_ref[...] = ahead_x
    back_x_ref[...] = back_x
    ahead_y_ref[...] = ahead_y
    back_y_ref[...] = back_y

    row, lane = iotas((2 * row_size, depth))
    spot = row % row_size
    wanted = (spot // zs) * sites + spot % zs + jnp.where(row < row_size, 0, sites - zs)
    ends = (lane == wanted).astype(jnp.bfloat16)
    filler = jnp.zeros((8, width - 128), jnp.float32)
    spare = ends_ref.shape[1] - 2 * row_size - 8
    for x in range(planes):
        plane = plane_rows(raw_ref.at[:, x], ys)
        rows_ref[place_of(x, planes)] = plane
        tail = jnp.concatenate([back_y[x, :, lanes - 128 :], filler], axis=1)
        pieces = [dot(ends, plane), tail]
        if spare:
            pieces.append(jnp.zeros((spare, width), jnp.float32))
        ends_ref[x] = jnp.concatenate(pieces, axis=0).astype(jnp.bfloat16)


def turn_kernel(raw_ref, rows_ref, turned_ref):
    planes, depth, width = rows_ref.shape
    for x in range(planes):
        rows_ref[place_of(x, planes)] = plane_rows(raw_ref.at[:, x], raw_ref.shape[2])
    turned_ref[...] = rows_ref[...].reshape(planes * depth, width).T


def move_plane(same, count, ahead, back, above, below):
    depth = same.shape[1]
    moved = dot(site_matrix([(ahead[:, :depth], same)], count), above)
    return (moved + dot(site_matrix([(back[:, :depth], same)], count), below)).astype(jnp.bfloat16)


def same_site(sites, depth):
    site, lane = iotas((sites, depth))
    return (lane % sites == site).astype(jnp.float32)


def set_right(right_ref, place, moved):
    depth, width = moved.shape
    half = depth // 2
    start = place * depth
    real, imag = moved[:half], moved[half:]
    right_ref[start : start + half, :width] = real
    right_ref[start : start + half, width:] = imag
    right_ref[start + half : start + depth, :width] = imag
    right_ref[start + half : start + depth, width:] = -real


def inner_kernel(sites, rows_ref, ahead_ref, back_ref, right_ref, turned_ref):
    planes, depth, width = rows_ref.shape
    same = same_site(sites, depth)
    for x in range(1, planes - 1):
        above = rows_ref[place_of(x + 1, planes)]
        below = rows_ref[place_of(x - 1, planes)]
        moved = move_plane(same, depth // sites, ahead_ref[x], back_ref[x - 1], above, below)
        set_right(right_ref, place_of(x, planes), moved)
    turned_ref[...] = rows_ref[...].reshape(planes * depth, width).T


def begin_first_kernel(own_ref, others_ref, right_ref, total_ref):
    inner = right_ref.shape[0]
    right = right_ref[...]
    total_ref[0] = dot(own_ref[:, :inner], right)
    for k in range(others_ref.shape[0]):
        total_ref[k + 1] = dot(others_ref[k, :, :inner], right)


def begin_second_kernel(lefts_ref, right_ref, total_ref):
    inner = right_ref.shape[0]
    right = right_ref[...]
    for k in range(lefts_ref.shape[0]):
        total_ref[k] = dot(lefts_ref[k, :, :inner], right)


def project(lefts, right, halved, begun_ref, keep_ref, send_ref, total_ref):
    my_bit = lax.bitwise_and(lax.axis_index("gy" if halved else "gx"), 1)
    my_modes = lax.axis_index("ma")
    for k, left in enumerate(lefts):
        total_ref[k] = begun_ref[k] + dot(left, right)
    groups, own_modes, _ = total_ref.shape
    parts, across_x, across_y, rows, width = keep_ref.shape

    def piece(index):
        start = index * rows
        group = lax.rem(start // own_modes + groups - my_modes, groups)
        begin = start % own_modes
        return total_ref[group, begin : begin + rows]

    for gx in range(across_x):
        for gy in range(across_y):
            if halved:
                base = gx * 2 * across_y + 2 * gy
                even, odd = piece(base), piece(base + 1)
            else:
                even, odd = piece(2 * gx * across_y + gy), piece((2 * gx + 1) * across_y + gy)
            keep = jnp.where(my_bit == 0, even, odd)
            send = jnp.where(my_bit == 0, odd, even).astype(send_ref.dtype)
            for p in range(parts):
                keep_ref[p, gx, gy] = keep[:, p * width : (p + 1) * width]
                send_ref[p, gx, gy] = send[:, p * width : (p + 1) * width]


def first_kernel(
    sites, rows_ref, high_ref, low_ref, ahead_ref, back_ref, past_maps_ref, own_ref, others_ref, begun_ref,
    keep_ref, send_ref, right_ref, total_ref,
):
    planes, depth, _ = rows_ref.shape
    same = same_site(sites, depth)
    count = depth // sites
    _, ys, colours, zs, _ = high_ref.shape
    links = low_ref[:, ys:, :, :, :ys].reshape(-1, ys)
    lanes = past_maps_ref.shape[1] // 2
    count = links.shape[0]
    spread = past_maps_ref[:ys, :lanes].astype(jnp.bfloat16)
    match = past_maps_ref[ys : ys + count, lanes:]
    start = past_maps_ref.shape[0] - 24
    choose = past_maps_ref[start : start + 16, :count].astype(jnp.bfloat16)
    past = dot(choose, (dot(links, spread) * match).astype(jnp.bfloat16))
    past = jnp.where(past_maps_ref[start + 16 : start + 17, :lanes] > 0.5, past[:8], past[8:])
    count = depth // sites
    above = rows_ref[place_of(1, planes)]
    set_right(right_ref, 0, move_plane(same, count, ahead_ref[0], past, above, plane_rows(low_ref, ys)))
    x = planes - 1
    below = rows_ref[place_of(x - 1, planes)]
    moved = move_plane(same, count, ahead_ref[x], back_ref[x - 1], plane_rows(high_ref, ys), below)
    set_right(right_ref, 1, moved)
    inner = (planes - 2) * depth
    lefts = [own_ref[:, inner:]] + [others_ref[k, :, inner:] for k in range(others_ref.shape[0])]
    project(lefts, right_ref[...], True, begun_ref, keep_ref, send_ref, total_ref)


def move_y_kernel(
    sites, zs, rows_ref, others_ref, near_ref, far_ref, ahead_ref, back_ref, turned_ref, field_ref
):
    planes, depth, width = rows_ref.shape
    groups = others_ref.shape[0] + 1
    row_size = depth // sites * zs
    reach = depth + near_ref.shape[1]
    head = back_ref.shape[2] - 128
    site, lane = iotas((sites, reach))
    inner = lane < depth
    upper = (lane >= depth) & (lane < depth + row_size)
    lower = (lane >= depth + row_size) & (lane < depth + 2 * row_size)
    lane_z = lane % zs
    to_next = (inner & (lane % sites == site + zs)) | (upper & (site == sites - zs + lane_z))
    to_last = (inner & (lane % sites == site - zs)) | (lower & (site == lane_z))
    to_next = jnp.where(to_next, -1.0, 0.0)
    to_last = jnp.where(to_last, -1.0, 0.0)
    _, lane = iotas((8, 128))
    for x in range(planes):
        past = near_ref[x, 2 * row_size : 2 * row_size + 8, :128].astype(jnp.float32)
        mixed = jnp.where(lane >= depth + row_size - head, past, back_ref[x, :, head:])
        back = jnp.concatenate([back_ref[x, :, :head], mixed], axis=1)[:, :reach]
        matrix = site_matrix([(ahead_ref[x, :, :reach], to_next), (back, to_last)], depth // sites)
        place = place_of(x, planes)
        column = jnp.concatenate([rows_ref[place], near_ref[x]], axis=0)
        field_ref[0, place] = dot(matrix, column).astype(jnp.bfloat16)
        for k in range(groups - 1):
            column = jnp.concatenate([others_ref[k, place], far_ref[k, x]], axis=0)
            field_ref[k + 1, place] = dot(matrix, column).astype(jnp.bfloat16)
    for k in range(groups):
        turned_ref[k] = field_ref[k].reshape(planes * depth, width).T


def second_kernel(lefts_ref, right_ref, begun_ref, keep_ref, send_ref, total_ref):
    inner = lefts_ref.shape[2] - right_ref.shape[0]
    lefts = [lefts_ref[k, :, inner:] for k in range(lefts_ref.shape[0])]
    project(lefts, right_ref[...], False, begun_ref, keep_ref, send_ref, total_ref)


def swap(block, axis, bit):
    return lax.ppermute(block, axis, [(i, i ^ (1 << bit)) for i in range(lax.axis_size(axis))])


def merge_kernel(dim, axis, bit, kept_ref, came_ref, keep_ref, send_ref):
    mine = lax.bitwise_and(lax.shift_right_logical(lax.axis_index(axis), bit), 1)
    for gx in range(keep_ref.shape[1]):
        for gy in range(keep_ref.shape[2]):
            pair = []
            for odd in range(2):
                at = (slice(None), 2 * gx + odd, gy) if dim == 1 else (slice(None), gx, 2 * gy + odd)
                pair.append(kept_ref[at] + came_ref[at].astype(jnp.float32))
            keep_ref[:, gx, gy] = jnp.where(mine == 0, pair[0], pair[1])
            send_ref[:, gx, gy] = jnp.where(mine == 0, pair[1], pair[0]).astype(send_ref.dtype)


def halve(kept, came, axis, bit):
    dim = ("gx", "gy").index(axis) + 1
    dims = kept.shape[:dim] + (kept.shape[dim] // 2,) + kept.shape[dim + 1 :]

    def merge(*refs):
        merge_kernel(dim, axis, bit, *refs)

    keep, send = call(
        merge, (pltpu.VMEM(dims, jnp.float32), pltpu.VMEM(dims, jnp.bfloat16)), kept.size, [kept, came]
    )
    return keep, swap(send, axis, bit)


def finish_kernel(*refs):
    out_ref = refs[-1]
    for d in range(out_ref.shape[0]):
        kept_ref, came_ref = refs[2 * d : 2 * d + 2]
        out_ref[d] = kept_ref[:, 0, 0] + came_ref[:, 0, 0].astype(jnp.float32)


def bits(axis):
    return range(lax.axis_size(axis).bit_length() - 1)


def local(eigen_modes, links_first, links_second):
    f32, bf16 = jnp.float32, jnp.bfloat16
    parts, planes, ys, zs, colours, width = eigen_modes.shape
    sites = ys * zs
    depth = parts * colours * sites
    row_size = parts * colours * zs
    edge = -(-(2 * row_size + 8) // 16) * 16
    lanes = -(-(depth + 2 * row_size) // 128) * 128
    across_x, across_y, groups = (lax.axis_size(a) for a in ("gx", "gy", "ma"))
    rows = groups * width // (across_x * across_y)
    inner_depth = (planes - 2) * depth
    raw = eigen_modes.transpose(0, 1, 2, 4, 3, 5)

    def shape(*dims, dtype=bf16):
        return pltpu.VMEM(dims, dtype)

    field_shape = shape(planes, depth, width)
    turned_shape = shape(width, planes * depth)
    total_shape = shape(groups, width, parts * width, dtype=f32)
    link_shape = shape(planes, 8, lanes, dtype=f32)
    total = pltpu.VMEM(total_shape.shape, f32)
    step_flops = 2 * planes * depth * depth * width
    project_flops = 2 * groups * width * planes * depth * parts * width

    raw_others = [shifted(raw, "ma", -step) for step in range(1, groups)]
    raw_links_x, raw_links_y = (a.transpose(0, 1, 2, 3, 5, 4) for a in (links_first, links_second))
    maps = jnp.asarray(np.concatenate(lane_maps(parts, colours, planes, ys, zs, lanes)))
    past_maps = jnp.asarray(np.concatenate(lane_maps(parts, colours, 1, ys, zs, lanes)))
    inputs = [raw, raw_links_x, raw_links_y, maps]
    first_plane, last_plane, *inputs = call(
        edges_kernel,
        (
            shape(parts, ys, colours, zs, width), shape(parts, ys + colours, colours, zs, width),
            *(shape(*a.shape, dtype=a.dtype) for a in inputs),
        ),
        0,
        inputs,
        [pltpu.SemaphoreType.DMA((6,))],
        [pltpu.HBM] * len(inputs),
    )
    low = shifted(last_plane, "gx", 1)
    high = shifted(first_plane, "gx", -1)
    field, ends, ahead_x, back_x, ahead_y, back_y = call(
        prepare_kernel,
        (field_shape, shape(planes, edge, width), link_shape, link_shape, link_shape, link_shape),
        0,
        inputs,
    )
    near = shifted(ends, "gy", 1)
    if across_y != 2:
        ahead_row = lax.broadcasted_iota(jnp.int32, ends.shape, 1) < row_size
        near = jnp.where(ahead_row, shifted(ends, "gy", -1), near)

    def inner(*refs):
        inner_kernel(sites, *refs)

    def first(*refs):
        first_kernel(sites, *refs)

    def move_y(*refs):
        move_y_kernel(sites, zs, *refs)

    right, own = call(
        inner, (shape(inner_depth, parts * width), turned_shape), 2 * step_flops, [field, ahead_x, back_x]
    )
    turned = [call(turn_kernel, (field_shape, turned_shape), step_flops // 4, [r]) for r in raw_others]
    fields = jnp.stack([t[0] for t in turned])
    others = jnp.stack([t[1] for t in turned])
    begun_first = call(begin_first_kernel, total_shape, project_flops, [own, others, right])
    keep_first, send_first, right_edge = call(
        first,
        (
            shape(parts, across_x, across_y // 2, rows, width, dtype=f32),
            shape(parts, across_x, across_y // 2, rows, width),
            shape(2 * depth, parts * width),
        ),
        project_flops,
        [field, high, low, ahead_x, back_x, past_maps, own, others, begun_first],
        [total],
    )
    near, right_edge = lax.optimization_barrier((near, right_edge))
    far = jnp.stack([shifted(near, "ma", -step) for step in range(1, groups)])
    lefts = call(
        move_y, shape(groups, width, planes * depth), 2 * step_flops,
        [field, fields, near, far, ahead_y, back_y],
        [pltpu.VMEM((groups,) + field_shape.shape, bf16)],
    )
    begun_second = call(begin_second_kernel, total_shape, project_flops, [lefts, right])
    keep_second, send_second = call(
        second_kernel,
        (
            shape(parts, across_x // 2, across_y, rows, width, dtype=f32),
            shape(parts, across_x // 2, across_y, rows, width),
        ),
        project_flops,
        [lefts, right_edge, begun_second],
        [total],
    )
    first_came = swap(send_first, "gy", 0)
    second_came = swap(send_second, "gx", 0)
    for bit in list(bits("gy"))[1:]:
        keep_first, first_came = halve(keep_first, first_came, "gy", bit)
    for bit in bits("gy"):
        keep_second, second_came = halve(keep_second, second_came, "gy", bit)
    for bit in bits("gx"):
        keep_first, first_came = halve(keep_first, first_came, "gx", bit)
    for bit in list(bits("gx"))[1:]:
        keep_second, second_came = halve(keep_second, second_came, "gx", bit)
    return call(
        finish_kernel, jax.ShapeDtypeStruct((2, parts, rows, width), f32), keep_first.size * 2,
        [keep_first, first_came, keep_second, second_came],
    )


def solution(mesh):
    return jax.shard_map(
        local,
        mesh=mesh,
        in_specs=(
            P("cuts", "gx", "gy", None, None, "ma"),
            P("cuts", None, None, "gx", "gy", None),
            P("cuts", None, None, "gx", "gy", None),
        ),
        out_specs=P("cuts", None, ("gx", "gy"), "ma"),
        check_vma=False,
    )
```

```python
import jax
import jax.numpy as jnp
import numpy as np
from jax import lax
from jax.experimental import pallas as pl
from jax.experimental.pallas import tpu as pltpu
from jax.sharding import PartitionSpec as P

VMEM_LIMIT = 16 * 1024 * 1024


def shifted(block, axis, distance):
    devices = range(lax.axis_size(axis))
    route = [((i - distance) % len(devices), i) for i in devices]
    return lax.ppermute(block, axis, route)


def call(body, out_shape, flops, operands, scratch=(), places=None):
    places = places or [pltpu.VMEM] * len(operands)
    return pl.pallas_call(
        body,
        out_shape=out_shape,
        in_specs=[pl.BlockSpec(memory_space=place) for place in places],
        scratch_shapes=scratch,
        cost_estimate=pl.CostEstimate(flops=flops // 2, bytes_accessed=0, transcendentals=0),
        compiler_params=pltpu.CompilerParams(vmem_limit_bytes=VMEM_LIMIT),
    )(*(pltpu.with_memory_space_constraint(a, place) for a, place in zip(operands, places)))


def dot(a, b):
    return jnp.dot(a, b, preferred_element_type=jnp.float32)


def iotas(shape):
    return (
        lax.broadcasted_iota(jnp.int32, shape, 0),
        lax.broadcasted_iota(jnp.int32, shape, 1),
    )


def place_of(x, planes):
    return planes - 2 if x == 0 else x if x == planes - 1 else x - 1


def lane_maps(parts, colours, planes, ys, zs, lanes):
    sites = ys * zs
    depth = parts * colours * sites
    row_size = parts * colours * zs
    lane = np.arange(lanes)
    inner = lane < depth
    past = (lane - depth) % row_size
    used = lane < depth + 2 * row_size
    part = np.where(inner, lane // (colours * sites), past // (colours * zs))
    colour = np.where(inner, lane // sites, past // zs) % colours
    z = np.where(inner, lane, past) % zs
    y = np.where(inner, lane % sites // zs, ys - 1)
    y_ahead = np.where(inner, lane % sites // zs, ys) - 1
    spread = y == np.arange(ys)[:, None]
    spread_ahead = y_ahead == np.arange(ys)[:, None]

    row = np.arange(parts * colours * colours * planes * zs)[:, None]
    row_z = row % zs
    row_x = row // zs % planes
    row_right = row // (zs * planes) % colours
    row_left = row // (zs * planes * colours) % colours
    row_part = row // (zs * planes * colours * colours)
    match_ahead = (row_z == z) & (row_right == colour) & used
    match_back = (row_z == z) & (row_left == colour) & used

    out = np.arange(parts * planes * 8)[:, None]
    field_part = out // (planes * 8)
    out_x = out // 8 % planes
    out_part = out % 8 // colours
    out_colour = out % 8 % colours
    source = (out_x == row_x.T) & (row_part.T == (out_part + field_part) % 2) & (out_part < parts)
    choose_ahead = source & (row_left.T == out_colour)
    choose_back = source & (row_right.T == out_colour)
    sign_ahead = np.where((field_part == 1) & (out_part == 0), -1.0, 1.0)
    sign_back = np.where((field_part == 0) & (out_part == 1), 1.0, -1.0)
    maps = (
        np.concatenate([spread, spread_ahead], axis=1), np.concatenate([match_ahead, match_back], axis=1),
        np.concatenate([choose_ahead * sign_ahead, choose_back * sign_back], axis=0),
        np.broadcast_to(part == 0, (8, lanes)),
    )
    return [np.pad(m, ((0, -len(m) % 8), (0, 2 * lanes - m.shape[1]))).astype(np.float32) for m in maps]


def coefficients(links_x, links_y, maps_ref, planes):
    lanes = maps_ref.shape[1] // 2
    ys = links_x.shape[1]
    count = links_x.shape[0]
    half = 2 * planes * 8
    wide = dot(jnp.concatenate([links_x, links_y], axis=0), maps_ref[:ys].astype(jnp.bfloat16))
    match = maps_ref[ys : ys + count]
    match_ahead, match_back = match[:, :lanes], match[:, lanes:]
    choose = maps_ref[ys + count : ys + count + 2 * half, :count].astype(jnp.bfloat16)
    first_part = maps_ref[ys + count + 2 * half : ys + count + 2 * half + 1, :lanes] > 0.5
    ahead = jnp.concatenate([wide[:count, :lanes] * match_ahead, wide[count:, lanes:] * match_ahead], axis=1)
    back = jnp.concatenate([wide[:count, :lanes] * match_back, wide[count:, :lanes] * match_back], axis=1)
    out = []
    for chosen in (
        dot(choose[:half], ahead.astype(jnp.bfloat16)), dot(choose[half:], back.astype(jnp.bfloat16))
    ):
        for start in (0, lanes):
            part = chosen[:, start : start + lanes]
            rows = jnp.where(first_part, part[: half // 2], part[half // 2 :])
            out.append(rows.reshape(planes, 8, lanes))
    return out


def plane_rows(ref, ys):
    parts, _, colours, zs, width = ref.shape
    return jnp.concatenate(
        [ref[p, :ys, c].reshape(ys * zs, width) for p in range(parts) for c in range(colours)],
        axis=0,
    )


def edges_kernel(
    raw_hbm, links_x_hbm, links_y_hbm, maps_hbm,
    first_ref, last_ref, raw_ref, links_x_ref, links_y_ref, maps_ref, arrived,
):
    parts, planes, ys, colours, zs, _ = raw_hbm.shape
    sources = (
        raw_hbm.at[:, planes - 1], raw_hbm.at[:, 0], links_x_hbm, links_y_hbm, maps_hbm, raw_hbm
    )
    targets = (last_ref.at[:, :ys], first_ref, links_x_ref, links_y_ref, maps_ref, raw_ref)
    copies = [
        pltpu.make_async_copy(source, target, arrived.at[i])
        for i, (source, target) in enumerate(zip(sources, targets))
    ]
    for copy in copies:
        copy.start()
    last_ref[:, ys:] = jnp.zeros((parts, colours) + last_ref.shape[2:], last_ref.dtype)
    copies[2].wait()
    last_ref[:, ys:, :, :, :ys] = links_x_ref[:, :, :, planes - 1]
    for copy in copies[:2] + copies[3:]:
        copy.wait()


def site_matrix(rows_and_masks, count):
    blocks = []
    for q in range(count):
        block = None
        for rows, mask in rows_and_masks:
            term = rows[q : q + 1] * mask
            block = term if block is None else block + term
        blocks.append(block.astype(jnp.bfloat16))
    return jnp.concatenate(blocks, axis=0)


def prepare_kernel(
    raw_ref, links_x_ref, links_y_ref, maps_ref,
    rows_ref, ends_ref, ahead_x_ref, back_x_ref, ahead_y_ref, back_y_ref,
):
    planes, depth, width = rows_ref.shape
    zs = raw_ref.shape[4]
    ys = raw_ref.shape[2]
    sites = ys * zs
    row_size = depth // sites * zs
    lanes = ahead_y_ref.shape[2]
    ahead_x, ahead_y, back_x, back_y = coefficients(
        links_x_ref[...].reshape(-1, ys), links_y_ref[...].reshape(-1, ys), maps_ref, planes
    )
    ahead_x_ref[...] = ahead_x
    back_x_ref[...] = back_x
    ahead_y_ref[...] = ahead_y
    back_y_ref[...] = back_y

    row, lane = iotas((2 * row_size, depth))
    spot = row % row_size
    wanted = (spot // zs) * sites + spot % zs + jnp.where(row < row_size, 0, sites - zs)
    ends = (lane == wanted).astype(jnp.bfloat16)
    filler = jnp.zeros((8, width - 128), jnp.float32)
    spare = ends_ref.shape[1] - 2 * row_size - 8
    for x in range(planes):
        plane = plane_rows(raw_ref.at[:, x], ys)
        rows_ref[place_of(x, planes)] = plane
        tail = jnp.concatenate([back_y[x, :, lanes - 128 :], filler], axis=1)
        pieces = [dot(ends, plane), tail]
        if spare:
            pieces.append(jnp.zeros((spare, width), jnp.float32))
        ends_ref[x] = jnp.concatenate(pieces, axis=0).astype(jnp.bfloat16)


def turn_kernel(raw_ref, rows_ref, turned_ref):
    planes, depth, width = rows_ref.shape
    for x in range(planes):
        rows_ref[place_of(x, planes)] = plane_rows(raw_ref.at[:, x], raw_ref.shape[2])
    turned_ref[...] = rows_ref[...].reshape(planes * depth, width).T


def move_plane(same, count, ahead, back, above, below):
    depth = same.shape[1]
    moved = dot(site_matrix([(ahead[:, :depth], same)], count), above)
    return (moved + dot(site_matrix([(back[:, :depth], same)], count), below)).astype(jnp.bfloat16)


def same_site(sites, depth):
    site, lane = iotas((sites, depth))
    return (lane % sites == site).astype(jnp.float32)


def set_right(right_ref, place, moved):
    depth, width = moved.shape
    half = depth // 2
    start = place * depth
    real, imag = moved[:half], moved[half:]
    right_ref[start : start + half, :width] = real
    right_ref[start : start + half, width:] = imag
    right_ref[start + half : start + depth, :width] = imag
    right_ref[start + half : start + depth, width:] = -real


def inner_kernel(sites, rows_ref, ahead_ref, back_ref, right_ref, turned_ref):
    planes, depth, width = rows_ref.shape
    same = same_site(sites, depth)
    for x in range(1, planes - 1):
        above = rows_ref[place_of(x + 1, planes)]
        below = rows_ref[place_of(x - 1, planes)]
        moved = move_plane(same, depth // sites, ahead_ref[x], back_ref[x - 1], above, below)
        set_right(right_ref, place_of(x, planes), moved)
    turned_ref[...] = rows_ref[...].reshape(planes * depth, width).T


def begin_first_kernel(own_ref, others_ref, right_ref, total_ref):
    inner = right_ref.shape[0]
    right = right_ref[...]
    total_ref[0] = dot(own_ref[:, :inner], right)
    for k in range(others_ref.shape[0]):
        total_ref[k + 1] = dot(others_ref[k, :, :inner], right)


def begin_second_kernel(lefts_ref, right_ref, total_ref):
    inner = right_ref.shape[0]
    right = right_ref[...]
    for k in range(lefts_ref.shape[0]):
        total_ref[k] = dot(lefts_ref[k, :, :inner], right)


def bits(axis):
    return range(lax.axis_size(axis).bit_length() - 1)


def my_bit(axis, bit):
    return lax.bitwise_and(lax.shift_right_logical(lax.axis_index(axis), bit), 1)


def project(lefts, right, begun_ref, steps, refs, total_ref):
    for k, left in enumerate(lefts):
        total_ref[k] = begun_ref[k] + dot(left, right)
    groups, own_modes, _ = total_ref.shape
    my_modes = lax.axis_index("ma")
    top = my_bit("gx", bits("gx")[-1])
    across_x, across_y = lax.axis_size("gx"), lax.axis_size("gy")
    rows, width = refs[0].shape[3:]

    def piece(gx, gy):
        start = (gx * across_y + gy) * rows
        group = lax.rem(start // own_modes + groups - my_modes, groups)
        begin = start % own_modes
        return total_ref[group, begin : begin + rows]

    for kind, axis in enumerate(steps):
        keep_ref, send_ref = refs[2 * kind : 2 * kind + 2]
        mine = my_bit(axis, 0)
        half = lax.bitwise_xor(top, 1 - kind)

        def chosen(gx, gy):
            return jnp.where(half == 0, piece(gx, gy), piece(gx + across_x // 2, gy))

        for gx in range(keep_ref.shape[1]):
            for gy in range(keep_ref.shape[2]):
                if axis == "gx":
                    even, odd = chosen(2 * gx, gy), chosen(2 * gx + 1, gy)
                else:
                    even, odd = chosen(gx, 2 * gy), chosen(gx, 2 * gy + 1)
                keep = jnp.where(mine == 0, even, odd)
                send = jnp.where(mine == 0, odd, even).astype(send_ref.dtype)
                for p in range(keep_ref.shape[0]):
                    keep_ref[p, gx, gy] = keep[:, p * width : (p + 1) * width]
                    send_ref[p, gx, gy] = send[:, p * width : (p + 1) * width]


def first_kernel(
    sites, steps, rows_ref, high_ref, low_ref, ahead_ref, back_ref, past_maps_ref, own_ref, others_ref, begun_ref,
    *refs,
):
    *refs, right_ref, total_ref = refs
    planes, depth, _ = rows_ref.shape
    same = same_site(sites, depth)
    count = depth // sites
    _, ys, colours, zs, _ = high_ref.shape
    links = low_ref[:, ys:, :, :, :ys].reshape(-1, ys)
    lanes = past_maps_ref.shape[1] // 2
    count = links.shape[0]
    spread = past_maps_ref[:ys, :lanes].astype(jnp.bfloat16)
    match = past_maps_ref[ys : ys + count, lanes:]
    start = past_maps_ref.shape[0] - 24
    choose = past_maps_ref[start : start + 16, :count].astype(jnp.bfloat16)
    past = dot(choose, (dot(links, spread) * match).astype(jnp.bfloat16))
    past = jnp.where(past_maps_ref[start + 16 : start + 17, :lanes] > 0.5, past[:8], past[8:])
    count = depth // sites
    above = rows_ref[place_of(1, planes)]
    set_right(right_ref, 0, move_plane(same, count, ahead_ref[0], past, above, plane_rows(low_ref, ys)))
    x = planes - 1
    below = rows_ref[place_of(x - 1, planes)]
    moved = move_plane(same, count, ahead_ref[x], back_ref[x - 1], plane_rows(high_ref, ys), below)
    set_right(right_ref, 1, moved)
    inner = (planes - 2) * depth
    lefts = [own_ref[:, inner:]] + [others_ref[k, :, inner:] for k in range(others_ref.shape[0])]
    project(lefts, right_ref[...], begun_ref, steps, refs, total_ref)


def move_y_kernel(
    sites, zs, rows_ref, others_ref, near_ref, far_ref, ahead_ref, back_ref, turned_ref, field_ref
):
    planes, depth, width = rows_ref.shape
    groups = others_ref.shape[0] + 1
    row_size = depth // sites * zs
    reach = depth + near_ref.shape[1]
    head = back_ref.shape[2] - 128
    site, lane = iotas((sites, reach))
    inner = lane < depth
    upper = (lane >= depth) & (lane < depth + row_size)
    lower = (lane >= depth + row_size) & (lane < depth + 2 * row_size)
    lane_z = lane % zs
    to_next = (inner & (lane % sites == site + zs)) | (upper & (site == sites - zs + lane_z))
    to_last = (inner & (lane % sites == site - zs)) | (lower & (site == lane_z))
    to_next = jnp.where(to_next, -1.0, 0.0)
    to_last = jnp.where(to_last, -1.0, 0.0)
    _, lane = iotas((8, 128))
    for x in range(planes):
        past = near_ref[x, 2 * row_size : 2 * row_size + 8, :128].astype(jnp.float32)
        mixed = jnp.where(lane >= depth + row_size - head, past, back_ref[x, :, head:])
        back = jnp.concatenate([back_ref[x, :, :head], mixed], axis=1)[:, :reach]
        matrix = site_matrix([(ahead_ref[x, :, :reach], to_next), (back, to_last)], depth // sites)
        place = place_of(x, planes)
        column = jnp.concatenate([rows_ref[place], near_ref[x]], axis=0)
        field_ref[0, place] = dot(matrix, column).astype(jnp.bfloat16)
        for k in range(groups - 1):
            column = jnp.concatenate([others_ref[k, place], far_ref[k, x]], axis=0)
            field_ref[k + 1, place] = dot(matrix, column).astype(jnp.bfloat16)
    for k in range(groups):
        turned_ref[k] = field_ref[k].reshape(planes * depth, width).T


def second_kernel(steps, lefts_ref, right_ref, begun_ref, *refs):
    *refs, total_ref = refs
    inner = lefts_ref.shape[2] - right_ref.shape[0]
    lefts = [lefts_ref[k, :, inner:] for k in range(lefts_ref.shape[0])]
    project(lefts, right_ref[...], begun_ref, steps, refs, total_ref)


def swap(block, axis, bit):
    return lax.ppermute(block, axis, [(i, i ^ (1 << bit)) for i in range(lax.axis_size(axis))])


def merge_kernel(axis, bit, kept_ref, came_ref, keep_ref, send_ref):
    mine = my_bit(axis, bit)
    for gx in range(keep_ref.shape[1]):
        for gy in range(keep_ref.shape[2]):
            pair = []
            for odd in range(2):
                at = (slice(None), 2 * gx + odd, gy) if axis == "gx" else (slice(None), gx, 2 * gy + odd)
                pair.append(kept_ref[at] + came_ref[at].astype(jnp.float32))
            keep_ref[:, gx, gy] = jnp.where(mine == 0, pair[0], pair[1])
            send_ref[:, gx, gy] = jnp.where(mine == 0, pair[1], pair[0]).astype(send_ref.dtype)


def sum_kernel(kept_ref, came_ref, send_ref):
    send_ref[...] = (kept_ref[...] + came_ref[...].astype(jnp.float32)).astype(send_ref.dtype)


def finish_kernel(*refs):
    out_ref = refs[-1]
    for d in range(out_ref.shape[0]):
        kept_ref, came_ref, crossed_ref = refs[3 * d : 3 * d + 3]
        total = kept_ref[:, 0, 0] + came_ref[:, 0, 0].astype(jnp.float32)
        out_ref[d] = total + crossed_ref[:, 0, 0].astype(jnp.float32)


class Reduction:
    def __init__(self, kept, sent, axis):
        *low, self.top = [("gx", bit) for bit in bits("gx")]
        across = [("gy", bit) for bit in bits("gy")]
        self.steps = across + low[1:] if axis == "gx" else across[1:] + low
        self.kept, self.came = kept, swap(sent, axis, 0)

    def halve(self, after):
        (axis, bit), *self.steps = self.steps
        dim = ("gx", "gy").index(axis) + 1
        shape = self.kept.shape
        shape = shape[:dim] + (shape[dim] // 2,) + shape[dim + 1 :]

        def merge(*refs):
            merge_kernel(axis, bit, *refs)

        self.came, _ = lax.optimization_barrier((self.came, after))
        self.kept, sent = call(
            merge, (pltpu.VMEM(shape, jnp.float32), pltpu.VMEM(shape, jnp.bfloat16)), 0, [self.kept, self.came]
        )
        self.came = swap(sent, axis, bit)
        return self.kept

    def cross(self, after):
        self.came, _ = lax.optimization_barrier((self.came, after))
        sent = call(sum_kernel, pltpu.VMEM(self.kept.shape, jnp.bfloat16), 0, [self.kept, self.came])
        self.came = swap(sent, *self.top)
        return sent


def local(eigen_modes, links_first, links_second):
    f32, bf16 = jnp.float32, jnp.bfloat16
    parts, planes, ys, zs, colours, width = eigen_modes.shape
    sites = ys * zs
    depth = parts * colours * sites
    row_size = parts * colours * zs
    edge = -(-(2 * row_size + 8) // 16) * 16
    lanes = -(-(depth + 2 * row_size) // 128) * 128
    across_x, across_y, groups = (lax.axis_size(a) for a in ("gx", "gy", "ma"))
    rows = groups * width // (across_x * across_y)
    inner_depth = (planes - 2) * depth
    raw = eigen_modes.transpose(0, 1, 2, 4, 3, 5)

    def shape(*dims, dtype=bf16):
        return pltpu.VMEM(dims, dtype)

    field_shape = shape(planes, depth, width)
    turned_shape = shape(width, planes * depth)
    total_shape = shape(groups, width, parts * width, dtype=f32)
    link_shape = shape(planes, 8, lanes, dtype=f32)
    total = pltpu.VMEM(total_shape.shape, f32)
    step_flops = 2 * planes * depth * depth * width
    project_flops = 2 * groups * width * planes * depth * parts * width

    raw_others = [shifted(raw, "ma", -step) for step in range(1, groups)]
    raw_links_x, raw_links_y = (a.transpose(0, 1, 2, 3, 5, 4) for a in (links_first, links_second))
    maps = jnp.asarray(np.concatenate(lane_maps(parts, colours, planes, ys, zs, lanes)))
    past_maps = jnp.asarray(np.concatenate(lane_maps(parts, colours, 1, ys, zs, lanes)))
    inputs = [raw, raw_links_x, raw_links_y, maps]
    first_plane, last_plane, *inputs = call(
        edges_kernel,
        (
            shape(parts, ys, colours, zs, width), shape(parts, ys + colours, colours, zs, width),
            *(shape(*a.shape, dtype=a.dtype) for a in inputs),
        ),
        0,
        inputs,
        [pltpu.SemaphoreType.DMA((6,))],
        [pltpu.HBM] * len(inputs),
    )
    low = shifted(last_plane, "gx", 1)
    high = shifted(first_plane, "gx", -1)
    field, ends, ahead_x, back_x, ahead_y, back_y = call(
        prepare_kernel,
        (field_shape, shape(planes, edge, width), link_shape, link_shape, link_shape, link_shape),
        0,
        inputs,
    )
    near = shifted(ends, "gy", 1)
    if across_y != 2:
        ahead_row = lax.broadcasted_iota(jnp.int32, ends.shape, 1) < row_size
        near = jnp.where(ahead_row, shifted(ends, "gy", -1), near)

    first_steps, second_steps = ("gx", "gx"), ("gy", "gx")

    def split(steps):
        shapes = []
        for axis in steps:
            dims = (across_x // 4, across_y) if axis == "gx" else (across_x // 2, across_y // 2)
            shapes += [shape(parts, *dims, rows, width, dtype=dtype) for dtype in (f32, bf16)]
        return shapes

    def inner(*refs):
        inner_kernel(sites, *refs)

    def first(*refs):
        first_kernel(sites, first_steps, *refs)

    def second(*refs):
        second_kernel(second_steps, *refs)

    def move_y(*refs):
        move_y_kernel(sites, zs, *refs)

    right, own = call(
        inner, (shape(inner_depth, parts * width), turned_shape), 2 * step_flops, [field, ahead_x, back_x]
    )
    turned = [call(turn_kernel, (field_shape, turned_shape), step_flops // 4, [r]) for r in raw_others]
    fields = jnp.stack([t[0] for t in turned])
    others = jnp.stack([t[1] for t in turned])
    begun_first = call(begin_first_kernel, total_shape, project_flops, [own, others, right])
    *parts_first, right_edge = call(
        first,
        (*split(first_steps), shape(2 * depth, parts * width)),
        project_flops,
        [field, high, low, ahead_x, back_x, past_maps, own, others, begun_first],
        [total],
    )
    near, right_edge = lax.optimization_barrier((near, right_edge))
    far = jnp.stack([shifted(near, "ma", -step) for step in range(1, groups)])
    lefts = call(
        move_y, shape(groups, width, planes * depth), 2 * step_flops,
        [field, fields, near, far, ahead_y, back_y],
        [pltpu.VMEM((groups,) + field_shape.shape, bf16)],
    )
    begun_second = call(begin_second_kernel, total_shape, project_flops, [lefts, right])
    parts_second = call(
        second, split(second_steps), project_flops, [lefts, right_edge, begun_second], [total]
    )
    crossing, staying = (
        [
            Reduction(*parts_first[k : k + 2], first_steps[k // 2]),
            Reduction(*parts_second[k : k + 2], second_steps[k // 2]),
        ]
        for k in (0, 2)
    )
    after = parts_second[0]
    while any(r.steps for r in crossing):
        for r in crossing:
            if r.steps:
                after = r.halve(after)
    for r in crossing:
        after = r.cross(after)
    while any(r.steps for r in staying):
        for r in staying:
            if r.steps:
                after = r.halve(after)
    sums = []
    for stay, cross in zip(staying, crossing):
        sums += [stay.kept, stay.came, cross.came]
    return call(finish_kernel, jax.ShapeDtypeStruct((2, parts, rows, width), f32), 0, sums)


def solution(mesh):
    return jax.shard_map(
        local,
        mesh=mesh,
        in_specs=(
            P("cuts", "gx", "gy", None, None, "ma"),
            P("cuts", None, None, "gx", "gy", None),
            P("cuts", None, None, "gx", "gy", None),
        ),
        out_specs=P("cuts", None, ("gx", "gy"), "ma"),
        check_vma=False,
    )
```

```python
import jax
import jax.numpy as jnp
import numpy as np
from jax import lax
from jax.experimental import pallas as pl
from jax.experimental.pallas import tpu as pltpu
from jax.sharding import PartitionSpec as P

VMEM_LIMIT = 16 * 1024 * 1024


def shifted(block, axis, distance):
    devices = range(lax.axis_size(axis))
    route = [((i - distance) % len(devices), i) for i in devices]
    return lax.ppermute(block, axis, route)


def call(body, out_shape, flops, operands, scratch=(), places=None):
    places = places or [pltpu.VMEM] * len(operands)
    return pl.pallas_call(
        body,
        out_shape=out_shape,
        in_specs=[pl.BlockSpec(memory_space=place) for place in places],
        scratch_shapes=scratch,
        cost_estimate=pl.CostEstimate(flops=flops // 2, bytes_accessed=0, transcendentals=0),
        compiler_params=pltpu.CompilerParams(vmem_limit_bytes=VMEM_LIMIT),
    )(*(pltpu.with_memory_space_constraint(a, place) for a, place in zip(operands, places)))


def dot(a, b):
    return jnp.dot(a, b, preferred_element_type=jnp.float32)


def iotas(shape):
    return (
        lax.broadcasted_iota(jnp.int32, shape, 0),
        lax.broadcasted_iota(jnp.int32, shape, 1),
    )


def place_of(x, planes):
    return planes - 2 if x == 0 else x if x == planes - 1 else x - 1


def lane_maps(parts, colours, planes, ys, zs, lanes):
    sites = ys * zs
    depth = parts * colours * sites
    row_size = parts * colours * zs
    lane = np.arange(lanes)
    inner = lane < depth
    past = (lane - depth) % row_size
    used = lane < depth + 2 * row_size
    part = np.where(inner, lane // (colours * sites), past // (colours * zs))
    colour = np.where(inner, lane // sites, past // zs) % colours
    z = np.where(inner, lane, past) % zs
    y = np.where(inner, lane % sites // zs, ys - 1)
    y_ahead = np.where(inner, lane % sites // zs, ys) - 1
    spread = y == np.arange(ys)[:, None]
    spread_ahead = y_ahead == np.arange(ys)[:, None]

    row = np.arange(parts * colours * colours * planes * zs)[:, None]
    row_z = row % zs
    row_x = row // zs % planes
    row_right = row // (zs * planes) % colours
    row_left = row // (zs * planes * colours) % colours
    row_part = row // (zs * planes * colours * colours)
    match_ahead = (row_z == z) & (row_right == colour) & used
    match_back = (row_z == z) & (row_left == colour) & used

    out = np.arange(parts * planes * 8)[:, None]
    field_part = out // (planes * 8)
    out_x = out // 8 % planes
    out_part = out % 8 // colours
    out_colour = out % 8 % colours
    source = (out_x == row_x.T) & (row_part.T == (out_part + field_part) % 2) & (out_part < parts)
    choose_ahead = source & (row_left.T == out_colour)
    choose_back = source & (row_right.T == out_colour)
    sign_ahead = np.where((field_part == 1) & (out_part == 0), -1.0, 1.0)
    sign_back = np.where((field_part == 0) & (out_part == 1), 1.0, -1.0)
    maps = (
        np.concatenate([spread, spread_ahead], axis=1), np.concatenate([match_ahead, match_back], axis=1),
        np.concatenate([choose_ahead * sign_ahead, choose_back * sign_back], axis=0),
        np.broadcast_to(part == 0, (8, lanes)),
    )
    return [np.pad(m, ((0, -len(m) % 8), (0, 2 * lanes - m.shape[1]))).astype(np.float32) for m in maps]


def coefficients(links_x, links_y, maps_ref, planes):
    lanes = maps_ref.shape[1] // 2
    ys = links_x.shape[1]
    count = links_x.shape[0]
    half = 2 * planes * 8
    wide = dot(jnp.concatenate([links_x, links_y], axis=0), maps_ref[:ys].astype(jnp.bfloat16))
    match = maps_ref[ys : ys + count]
    match_ahead, match_back = match[:, :lanes], match[:, lanes:]
    choose = maps_ref[ys + count : ys + count + 2 * half, :count].astype(jnp.bfloat16)
    first_part = maps_ref[ys + count + 2 * half : ys + count + 2 * half + 1, :lanes] > 0.5
    ahead = jnp.concatenate([wide[:count, :lanes] * match_ahead, wide[count:, lanes:] * match_ahead], axis=1)
    back = jnp.concatenate([wide[:count, :lanes] * match_back, wide[count:, :lanes] * match_back], axis=1)
    out = []
    for chosen in (
        dot(choose[:half], ahead.astype(jnp.bfloat16)), dot(choose[half:], back.astype(jnp.bfloat16))
    ):
        for start in (0, lanes):
            part = chosen[:, start : start + lanes]
            rows = jnp.where(first_part, part[: half // 2], part[half // 2 :])
            out.append(rows.reshape(planes, 8, lanes))
    return out


def plane_rows(ref, ys):
    parts, _, colours, zs, width = ref.shape
    return jnp.concatenate(
        [ref[p, :ys, c].reshape(ys * zs, width) for p in range(parts) for c in range(colours)],
        axis=0,
    )


def edges_kernel(
    raw_hbm, links_x_hbm, links_y_hbm, maps_hbm,
    first_ref, last_ref, links_x_ref, links_y_ref, maps_ref, arrived,
):
    parts, planes, ys, colours, zs, _ = raw_hbm.shape
    sources = (raw_hbm.at[:, planes - 1], raw_hbm.at[:, 0], links_x_hbm, links_y_hbm, maps_hbm)
    targets = (last_ref.at[:, :ys], first_ref, links_x_ref, links_y_ref, maps_ref)
    copies = [
        pltpu.make_async_copy(source, target, arrived.at[i])
        for i, (source, target) in enumerate(zip(sources, targets))
    ]
    for copy in copies:
        copy.start()
    last_ref[:, ys:] = jnp.zeros((parts, colours) + last_ref.shape[2:], last_ref.dtype)
    copies[2].wait()
    last_ref[:, ys:, :, :, :ys] = links_x_ref[:, :, :, planes - 1]
    for copy in copies[:2] + copies[3:]:
        copy.wait()


def site_matrix(rows_and_masks, count):
    blocks = []
    for q in range(count):
        block = None
        for rows, mask in rows_and_masks:
            term = rows[q : q + 1] * mask
            block = term if block is None else block + term
        blocks.append(block.astype(jnp.bfloat16))
    return jnp.concatenate(blocks, axis=0)


def prepare_kernel(
    raw_hbm, links_x_ref, links_y_ref, maps_ref,
    rows_ref, ends_ref, ahead_x_ref, back_x_ref, ahead_y_ref, back_y_ref, raw_ref, arrived,
):
    copy = pltpu.make_async_copy(raw_hbm, raw_ref, arrived)
    copy.start()
    planes, depth, width = rows_ref.shape
    zs = raw_ref.shape[4]
    ys = raw_ref.shape[2]
    sites = ys * zs
    row_size = depth // sites * zs
    lanes = ahead_y_ref.shape[2]
    ahead_x, ahead_y, back_x, back_y = coefficients(
        links_x_ref[...].reshape(-1, ys), links_y_ref[...].reshape(-1, ys), maps_ref, planes
    )
    ahead_x_ref[...] = ahead_x
    back_x_ref[...] = back_x
    ahead_y_ref[...] = ahead_y
    back_y_ref[...] = back_y

    row, lane = iotas((2 * row_size, depth))
    spot = row % row_size
    wanted = (spot // zs) * sites + spot % zs + jnp.where(row < row_size, 0, sites - zs)
    ends = (lane == wanted).astype(jnp.bfloat16)
    filler = jnp.zeros((8, width - 128), jnp.float32)
    spare = ends_ref.shape[1] - 2 * row_size - 8
    copy.wait()
    for x in range(planes):
        plane = plane_rows(raw_ref.at[:, x], ys)
        rows_ref[place_of(x, planes)] = plane
        tail = jnp.concatenate([back_y[x, :, lanes - 128 :], filler], axis=1)
        pieces = [dot(ends, plane), tail]
        if spare:
            pieces.append(jnp.zeros((spare, width), jnp.float32))
        ends_ref[x] = jnp.concatenate(pieces, axis=0).astype(jnp.bfloat16)


def turn_kernel(raw_ref, rows_ref, turned_ref):
    planes, depth, width = rows_ref.shape
    for x in range(planes):
        rows_ref[place_of(x, planes)] = plane_rows(raw_ref.at[:, x], raw_ref.shape[2])
    turned_ref[...] = rows_ref[...].reshape(planes * depth, width).T


def move_plane(same, count, ahead, back, above, below):
    depth = same.shape[1]
    moved = dot(site_matrix([(ahead[:, :depth], same)], count), above)
    return (moved + dot(site_matrix([(back[:, :depth], same)], count), below)).astype(jnp.bfloat16)


def same_site(sites, depth):
    site, lane = iotas((sites, depth))
    return (lane % sites == site).astype(jnp.float32)


def set_right(right_ref, place, moved):
    depth, width = moved.shape
    half = depth // 2
    start = place * depth
    real, imag = moved[:half], moved[half:]
    right_ref[start : start + half, :width] = real
    right_ref[start : start + half, width:] = imag
    right_ref[start + half : start + depth, :width] = imag
    right_ref[start + half : start + depth, width:] = -real


def inner_kernel(sites, rows_ref, ahead_ref, back_ref, right_ref, turned_ref):
    planes, depth, width = rows_ref.shape
    same = same_site(sites, depth)
    for x in range(1, planes - 1):
        above = rows_ref[place_of(x + 1, planes)]
        below = rows_ref[place_of(x - 1, planes)]
        moved = move_plane(same, depth // sites, ahead_ref[x], back_ref[x - 1], above, below)
        set_right(right_ref, place_of(x, planes), moved)
    turned_ref[...] = rows_ref[...].reshape(planes * depth, width).T


def begin_first_kernel(own_ref, others_ref, right_ref, total_ref):
    inner = right_ref.shape[0]
    right = right_ref[...]
    total_ref[0] = dot(own_ref[:, :inner], right)
    for k in range(others_ref.shape[0]):
        total_ref[k + 1] = dot(others_ref[k, :, :inner], right)


def begin_second_kernel(lefts_ref, right_ref, total_ref):
    inner = right_ref.shape[0]
    right = right_ref[...]
    for k in range(lefts_ref.shape[0]):
        total_ref[k] = dot(lefts_ref[k, :, :inner], right)


def bits(axis):
    return range(lax.axis_size(axis).bit_length() - 1)


def my_bit(axis, bit):
    return lax.bitwise_and(lax.shift_right_logical(lax.axis_index(axis), bit), 1)


def project(lefts, right, begun_ref, steps, refs, total_ref):
    for k, left in enumerate(lefts):
        total_ref[k] = begun_ref[k] + dot(left, right)
    groups, own_modes, _ = total_ref.shape
    my_modes = lax.axis_index("ma")
    top = my_bit("gx", bits("gx")[-1])
    across_x, across_y = lax.axis_size("gx"), lax.axis_size("gy")
    rows, width = refs[0].shape[3:]

    def piece(gx, gy):
        start = (gx * across_y + gy) * rows
        group = lax.rem(start // own_modes + groups - my_modes, groups)
        begin = start % own_modes
        return total_ref[group, begin : begin + rows]

    for kind, axis in enumerate(steps):
        keep_ref, send_ref = refs[2 * kind : 2 * kind + 2]
        mine = my_bit(axis, 0)
        half = lax.bitwise_xor(top, 1 - kind)

        def chosen(gx, gy):
            return jnp.where(half == 0, piece(gx, gy), piece(gx + across_x // 2, gy))

        for gx in range(keep_ref.shape[1]):
            for gy in range(keep_ref.shape[2]):
                if axis == "gx":
                    even, odd = chosen(2 * gx, gy), chosen(2 * gx + 1, gy)
                else:
                    even, odd = chosen(gx, 2 * gy), chosen(gx, 2 * gy + 1)
                keep = jnp.where(mine == 0, even, odd)
                send = jnp.where(mine == 0, odd, even).astype(send_ref.dtype)
                for p in range(keep_ref.shape[0]):
                    keep_ref[p, gx, gy] = keep[:, p * width : (p + 1) * width]
                    send_ref[p, gx, gy] = send[:, p * width : (p + 1) * width]


def first_kernel(
    sites, steps, rows_ref, high_ref, low_ref, ahead_ref, back_ref, past_maps_ref, own_ref, others_ref, begun_ref,
    *refs,
):
    *refs, right_ref, total_ref = refs
    planes, depth, _ = rows_ref.shape
    same = same_site(sites, depth)
    count = depth // sites
    _, ys, colours, zs, _ = high_ref.shape
    links = low_ref[:, ys:, :, :, :ys].reshape(-1, ys)
    lanes = past_maps_ref.shape[1] // 2
    count = links.shape[0]
    spread = past_maps_ref[:ys, :lanes].astype(jnp.bfloat16)
    match = past_maps_ref[ys : ys + count, lanes:]
    start = past_maps_ref.shape[0] - 24
    choose = past_maps_ref[start : start + 16, :count].astype(jnp.bfloat16)
    past = dot(choose, (dot(links, spread) * match).astype(jnp.bfloat16))
    past = jnp.where(past_maps_ref[start + 16 : start + 17, :lanes] > 0.5, past[:8], past[8:])
    count = depth // sites
    above = rows_ref[place_of(1, planes)]
    set_right(right_ref, 0, move_plane(same, count, ahead_ref[0], past, above, plane_rows(low_ref, ys)))
    x = planes - 1
    below = rows_ref[place_of(x - 1, planes)]
    moved = move_plane(same, count, ahead_ref[x], back_ref[x - 1], plane_rows(high_ref, ys), below)
    set_right(right_ref, 1, moved)
    inner = (planes - 2) * depth
    lefts = [own_ref[:, inner:]] + [others_ref[k, :, inner:] for k in range(others_ref.shape[0])]
    project(lefts, right_ref[...], begun_ref, steps, refs, total_ref)


def move_y_kernel(
    sites, zs, rows_ref, others_ref, near_ref, far_ref, ahead_ref, back_ref, turned_ref, field_ref
):
    planes, depth, width = rows_ref.shape
    groups = others_ref.shape[0] + 1
    row_size = depth // sites * zs
    reach = depth + near_ref.shape[1]
    head = back_ref.shape[2] - 128
    site, lane = iotas((sites, reach))
    inner = lane < depth
    upper = (lane >= depth) & (lane < depth + row_size)
    lower = (lane >= depth + row_size) & (lane < depth + 2 * row_size)
    lane_z = lane % zs
    to_next = (inner & (lane % sites == site + zs)) | (upper & (site == sites - zs + lane_z))
    to_last = (inner & (lane % sites == site - zs)) | (lower & (site == lane_z))
    to_next = jnp.where(to_next, -1.0, 0.0)
    to_last = jnp.where(to_last, -1.0, 0.0)
    _, lane = iotas((8, 128))
    for x in range(planes):
        past = near_ref[x, 2 * row_size : 2 * row_size + 8, :128].astype(jnp.float32)
        mixed = jnp.where(lane >= depth + row_size - head, past, back_ref[x, :, head:])
        back = jnp.concatenate([back_ref[x, :, :head], mixed], axis=1)[:, :reach]
        matrix = site_matrix([(ahead_ref[x, :, :reach], to_next), (back, to_last)], depth // sites)
        place = place_of(x, planes)
        column = jnp.concatenate([rows_ref[place], near_ref[x]], axis=0)
        field_ref[0, place] = dot(matrix, column).astype(jnp.bfloat16)
        for k in range(groups - 1):
            column = jnp.concatenate([others_ref[k, place], far_ref[k, x]], axis=0)
            field_ref[k + 1, place] = dot(matrix, column).astype(jnp.bfloat16)
    for k in range(groups):
        turned_ref[k] = field_ref[k].reshape(planes * depth, width).T


def second_kernel(steps, lefts_ref, right_ref, begun_ref, *refs):
    *refs, total_ref = refs
    inner = lefts_ref.shape[2] - right_ref.shape[0]
    lefts = [lefts_ref[k, :, inner:] for k in range(lefts_ref.shape[0])]
    project(lefts, right_ref[...], begun_ref, steps, refs, total_ref)


def swap(block, axis, bit):
    return lax.ppermute(block, axis, [(i, i ^ (1 << bit)) for i in range(lax.axis_size(axis))])


def merge_kernel(axis, bit, kept_ref, came_ref, keep_ref, send_ref):
    mine = my_bit(axis, bit)
    for gx in range(keep_ref.shape[1]):
        for gy in range(keep_ref.shape[2]):
            pair = []
            for odd in range(2):
                at = (slice(None), 2 * gx + odd, gy) if axis == "gx" else (slice(None), gx, 2 * gy + odd)
                pair.append(kept_ref[at] + came_ref[at].astype(jnp.float32))
            keep_ref[:, gx, gy] = jnp.where(mine == 0, pair[0], pair[1])
            send_ref[:, gx, gy] = jnp.where(mine == 0, pair[1], pair[0]).astype(send_ref.dtype)


def sum_kernel(kept_ref, came_ref, send_ref):
    send_ref[...] = (kept_ref[...] + came_ref[...].astype(jnp.float32)).astype(send_ref.dtype)


def finish_kernel(*refs):
    out_ref = refs[-1]
    for d in range(out_ref.shape[0]):
        kept_ref, came_ref, crossed_ref = refs[3 * d : 3 * d + 3]
        total = kept_ref[:, 0, 0] + came_ref[:, 0, 0].astype(jnp.float32)
        out_ref[d] = total + crossed_ref[:, 0, 0].astype(jnp.float32)


class Reduction:
    def __init__(self, kept, sent, axis):
        *low, self.top = [("gx", bit) for bit in bits("gx")]
        across = [("gy", bit) for bit in bits("gy")]
        self.steps = across + low[1:] if axis == "gx" else across[1:] + low
        self.kept, self.came = kept, swap(sent, axis, 0)

    def halve(self, after, weight=0):
        (axis, bit), *self.steps = self.steps
        dim = ("gx", "gy").index(axis) + 1
        shape = self.kept.shape
        shape = shape[:dim] + (shape[dim] // 2,) + shape[dim + 1 :]

        def merge(*refs):
            merge_kernel(axis, bit, *refs)

        self.came, _ = lax.optimization_barrier((self.came, after))
        self.kept, sent = call(
            merge, (pltpu.VMEM(shape, jnp.float32), pltpu.VMEM(shape, jnp.bfloat16)), weight, [self.kept, self.came]
        )
        self.came = swap(sent, axis, bit)
        return self.kept

    def cross(self, after):
        self.came, _ = lax.optimization_barrier((self.came, after))
        sent = call(sum_kernel, pltpu.VMEM(self.kept.shape, jnp.bfloat16), 0, [self.kept, self.came])
        self.came = swap(sent, *self.top)
        return sent


def local(eigen_modes, links_first, links_second):
    f32, bf16 = jnp.float32, jnp.bfloat16
    parts, planes, ys, zs, colours, width = eigen_modes.shape
    sites = ys * zs
    depth = parts * colours * sites
    row_size = parts * colours * zs
    edge = -(-(2 * row_size + 8) // 16) * 16
    lanes = -(-(depth + 2 * row_size) // 128) * 128
    across_x, across_y, groups = (lax.axis_size(a) for a in ("gx", "gy", "ma"))
    rows = groups * width // (across_x * across_y)
    inner_depth = (planes - 2) * depth
    raw = eigen_modes.transpose(0, 1, 2, 4, 3, 5)

    def shape(*dims, dtype=bf16):
        return pltpu.VMEM(dims, dtype)

    field_shape = shape(planes, depth, width)
    turned_shape = shape(width, planes * depth)
    total_shape = shape(groups, width, parts * width, dtype=f32)
    link_shape = shape(planes, 8, lanes, dtype=f32)
    total = pltpu.VMEM(total_shape.shape, f32)
    step_flops = 2 * planes * depth * depth * width
    project_flops = 2 * groups * width * planes * depth * parts * width

    raw_others = [shifted(raw, "ma", -step) for step in range(1, groups)]
    raw_links_x, raw_links_y = (a.transpose(0, 1, 2, 3, 5, 4) for a in (links_first, links_second))
    maps = jnp.asarray(np.concatenate(lane_maps(parts, colours, planes, ys, zs, lanes)))
    past_maps = jnp.asarray(np.concatenate(lane_maps(parts, colours, 1, ys, zs, lanes)))
    inputs = [raw, raw_links_x, raw_links_y, maps]
    first_plane, last_plane, *inputs = call(
        edges_kernel,
        (
            shape(parts, ys, colours, zs, width), shape(parts, ys + colours, colours, zs, width),
            *(shape(*a.shape, dtype=a.dtype) for a in inputs[1:]),
        ),
        0,
        inputs,
        [pltpu.SemaphoreType.DMA((5,))],
        [pltpu.HBM] * len(inputs),
    )
    low = shifted(last_plane, "gx", 1)
    high = shifted(first_plane, "gx", -1)
    field, ends, ahead_x, back_x, ahead_y, back_y = call(
        prepare_kernel,
        (field_shape, shape(planes, edge, width), link_shape, link_shape, link_shape, link_shape),
        0,
        [raw] + inputs,
        [pltpu.VMEM(raw.shape, bf16), pltpu.SemaphoreType.DMA],
        [pltpu.HBM] + [pltpu.VMEM] * len(inputs),
    )
    near = shifted(ends, "gy", 1)
    if across_y != 2:
        ahead_row = lax.broadcasted_iota(jnp.int32, ends.shape, 1) < row_size
        near = jnp.where(ahead_row, shifted(ends, "gy", -1), near)

    first_steps, second_steps = ("gx", "gy"), ("gy", "gx")

    def split(steps):
        shapes = []
        for axis in steps:
            dims = (across_x // 4, across_y) if axis == "gx" else (across_x // 2, across_y // 2)
            shapes += [shape(parts, *dims, rows, width, dtype=dtype) for dtype in (f32, bf16)]
        return shapes

    def inner(*refs):
        inner_kernel(sites, *refs)

    def first(*refs):
        first_kernel(sites, first_steps, *refs)

    def second(*refs):
        second_kernel(second_steps, *refs)

    def move_y(*refs):
        move_y_kernel(sites, zs, *refs)

    right, own = call(
        inner, (shape(inner_depth, parts * width), turned_shape), 2 * step_flops, [field, ahead_x, back_x]
    )
    turned = [call(turn_kernel, (field_shape, turned_shape), step_flops // 4, [r]) for r in raw_others]
    fields = jnp.stack([t[0] for t in turned])
    others = jnp.stack([t[1] for t in turned])
    begun_first = call(begin_first_kernel, total_shape, project_flops, [own, others, right])
    *parts_first, right_edge = call(
        first,
        (*split(first_steps), shape(2 * depth, parts * width)),
        project_flops,
        [field, high, low, ahead_x, back_x, past_maps, own, others, begun_first],
        [total],
    )
    near, right_edge = lax.optimization_barrier((near, right_edge))
    far = jnp.stack([shifted(near, "ma", -step) for step in range(1, groups)])
    lefts = call(
        move_y, shape(groups, width, planes * depth), 2 * step_flops,
        [field, fields, near, far, ahead_y, back_y],
        [pltpu.VMEM((groups,) + field_shape.shape, bf16)],
    )
    begun_second = call(begin_second_kernel, total_shape, project_flops, [lefts, right])
    parts_second = call(
        second, split(second_steps), project_flops, [lefts, right_edge, begun_second], [total]
    )
    crossing = [
        Reduction(*parts_first[:2], first_steps[0]), Reduction(*parts_second[:2], second_steps[0])
    ]
    after = crossing[0].halve(parts_second[0])
    kept, sent = parts_first[2:]
    sent, _ = lax.optimization_barrier((sent, after))
    staying = [Reduction(kept, sent, first_steps[1]), Reduction(*parts_second[2:], second_steps[1])]
    after = crossing[1].halve(after)
    while any(r.steps for r in crossing):
        for r in crossing:
            if r.steps:
                after = r.halve(after)
    for r in crossing:
        after = r.cross(after)
    weights = (0, 4 * project_flops)
    while any(r.steps for r in staying):
        for r in staying[::-1]:
            if r.steps:
                after = r.halve(after, weights[r is staying[1]])
    sums = []
    for stay, cross in zip(staying, crossing):
        sums += [stay.kept, stay.came, cross.came]
    return call(finish_kernel, jax.ShapeDtypeStruct((2, parts, rows, width), f32), 0, sums)


def solution(mesh):
    return jax.shard_map(
        local,
        mesh=mesh,
        in_specs=(
            P("cuts", "gx", "gy", None, None, "ma"),
            P("cuts", None, None, "gx", "gy", None),
            P("cuts", None, None, "gx", "gy", None),
        ),
        out_specs=P("cuts", None, ("gx", "gy"), "ma"),
        check_vma=False,
    )
```

```python
import jax
import jax.numpy as jnp
from jax import lax
from jax.experimental import pallas as pl
from jax.experimental.pallas import tpu as pltpu
from jax.sharding import PartitionSpec as P

VMEM_LIMIT = 16 * 1024 * 1024


def shifted(block, axis, distance):
    devices = range(lax.axis_size(axis))
    route = [((i - distance) % len(devices), i) for i in devices]
    return lax.ppermute(block, axis, route)


def call(body, out_shape, flops, operands, scratch=(), places=None):
    places = places or [pltpu.VMEM] * len(operands)
    return pl.pallas_call(
        body,
        out_shape=out_shape,
        in_specs=[pl.BlockSpec(memory_space=place) for place in places],
        scratch_shapes=scratch,
        cost_estimate=pl.CostEstimate(flops=flops // 2, bytes_accessed=0, transcendentals=0),
        compiler_params=pltpu.CompilerParams(vmem_limit_bytes=VMEM_LIMIT),
    )(*(pltpu.with_memory_space_constraint(a, place) for a, place in zip(operands, places)))


def dot(a, b):
    return jnp.dot(a, b, preferred_element_type=jnp.float32)


def iotas(shape):
    return (
        lax.broadcasted_iota(jnp.int32, shape, 0),
        lax.broadcasted_iota(jnp.int32, shape, 1),
    )


def place_of(x, planes):
    return planes - 2 if x == 0 else x if x == planes - 1 else x - 1


def map_rows(parts, colours, planes, ys, zs):
    match = ys
    choose = match + -(-parts * colours * colours * planes * zs // 8) * 8
    first_part = choose + 2 * parts * planes * 8
    return match, choose, first_part, first_part + 8


def write_maps(ref, parts, colours, planes, ys, zs):
    lanes = ref.shape[1] // 2
    sites = ys * zs
    depth = parts * colours * sites
    row_size = parts * colours * zs
    match, choose, first_part, _ = map_rows(parts, colours, planes, ys, zs)

    def ones(mask):
        return jnp.where(mask, 1.0, 0.0)

    def column(count):
        return lax.broadcasted_iota(jnp.int32, (count, 1), 0)

    def line(count):
        return lax.broadcasted_iota(jnp.int32, (1, count), 1)

    lane = line(lanes)
    inner = lane < depth
    past = lax.rem(jnp.maximum(lane - depth, 0), row_size)
    used = lane < depth + 2 * row_size
    part = jnp.where(inner, lax.div(lane, colours * sites), lax.div(past, colours * zs))
    colour = lax.rem(jnp.where(inner, lax.div(lane, sites), lax.div(past, zs)), colours)
    z = lax.rem(jnp.where(inner, lane, past), zs)
    y = lax.div(lax.rem(lane, sites), zs)
    ref[:ys, :lanes] = ones(column(ys) == jnp.where(inner, y, ys - 1))
    ref[:ys, lanes:] = ones(column(ys) == jnp.where(inner, y, ys) - 1)

    count = parts * colours * colours * planes * zs

    def link(index):
        x = lax.rem(lax.div(index, zs), planes)
        right = lax.rem(lax.div(index, zs * planes), colours)
        left = lax.rem(lax.div(index, zs * planes * colours), colours)
        return x, right, left, lax.div(index, zs * planes * colours * colours)

    row = column(count)
    _, right, left, _ = link(row)
    row_z = lax.rem(row, zs)
    key = jnp.where(used, colour * zs + z, -1)
    ref[match : match + count, :lanes] = ones(right * zs + row_z == key)
    ref[match : match + count, lanes:] = ones(left * zs + row_z == key)

    out = column(parts * planes * 8)
    field_part = lax.div(out, planes * 8)
    out_x = lax.rem(lax.div(out, 8), planes)
    out_part = lax.div(lax.rem(out, 8), colours)
    out_colour = lax.rem(lax.rem(out, 8), colours)
    x, right, left, source_part = link(line(count))
    source = source_part * planes + x
    wanted = jnp.where(out_part < parts, lax.rem(out_part + field_part, 2) * planes + out_x, -1)
    sign_ahead = jnp.where((field_part == 1) & (out_part == 0), -1.0, 1.0)
    sign_back = jnp.where((field_part == 0) & (out_part == 1), 1.0, -1.0)
    half = parts * planes * 8
    for start, end, sign in ((choose, left, sign_ahead), (choose + half, right, sign_back)):
        hit = source * colours + end == wanted * colours + jnp.where(wanted < 0, -1, out_colour)
        ref[start : start + half, :count] = jnp.where(hit, sign, 0.0)
    ref[first_part:, :lanes] = jnp.broadcast_to(ones(part == 0), (8, lanes))


def coefficients(links_x, links_y, maps_ref, planes):
    lanes = maps_ref.shape[1] // 2
    ys = links_x.shape[1]
    count = links_x.shape[0]
    half = 2 * planes * 8
    wide = dot(jnp.concatenate([links_x, links_y], axis=0), maps_ref[:ys].astype(jnp.bfloat16))
    match = maps_ref[ys : ys + count]
    match_ahead, match_back = match[:, :lanes], match[:, lanes:]
    choose = maps_ref[ys + count : ys + count + 2 * half, :count].astype(jnp.bfloat16)
    first_part = maps_ref[ys + count + 2 * half : ys + count + 2 * half + 1, :lanes] > 0.5
    ahead = jnp.concatenate([wide[:count, :lanes] * match_ahead, wide[count:, lanes:] * match_ahead], axis=1)
    back = jnp.concatenate([wide[:count, :lanes] * match_back, wide[count:, :lanes] * match_back], axis=1)
    out = []
    for chosen in (
        dot(choose[:half], ahead.astype(jnp.bfloat16)), dot(choose[half:], back.astype(jnp.bfloat16))
    ):
        for start in (0, lanes):
            part = chosen[:, start : start + lanes]
            rows = jnp.where(first_part, part[: half // 2], part[half // 2 :])
            out.append(rows.reshape(planes, 8, lanes))
    return out


def plane_rows(ref, ys):
    parts, _, colours, zs, width = ref.shape
    return jnp.concatenate(
        [ref[p, :ys, c].reshape(ys * zs, width) for p in range(parts) for c in range(colours)],
        axis=0,
    )


def edges_kernel(
    raw_hbm, links_x_hbm, links_y_hbm,
    first_ref, last_ref, raw_ref, links_x_ref, links_y_ref, maps_ref, past_maps_ref, arrived,
):
    parts, planes, ys, colours, zs, _ = raw_hbm.shape
    sources = (raw_hbm.at[:, planes - 1], raw_hbm.at[:, 0], links_x_hbm, links_y_hbm, raw_hbm)
    targets = (last_ref.at[:, :ys], first_ref, links_x_ref, links_y_ref, raw_ref)
    copies = [
        pltpu.make_async_copy(source, target, arrived.at[i])
        for i, (source, target) in enumerate(zip(sources, targets))
    ]
    for copy in copies:
        copy.start()
    last_ref[:, ys:] = jnp.zeros((parts, colours) + last_ref.shape[2:], last_ref.dtype)
    write_maps(maps_ref, parts, colours, planes, ys, zs)
    write_maps(past_maps_ref, parts, colours, 1, ys, zs)
    copies[2].wait()
    last_ref[:, ys:, :, :, :ys] = links_x_ref[:, :, :, planes - 1]
    for copy in copies[:2] + copies[3:]:
        copy.wait()


def site_matrix(rows_and_masks, count):
    blocks = []
    for q in range(count):
        block = None
        for rows, mask in rows_and_masks:
            term = rows[q : q + 1] * mask
            block = term if block is None else block + term
        blocks.append(block.astype(jnp.bfloat16))
    return jnp.concatenate(blocks, axis=0)


def prepare_kernel(
    raw_ref, links_x_ref, links_y_ref, maps_ref,
    rows_ref, ends_ref, ahead_x_ref, back_x_ref, ahead_y_ref, back_y_ref,
):
    planes, depth, width = rows_ref.shape
    zs = raw_ref.shape[4]
    ys = raw_ref.shape[2]
    sites = ys * zs
    row_size = depth // sites * zs
    lanes = ahead_y_ref.shape[2]
    ahead_x, ahead_y, back_x, back_y = coefficients(
        links_x_ref[...].reshape(-1, ys), links_y_ref[...].reshape(-1, ys), maps_ref, planes
    )
    ahead_x_ref[...] = ahead_x
    back_x_ref[...] = back_x
    ahead_y_ref[...] = ahead_y
    back_y_ref[...] = back_y

    row, lane = iotas((2 * row_size, depth))
    spot = row % row_size
    wanted = (spot // zs) * sites + spot % zs + jnp.where(row < row_size, 0, sites - zs)
    ends = (lane == wanted).astype(jnp.bfloat16)
    filler = jnp.zeros((8, width - 128), jnp.float32)
    spare = ends_ref.shape[1] - 2 * row_size - 8
    for x in range(planes):
        plane = plane_rows(raw_ref.at[:, x], ys)
        rows_ref[place_of(x, planes)] = plane
        tail = jnp.concatenate([back_y[x, :, lanes - 128 :], filler], axis=1)
        pieces = [dot(ends, plane), tail]
        if spare:
            pieces.append(jnp.zeros((spare, width), jnp.float32))
        ends_ref[x] = jnp.concatenate(pieces, axis=0).astype(jnp.bfloat16)


def turn_kernel(raw_ref, rows_ref, turned_ref):
    planes, depth, width = rows_ref.shape
    for x in range(planes):
        rows_ref[place_of(x, planes)] = plane_rows(raw_ref.at[:, x], raw_ref.shape[2])
    turned_ref[...] = rows_ref[...].reshape(planes * depth, width).T


def move_plane(same, count, ahead, back, above, below):
    depth = same.shape[1]
    moved = dot(site_matrix([(ahead[:, :depth], same)], count), above)
    return (moved + dot(site_matrix([(back[:, :depth], same)], count), below)).astype(jnp.bfloat16)


def same_site(sites, depth):
    site, lane = iotas((sites, depth))
    return (lane % sites == site).astype(jnp.float32)


def set_right(right_ref, place, moved):
    depth, width = moved.shape
    half = depth // 2
    start = place * depth
    real, imag = moved[:half], moved[half:]
    right_ref[start : start + half, :width] = real
    right_ref[start : start + half, width:] = imag
    right_ref[start + half : start + depth, :width] = imag
    right_ref[start + half : start + depth, width:] = -real


def inner_kernel(sites, rows_ref, ahead_ref, back_ref, right_ref, turned_ref):
    planes, depth, width = rows_ref.shape
    same = same_site(sites, depth)
    for x in range(1, planes - 1):
        above = rows_ref[place_of(x + 1, planes)]
        below = rows_ref[place_of(x - 1, planes)]
        moved = move_plane(same, depth // sites, ahead_ref[x], back_ref[x - 1], above, below)
        set_right(right_ref, place_of(x, planes), moved)
    turned_ref[...] = rows_ref[...].reshape(planes * depth, width).T


def begin_first_kernel(own_ref, others_ref, right_ref, total_ref):
    inner = right_ref.shape[0]
    right = right_ref[...]
    total_ref[0] = dot(own_ref[:, :inner], right)
    for k in range(others_ref.shape[0]):
        total_ref[k + 1] = dot(others_ref[k, :, :inner], right)


def begin_second_kernel(lefts_ref, right_ref, total_ref):
    inner = right_ref.shape[0]
    right = right_ref[...]
    for k in range(lefts_ref.shape[0]):
        total_ref[k] = dot(lefts_ref[k, :, :inner], right)


def bits(axis):
    return range(lax.axis_size(axis).bit_length() - 1)


def my_bit(axis, bit):
    return lax.bitwise_and(lax.shift_right_logical(lax.axis_index(axis), bit), 1)


def project(lefts, right, begun_ref, steps, refs, total_ref):
    for k, left in enumerate(lefts):
        total_ref[k] = begun_ref[k] + dot(left, right)
    groups, own_modes, _ = total_ref.shape
    my_modes = lax.axis_index("ma")
    top = my_bit("gx", bits("gx")[-1])
    across_x, across_y = lax.axis_size("gx"), lax.axis_size("gy")
    rows, width = refs[0].shape[3:]

    def piece(gx, gy):
        start = (gx * across_y + gy) * rows
        group = lax.rem(start // own_modes + groups - my_modes, groups)
        begin = start % own_modes
        return total_ref[group, begin : begin + rows]

    for kind, axis in enumerate(steps):
        keep_ref, send_ref = refs[2 * kind : 2 * kind + 2]
        mine = my_bit(axis, 0)
        half = lax.bitwise_xor(top, 1 - kind)

        def chosen(gx, gy):
            return jnp.where(half == 0, piece(gx, gy), piece(gx + across_x // 2, gy))

        for gx in range(keep_ref.shape[1]):
            for gy in range(keep_ref.shape[2]):
                if axis == "gx":
                    even, odd = chosen(2 * gx, gy), chosen(2 * gx + 1, gy)
                else:
                    even, odd = chosen(gx, 2 * gy), chosen(gx, 2 * gy + 1)
                keep = jnp.where(mine == 0, even, odd)
                send = jnp.where(mine == 0, odd, even).astype(send_ref.dtype)
                for p in range(keep_ref.shape[0]):
                    keep_ref[p, gx, gy] = keep[:, p * width : (p + 1) * width]
                    send_ref[p, gx, gy] = send[:, p * width : (p + 1) * width]


def first_kernel(
    sites, steps, rows_ref, high_ref, low_ref, ahead_ref, back_ref, past_maps_ref, own_ref, others_ref, begun_ref,
    *refs,
):
    *refs, right_ref, total_ref = refs
    planes, depth, _ = rows_ref.shape
    same = same_site(sites, depth)
    count = depth // sites
    _, ys, colours, zs, _ = high_ref.shape
    links = low_ref[:, ys:, :, :, :ys].reshape(-1, ys)
    lanes = past_maps_ref.shape[1] // 2
    count = links.shape[0]
    spread = past_maps_ref[:ys, :lanes].astype(jnp.bfloat16)
    match = past_maps_ref[ys : ys + count, lanes:]
    start = past_maps_ref.shape[0] - 24
    choose = past_maps_ref[start : start + 16, :count].astype(jnp.bfloat16)
    past = dot(choose, (dot(links, spread) * match).astype(jnp.bfloat16))
    past = jnp.where(past_maps_ref[start + 16 : start + 17, :lanes] > 0.5, past[:8], past[8:])
    count = depth // sites
    above = rows_ref[place_of(1, planes)]
    set_right(right_ref, 0, move_plane(same, count, ahead_ref[0], past, above, plane_rows(low_ref, ys)))
    x = planes - 1
    below = rows_ref[place_of(x - 1, planes)]
    moved = move_plane(same, count, ahead_ref[x], back_ref[x - 1], plane_rows(high_ref, ys), below)
    set_right(right_ref, 1, moved)
    inner = (planes - 2) * depth
    lefts = [own_ref[:, inner:]] + [others_ref[k, :, inner:] for k in range(others_ref.shape[0])]
    project(lefts, right_ref[...], begun_ref, steps, refs, total_ref)


def move_y_kernel(
    sites, zs, rows_ref, others_ref, near_ref, far_ref, ahead_ref, back_ref, turned_ref, field_ref
):
    planes, depth, width = rows_ref.shape
    groups = others_ref.shape[0] + 1
    row_size = depth // sites * zs
    reach = depth + near_ref.shape[1]
    head = back_ref.shape[2] - 128
    site, lane = iotas((sites, reach))
    inner = lane < depth
    upper = (lane >= depth) & (lane < depth + row_size)
    lower = (lane >= depth + row_size) & (lane < depth + 2 * row_size)
    lane_z = lane % zs
    to_next = (inner & (lane % sites == site + zs)) | (upper & (site == sites - zs + lane_z))
    to_last = (inner & (lane % sites == site - zs)) | (lower & (site == lane_z))
    to_next = jnp.where(to_next, -1.0, 0.0)
    to_last = jnp.where(to_last, -1.0, 0.0)
    _, lane = iotas((8, 128))
    spare = jnp.zeros((near_ref.shape[1] - far_ref.shape[2], width), far_ref.dtype)
    for x in range(planes):
        past = near_ref[x, 2 * row_size : 2 * row_size + 8, :128].astype(jnp.float32)
        mixed = jnp.where(lane >= depth + row_size - head, past, back_ref[x, :, head:])
        back = jnp.concatenate([back_ref[x, :, :head], mixed], axis=1)[:, :reach]
        matrix = site_matrix([(ahead_ref[x, :, :reach], to_next), (back, to_last)], depth // sites)
        place = place_of(x, planes)
        column = jnp.concatenate([rows_ref[place], near_ref[x]], axis=0)
        field_ref[0, place] = dot(matrix, column).astype(jnp.bfloat16)
        for k in range(groups - 1):
            column = jnp.concatenate([others_ref[k, place], far_ref[k, x], spare], axis=0)
            field_ref[k + 1, place] = dot(matrix, column).astype(jnp.bfloat16)
    for k in range(groups):
        turned_ref[k] = field_ref[k].reshape(planes * depth, width).T


def second_kernel(steps, lefts_ref, right_ref, begun_ref, *refs):
    *refs, total_ref = refs
    inner = lefts_ref.shape[2] - right_ref.shape[0]
    lefts = [lefts_ref[k, :, inner:] for k in range(lefts_ref.shape[0])]
    project(lefts, right_ref[...], begun_ref, steps, refs, total_ref)


def swap(block, axis, bit):
    return lax.ppermute(block, axis, [(i, i ^ (1 << bit)) for i in range(lax.axis_size(axis))])


def merge_kernel(axis, bit, kept_ref, came_ref, keep_ref, send_ref):
    mine = my_bit(axis, bit)
    for gx in range(keep_ref.shape[1]):
        for gy in range(keep_ref.shape[2]):
            pair = []
            for odd in range(2):
                at = (slice(None), 2 * gx + odd, gy) if axis == "gx" else (slice(None), gx, 2 * gy + odd)
                pair.append(kept_ref[at] + came_ref[at].astype(jnp.float32))
            keep_ref[:, gx, gy] = jnp.where(mine == 0, pair[0], pair[1])
            send_ref[:, gx, gy] = jnp.where(mine == 0, pair[1], pair[0]).astype(send_ref.dtype)


def sum_kernel(kept_ref, came_ref, send_ref):
    send_ref[...] = (kept_ref[...] + came_ref[...].astype(jnp.float32)).astype(send_ref.dtype)


def finish_kernel(*refs):
    out_ref = refs[-1]
    for d in range(out_ref.shape[0]):
        kept_ref, came_ref, crossed_ref = refs[3 * d : 3 * d + 3]
        total = kept_ref[:, 0, 0] + came_ref[:, 0, 0].astype(jnp.float32)
        out_ref[d] = total + crossed_ref[:, 0, 0].astype(jnp.float32)


class Reduction:
    def __init__(self, kept, sent, axis):
        *low, self.top = [("gx", bit) for bit in bits("gx")]
        across = [("gy", bit) for bit in bits("gy")]
        self.steps = across + low[1:] if axis == "gx" else across[1:] + low
        self.kept, self.came = kept, swap(sent, axis, 0)

    def halve(self, after, weight=0):
        (axis, bit), *self.steps = self.steps
        dim = ("gx", "gy").index(axis) + 1
        shape = self.kept.shape
        shape = shape[:dim] + (shape[dim] // 2,) + shape[dim + 1 :]

        def merge(*refs):
            merge_kernel(axis, bit, *refs)

        self.came, _ = lax.optimization_barrier((self.came, after))
        self.kept, sent = call(
            merge, (pltpu.VMEM(shape, jnp.float32), pltpu.VMEM(shape, jnp.bfloat16)), weight, [self.kept, self.came]
        )
        self.came = swap(sent, axis, bit)
        return self.kept

    def cross(self, after):
        self.came, _ = lax.optimization_barrier((self.came, after))
        sent = call(sum_kernel, pltpu.VMEM(self.kept.shape, jnp.bfloat16), 0, [self.kept, self.came])
        self.came = swap(sent, *self.top)
        return sent


def local(eigen_modes, links_first, links_second):
    f32, bf16 = jnp.float32, jnp.bfloat16
    parts, planes, ys, zs, colours, width = eigen_modes.shape
    sites = ys * zs
    depth = parts * colours * sites
    row_size = parts * colours * zs
    edge = -(-(2 * row_size + 8) // 16) * 16
    lanes = -(-(depth + 2 * row_size) // 128) * 128
    across_x, across_y, groups = (lax.axis_size(a) for a in ("gx", "gy", "ma"))
    rows = groups * width // (across_x * across_y)
    inner_depth = (planes - 2) * depth
    raw = eigen_modes.transpose(0, 1, 2, 4, 3, 5)

    def shape(*dims, dtype=bf16):
        return pltpu.VMEM(dims, dtype)

    field_shape = shape(planes, depth, width)
    turned_shape = shape(width, planes * depth)
    total_shape = shape(groups, width, parts * width, dtype=f32)
    link_shape = shape(planes, 8, lanes, dtype=f32)
    total = pltpu.VMEM(total_shape.shape, f32)
    step_flops = 2 * planes * depth * depth * width
    project_flops = 2 * groups * width * planes * depth * parts * width

    raw_others = [shifted(raw, "ma", -step) for step in range(1, groups)]
    raw_links_x, raw_links_y = (a.transpose(0, 1, 2, 3, 5, 4) for a in (links_first, links_second))
    inputs = [raw, raw_links_x, raw_links_y]
    first_plane, last_plane, *inputs, past_maps = call(
        edges_kernel,
        (
            shape(parts, ys, colours, zs, width), shape(parts, ys + colours, colours, zs, width),
            *(shape(*a.shape) for a in inputs),
            shape(map_rows(parts, colours, planes, ys, zs)[-1], 2 * lanes, dtype=f32),
            shape(map_rows(parts, colours, 1, ys, zs)[-1], 2 * lanes, dtype=f32),
        ),
        0,
        inputs,
        [pltpu.SemaphoreType.DMA((5,))],
        [pltpu.HBM] * len(inputs),
    )
    low = shifted(last_plane, "gx", 1)
    high = shifted(first_plane, "gx", -1)
    field, ends, ahead_x, back_x, ahead_y, back_y = call(
        prepare_kernel,
        (field_shape, shape(planes, edge, width), link_shape, link_shape, link_shape, link_shape),
        0,
        inputs,
    )
    near = shifted(ends, "gy", 1)
    if across_y != 2:
        ahead_row = lax.broadcasted_iota(jnp.int32, ends.shape, 1) < row_size
        near = jnp.where(ahead_row, shifted(ends, "gy", -1), near)

    first_steps, second_steps = ("gx", "gy"), ("gy", "gx")

    def split(steps):
        shapes = []
        for axis in steps:
            dims = (across_x // 4, across_y) if axis == "gx" else (across_x // 2, across_y // 2)
            shapes += [shape(parts, *dims, rows, width, dtype=dtype) for dtype in (f32, bf16)]
        return shapes

    def inner(*refs):
        inner_kernel(sites, *refs)

    def first(*refs):
        first_kernel(sites, first_steps, *refs)

    def second(*refs):
        second_kernel(second_steps, *refs)

    def move_y(*refs):
        move_y_kernel(sites, zs, *refs)

    right, own = call(
        inner, (shape(inner_depth, parts * width), turned_shape), 2 * step_flops, [field, ahead_x, back_x]
    )
    turned = [call(turn_kernel, (field_shape, turned_shape), step_flops // 4, [r]) for r in raw_others]
    fields = jnp.stack([t[0] for t in turned])
    others = jnp.stack([t[1] for t in turned])
    begun_first = call(begin_first_kernel, total_shape, project_flops, [own, others, right])
    *parts_first, right_edge = call(
        first,
        (*split(first_steps), shape(2 * depth, parts * width)),
        project_flops,
        [field, high, low, ahead_x, back_x, past_maps, own, others, begun_first],
        [total],
    )
    near, right_edge = lax.optimization_barrier((near, right_edge))
    near_rows = near[:, : 2 * row_size]
    far = jnp.stack([shifted(near_rows, "ma", -step) for step in range(1, groups)])
    lefts = call(
        move_y, shape(groups, width, planes * depth), 2 * step_flops,
        [field, fields, near, far, ahead_y, back_y],
        [pltpu.VMEM((groups,) + field_shape.shape, bf16)],
    )
    begun_second = call(begin_second_kernel, total_shape, project_flops, [lefts, right])
    parts_second = call(
        second, split(second_steps), project_flops, [lefts, right_edge, begun_second], [total]
    )
    crossing = [
        Reduction(*parts_first[:2], first_steps[0]), Reduction(*parts_second[:2], second_steps[0])
    ]
    after = crossing[0].halve(parts_second[0])
    kept, sent = parts_first[2:]
    sent, _ = lax.optimization_barrier((sent, after))
    staying = [Reduction(kept, sent, first_steps[1]), Reduction(*parts_second[2:], second_steps[1])]
    after = crossing[1].halve(after)
    while any(r.steps for r in crossing):
        for r in crossing:
            if r.steps:
                after = r.halve(after)
    for r in crossing:
        after = r.cross(after)
    weights = (0, 4 * project_flops)
    while any(r.steps for r in staying):
        for r in staying[::-1]:
            if r.steps:
                after = r.halve(after, weights[r is staying[1]])
    sums = []
    for stay, cross in zip(staying, crossing):
        sums += [stay.kept, stay.came, cross.came]
    return call(finish_kernel, jax.ShapeDtypeStruct((2, parts, rows, width), f32), 0, sums)


def solution(mesh):
    return jax.shard_map(
        local,
        mesh=mesh,
        in_specs=(
            P("cuts", "gx", "gy", None, None, "ma"),
            P("cuts", None, None, "gx", "gy", None),
            P("cuts", None, None, "gx", "gy", None),
        ),
        out_specs=P("cuts", None, ("gx", "gy"), "ma"),
        check_vma=False,
    )
```

```python
import jax
import jax.numpy as jnp
from jax import lax
from jax.experimental import pallas as pl
from jax.experimental.pallas import tpu as pltpu
from jax.sharding import PartitionSpec as P

VMEM_LIMIT = 16 * 1024 * 1024


def shifted(block, axis, distance):
    devices = range(lax.axis_size(axis))
    route = [((i - distance) % len(devices), i) for i in devices]
    return lax.ppermute(block, axis, route)


def call(body, out_shape, flops, operands, scratch=(), places=None):
    places = places or [pltpu.VMEM] * len(operands)
    return pl.pallas_call(
        body,
        out_shape=out_shape,
        in_specs=[pl.BlockSpec(memory_space=place) for place in places],
        scratch_shapes=scratch,
        cost_estimate=pl.CostEstimate(flops=flops // 2, bytes_accessed=0, transcendentals=0),
        compiler_params=pltpu.CompilerParams(vmem_limit_bytes=VMEM_LIMIT),
    )(*(pltpu.with_memory_space_constraint(a, place) for a, place in zip(operands, places)))


def dot(a, b):
    return jnp.dot(a, b, preferred_element_type=jnp.float32)


def iotas(shape):
    return (
        lax.broadcasted_iota(jnp.int32, shape, 0),
        lax.broadcasted_iota(jnp.int32, shape, 1),
    )


def place_of(x, planes):
    return planes - 2 if x == 0 else x if x == planes - 1 else x - 1


def map_rows(parts, colours, planes, ys, zs):
    match = ys
    choose = match + -(-parts * colours * colours * planes * zs // 8) * 8
    first_part = choose + 2 * parts * planes * 8
    return match, choose, first_part, first_part + 8


def write_maps(ref, parts, colours, planes, ys, zs):
    lanes = ref.shape[1] // 2
    sites = ys * zs
    depth = parts * colours * sites
    row_size = parts * colours * zs
    match, choose, first_part, _ = map_rows(parts, colours, planes, ys, zs)

    def ones(mask):
        return jnp.where(mask, 1.0, 0.0)

    def column(count):
        return lax.broadcasted_iota(jnp.int32, (count, 1), 0)

    def line(count):
        return lax.broadcasted_iota(jnp.int32, (1, count), 1)

    lane = line(lanes)
    inner = lane < depth
    past = lax.rem(jnp.maximum(lane - depth, 0), row_size)
    used = lane < depth + 2 * row_size
    part = jnp.where(inner, lax.div(lane, colours * sites), lax.div(past, colours * zs))
    colour = lax.rem(jnp.where(inner, lax.div(lane, sites), lax.div(past, zs)), colours)
    z = lax.rem(jnp.where(inner, lane, past), zs)
    y = lax.div(lax.rem(lane, sites), zs)
    ref[:ys, :lanes] = ones(column(ys) == jnp.where(inner, y, ys - 1))
    ref[:ys, lanes:] = ones(column(ys) == jnp.where(inner, y, ys) - 1)

    count = parts * colours * colours * planes * zs

    def link(index):
        x = lax.rem(lax.div(index, zs), planes)
        right = lax.rem(lax.div(index, zs * planes), colours)
        left = lax.rem(lax.div(index, zs * planes * colours), colours)
        return x, right, left, lax.div(index, zs * planes * colours * colours)

    row = column(count)
    _, right, left, _ = link(row)
    row_z = lax.rem(row, zs)
    key = jnp.where(used, colour * zs + z, -1)
    ref[match : match + count, :lanes] = ones(right * zs + row_z == key)
    ref[match : match + count, lanes:] = ones(left * zs + row_z == key)

    out = column(parts * planes * 8)
    field_part = lax.div(out, planes * 8)
    out_x = lax.rem(lax.div(out, 8), planes)
    out_part = lax.div(lax.rem(out, 8), colours)
    out_colour = lax.rem(lax.rem(out, 8), colours)
    x, right, left, source_part = link(line(count))
    source = source_part * planes + x
    wanted = jnp.where(out_part < parts, lax.rem(out_part + field_part, 2) * planes + out_x, -1)
    sign_ahead = jnp.where((field_part == 1) & (out_part == 0), -1.0, 1.0)
    sign_back = jnp.where((field_part == 0) & (out_part == 1), 1.0, -1.0)
    half = parts * planes * 8
    for start, end, sign in ((choose, left, sign_ahead), (choose + half, right, sign_back)):
        hit = source * colours + end == wanted * colours + jnp.where(wanted < 0, -1, out_colour)
        ref[start : start + half, :count] = jnp.where(hit, sign, 0.0)
    ref[first_part:, :lanes] = jnp.broadcast_to(ones(part == 0), (8, lanes))


def coefficients(links_x, links_y, maps_ref, planes):
    lanes = maps_ref.shape[1] // 2
    ys = links_x.shape[1]
    count = links_x.shape[0]
    half = 2 * planes * 8
    wide = dot(jnp.concatenate([links_x, links_y], axis=0), maps_ref[:ys].astype(jnp.bfloat16))
    match = maps_ref[ys : ys + count]
    match_ahead, match_back = match[:, :lanes], match[:, lanes:]
    choose = maps_ref[ys + count : ys + count + 2 * half, :count].astype(jnp.bfloat16)
    first_part = maps_ref[ys + count + 2 * half : ys + count + 2 * half + 1, :lanes] > 0.5
    ahead = jnp.concatenate([wide[:count, :lanes] * match_ahead, wide[count:, lanes:] * match_ahead], axis=1)
    back = jnp.concatenate([wide[:count, :lanes] * match_back, wide[count:, :lanes] * match_back], axis=1)
    out = []
    for chosen in (
        dot(choose[:half], ahead.astype(jnp.bfloat16)), dot(choose[half:], back.astype(jnp.bfloat16))
    ):
        for start in (0, lanes):
            part = chosen[:, start : start + lanes]
            rows = jnp.where(first_part, part[: half // 2], part[half // 2 :])
            out.append(rows.reshape(planes, 8, lanes))
    return out


def plane_rows(ref, ys):
    parts, _, colours, zs, width = ref.shape
    return jnp.concatenate(
        [ref[p, :ys, c].reshape(ys * zs, width) for p in range(parts) for c in range(colours)],
        axis=0,
    )


def edges_kernel(
    raw_hbm, links_x_hbm, links_y_hbm,
    first_ref, last_ref, raw_ref, links_x_ref, links_y_ref, maps_ref, past_maps_ref, arrived,
):
    parts, planes, ys, colours, zs, _ = raw_hbm.shape
    sources = (raw_hbm.at[:, planes - 1], raw_hbm.at[:, 0], links_x_hbm, links_y_hbm, raw_hbm)
    targets = (last_ref.at[:, :ys], first_ref, links_x_ref, links_y_ref, raw_ref)
    copies = [
        pltpu.make_async_copy(source, target, arrived.at[i])
        for i, (source, target) in enumerate(zip(sources, targets))
    ]
    for copy in copies:
        copy.start()
    last_ref[:, ys:] = jnp.zeros((parts, colours) + last_ref.shape[2:], last_ref.dtype)
    write_maps(maps_ref, parts, colours, planes, ys, zs)
    write_maps(past_maps_ref, parts, colours, 1, ys, zs)
    copies[2].wait()
    last_ref[:, ys:, :, :, :ys] = links_x_ref[:, :, :, planes - 1]
    for copy in copies[:2] + copies[3:]:
        copy.wait()


def site_matrix(rows_and_masks, count):
    blocks = []
    for q in range(count):
        block = None
        for rows, mask in rows_and_masks:
            term = rows[q : q + 1] * mask
            block = term if block is None else block + term
        blocks.append(block.astype(jnp.bfloat16))
    return jnp.concatenate(blocks, axis=0)


def prepare_kernel(
    raw_ref, links_x_ref, links_y_ref, maps_ref,
    rows_ref, ends_ref, ahead_x_ref, back_x_ref, ahead_y_ref, back_y_ref,
):
    planes, depth, width = rows_ref.shape
    zs = raw_ref.shape[4]
    ys = raw_ref.shape[2]
    sites = ys * zs
    row_size = depth // sites * zs
    lanes = ahead_y_ref.shape[2]
    ahead_x, ahead_y, back_x, back_y = coefficients(
        links_x_ref[...].reshape(-1, ys), links_y_ref[...].reshape(-1, ys), maps_ref, planes
    )
    ahead_x_ref[...] = ahead_x
    back_x_ref[...] = back_x
    ahead_y_ref[...] = ahead_y
    back_y_ref[...] = back_y

    row, lane = iotas((2 * row_size, depth))
    spot = row % row_size
    wanted = (spot // zs) * sites + spot % zs + jnp.where(row < row_size, 0, sites - zs)
    ends = (lane == wanted).astype(jnp.bfloat16)
    filler = jnp.zeros((8, width - 128), jnp.float32)
    spare = ends_ref.shape[1] - 2 * row_size - 8
    for x in range(planes):
        plane = plane_rows(raw_ref.at[:, x], ys)
        rows_ref[place_of(x, planes)] = plane
        tail = jnp.concatenate([back_y[x, :, lanes - 128 :], filler], axis=1)
        pieces = [dot(ends, plane), tail]
        if spare:
            pieces.append(jnp.zeros((spare, width), jnp.float32))
        ends_ref[x] = jnp.concatenate(pieces, axis=0).astype(jnp.bfloat16)


def turn_kernel(raw_ref, rows_ref, turned_ref):
    planes, depth, width = rows_ref.shape
    for x in range(planes):
        rows_ref[place_of(x, planes)] = plane_rows(raw_ref.at[:, x], raw_ref.shape[2])
    turned_ref[...] = rows_ref[...].reshape(planes * depth, width).T


def move_plane(same, count, ahead, back, above, below):
    depth = same.shape[1]
    moved = dot(site_matrix([(ahead[:, :depth], same)], count), above)
    return (moved + dot(site_matrix([(back[:, :depth], same)], count), below)).astype(jnp.bfloat16)


def same_site(sites, depth):
    site, lane = iotas((sites, depth))
    return (lane % sites == site).astype(jnp.float32)


def set_right(right_ref, place, moved):
    depth, width = moved.shape
    half = depth // 2
    start = place * depth
    real, imag = moved[:half], moved[half:]
    right_ref[start : start + half, :width] = real
    right_ref[start : start + half, width:] = imag
    right_ref[start + half : start + depth, :width] = imag
    right_ref[start + half : start + depth, width:] = -real


def inner_kernel(sites, rows_ref, ahead_ref, back_ref, right_ref, turned_ref):
    planes, depth, width = rows_ref.shape
    same = same_site(sites, depth)
    for x in range(1, planes - 1):
        above = rows_ref[place_of(x + 1, planes)]
        below = rows_ref[place_of(x - 1, planes)]
        moved = move_plane(same, depth // sites, ahead_ref[x], back_ref[x - 1], above, below)
        set_right(right_ref, place_of(x, planes), moved)
    turned_ref[...] = rows_ref[...].reshape(planes * depth, width).T


def begin_first_kernel(own_ref, others_ref, right_ref, total_ref):
    inner = right_ref.shape[0]
    right = right_ref[...]
    total_ref[0] = dot(own_ref[:, :inner], right)
    for k in range(others_ref.shape[0]):
        total_ref[k + 1] = dot(others_ref[k, :, :inner], right)


def begin_second_kernel(lefts_ref, right_ref, total_ref):
    inner = right_ref.shape[0]
    right = right_ref[...]
    for k in range(lefts_ref.shape[0]):
        total_ref[k] = dot(lefts_ref[k, :, :inner], right)


def bits(axis):
    return range(lax.axis_size(axis).bit_length() - 1)


def my_bit(axis, bit):
    return lax.bitwise_and(lax.shift_right_logical(lax.axis_index(axis), bit), 1)


def project(terms, begun_ref, steps, refs, total_ref):
    for k, term in enumerate(terms):
        total_ref[k] = begun_ref[k] + term
    groups, own_modes, _ = total_ref.shape
    my_modes = lax.axis_index("ma")
    top = my_bit("gx", bits("gx")[-1])
    across_x, across_y = lax.axis_size("gx"), lax.axis_size("gy")
    rows, width = refs[0].shape[3:]

    def piece(gx, gy):
        start = (gx * across_y + gy) * rows
        group = lax.rem(start // own_modes + groups - my_modes, groups)
        begin = start % own_modes
        return total_ref[group, begin : begin + rows]

    for kind, axis in enumerate(steps):
        keep_ref, send_ref = refs[2 * kind : 2 * kind + 2]
        mine = my_bit(axis, 0)
        half = lax.bitwise_xor(top, 1 - kind)

        def chosen(gx, gy):
            return jnp.where(half == 0, piece(gx, gy), piece(gx + across_x // 2, gy))

        for gx in range(keep_ref.shape[1]):
            for gy in range(keep_ref.shape[2]):
                if axis == "gx":
                    even, odd = chosen(2 * gx, gy), chosen(2 * gx + 1, gy)
                else:
                    even, odd = chosen(gx, 2 * gy), chosen(gx, 2 * gy + 1)
                keep = jnp.where(mine == 0, even, odd)
                send = jnp.where(mine == 0, odd, even).astype(send_ref.dtype)
                for p in range(keep_ref.shape[0]):
                    keep_ref[p, gx, gy] = keep[:, p * width : (p + 1) * width]
                    send_ref[p, gx, gy] = send[:, p * width : (p + 1) * width]


def first_kernel(
    sites, steps, rows_ref, high_ref, high_others_ref, ahead_ref, back_ref, own_ref, others_ref, begun_ref, *refs
):
    *refs, right_ref, past_ref, total_ref = refs
    planes, depth, _ = rows_ref.shape
    ys = high_ref.shape[1]
    same = same_site(sites, depth)
    count = depth // sites
    x = planes - 1
    low, high = rows_ref[place_of(1, planes)], plane_rows(high_ref, ys)
    ahead = dot(site_matrix([(ahead_ref[0, :, :depth], same)], count), low)
    set_right(right_ref, 0, ahead.astype(jnp.bfloat16))
    below = rows_ref[place_of(x - 1, planes)]
    set_right(right_ref, 1, move_plane(same, count, ahead_ref[x], back_ref[x - 1], high, below))
    back = dot(site_matrix([(back_ref[x, :, :depth], same)], count), rows_ref[place_of(x, planes)])
    set_right(past_ref, 0, back.astype(jnp.bfloat16))
    inner = (planes - 2) * depth
    lefts = [own_ref[:, inner:]] + [others_ref[k, :, inner:] for k in range(others_ref.shape[0])]
    highs = [high] + [plane_rows(high_others_ref.at[k], ys) for k in range(others_ref.shape[0])]
    terms = [
        dot(left, right_ref[...]) + dot(above.T, past_ref[...]) for left, above in zip(lefts, highs)
    ]
    project(terms, begun_ref, steps, refs, total_ref)


def plane_kernel(sites, rows_ref, low_ref, ahead_ref, past_maps_ref, right_ref):
    planes, depth, _ = rows_ref.shape
    ys = low_ref.shape[1] - low_ref.shape[2]
    links = low_ref[:, ys:, :, :, :ys].reshape(-1, ys)
    lanes = past_maps_ref.shape[1] // 2
    count = links.shape[0]
    spread = past_maps_ref[:ys, :lanes].astype(jnp.bfloat16)
    match = past_maps_ref[ys : ys + count, lanes:]
    start = past_maps_ref.shape[0] - 24
    choose = past_maps_ref[start : start + 16, :count].astype(jnp.bfloat16)
    past = dot(choose, (dot(links, spread) * match).astype(jnp.bfloat16))
    past = jnp.where(past_maps_ref[start + 16 : start + 17, :lanes] > 0.5, past[:8], past[8:])
    above = rows_ref[place_of(1, planes)]
    same = same_site(sites, depth)
    moved = move_plane(same, depth // sites, ahead_ref[0], past, above, plane_rows(low_ref, ys))
    set_right(right_ref, 0, moved)


def move_y_kernel(
    sites, zs, rows_ref, others_ref, near_ref, far_ref, ahead_ref, back_ref, turned_ref, field_ref
):
    planes, depth, width = rows_ref.shape
    groups = others_ref.shape[0] + 1
    row_size = depth // sites * zs
    reach = depth + near_ref.shape[1]
    head = back_ref.shape[2] - 128
    site, lane = iotas((sites, reach))
    inner = lane < depth
    upper = (lane >= depth) & (lane < depth + row_size)
    lower = (lane >= depth + row_size) & (lane < depth + 2 * row_size)
    lane_z = lane % zs
    to_next = (inner & (lane % sites == site + zs)) | (upper & (site == sites - zs + lane_z))
    to_last = (inner & (lane % sites == site - zs)) | (lower & (site == lane_z))
    to_next = jnp.where(to_next, -1.0, 0.0)
    to_last = jnp.where(to_last, -1.0, 0.0)
    _, lane = iotas((8, 128))
    spare = jnp.zeros((near_ref.shape[1] - far_ref.shape[2], width), far_ref.dtype)
    for x in range(planes):
        past = near_ref[x, 2 * row_size : 2 * row_size + 8, :128].astype(jnp.float32)
        mixed = jnp.where(lane >= depth + row_size - head, past, back_ref[x, :, head:])
        back = jnp.concatenate([back_ref[x, :, :head], mixed], axis=1)[:, :reach]
        matrix = site_matrix([(ahead_ref[x, :, :reach], to_next), (back, to_last)], depth // sites)
        place = place_of(x, planes)
        column = jnp.concatenate([rows_ref[place], near_ref[x]], axis=0)
        field_ref[0, place] = dot(matrix, column).astype(jnp.bfloat16)
        for k in range(groups - 1):
            column = jnp.concatenate([others_ref[k, place], far_ref[k, x], spare], axis=0)
            field_ref[k + 1, place] = dot(matrix, column).astype(jnp.bfloat16)
    for k in range(groups):
        turned_ref[k] = field_ref[k].reshape(planes * depth, width).T


def second_kernel(steps, lefts_ref, plane_ref, right_ref, begun_ref, *refs):
    *refs, total_ref = refs
    inner = lefts_ref.shape[2] - right_ref.shape[0]
    right = jnp.concatenate([plane_ref[...], right_ref[plane_ref.shape[0] :]], axis=0)
    terms = [dot(lefts_ref[k, :, inner:], right) for k in range(lefts_ref.shape[0])]
    project(terms, begun_ref, steps, refs, total_ref)


def swap(block, axis, bit):
    return lax.ppermute(block, axis, [(i, i ^ (1 << bit)) for i in range(lax.axis_size(axis))])


def merge_kernel(axis, bit, kept_ref, came_ref, keep_ref, send_ref):
    mine = my_bit(axis, bit)
    for gx in range(keep_ref.shape[1]):
        for gy in range(keep_ref.shape[2]):
            pair = []
            for odd in range(2):
                at = (slice(None), 2 * gx + odd, gy) if axis == "gx" else (slice(None), gx, 2 * gy + odd)
                pair.append(kept_ref[at] + came_ref[at].astype(jnp.float32))
            keep_ref[:, gx, gy] = jnp.where(mine == 0, pair[0], pair[1])
            send_ref[:, gx, gy] = jnp.where(mine == 0, pair[1], pair[0]).astype(send_ref.dtype)


def sum_kernel(kept_ref, came_ref, send_ref):
    send_ref[...] = (kept_ref[...] + came_ref[...].astype(jnp.float32)).astype(send_ref.dtype)


def finish_kernel(*refs):
    out_ref = refs[-1]
    for d in range(out_ref.shape[0]):
        kept_ref, came_ref, crossed_ref = refs[3 * d : 3 * d + 3]
        total = kept_ref[:, 0, 0] + came_ref[:, 0, 0].astype(jnp.float32)
        out_ref[d] = total + crossed_ref[:, 0, 0].astype(jnp.float32)


class Reduction:
    def __init__(self, kept, sent, axis):
        *low, self.top = [("gx", bit) for bit in bits("gx")]
        across = [("gy", bit) for bit in bits("gy")]
        self.steps = across + low[1:] if axis == "gx" else across[1:] + low
        self.kept, self.came = kept, swap(sent, axis, 0)

    def halve(self, after, weight=0):
        (axis, bit), *self.steps = self.steps
        dim = ("gx", "gy").index(axis) + 1
        shape = self.kept.shape
        shape = shape[:dim] + (shape[dim] // 2,) + shape[dim + 1 :]

        def merge(*refs):
            merge_kernel(axis, bit, *refs)

        self.came, _ = lax.optimization_barrier((self.came, after))
        self.kept, sent = call(
            merge, (pltpu.VMEM(shape, jnp.float32), pltpu.VMEM(shape, jnp.bfloat16)), weight, [self.kept, self.came]
        )
        self.came = swap(sent, axis, bit)
        return self.kept

    def cross(self, after):
        self.came, _ = lax.optimization_barrier((self.came, after))
        sent = call(sum_kernel, pltpu.VMEM(self.kept.shape, jnp.bfloat16), 0, [self.kept, self.came])
        self.came = swap(sent, *self.top)
        return sent


def local(eigen_modes, links_first, links_second):
    f32, bf16 = jnp.float32, jnp.bfloat16
    parts, planes, ys, zs, colours, width = eigen_modes.shape
    sites = ys * zs
    depth = parts * colours * sites
    row_size = parts * colours * zs
    edge = -(-(2 * row_size + 8) // 16) * 16
    lanes = -(-(depth + 2 * row_size) // 128) * 128
    across_x, across_y, groups = (lax.axis_size(a) for a in ("gx", "gy", "ma"))
    rows = groups * width // (across_x * across_y)
    inner_depth = (planes - 2) * depth
    raw = eigen_modes.transpose(0, 1, 2, 4, 3, 5)

    def shape(*dims, dtype=bf16):
        return pltpu.VMEM(dims, dtype)

    field_shape = shape(planes, depth, width)
    turned_shape = shape(width, planes * depth)
    total_shape = shape(groups, width, parts * width, dtype=f32)
    link_shape = shape(planes, 8, lanes, dtype=f32)
    total = pltpu.VMEM(total_shape.shape, f32)
    step_flops = 2 * planes * depth * depth * width
    project_flops = 2 * groups * width * planes * depth * parts * width

    raw_others = [shifted(raw, "ma", -step) for step in range(1, groups)]
    raw_links_x, raw_links_y = (a.transpose(0, 1, 2, 3, 5, 4) for a in (links_first, links_second))
    inputs = [raw, raw_links_x, raw_links_y]
    first_plane, last_plane, *inputs, past_maps = call(
        edges_kernel,
        (
            shape(parts, ys, colours, zs, width), shape(parts, ys + colours, colours, zs, width),
            *(shape(*a.shape) for a in inputs),
            shape(map_rows(parts, colours, planes, ys, zs)[-1], 2 * lanes, dtype=f32),
            shape(map_rows(parts, colours, 1, ys, zs)[-1], 2 * lanes, dtype=f32),
        ),
        0,
        inputs,
        [pltpu.SemaphoreType.DMA((5,))],
        [pltpu.HBM] * len(inputs),
    )
    low = shifted(last_plane, "gx", 1)
    high = shifted(first_plane, "gx", -1)
    field, ends, ahead_x, back_x, ahead_y, back_y = call(
        prepare_kernel,
        (field_shape, shape(planes, edge, width), link_shape, link_shape, link_shape, link_shape),
        0,
        inputs,
    )
    near = shifted(ends, "gy", 1)
    if across_y != 2:
        ahead_row = lax.broadcasted_iota(jnp.int32, ends.shape, 1) < row_size
        near = jnp.where(ahead_row, shifted(ends, "gy", -1), near)

    first_steps, second_steps = ("gx", "gy"), ("gy", "gx")

    def split(steps):
        shapes = []
        for axis in steps:
            dims = (across_x // 4, across_y) if axis == "gx" else (across_x // 2, across_y // 2)
            shapes += [shape(parts, *dims, rows, width, dtype=dtype) for dtype in (f32, bf16)]
        return shapes

    def inner(*refs):
        inner_kernel(sites, *refs)

    def first(*refs):
        first_kernel(sites, first_steps, *refs)

    def second(*refs):
        second_kernel(second_steps, *refs)

    def move_y(*refs):
        move_y_kernel(sites, zs, *refs)

    right, own = call(
        inner, (shape(inner_depth, parts * width), turned_shape), 0, [field, ahead_x, back_x]
    )
    turned = [call(turn_kernel, (field_shape, turned_shape), 0, [r]) for r in raw_others]
    fields = jnp.stack([t[0] for t in turned])
    others = jnp.stack([t[1] for t in turned])
    own, others, high = lax.optimization_barrier((own, others, high))
    high_others = jnp.stack([shifted(high, "ma", -step) for step in range(1, groups)])
    begun_first = call(begin_first_kernel, total_shape, 0, [own, others, right])
    *parts_first, right_edge = call(
        first,
        (*split(first_steps), shape(2 * depth, parts * width)),
        0,
        [field, high, high_others, ahead_x, back_x, own, others, begun_first],
        [pltpu.VMEM((depth, parts * width), bf16), total],
    )
    near, right_edge = lax.optimization_barrier((near, right_edge))
    near_rows = near[:, : 2 * row_size]
    far = jnp.stack([shifted(near_rows, "ma", -step) for step in range(1, groups)])
    lefts = call(
        move_y, shape(groups, width, planes * depth), 2 * step_flops,
        [field, fields, near, far, ahead_y, back_y],
        [pltpu.VMEM((groups,) + field_shape.shape, bf16)],
    )
    def plane(*refs):
        plane_kernel(sites, *refs)

    low, lefts = lax.optimization_barrier((low, lefts))
    plane_first = call(plane, shape(depth, parts * width), 0, [field, low, ahead_x, past_maps])
    begun_second = call(begin_second_kernel, total_shape, project_flops, [lefts, right])
    parts_second = call(
        second, split(second_steps), project_flops, [lefts, plane_first, right_edge, begun_second], [total]
    )
    crossing = [
        Reduction(*parts_first[:2], first_steps[0]), Reduction(*parts_second[:2], second_steps[0])
    ]
    after = crossing[0].halve(parts_second[0])
    kept, sent = parts_first[2:]
    sent, _ = lax.optimization_barrier((sent, after))
    staying = [Reduction(kept, sent, first_steps[1]), Reduction(*parts_second[2:], second_steps[1])]
    after = crossing[1].halve(after)
    while any(r.steps for r in crossing):
        for r in crossing:
            if r.steps:
                after = r.halve(after)
    for r in crossing:
        after = r.cross(after)
    weights = (0, 4 * project_flops)
    while any(r.steps for r in staying):
        for r in staying[::-1]:
            if r.steps:
                after = r.halve(after, weights[r is staying[1]])
    sums = []
    for stay, cross in zip(staying, crossing):
        sums += [stay.kept, stay.came, cross.came]
    return call(finish_kernel, jax.ShapeDtypeStruct((2, parts, rows, width), f32), 0, sums)


def solution(mesh):
    return jax.shard_map(
        local,
        mesh=mesh,
        in_specs=(
            P("cuts", "gx", "gy", None, None, "ma"),
            P("cuts", None, None, "gx", "gy", None),
            P("cuts", None, None, "gx", "gy", None),
        ),
        out_specs=P("cuts", None, ("gx", "gy"), "ma"),
        check_vma=False,
    )
```

```python
import jax
import jax.numpy as jnp
from jax import lax
from jax.experimental import pallas as pl
from jax.experimental.pallas import tpu as pltpu
from jax.sharding import PartitionSpec as P

VMEM_LIMIT = 16 * 1024 * 1024


def shifted(block, axis, distance):
    devices = range(lax.axis_size(axis))
    route = [((i - distance) % len(devices), i) for i in devices]
    return lax.ppermute(block, axis, route)


def call(body, out_shape, flops, operands, scratch=(), places=None):
    places = places or [pltpu.VMEM] * len(operands)
    return pl.pallas_call(
        body,
        out_shape=out_shape,
        in_specs=[pl.BlockSpec(memory_space=place) for place in places],
        scratch_shapes=scratch,
        cost_estimate=pl.CostEstimate(flops=flops // 2, bytes_accessed=0, transcendentals=0),
        compiler_params=pltpu.CompilerParams(vmem_limit_bytes=VMEM_LIMIT),
    )(*(pltpu.with_memory_space_constraint(a, place) for a, place in zip(operands, places)))


def dot(a, b):
    return jnp.dot(a, b, preferred_element_type=jnp.float32)


def iotas(shape):
    return (
        lax.broadcasted_iota(jnp.int32, shape, 0),
        lax.broadcasted_iota(jnp.int32, shape, 1),
    )


def place_of(x, planes):
    return planes - 2 if x == 0 else x if x == planes - 1 else x - 1


def map_rows(parts, colours, planes, ys, zs):
    match = ys
    choose = match + -(-parts * colours * colours * planes * zs // 8) * 8
    first_part = choose + 2 * parts * planes * 8
    return match, choose, first_part, first_part + 8


def write_maps(ref, parts, colours, planes, ys, zs):
    lanes = ref.shape[1] // 2
    sites = ys * zs
    depth = parts * colours * sites
    row_size = parts * colours * zs
    match, choose, first_part, _ = map_rows(parts, colours, planes, ys, zs)

    def ones(mask):
        return jnp.where(mask, 1.0, 0.0)

    def column(count):
        return lax.broadcasted_iota(jnp.int32, (count, 1), 0)

    def line(count):
        return lax.broadcasted_iota(jnp.int32, (1, count), 1)

    lane = line(lanes)
    inner = lane < depth
    past = lax.rem(jnp.maximum(lane - depth, 0), row_size)
    used = lane < depth + 2 * row_size
    part = jnp.where(inner, lax.div(lane, colours * sites), lax.div(past, colours * zs))
    colour = lax.rem(jnp.where(inner, lax.div(lane, sites), lax.div(past, zs)), colours)
    z = lax.rem(jnp.where(inner, lane, past), zs)
    y = lax.div(lax.rem(lane, sites), zs)
    ref[:ys, :lanes] = ones(column(ys) == jnp.where(inner, y, ys - 1))
    ref[:ys, lanes:] = ones(column(ys) == jnp.where(inner, y, ys) - 1)

    count = parts * colours * colours * planes * zs

    def link(index):
        x = lax.rem(lax.div(index, zs), planes)
        right = lax.rem(lax.div(index, zs * planes), colours)
        left = lax.rem(lax.div(index, zs * planes * colours), colours)
        return x, right, left, lax.div(index, zs * planes * colours * colours)

    row = column(count)
    _, right, left, _ = link(row)
    row_z = lax.rem(row, zs)
    key = jnp.where(used, colour * zs + z, -1)
    ref[match : match + count, :lanes] = ones(right * zs + row_z == key)
    ref[match : match + count, lanes:] = ones(left * zs + row_z == key)

    out = column(parts * planes * 8)
    field_part = lax.div(out, planes * 8)
    out_x = lax.rem(lax.div(out, 8), planes)
    out_part = lax.div(lax.rem(out, 8), colours)
    out_colour = lax.rem(lax.rem(out, 8), colours)
    x, right, left, source_part = link(line(count))
    source = source_part * planes + x
    wanted = jnp.where(out_part < parts, lax.rem(out_part + field_part, 2) * planes + out_x, -1)
    sign_ahead = jnp.where((field_part == 1) & (out_part == 0), -1.0, 1.0)
    sign_back = jnp.where((field_part == 0) & (out_part == 1), 1.0, -1.0)
    half = parts * planes * 8
    for start, end, sign in ((choose, left, sign_ahead), (choose + half, right, sign_back)):
        hit = source * colours + end == wanted * colours + jnp.where(wanted < 0, -1, out_colour)
        ref[start : start + half, :count] = jnp.where(hit, sign, 0.0)
    ref[first_part:, :lanes] = jnp.broadcast_to(ones(part == 0), (8, lanes))


def coefficients(links_x, links_y, maps_ref, planes):
    lanes = maps_ref.shape[1] // 2
    ys = links_x.shape[1]
    count = links_x.shape[0]
    half = 2 * planes * 8
    wide = dot(jnp.concatenate([links_x, links_y], axis=0), maps_ref[:ys].astype(jnp.bfloat16))
    match = maps_ref[ys : ys + count]
    match_ahead, match_back = match[:, :lanes], match[:, lanes:]
    choose = maps_ref[ys + count : ys + count + 2 * half, :count].astype(jnp.bfloat16)
    first_part = maps_ref[ys + count + 2 * half : ys + count + 2 * half + 1, :lanes] > 0.5
    ahead = jnp.concatenate([wide[:count, :lanes] * match_ahead, wide[count:, lanes:] * match_ahead], axis=1)
    back = jnp.concatenate([wide[:count, :lanes] * match_back, wide[count:, :lanes] * match_back], axis=1)
    out = []
    for chosen in (
        dot(choose[:half], ahead.astype(jnp.bfloat16)), dot(choose[half:], back.astype(jnp.bfloat16))
    ):
        for start in (0, lanes):
            part = chosen[:, start : start + lanes]
            rows = jnp.where(first_part, part[: half // 2], part[half // 2 :])
            out.append(rows.reshape(planes, 8, lanes))
    return out


def plane_rows(ref, ys):
    parts, _, colours, zs, width = ref.shape
    return jnp.concatenate(
        [ref[p, :ys, c].reshape(ys * zs, width) for p in range(parts) for c in range(colours)],
        axis=0,
    )


def edges_kernel(
    raw_hbm, links_x_hbm, links_y_hbm,
    first_ref, last_ref, raw_ref, links_x_ref, links_y_ref, maps_ref, past_maps_ref, arrived,
):
    parts, planes, ys, colours, zs, _ = raw_hbm.shape
    sources = (raw_hbm.at[:, planes - 1], raw_hbm.at[:, 0], links_x_hbm, links_y_hbm, raw_hbm)
    targets = (last_ref.at[:, :ys], first_ref, links_x_ref, links_y_ref, raw_ref)
    copies = [
        pltpu.make_async_copy(source, target, arrived.at[i])
        for i, (source, target) in enumerate(zip(sources, targets))
    ]
    for copy in copies:
        copy.start()
    last_ref[:, ys:] = jnp.zeros((parts, colours) + last_ref.shape[2:], last_ref.dtype)
    write_maps(maps_ref, parts, colours, planes, ys, zs)
    write_maps(past_maps_ref, parts, colours, 1, ys, zs)
    copies[2].wait()
    last_ref[:, ys:, :, :, :ys] = links_x_ref[:, :, :, planes - 1]
    for copy in copies[:2] + copies[3:]:
        copy.wait()


def site_matrix(rows_and_masks, count):
    blocks = []
    for q in range(count):
        block = None
        for rows, mask in rows_and_masks:
            term = rows[q : q + 1] * mask
            block = term if block is None else block + term
        blocks.append(block.astype(jnp.bfloat16))
    return jnp.concatenate(blocks, axis=0)


def prepare_kernel(
    raw_ref, links_x_ref, links_y_ref, maps_ref,
    rows_ref, ends_ref, ahead_x_ref, back_x_ref, ahead_y_ref, back_y_ref,
):
    planes, depth, width = rows_ref.shape
    zs = raw_ref.shape[4]
    ys = raw_ref.shape[2]
    sites = ys * zs
    row_size = depth // sites * zs
    lanes = ahead_y_ref.shape[2]
    ahead_x, ahead_y, back_x, back_y = coefficients(
        links_x_ref[...].reshape(-1, ys), links_y_ref[...].reshape(-1, ys), maps_ref, planes
    )
    ahead_x_ref[...] = ahead_x
    back_x_ref[...] = back_x
    ahead_y_ref[...] = ahead_y
    back_y_ref[...] = back_y

    row, lane = iotas((2 * row_size, depth))
    spot = row % row_size
    wanted = (spot // zs) * sites + spot % zs + jnp.where(row < row_size, 0, sites - zs)
    ends = (lane == wanted).astype(jnp.bfloat16)
    filler = jnp.zeros((8, width - 128), jnp.float32)
    spare = ends_ref.shape[1] - 2 * row_size - 8
    for x in range(planes):
        plane = plane_rows(raw_ref.at[:, x], ys)
        rows_ref[place_of(x, planes)] = plane
        tail = jnp.concatenate([back_y[x, :, lanes - 128 :], filler], axis=1)
        pieces = [dot(ends, plane), tail]
        if spare:
            pieces.append(jnp.zeros((spare, width), jnp.float32))
        ends_ref[x] = jnp.concatenate(pieces, axis=0).astype(jnp.bfloat16)


def turn_kernel(raw_ref, rows_ref, turned_ref):
    planes, depth, width = rows_ref.shape
    for x in range(planes):
        rows_ref[place_of(x, planes)] = plane_rows(raw_ref.at[:, x], raw_ref.shape[2])
    turned_ref[...] = rows_ref[...].reshape(planes * depth, width).T


def move_plane(same, count, ahead, back, above, below):
    depth = same.shape[1]
    moved = dot(site_matrix([(ahead[:, :depth], same)], count), above)
    return (moved + dot(site_matrix([(back[:, :depth], same)], count), below)).astype(jnp.bfloat16)


def same_site(sites, depth):
    site, lane = iotas((sites, depth))
    return (lane % sites == site).astype(jnp.float32)


def set_right(right_ref, place, moved):
    depth, width = moved.shape
    half = depth // 2
    start = place * depth
    real, imag = moved[:half], moved[half:]
    right_ref[start : start + half, :width] = real
    right_ref[start : start + half, width:] = imag
    right_ref[start + half : start + depth, :width] = imag
    right_ref[start + half : start + depth, width:] = -real


def inner_kernel(sites, rows_ref, ahead_ref, back_ref, right_ref, turned_ref):
    planes, depth, width = rows_ref.shape
    same = same_site(sites, depth)
    for x in range(1, planes - 1):
        above = rows_ref[place_of(x + 1, planes)]
        below = rows_ref[place_of(x - 1, planes)]
        moved = move_plane(same, depth // sites, ahead_ref[x], back_ref[x - 1], above, below)
        set_right(right_ref, place_of(x, planes), moved)
    turned_ref[...] = rows_ref[...].reshape(planes * depth, width).T


def begin_first_kernel(own_ref, others_ref, right_ref, total_ref):
    inner = right_ref.shape[0]
    right = right_ref[...]
    total_ref[0] = dot(own_ref[:, :inner], right)
    for k in range(others_ref.shape[0]):
        total_ref[k + 1] = dot(others_ref[k, :, :inner], right)


def begin_second_kernel(lefts_ref, right_ref, total_ref):
    inner = right_ref.shape[0]
    right = right_ref[...]
    for k in range(lefts_ref.shape[0]):
        total_ref[k] = dot(lefts_ref[k, :, :inner], right)


def bits(axis):
    return range(lax.axis_size(axis).bit_length() - 1)


def steps():
    one = [("gx", bit) for bit in bits("gx")[:-1]]
    two = [("gy", bit) for bit in bits("gy")]
    both = min(len(one), len(two))
    pairs = [pair for ends in zip(one, two) for pair in (ends, ends[::-1])]
    return pairs + [(step, step) for step in one[both:] + two[both:]]


def my_bit(axis, bit):
    return lax.bitwise_and(lax.shift_right_logical(lax.axis_index(axis), bit), 1)


def my_side(step):
    even, odd = (my_bit(*way) for way in step)
    return jnp.where(my_bit("ma", 0) == 0, even, odd)


def project(terms, begun_ref, keep_refs, send_refs, total_ref):
    for k, term in enumerate(terms):
        total_ref[k] = begun_ref[k] + term
    groups, own_modes, _ = total_ref.shape
    my_modes = lax.axis_index("ma")
    odd_core = my_bit("ma", 0)
    top = my_bit("gx", bits("gx")[-1])
    across_x, across_y = lax.axis_size("gx"), lax.axis_size("gy")
    parts, count, rows, width = keep_refs[0].shape
    plan = steps()
    mine = my_side(plan[0])

    def piece(gx, gy):
        start = (gx * across_y + gy) * rows
        group = lax.rem(start // own_modes + groups - my_modes, groups)
        begin = start % own_modes
        return total_ref[group, begin : begin + rows]

    for kind in range(2):
        half = lax.bitwise_xor(top, 1 - kind)

        def chosen(gx, gy):
            return jnp.where(half == 0, piece(gx, gy), piece(gx + across_x // 2, gy))

        def at(index):
            places = []
            for core in range(2):
                place = {"gx": 0, "gy": 0}
                for k, step in enumerate(plan):
                    axis, bit = step[core]
                    place[axis] |= (index >> (len(plan) - 1 - k) & 1) << bit
                places.append((place["gx"], place["gy"]))
            if places[0] == places[1]:
                return chosen(*places[0])
            return jnp.where(odd_core == 0, chosen(*places[0]), chosen(*places[1]))

        for index in range(count):
            low, high = at(index), at(index + count)
            keep = jnp.where(mine == 0, low, high)
            send = jnp.where(mine == 0, high, low).astype(jnp.bfloat16)
            for p in range(parts):
                keep_refs[kind][p, index] = keep[:, p * width : (p + 1) * width]
                send_refs[kind][p, index] = send[:, p * width : (p + 1) * width]


def first_kernel(
    sites, rows_ref, high_ref, low_ref, ahead_ref, back_ref, past_maps_ref, own_ref, others_ref, begun_ref,
    *refs,
):
    *refs, right_ref, total_ref = refs
    planes, depth, _ = rows_ref.shape
    same = same_site(sites, depth)
    count = depth // sites
    _, ys, colours, zs, _ = high_ref.shape
    links = low_ref[:, ys:, :, :, :ys].reshape(-1, ys)
    lanes = past_maps_ref.shape[1] // 2
    count = links.shape[0]
    spread = past_maps_ref[:ys, :lanes].astype(jnp.bfloat16)
    match = past_maps_ref[ys : ys + count, lanes:]
    start = past_maps_ref.shape[0] - 24
    choose = past_maps_ref[start : start + 16, :count].astype(jnp.bfloat16)
    past = dot(choose, (dot(links, spread) * match).astype(jnp.bfloat16))
    past = jnp.where(past_maps_ref[start + 16 : start + 17, :lanes] > 0.5, past[:8], past[8:])
    count = depth // sites
    above = rows_ref[place_of(1, planes)]
    set_right(right_ref, 0, move_plane(same, count, ahead_ref[0], past, above, plane_rows(low_ref, ys)))
    x = planes - 1
    below = rows_ref[place_of(x - 1, planes)]
    moved = move_plane(same, count, ahead_ref[x], back_ref[x - 1], plane_rows(high_ref, ys), below)
    set_right(right_ref, 1, moved)
    inner = (planes - 2) * depth
    lefts = [own_ref[:, inner:]] + [others_ref[k, :, inner:] for k in range(others_ref.shape[0])]
    terms = [dot(left, right_ref[...]) for left in lefts]
    keep_other, keep_own, send_ref = refs
    project(terms, begun_ref, (keep_other, keep_own), (send_ref.at[0], send_ref.at[1]), total_ref)


def move_y_kernel(
    sites, zs, rows_ref, others_ref, near_ref, far_ref, ahead_ref, back_ref, turned_ref, field_ref
):
    planes, depth, width = rows_ref.shape
    groups = others_ref.shape[0] + 1
    row_size = depth // sites * zs
    reach = depth + near_ref.shape[1]
    head = back_ref.shape[2] - 128
    site, lane = iotas((sites, reach))
    inner = lane < depth
    upper = (lane >= depth) & (lane < depth + row_size)
    lower = (lane >= depth + row_size) & (lane < depth + 2 * row_size)
    lane_z = lane % zs
    to_next = (inner & (lane % sites == site + zs)) | (upper & (site == sites - zs + lane_z))
    to_last = (inner & (lane % sites == site - zs)) | (lower & (site == lane_z))
    to_next = jnp.where(to_next, -1.0, 0.0)
    to_last = jnp.where(to_last, -1.0, 0.0)
    _, lane = iotas((8, 128))
    spare = jnp.zeros((near_ref.shape[1] - far_ref.shape[2], width), far_ref.dtype)
    for x in range(planes):
        past = near_ref[x, 2 * row_size : 2 * row_size + 8, :128].astype(jnp.float32)
        mixed = jnp.where(lane >= depth + row_size - head, past, back_ref[x, :, head:])
        back = jnp.concatenate([back_ref[x, :, :head], mixed], axis=1)[:, :reach]
        matrix = site_matrix([(ahead_ref[x, :, :reach], to_next), (back, to_last)], depth // sites)
        place = place_of(x, planes)
        column = jnp.concatenate([rows_ref[place], near_ref[x]], axis=0)
        field_ref[0, place] = dot(matrix, column).astype(jnp.bfloat16)
        for k in range(groups - 1):
            column = jnp.concatenate([others_ref[k, place], far_ref[k, x], spare], axis=0)
            field_ref[k + 1, place] = dot(matrix, column).astype(jnp.bfloat16)
    for k in range(groups):
        turned_ref[k] = field_ref[k].reshape(planes * depth, width).T


def second_kernel(lefts_ref, right_ref, begun_ref, *refs):
    *refs, total_ref = refs
    inner = lefts_ref.shape[2] - right_ref.shape[0]
    lefts = [lefts_ref[k, :, inner:] for k in range(lefts_ref.shape[0])]
    terms = [dot(left, right_ref[...]) for left in lefts]
    project(terms, begun_ref, refs[:2], refs[2:], total_ref)


def exchange(block, step):
    axes = ("gx", "gy", "ma")
    sizes = [lax.axis_size(axis) for axis in axes]
    route = []
    for source in range(sizes[0] * sizes[1] * sizes[2]):
        where = [source // (sizes[1] * sizes[2]), source // sizes[2] % sizes[1], source % sizes[2]]
        axis, bit = step[where[2] % 2]
        where[axes.index(axis)] ^= 1 << bit
        route.append((source, (where[0] * sizes[1] + where[1]) * sizes[2] + where[2]))
    return lax.ppermute(block, axes, route)


def halve(sums, step, weight=0):
    parts = sum(kept.shape[0] for kept, _, _ in sums)
    count, rows, width = sums[0][0].shape[1:]
    dims = (parts, count // 2, rows, width)

    def merge(*refs):
        *refs, keep_ref, send_ref = refs
        mine = my_side(step)
        start = 0
        for k, (_, _, which) in enumerate(sums):
            kept_ref, came_ref = refs[2 * k : 2 * k + 2]
            came_ref = came_ref if which is None else came_ref.at[which]
            end = start + kept_ref.shape[0]
            for index in range(count // 2):
                low, high = (
                    kept_ref[:, at] + came_ref[:, at].astype(jnp.float32) for at in (index, index + count // 2)
                )
                keep_ref[start:end, index] = jnp.where(mine == 0, low, high)
                send_ref[start:end, index] = jnp.where(mine == 0, high, low).astype(send_ref.dtype)
            start = end

    operands = [a for kept, came, _ in sums for a in (kept, came)]
    keep, send = call(merge, (pltpu.VMEM(dims, jnp.float32), pltpu.VMEM(dims, jnp.bfloat16)), weight, operands)
    return keep, exchange(send, step)


def sum_kernel(kept_ref, came_ref, send_ref):
    send_ref[...] = (kept_ref[...] + came_ref[...].astype(jnp.float32)).astype(send_ref.dtype)


def finish_kernel(kept_ref, came_ref, *refs):
    *crossed_refs, out_ref = refs
    parts = out_ref.shape[1]
    for d, crossed_ref in enumerate(crossed_refs):
        own = slice(d * parts, (d + 1) * parts)
        total = kept_ref[own, 0] + came_ref[own, 0].astype(jnp.float32)
        out_ref[d] = total + crossed_ref[:, 0].astype(jnp.float32)


def local(eigen_modes, links_first, links_second):
    f32, bf16 = jnp.float32, jnp.bfloat16
    parts, planes, ys, zs, colours, width = eigen_modes.shape
    sites = ys * zs
    depth = parts * colours * sites
    row_size = parts * colours * zs
    edge = -(-(2 * row_size + 8) // 16) * 16
    lanes = -(-(depth + 2 * row_size) // 128) * 128
    across_x, across_y, groups = (lax.axis_size(a) for a in ("gx", "gy", "ma"))
    rows = groups * width // (across_x * across_y)
    inner_depth = (planes - 2) * depth
    raw = eigen_modes.transpose(0, 1, 2, 4, 3, 5)

    def shape(*dims, dtype=bf16):
        return pltpu.VMEM(dims, dtype)

    field_shape = shape(planes, depth, width)
    turned_shape = shape(width, planes * depth)
    total_shape = shape(groups, width, parts * width, dtype=f32)
    link_shape = shape(planes, 8, lanes, dtype=f32)
    total = pltpu.VMEM(total_shape.shape, f32)
    step_flops = 2 * planes * depth * depth * width
    project_flops = 2 * groups * width * planes * depth * parts * width

    raw_others = [shifted(raw, "ma", -step) for step in range(1, groups)]
    raw_links_x, raw_links_y = (a.transpose(0, 1, 2, 3, 5, 4) for a in (links_first, links_second))
    inputs = [raw, raw_links_x, raw_links_y]
    first_plane, last_plane, *inputs, past_maps = call(
        edges_kernel,
        (
            shape(parts, ys, colours, zs, width), shape(parts, ys + colours, colours, zs, width),
            *(shape(*a.shape) for a in inputs),
            shape(map_rows(parts, colours, planes, ys, zs)[-1], 2 * lanes, dtype=f32),
            shape(map_rows(parts, colours, 1, ys, zs)[-1], 2 * lanes, dtype=f32),
        ),
        0,
        inputs,
        [pltpu.SemaphoreType.DMA((5,))],
        [pltpu.HBM] * len(inputs),
    )
    low = shifted(last_plane, "gx", 1)
    high = shifted(first_plane, "gx", -1)
    field, ends, ahead_x, back_x, ahead_y, back_y = call(
        prepare_kernel,
        (field_shape, shape(planes, edge, width), link_shape, link_shape, link_shape, link_shape),
        0,
        inputs,
    )
    near = shifted(ends, "gy", 1)
    if across_y != 2:
        ahead_row = lax.broadcasted_iota(jnp.int32, ends.shape, 1) < row_size
        near = jnp.where(ahead_row, shifted(ends, "gy", -1), near)

    plan = steps()
    top = ("gx", bits("gx")[-1])
    pieces = across_x * across_y // 4
    kept_shape = shape(parts, pieces, rows, width, dtype=f32)

    def inner(*refs):
        inner_kernel(sites, *refs)

    def first(*refs):
        first_kernel(sites, *refs)

    def move_y(*refs):
        move_y_kernel(sites, zs, *refs)

    right, own = call(
        inner, (shape(inner_depth, parts * width), turned_shape), 2 * step_flops, [field, ahead_x, back_x]
    )
    turned = [call(turn_kernel, (field_shape, turned_shape), step_flops // 4, [r]) for r in raw_others]
    fields = jnp.stack([t[0] for t in turned])
    others = jnp.stack([t[1] for t in turned])
    begun_first = call(begin_first_kernel, total_shape, project_flops, [own, others, right])
    kept_first, own_first, sent_first, right_edge = call(
        first,
        (kept_shape, kept_shape, shape(2, parts, pieces, rows, width), shape(2 * depth, parts * width)),
        project_flops,
        [field, high, low, ahead_x, back_x, past_maps, own, others, begun_first],
        [total],
    )
    near, right_edge = lax.optimization_barrier((near, right_edge))
    near_rows = near[:, : 2 * row_size]
    far = jnp.stack([shifted(near_rows, "ma", -step) for step in range(1, groups)])
    lefts = call(
        move_y, shape(groups, width, planes * depth), 2 * step_flops,
        [field, fields, near, far, ahead_y, back_y],
        [pltpu.VMEM((groups,) + field_shape.shape, bf16)],
    )
    begun_second = call(begin_second_kernel, total_shape, project_flops, [lefts, right])
    sent_shape = shape(parts, pieces, rows, width)
    kept_second, own_second, sent_second, sent_own = call(
        second_kernel, (kept_shape, kept_shape, sent_shape, sent_shape), project_flops,
        [lefts, right_edge, begun_second], [total],
    )
    came_first = exchange(sent_first, plan[0])
    crossing = [(kept_first, came_first, 0), (kept_second, exchange(sent_second, plan[0]), None)]
    staying = [(own_first, came_first, 1), (own_second, exchange(sent_own, plan[0]), None)]
    after = kept_second
    for step in plan[1:]:
        for d, (kept, came, which) in enumerate(crossing):
            came, after = lax.optimization_barrier((came, after))
            kept, came = halve([(kept, came, which)], step)
            crossing[d], after = (kept, came, None), kept
    crossed = []
    for kept, came, _ in crossing:
        came, after = lax.optimization_barrier((came, after))
        after = call(sum_kernel, pltpu.VMEM(kept.shape, bf16), 0, [kept, came])
        crossed.append(exchange(after, (top, top)))
    for step in plan[1:]:
        kept, came, which = staying[-1]
        came, after = lax.optimization_barrier((came, after))
        kept, came = halve(staying[:-1] + [(kept, came, which)], step)
        staying, after = [(kept, came, None)], kept
    kept, came, _ = staying[0]
    return call(
        finish_kernel, jax.ShapeDtypeStruct((2, parts, rows, width), f32), 0, [kept, came, *crossed]
    )


def solution(mesh):
    return jax.shard_map(
        local,
        mesh=mesh,
        in_specs=(
            P("cuts", "gx", "gy", None, None, "ma"),
            P("cuts", None, None, "gx", "gy", None),
            P("cuts", None, None, "gx", "gy", None),
        ),
        out_specs=P("cuts", None, ("gx", "gy"), "ma"),
        check_vma=False,
    )
```

```python
import jax
import jax.numpy as jnp
from jax import lax
from jax.experimental import pallas as pl
from jax.experimental.pallas import tpu as pltpu
from jax.sharding import PartitionSpec as P

VMEM_LIMIT = 16 * 1024 * 1024


def shifted(block, axis, distance):
    devices = range(lax.axis_size(axis))
    route = [((i - distance) % len(devices), i) for i in devices]
    return lax.ppermute(block, axis, route)


def call(body, out_shape, flops, operands, scratch=(), places=None):
    places = places or [pltpu.VMEM] * len(operands)
    return pl.pallas_call(
        body,
        out_shape=out_shape,
        in_specs=[pl.BlockSpec(memory_space=place) for place in places],
        scratch_shapes=scratch,
        cost_estimate=pl.CostEstimate(flops=flops // 2, bytes_accessed=0, transcendentals=0),
        compiler_params=pltpu.CompilerParams(vmem_limit_bytes=VMEM_LIMIT),
    )(*(pltpu.with_memory_space_constraint(a, place) for a, place in zip(operands, places)))


def dot(a, b):
    return jnp.dot(a, b, preferred_element_type=jnp.float32)


def iotas(shape):
    return (
        lax.broadcasted_iota(jnp.int32, shape, 0),
        lax.broadcasted_iota(jnp.int32, shape, 1),
    )


def place_of(x, planes):
    return planes - 2 if x == 0 else x if x == planes - 1 else x - 1


def map_rows(parts, colours, planes, ys, zs):
    match = ys
    choose = match + -(-parts * colours * colours * planes * zs // 8) * 8
    first_part = choose + 2 * parts * planes * 8
    return match, choose, first_part, first_part + 8


def write_maps(ref, parts, colours, planes, ys, zs):
    lanes = ref.shape[1] // 2
    sites = ys * zs
    depth = parts * colours * sites
    row_size = parts * colours * zs
    match, choose, first_part, _ = map_rows(parts, colours, planes, ys, zs)

    def ones(mask):
        return jnp.where(mask, 1.0, 0.0)

    def column(count):
        return lax.broadcasted_iota(jnp.int32, (count, 1), 0)

    def line(count):
        return lax.broadcasted_iota(jnp.int32, (1, count), 1)

    lane = line(lanes)
    inner = lane < depth
    past = lax.rem(jnp.maximum(lane - depth, 0), row_size)
    used = lane < depth + 2 * row_size
    part = jnp.where(inner, lax.div(lane, colours * sites), lax.div(past, colours * zs))
    colour = lax.rem(jnp.where(inner, lax.div(lane, sites), lax.div(past, zs)), colours)
    z = lax.rem(jnp.where(inner, lane, past), zs)
    y = lax.div(lax.rem(lane, sites), zs)
    ref[:ys, :lanes] = ones(column(ys) == jnp.where(inner, y, ys - 1))
    ref[:ys, lanes:] = ones(column(ys) == jnp.where(inner, y, ys) - 1)

    count = parts * colours * colours * planes * zs

    def link(index):
        x = lax.rem(lax.div(index, zs), planes)
        right = lax.rem(lax.div(index, zs * planes), colours)
        left = lax.rem(lax.div(index, zs * planes * colours), colours)
        return x, right, left, lax.div(index, zs * planes * colours * colours)

    row = column(count)
    _, right, left, _ = link(row)
    row_z = lax.rem(row, zs)
    key = jnp.where(used, colour * zs + z, -1)
    ref[match : match + count, :lanes] = ones(right * zs + row_z == key)
    ref[match : match + count, lanes:] = ones(left * zs + row_z == key)

    out = column(parts * planes * 8)
    field_part = lax.div(out, planes * 8)
    out_x = lax.rem(lax.div(out, 8), planes)
    out_part = lax.div(lax.rem(out, 8), colours)
    out_colour = lax.rem(lax.rem(out, 8), colours)
    x, right, left, source_part = link(line(count))
    source = source_part * planes + x
    wanted = jnp.where(out_part < parts, lax.rem(out_part + field_part, 2) * planes + out_x, -1)
    sign_ahead = jnp.where((field_part == 1) & (out_part == 0), -1.0, 1.0)
    sign_back = jnp.where((field_part == 0) & (out_part == 1), 1.0, -1.0)
    half = parts * planes * 8
    for start, end, sign in ((choose, left, sign_ahead), (choose + half, right, sign_back)):
        hit = source * colours + end == wanted * colours + jnp.where(wanted < 0, -1, out_colour)
        ref[start : start + half, :count] = jnp.where(hit, sign, 0.0)
    ref[first_part:, :lanes] = jnp.broadcast_to(ones(part == 0), (8, lanes))


def coefficients(links_x, links_y, maps_ref, planes):
    lanes = maps_ref.shape[1] // 2
    ys = links_x.shape[1]
    count = links_x.shape[0]
    half = 2 * planes * 8
    wide = dot(jnp.concatenate([links_x, links_y], axis=0), maps_ref[:ys].astype(jnp.bfloat16))
    match = maps_ref[ys : ys + count]
    match_ahead, match_back = match[:, :lanes], match[:, lanes:]
    choose = maps_ref[ys + count : ys + count + 2 * half, :count].astype(jnp.bfloat16)
    first_part = maps_ref[ys + count + 2 * half : ys + count + 2 * half + 1, :lanes] > 0.5
    ahead = jnp.concatenate([wide[:count, :lanes] * match_ahead, wide[count:, lanes:] * match_ahead], axis=1)
    back = jnp.concatenate([wide[:count, :lanes] * match_back, wide[count:, :lanes] * match_back], axis=1)
    out = []
    for chosen in (
        dot(choose[:half], ahead.astype(jnp.bfloat16)), dot(choose[half:], back.astype(jnp.bfloat16))
    ):
        for start in (0, lanes):
            part = chosen[:, start : start + lanes]
            rows = jnp.where(first_part, part[: half // 2], part[half // 2 :])
            out.append(rows.reshape(planes, 8, lanes))
    return out


def plane_rows(ref, ys):
    parts, _, colours, zs, width = ref.shape
    return jnp.concatenate(
        [ref[p, :ys, c].reshape(ys * zs, width) for p in range(parts) for c in range(colours)],
        axis=0,
    )


def edges_kernel(
    raw_hbm, links_x_hbm, links_y_hbm,
    first_ref, last_ref, raw_ref, links_x_ref, links_y_ref, maps_ref, past_maps_ref, arrived,
):
    parts, planes, ys, colours, zs, _ = raw_hbm.shape
    sources = (raw_hbm.at[:, planes - 1], raw_hbm.at[:, 0], links_x_hbm, links_y_hbm, raw_hbm)
    targets = (last_ref.at[:, :ys], first_ref, links_x_ref, links_y_ref, raw_ref)
    copies = [
        pltpu.make_async_copy(source, target, arrived.at[i])
        for i, (source, target) in enumerate(zip(sources, targets))
    ]
    for copy in copies:
        copy.start()
    last_ref[:, ys:] = jnp.zeros((parts, colours) + last_ref.shape[2:], last_ref.dtype)
    write_maps(maps_ref, parts, colours, planes, ys, zs)
    write_maps(past_maps_ref, parts, colours, 1, ys, zs)
    copies[2].wait()
    last_ref[:, ys:, :, :, :ys] = links_x_ref[:, :, :, planes - 1]
    for copy in copies[:2] + copies[3:]:
        copy.wait()


def site_matrix(rows_and_masks, count):
    blocks = []
    for q in range(count):
        block = None
        for rows, mask in rows_and_masks:
            term = rows[q : q + 1] * mask
            block = term if block is None else block + term
        blocks.append(block.astype(jnp.bfloat16))
    return jnp.concatenate(blocks, axis=0)


def prepare_kernel(
    raw_ref, links_x_ref, links_y_ref, maps_ref,
    rows_ref, ends_ref, ahead_x_ref, back_x_ref, ahead_y_ref, back_y_ref,
):
    planes, depth, width = rows_ref.shape
    zs = raw_ref.shape[4]
    ys = raw_ref.shape[2]
    sites = ys * zs
    row_size = depth // sites * zs
    lanes = ahead_y_ref.shape[2]
    ahead_x, ahead_y, back_x, back_y = coefficients(
        links_x_ref[...].reshape(-1, ys), links_y_ref[...].reshape(-1, ys), maps_ref, planes
    )
    ahead_x_ref[...] = ahead_x
    back_x_ref[...] = back_x
    ahead_y_ref[...] = ahead_y
    back_y_ref[...] = back_y

    row, lane = iotas((2 * row_size, depth))
    spot = row % row_size
    wanted = (spot // zs) * sites + spot % zs + jnp.where(row < row_size, 0, sites - zs)
    ends = (lane == wanted).astype(jnp.bfloat16)
    filler = jnp.zeros((8, width - 128), jnp.float32)
    spare = ends_ref.shape[1] - 2 * row_size - 8
    for x in range(planes):
        plane = plane_rows(raw_ref.at[:, x], ys)
        rows_ref[place_of(x, planes)] = plane
        tail = jnp.concatenate([back_y[x, :, lanes - 128 :], filler], axis=1)
        pieces = [dot(ends, plane), tail]
        if spare:
            pieces.append(jnp.zeros((spare, width), jnp.float32))
        ends_ref[x] = jnp.concatenate(pieces, axis=0).astype(jnp.bfloat16)


def turn_kernel(raw_ref, rows_ref, turned_ref):
    planes, depth, width = rows_ref.shape
    for x in range(planes):
        rows_ref[place_of(x, planes)] = plane_rows(raw_ref.at[:, x], raw_ref.shape[2])
    turned_ref[...] = rows_ref[...].reshape(planes * depth, width).T


def move_plane(same, count, ahead, back, above, below):
    depth = same.shape[1]
    moved = dot(site_matrix([(ahead[:, :depth], same)], count), above)
    return (moved + dot(site_matrix([(back[:, :depth], same)], count), below)).astype(jnp.bfloat16)


def same_site(sites, depth):
    site, lane = iotas((sites, depth))
    return (lane % sites == site).astype(jnp.float32)


def set_right(right_ref, place, moved):
    depth, width = moved.shape
    half = depth // 2
    start = place * depth
    real, imag = moved[:half], moved[half:]
    right_ref[start : start + half, :width] = real
    right_ref[start : start + half, width:] = imag
    right_ref[start + half : start + depth, :width] = imag
    right_ref[start + half : start + depth, width:] = -real


def inner_kernel(sites, rows_ref, ahead_ref, back_ref, right_ref, turned_ref):
    planes, depth, width = rows_ref.shape
    same = same_site(sites, depth)
    for x in range(1, planes - 1):
        above = rows_ref[place_of(x + 1, planes)]
        below = rows_ref[place_of(x - 1, planes)]
        moved = move_plane(same, depth // sites, ahead_ref[x], back_ref[x - 1], above, below)
        set_right(right_ref, place_of(x, planes), moved)
    turned_ref[...] = rows_ref[...].reshape(planes * depth, width).T


def begin_first_kernel(own_ref, others_ref, right_ref, total_ref):
    inner = right_ref.shape[0]
    right = right_ref[...]
    total_ref[0] = dot(own_ref[:, :inner], right)
    for k in range(others_ref.shape[0]):
        total_ref[k + 1] = dot(others_ref[k, :, :inner], right)


def begin_second_kernel(lefts_ref, right_ref, total_ref):
    inner = right_ref.shape[0]
    right = right_ref[...]
    for k in range(lefts_ref.shape[0]):
        total_ref[k] = dot(lefts_ref[k, :, :inner], right)


def bits(axis):
    return range(lax.axis_size(axis).bit_length() - 1)


def steps():
    one = [("gx", bit) for bit in bits("gx")[:-1]]
    two = [("gy", bit) for bit in bits("gy")]
    both = min(len(one), len(two))
    pairs = [pair for ends in zip(one, two) for pair in (ends, ends[::-1])]
    return pairs + [(step, step) for step in one[both:] + two[both:]]


def my_bit(axis, bit):
    return lax.bitwise_and(lax.shift_right_logical(lax.axis_index(axis), bit), 1)


def my_side(step):
    even, odd = (my_bit(*way) for way in step)
    return jnp.where(my_bit("ma", 0) == 0, even, odd)


def project(terms, begun_ref, keep_refs, send_refs, total_ref):
    for k, term in enumerate(terms):
        total_ref[k] = begun_ref[k] + term
    groups, own_modes, _ = total_ref.shape
    my_modes = lax.axis_index("ma")
    odd_core = my_bit("ma", 0)
    top = my_bit("gx", bits("gx")[-1])
    across_x, across_y = lax.axis_size("gx"), lax.axis_size("gy")
    parts, count, rows, width = keep_refs[0].shape
    plan = steps()
    mine = my_side(plan[0])

    def piece(gx, gy):
        start = (gx * across_y + gy) * rows
        group = lax.rem(start // own_modes + groups - my_modes, groups)
        begin = start % own_modes
        return total_ref[group, begin : begin + rows]

    for kind in range(2):
        half = lax.bitwise_xor(top, 1 - kind)

        def chosen(gx, gy):
            return jnp.where(half == 0, piece(gx, gy), piece(gx + across_x // 2, gy))

        def at(index):
            places = []
            for core in range(2):
                place = {"gx": 0, "gy": 0}
                for k, step in enumerate(plan):
                    axis, bit = step[core]
                    place[axis] |= (index >> (len(plan) - 1 - k) & 1) << bit
                places.append((place["gx"], place["gy"]))
            if places[0] == places[1]:
                return chosen(*places[0])
            return jnp.where(odd_core == 0, chosen(*places[0]), chosen(*places[1]))

        for index in range(count):
            low, high = at(index), at(index + count)
            keep = jnp.where(mine == 0, low, high)
            send = jnp.where(mine == 0, high, low).astype(jnp.bfloat16)
            for p in range(parts):
                keep_refs[kind][p, index] = keep[:, p * width : (p + 1) * width]
                send_refs[kind][p, index] = send[:, p * width : (p + 1) * width]


def first_kernel(
    sites, rows_ref, high_ref, low_ref, ahead_ref, back_ref, past_maps_ref, own_ref, others_ref, begun_ref,
    *refs,
):
    *refs, right_ref, total_ref = refs
    planes, depth, _ = rows_ref.shape
    same = same_site(sites, depth)
    count = depth // sites
    _, ys, colours, zs, _ = high_ref.shape
    links = low_ref[:, ys:, :, :, :ys].reshape(-1, ys)
    lanes = past_maps_ref.shape[1] // 2
    count = links.shape[0]
    spread = past_maps_ref[:ys, :lanes].astype(jnp.bfloat16)
    match = past_maps_ref[ys : ys + count, lanes:]
    start = past_maps_ref.shape[0] - 24
    choose = past_maps_ref[start : start + 16, :count].astype(jnp.bfloat16)
    past = dot(choose, (dot(links, spread) * match).astype(jnp.bfloat16))
    past = jnp.where(past_maps_ref[start + 16 : start + 17, :lanes] > 0.5, past[:8], past[8:])
    count = depth // sites
    above = rows_ref[place_of(1, planes)]
    set_right(right_ref, 0, move_plane(same, count, ahead_ref[0], past, above, plane_rows(low_ref, ys)))
    x = planes - 1
    below = rows_ref[place_of(x - 1, planes)]
    moved = move_plane(same, count, ahead_ref[x], back_ref[x - 1], plane_rows(high_ref, ys), below)
    set_right(right_ref, 1, moved)
    inner = (planes - 2) * depth
    lefts = [own_ref[:, inner:]] + [others_ref[k, :, inner:] for k in range(others_ref.shape[0])]
    terms = [dot(left, right_ref[...]) for left in lefts]
    keep_other, keep_own, send_ref = refs
    project(terms, begun_ref, (keep_other, keep_own), (send_ref.at[0], send_ref.at[1]), total_ref)


def move_y_kernel(
    sites, zs, rows_ref, others_ref, near_ref, far_ref, ahead_ref, back_ref, turned_ref, field_ref
):
    planes, depth, width = rows_ref.shape
    groups = others_ref.shape[0] + 1
    row_size = depth // sites * zs
    reach = depth + near_ref.shape[1]
    head = back_ref.shape[2] - 128
    site, lane = iotas((sites, reach))
    inner = lane < depth
    upper = (lane >= depth) & (lane < depth + row_size)
    lower = (lane >= depth + row_size) & (lane < depth + 2 * row_size)
    lane_z = lane % zs
    to_next = (inner & (lane % sites == site + zs)) | (upper & (site == sites - zs + lane_z))
    to_last = (inner & (lane % sites == site - zs)) | (lower & (site == lane_z))
    to_next = jnp.where(to_next, -1.0, 0.0)
    to_last = jnp.where(to_last, -1.0, 0.0)
    _, lane = iotas((8, 128))
    spare = jnp.zeros((near_ref.shape[1] - far_ref.shape[2], width), far_ref.dtype)
    for x in range(planes):
        past = near_ref[x, 2 * row_size : 2 * row_size + 8, :128].astype(jnp.float32)
        mixed = jnp.where(lane >= depth + row_size - head, past, back_ref[x, :, head:])
        back = jnp.concatenate([back_ref[x, :, :head], mixed], axis=1)[:, :reach]
        matrix = site_matrix([(ahead_ref[x, :, :reach], to_next), (back, to_last)], depth // sites)
        place = place_of(x, planes)
        column = jnp.concatenate([rows_ref[place], near_ref[x]], axis=0)
        field_ref[0, place] = dot(matrix, column).astype(jnp.bfloat16)
        for k in range(groups - 1):
            column = jnp.concatenate([others_ref[k, place], far_ref[k, x], spare], axis=0)
            field_ref[k + 1, place] = dot(matrix, column).astype(jnp.bfloat16)
    for k in range(groups):
        turned_ref[k] = field_ref[k].reshape(planes * depth, width).T


def second_kernel(lefts_ref, right_ref, begun_ref, *refs):
    *refs, total_ref = refs
    inner = lefts_ref.shape[2] - right_ref.shape[0]
    lefts = [lefts_ref[k, :, inner:] for k in range(lefts_ref.shape[0])]
    terms = [dot(left, right_ref[...]) for left in lefts]
    project(terms, begun_ref, refs[:2], refs[2:], total_ref)


def exchange(block, step):
    axes = ("gx", "gy", "ma")
    sizes = [lax.axis_size(axis) for axis in axes]
    route = []
    for source in range(sizes[0] * sizes[1] * sizes[2]):
        where = [source // (sizes[1] * sizes[2]), source // sizes[2] % sizes[1], source % sizes[2]]
        axis, bit = step[where[2] % 2]
        where[axes.index(axis)] ^= 1 << bit
        route.append((source, (where[0] * sizes[1] + where[1]) * sizes[2] + where[2]))
    return lax.ppermute(block, axes, route)


def halve(sums, step, weight=0):
    parts = sum(kept.shape[0] for kept, _, _ in sums)
    count, rows, width = sums[0][0].shape[1:]
    dims = (parts, count // 2, rows, width)

    def merge(*refs):
        *refs, keep_ref, send_ref = refs
        mine = my_side(step)
        start = 0
        for k, (_, _, which) in enumerate(sums):
            kept_ref, came_ref = refs[2 * k : 2 * k + 2]
            came_ref = came_ref if which is None else came_ref.at[which]
            end = start + kept_ref.shape[0]
            for index in range(count // 2):
                low, high = (
                    kept_ref[:, at] + came_ref[:, at].astype(jnp.float32) for at in (index, index + count // 2)
                )
                keep_ref[start:end, index] = jnp.where(mine == 0, low, high)
                send_ref[start:end, index] = jnp.where(mine == 0, high, low).astype(send_ref.dtype)
            start = end

    operands = [a for kept, came, _ in sums for a in (kept, came)]
    keep, send = call(merge, (pltpu.VMEM(dims, jnp.float32), pltpu.VMEM(dims, jnp.bfloat16)), weight, operands)
    return keep, exchange(send, step)


def sum_kernel(kept_ref, came_ref, send_ref):
    send_ref[...] = (kept_ref[...] + came_ref[...].astype(jnp.float32)).astype(send_ref.dtype)


def cross_kernel(start, kept_ref, crossed_ref, out_ref):
    kept = kept_ref[start : start + out_ref.shape[0]]
    out_ref[...] = kept + crossed_ref[...].astype(jnp.float32)


def finish_kernel(came_ref, *refs):
    *kept_refs, out_ref = refs
    parts = out_ref.shape[1]
    for d, kept_ref in enumerate(kept_refs):
        out_ref[d] = kept_ref[:, 0] + came_ref[d * parts : (d + 1) * parts, 0].astype(jnp.float32)


def local(eigen_modes, links_first, links_second):
    f32, bf16 = jnp.float32, jnp.bfloat16
    parts, planes, ys, zs, colours, width = eigen_modes.shape
    sites = ys * zs
    depth = parts * colours * sites
    row_size = parts * colours * zs
    edge = -(-(2 * row_size + 8) // 16) * 16
    lanes = -(-(depth + 2 * row_size) // 128) * 128
    across_x, across_y, groups = (lax.axis_size(a) for a in ("gx", "gy", "ma"))
    rows = groups * width // (across_x * across_y)
    inner_depth = (planes - 2) * depth
    raw = eigen_modes.transpose(0, 1, 2, 4, 3, 5)

    def shape(*dims, dtype=bf16):
        return pltpu.VMEM(dims, dtype)

    field_shape = shape(planes, depth, width)
    turned_shape = shape(width, planes * depth)
    total_shape = shape(groups, width, parts * width, dtype=f32)
    link_shape = shape(planes, 8, lanes, dtype=f32)
    total = pltpu.VMEM(total_shape.shape, f32)
    step_flops = 2 * planes * depth * depth * width
    project_flops = 2 * groups * width * planes * depth * parts * width

    raw_others = [shifted(raw, "ma", -step) for step in range(1, groups)]
    raw_links_x, raw_links_y = (a.transpose(0, 1, 2, 3, 5, 4) for a in (links_first, links_second))
    inputs = [raw, raw_links_x, raw_links_y]
    first_plane, last_plane, *inputs, past_maps = call(
        edges_kernel,
        (
            shape(parts, ys, colours, zs, width), shape(parts, ys + colours, colours, zs, width),
            *(shape(*a.shape) for a in inputs),
            shape(map_rows(parts, colours, planes, ys, zs)[-1], 2 * lanes, dtype=f32),
            shape(map_rows(parts, colours, 1, ys, zs)[-1], 2 * lanes, dtype=f32),
        ),
        0,
        inputs,
        [pltpu.SemaphoreType.DMA((5,))],
        [pltpu.HBM] * len(inputs),
    )
    low = shifted(last_plane, "gx", 1)
    high = shifted(first_plane, "gx", -1)
    field, ends, ahead_x, back_x, ahead_y, back_y = call(
        prepare_kernel,
        (field_shape, shape(planes, edge, width), link_shape, link_shape, link_shape, link_shape),
        0,
        inputs,
    )
    near = shifted(ends, "gy", 1)
    if across_y != 2:
        ahead_row = lax.broadcasted_iota(jnp.int32, ends.shape, 1) < row_size
        near = jnp.where(ahead_row, shifted(ends, "gy", -1), near)

    plan = steps()
    top = ("gx", bits("gx")[-1])
    pieces = across_x * across_y // 4
    kept_shape = shape(parts, pieces, rows, width, dtype=f32)

    def inner(*refs):
        inner_kernel(sites, *refs)

    def first(*refs):
        first_kernel(sites, *refs)

    def move_y(*refs):
        move_y_kernel(sites, zs, *refs)

    right, own = call(
        inner, (shape(inner_depth, parts * width), turned_shape), 2 * step_flops, [field, ahead_x, back_x]
    )
    turned = [call(turn_kernel, (field_shape, turned_shape), step_flops // 4, [r]) for r in raw_others]
    fields = jnp.stack([t[0] for t in turned])
    others = jnp.stack([t[1] for t in turned])
    begun_first = call(begin_first_kernel, total_shape, project_flops, [own, others, right])
    kept_first, own_first, sent_first, right_edge = call(
        first,
        (kept_shape, kept_shape, shape(2, parts, pieces, rows, width), shape(2 * depth, parts * width)),
        project_flops,
        [field, high, low, ahead_x, back_x, past_maps, own, others, begun_first],
        [total],
    )
    near, right_edge = lax.optimization_barrier((near, right_edge))
    near_rows = near[:, : 2 * row_size]
    far = jnp.stack([shifted(near_rows, "ma", -step) for step in range(1, groups)])
    lefts = call(
        move_y, shape(groups, width, planes * depth), 2 * step_flops,
        [field, fields, near, far, ahead_y, back_y],
        [pltpu.VMEM((groups,) + field_shape.shape, bf16)],
    )
    begun_second = call(begin_second_kernel, total_shape, project_flops, [lefts, right])
    sent_shape = shape(parts, pieces, rows, width)
    kept_second, own_second, sent_second, sent_own = call(
        second_kernel, (kept_shape, kept_shape, sent_shape, sent_shape), project_flops,
        [lefts, right_edge, begun_second], [total],
    )
    came_first = exchange(sent_first, plan[0])
    crossing = [(kept_first, came_first, 0), (kept_second, exchange(sent_second, plan[0]), None)]
    staying = [(own_first, came_first, 1), (own_second, exchange(sent_own, plan[0]), None)]
    after = kept_second
    for step in plan[1:]:
        for d, (kept, came, which) in enumerate(crossing):
            came, after = lax.optimization_barrier((came, after))
            kept, came = halve([(kept, came, which)], step)
            crossing[d], after = (kept, came, None), kept
    crossed = []
    for kept, came, _ in crossing:
        came, after = lax.optimization_barrier((came, after))
        after = call(sum_kernel, pltpu.VMEM(kept.shape, bf16), 0, [kept, came])
        crossed.append(exchange(after, (top, top)))
    for step in plan[1:]:
        kept, came, which = staying[-1]
        came, after = lax.optimization_barrier((came, after))
        kept, came = halve(staying[:-1] + [(kept, came, which)], step)
        staying, after = [(kept, came, None)], kept
    kept, came, _ = staying[0]
    totals = []
    for d, block in enumerate(crossed):

        def cross(*refs, start=d * parts):
            cross_kernel(start, *refs)

        block, after = lax.optimization_barrier((block, after))
        after = call(cross, shape(*block.shape, dtype=f32), 4 * project_flops, [kept, block])
        totals.append(after)
    came, after = lax.optimization_barrier((came, after))
    return call(
        finish_kernel, jax.ShapeDtypeStruct((2, parts, rows, width), f32), 0, [came, *totals]
    )


def solution(mesh):
    return jax.shard_map(
        local,
        mesh=mesh,
        in_specs=(
            P("cuts", "gx", "gy", None, None, "ma"),
            P("cuts", None, None, "gx", "gy", None),
            P("cuts", None, None, "gx", "gy", None),
        ),
        out_specs=P("cuts", None, ("gx", "gy"), "ma"),
        check_vma=False,
    )
```

```python
import jax
import jax.numpy as jnp
from jax import lax
from jax.experimental import pallas as pl
from jax.experimental.pallas import tpu as pltpu
from jax.sharding import PartitionSpec as P

VMEM_LIMIT = 16 * 1024 * 1024


def shifted(block, axis, distance):
    devices = range(lax.axis_size(axis))
    route = [((i - distance) % len(devices), i) for i in devices]
    return lax.ppermute(block, axis, route)


def call(body, out_shape, flops, operands, scratch=(), places=None):
    places = places or [pltpu.VMEM] * len(operands)
    return pl.pallas_call(
        body,
        out_shape=out_shape,
        in_specs=[pl.BlockSpec(memory_space=place) for place in places],
        scratch_shapes=scratch,
        cost_estimate=pl.CostEstimate(flops=flops // 2, bytes_accessed=0, transcendentals=0),
        compiler_params=pltpu.CompilerParams(vmem_limit_bytes=VMEM_LIMIT),
    )(*(pltpu.with_memory_space_constraint(a, place) for a, place in zip(operands, places)))


def dot(a, b):
    return jnp.dot(a, b, preferred_element_type=jnp.float32)


def iotas(shape):
    return (
        lax.broadcasted_iota(jnp.int32, shape, 0),
        lax.broadcasted_iota(jnp.int32, shape, 1),
    )


def place_of(x, planes):
    return planes - 2 if x == 0 else x if x == planes - 1 else x - 1


def map_rows(parts, colours, planes, ys, zs):
    match = ys
    choose = match + -(-parts * colours * colours * planes * zs // 8) * 8
    first_part = choose + 2 * parts * planes * 8
    return match, choose, first_part, first_part + 8


def write_maps(ref, parts, colours, planes, ys, zs):
    lanes = ref.shape[1] // 2
    sites = ys * zs
    depth = parts * colours * sites
    row_size = parts * colours * zs
    match, choose, first_part, _ = map_rows(parts, colours, planes, ys, zs)

    def ones(mask):
        return jnp.where(mask, 1.0, 0.0)

    def column(count):
        return lax.broadcasted_iota(jnp.int32, (count, 1), 0)

    def line(count):
        return lax.broadcasted_iota(jnp.int32, (1, count), 1)

    lane = line(lanes)
    inner = lane < depth
    past = lax.rem(jnp.maximum(lane - depth, 0), row_size)
    used = lane < depth + 2 * row_size
    part = jnp.where(inner, lax.div(lane, colours * sites), lax.div(past, colours * zs))
    colour = lax.rem(jnp.where(inner, lax.div(lane, sites), lax.div(past, zs)), colours)
    z = lax.rem(jnp.where(inner, lane, past), zs)
    y = lax.div(lax.rem(lane, sites), zs)
    ref[:ys, :lanes] = ones(column(ys) == jnp.where(inner, y, ys - 1))
    ref[:ys, lanes:] = ones(column(ys) == jnp.where(inner, y, ys) - 1)

    count = parts * colours * colours * planes * zs

    def link(index):
        x = lax.rem(lax.div(index, zs), planes)
        right = lax.rem(lax.div(index, zs * planes), colours)
        left = lax.rem(lax.div(index, zs * planes * colours), colours)
        return x, right, left, lax.div(index, zs * planes * colours * colours)

    row = column(count)
    _, right, left, _ = link(row)
    row_z = lax.rem(row, zs)
    key = jnp.where(used, colour * zs + z, -1)
    ref[match : match + count, :lanes] = ones(right * zs + row_z == key)
    ref[match : match + count, lanes:] = ones(left * zs + row_z == key)

    out = column(parts * planes * 8)
    field_part = lax.div(out, planes * 8)
    out_x = lax.rem(lax.div(out, 8), planes)
    out_part = lax.div(lax.rem(out, 8), colours)
    out_colour = lax.rem(lax.rem(out, 8), colours)
    x, right, left, source_part = link(line(count))
    source = source_part * planes + x
    wanted = jnp.where(out_part < parts, lax.rem(out_part + field_part, 2) * planes + out_x, -1)
    sign_ahead = jnp.where((field_part == 1) & (out_part == 0), -1.0, 1.0)
    sign_back = jnp.where((field_part == 0) & (out_part == 1), 1.0, -1.0)
    half = parts * planes * 8
    for start, end, sign in ((choose, left, sign_ahead), (choose + half, right, sign_back)):
        hit = source * colours + end == wanted * colours + jnp.where(wanted < 0, -1, out_colour)
        ref[start : start + half, :count] = jnp.where(hit, sign, 0.0)
    ref[first_part:, :lanes] = jnp.broadcast_to(ones(part == 0), (8, lanes))


def coefficients(links_x, links_y, maps_ref, planes):
    lanes = maps_ref.shape[1] // 2
    ys = links_x.shape[1]
    count = links_x.shape[0]
    half = 2 * planes * 8
    wide = dot(jnp.concatenate([links_x, links_y], axis=0), maps_ref[:ys].astype(jnp.bfloat16))
    match = maps_ref[ys : ys + count]
    match_ahead, match_back = match[:, :lanes], match[:, lanes:]
    choose = maps_ref[ys + count : ys + count + 2 * half, :count].astype(jnp.bfloat16)
    first_part = maps_ref[ys + count + 2 * half : ys + count + 2 * half + 1, :lanes] > 0.5
    ahead = jnp.concatenate([wide[:count, :lanes] * match_ahead, wide[count:, lanes:] * match_ahead], axis=1)
    back = jnp.concatenate([wide[:count, :lanes] * match_back, wide[count:, :lanes] * match_back], axis=1)
    out = []
    for chosen in (
        dot(choose[:half], ahead.astype(jnp.bfloat16)), dot(choose[half:], back.astype(jnp.bfloat16))
    ):
        for start in (0, lanes):
            part = chosen[:, start : start + lanes]
            rows = jnp.where(first_part, part[: half // 2], part[half // 2 :])
            out.append(rows.reshape(planes, 8, lanes))
    return out


def plane_rows(ref, ys):
    parts, _, colours, zs, width = ref.shape
    return jnp.concatenate(
        [ref[p, :ys, c].reshape(ys * zs, width) for p in range(parts) for c in range(colours)],
        axis=0,
    )


def edges_kernel(
    raw_hbm, links_x_hbm, links_y_hbm,
    first_ref, last_ref, raw_ref, links_x_ref, links_y_ref, maps_ref, past_maps_ref, arrived,
):
    parts, planes, ys, colours, zs, _ = raw_hbm.shape
    sources = (raw_hbm.at[:, planes - 1], raw_hbm.at[:, 0], links_x_hbm, links_y_hbm, raw_hbm)
    targets = (last_ref.at[:, :ys], first_ref, links_x_ref, links_y_ref, raw_ref)
    copies = [
        pltpu.make_async_copy(source, target, arrived.at[i])
        for i, (source, target) in enumerate(zip(sources, targets))
    ]
    for copy in copies:
        copy.start()
    last_ref[:, ys:] = jnp.zeros((parts, colours) + last_ref.shape[2:], last_ref.dtype)
    write_maps(maps_ref, parts, colours, planes, ys, zs)
    write_maps(past_maps_ref, parts, colours, 1, ys, zs)
    copies[2].wait()
    last_ref[:, ys:, :, :, :ys] = links_x_ref[:, :, :, planes - 1]
    for copy in copies[:2] + copies[3:]:
        copy.wait()


def site_matrix(rows_and_masks, count):
    blocks = []
    for q in range(count):
        block = None
        for rows, mask in rows_and_masks:
            term = rows[q : q + 1] * mask
            block = term if block is None else block + term
        blocks.append(block.astype(jnp.bfloat16))
    return jnp.concatenate(blocks, axis=0)


def prepare_kernel(
    raw_ref, links_x_ref, links_y_ref, maps_ref,
    rows_ref, ends_ref, ahead_x_ref, back_x_ref, ahead_y_ref, back_y_ref,
):
    planes, depth, width = rows_ref.shape
    zs = raw_ref.shape[4]
    ys = raw_ref.shape[2]
    sites = ys * zs
    row_size = depth // sites * zs
    lanes = ahead_y_ref.shape[2]
    ahead_x, ahead_y, back_x, back_y = coefficients(
        links_x_ref[...].reshape(-1, ys), links_y_ref[...].reshape(-1, ys), maps_ref, planes
    )
    ahead_x_ref[...] = ahead_x
    back_x_ref[...] = back_x
    ahead_y_ref[...] = ahead_y
    back_y_ref[...] = back_y

    row, lane = iotas((2 * row_size, depth))
    spot = row % row_size
    wanted = (spot // zs) * sites + spot % zs + jnp.where(row < row_size, 0, sites - zs)
    ends = (lane == wanted).astype(jnp.bfloat16)
    filler = jnp.zeros((8, width - 128), jnp.float32)
    spare = ends_ref.shape[1] - 2 * row_size - 8
    for x in range(planes):
        plane = plane_rows(raw_ref.at[:, x], ys)
        rows_ref[place_of(x, planes)] = plane
        tail = jnp.concatenate([back_y[x, :, lanes - 128 :], filler], axis=1)
        pieces = [dot(ends, plane), tail]
        if spare:
            pieces.append(jnp.zeros((spare, width), jnp.float32))
        ends_ref[x] = jnp.concatenate(pieces, axis=0).astype(jnp.bfloat16)


def turn_kernel(raw_ref, rows_ref, turned_ref):
    planes, depth, width = rows_ref.shape
    for x in range(planes):
        rows_ref[place_of(x, planes)] = plane_rows(raw_ref.at[:, x], raw_ref.shape[2])
    turned_ref[...] = rows_ref[...].reshape(planes * depth, width).T


def move_plane(same, count, ahead, back, above, below):
    depth = same.shape[1]
    moved = dot(site_matrix([(ahead[:, :depth], same)], count), above)
    return (moved + dot(site_matrix([(back[:, :depth], same)], count), below)).astype(jnp.bfloat16)


def same_site(sites, depth):
    site, lane = iotas((sites, depth))
    return (lane % sites == site).astype(jnp.float32)


def set_right(right_ref, place, moved):
    depth, width = moved.shape
    half = depth // 2
    start = place * depth
    real, imag = moved[:half], moved[half:]
    right_ref[start : start + half, :width] = real
    right_ref[start : start + half, width:] = imag
    right_ref[start + half : start + depth, :width] = imag
    right_ref[start + half : start + depth, width:] = -real


def inner_kernel(sites, rows_ref, ahead_ref, back_ref, right_ref, turned_ref):
    planes, depth, width = rows_ref.shape
    same = same_site(sites, depth)
    for x in range(1, planes - 1):
        above = rows_ref[place_of(x + 1, planes)]
        below = rows_ref[place_of(x - 1, planes)]
        moved = move_plane(same, depth // sites, ahead_ref[x], back_ref[x - 1], above, below)
        set_right(right_ref, place_of(x, planes), moved)
    turned_ref[...] = rows_ref[...].reshape(planes * depth, width).T


def begin_first_kernel(own_ref, others_ref, right_ref, total_ref):
    inner = right_ref.shape[0]
    right = right_ref[...]
    total_ref[0] = dot(own_ref[:, :inner], right)
    for k in range(others_ref.shape[0]):
        total_ref[k + 1] = dot(others_ref[k, :, :inner], right)


def begin_second_kernel(lefts_ref, right_ref, total_ref):
    inner = right_ref.shape[0]
    right = right_ref[...]
    for k in range(lefts_ref.shape[0]):
        total_ref[k] = dot(lefts_ref[k, :, :inner], right)


def bits(axis):
    return range(lax.axis_size(axis).bit_length() - 1)


def steps():
    one = [("gx", bit) for bit in bits("gx")[:-1]]
    two = [("gy", bit) for bit in bits("gy")]
    both = min(len(one), len(two))
    pairs = [pair for ends in zip(one, two) for pair in (ends, ends[::-1])]
    return pairs + [(step, step) for step in one[both:] + two[both:]]


def my_bit(axis, bit):
    return lax.bitwise_and(lax.shift_right_logical(lax.axis_index(axis), bit), 1)


def my_side(step):
    even, odd = (my_bit(*way) for way in step)
    return jnp.where(my_bit("ma", 0) == 0, even, odd)


def project(terms, begun_ref, keep_refs, send_refs, total_ref):
    for k, term in enumerate(terms):
        total_ref[k] = begun_ref[k] + term
    groups, own_modes, _ = total_ref.shape
    my_modes = lax.axis_index("ma")
    odd_core = my_bit("ma", 0)
    top = my_bit("gx", bits("gx")[-1])
    across_x, across_y = lax.axis_size("gx"), lax.axis_size("gy")
    parts, count, rows, width = keep_refs[0].shape
    plan = steps()
    mine = my_side(plan[0])

    def piece(gx, gy):
        start = (gx * across_y + gy) * rows
        group = lax.rem(start // own_modes + groups - my_modes, groups)
        begin = start % own_modes
        return total_ref[group, begin : begin + rows]

    for kind in range(2):
        half = lax.bitwise_xor(top, 1 - kind)

        def chosen(gx, gy):
            return jnp.where(half == 0, piece(gx, gy), piece(gx + across_x // 2, gy))

        def at(index):
            places = []
            for core in range(2):
                place = {"gx": 0, "gy": 0}
                for k, step in enumerate(plan):
                    axis, bit = step[core]
                    place[axis] |= (index >> (len(plan) - 1 - k) & 1) << bit
                places.append((place["gx"], place["gy"]))
            if places[0] == places[1]:
                return chosen(*places[0])
            return jnp.where(odd_core == 0, chosen(*places[0]), chosen(*places[1]))

        for index in range(count):
            low, high = at(index), at(index + count)
            keep = jnp.where(mine == 0, low, high)
            send = jnp.where(mine == 0, high, low).astype(jnp.bfloat16)
            for p in range(parts):
                keep_refs[kind][p, index] = keep[:, p * width : (p + 1) * width]
                send_refs[kind][p, index] = send[:, p * width : (p + 1) * width]


def first_kernel(
    sites, rows_ref, high_ref, low_ref, ahead_ref, back_ref, past_maps_ref, own_ref, others_ref, begun_ref,
    *refs,
):
    *refs, right_ref, total_ref = refs
    planes, depth, _ = rows_ref.shape
    same = same_site(sites, depth)
    count = depth // sites
    _, ys, colours, zs, _ = high_ref.shape
    links = low_ref[:, ys:, :, :, :ys].reshape(-1, ys)
    lanes = past_maps_ref.shape[1] // 2
    count = links.shape[0]
    spread = past_maps_ref[:ys, :lanes].astype(jnp.bfloat16)
    match = past_maps_ref[ys : ys + count, lanes:]
    start = past_maps_ref.shape[0] - 24
    choose = past_maps_ref[start : start + 16, :count].astype(jnp.bfloat16)
    past = dot(choose, (dot(links, spread) * match).astype(jnp.bfloat16))
    past = jnp.where(past_maps_ref[start + 16 : start + 17, :lanes] > 0.5, past[:8], past[8:])
    count = depth // sites
    above = rows_ref[place_of(1, planes)]
    set_right(right_ref, 0, move_plane(same, count, ahead_ref[0], past, above, plane_rows(low_ref, ys)))
    x = planes - 1
    below = rows_ref[place_of(x - 1, planes)]
    moved = move_plane(same, count, ahead_ref[x], back_ref[x - 1], plane_rows(high_ref, ys), below)
    set_right(right_ref, 1, moved)
    inner = (planes - 2) * depth
    lefts = [own_ref[:, inner:]] + [others_ref[k, :, inner:] for k in range(others_ref.shape[0])]
    terms = [dot(left, right_ref[...]) for left in lefts]
    keep_other, keep_own, send_ref = refs
    project(terms, begun_ref, (keep_other, keep_own), (send_ref.at[0], send_ref.at[1]), total_ref)


def move_y_kernel(
    sites, zs, rows_ref, others_ref, near_ref, far_ref, ahead_ref, back_ref, turned_ref, field_ref
):
    planes, depth, width = rows_ref.shape
    groups = others_ref.shape[0] + 1
    row_size = depth // sites * zs
    reach = depth + near_ref.shape[1]
    head = back_ref.shape[2] - 128
    site, lane = iotas((sites, reach))
    inner = lane < depth
    upper = (lane >= depth) & (lane < depth + row_size)
    lower = (lane >= depth + row_size) & (lane < depth + 2 * row_size)
    lane_z = lane % zs
    to_next = (inner & (lane % sites == site + zs)) | (upper & (site == sites - zs + lane_z))
    to_last = (inner & (lane % sites == site - zs)) | (lower & (site == lane_z))
    to_next = jnp.where(to_next, -1.0, 0.0)
    to_last = jnp.where(to_last, -1.0, 0.0)
    _, lane = iotas((8, 128))
    spare = jnp.zeros((near_ref.shape[1] - far_ref.shape[2], width), far_ref.dtype)
    for x in range(planes):
        past = near_ref[x, 2 * row_size : 2 * row_size + 8, :128].astype(jnp.float32)
        mixed = jnp.where(lane >= depth + row_size - head, past, back_ref[x, :, head:])
        back = jnp.concatenate([back_ref[x, :, :head], mixed], axis=1)[:, :reach]
        matrix = site_matrix([(ahead_ref[x, :, :reach], to_next), (back, to_last)], depth // sites)
        place = place_of(x, planes)
        column = jnp.concatenate([rows_ref[place], near_ref[x]], axis=0)
        field_ref[0, place] = dot(matrix, column).astype(jnp.bfloat16)
        for k in range(groups - 1):
            column = jnp.concatenate([others_ref[k, place], far_ref[k, x], spare], axis=0)
            field_ref[k + 1, place] = dot(matrix, column).astype(jnp.bfloat16)
    for k in range(groups):
        turned_ref[k] = field_ref[k].reshape(planes * depth, width).T


def second_kernel(lefts_ref, right_ref, begun_ref, *refs):
    *refs, total_ref = refs
    inner = lefts_ref.shape[2] - right_ref.shape[0]
    lefts = [lefts_ref[k, :, inner:] for k in range(lefts_ref.shape[0])]
    terms = [dot(left, right_ref[...]) for left in lefts]
    project(terms, begun_ref, refs[:2], refs[2:], total_ref)


def exchange(block, step):
    axes = ("gx", "gy", "ma")
    sizes = [lax.axis_size(axis) for axis in axes]
    route = []
    for source in range(sizes[0] * sizes[1] * sizes[2]):
        where = [source // (sizes[1] * sizes[2]), source // sizes[2] % sizes[1], source % sizes[2]]
        axis, bit = step[where[2] % 2]
        where[axes.index(axis)] ^= 1 << bit
        route.append((source, (where[0] * sizes[1] + where[1]) * sizes[2] + where[2]))
    return lax.ppermute(block, axes, route)


def halve(sums, step, weight=0):
    parts = sum(kept.shape[0] for kept, _, _ in sums)
    count, rows, width = sums[0][0].shape[1:]
    dims = (parts, count // 2, rows, width)

    def merge(*refs):
        *refs, keep_ref, send_ref = refs
        mine = my_side(step)
        start = 0
        for k, (_, _, which) in enumerate(sums):
            kept_ref, came_ref = refs[2 * k : 2 * k + 2]
            came_ref = came_ref if which is None else came_ref.at[which]
            end = start + kept_ref.shape[0]
            for index in range(count // 2):
                low, high = (
                    kept_ref[:, at] + came_ref[:, at].astype(jnp.float32) for at in (index, index + count // 2)
                )
                keep_ref[start:end, index] = jnp.where(mine == 0, low, high)
                send_ref[start:end, index] = jnp.where(mine == 0, high, low).astype(send_ref.dtype)
            start = end

    operands = [a for kept, came, _ in sums for a in (kept, came)]
    keep, send = call(merge, (pltpu.VMEM(dims, jnp.float32), pltpu.VMEM(dims, jnp.bfloat16)), weight, operands)
    return keep, exchange(send, step)


def sum_kernel(kept_ref, came_ref, send_ref):
    send_ref[...] = (kept_ref[...] + came_ref[...].astype(jnp.float32)).astype(send_ref.dtype)


def cross_kernel(start, kept_ref, crossed_ref, out_ref):
    kept = kept_ref[start : start + out_ref.shape[0]]
    out_ref[...] = kept + crossed_ref[...].astype(jnp.float32)


def finish_kernel(came_ref, *refs):
    *kept_refs, out_ref = refs
    parts = out_ref.shape[1]
    for d, kept_ref in enumerate(kept_refs):
        out_ref[d] = kept_ref[:, 0] + came_ref[d * parts : (d + 1) * parts, 0].astype(jnp.float32)


def local(eigen_modes, links_first, links_second):
    f32, bf16 = jnp.float32, jnp.bfloat16
    parts, planes, ys, zs, colours, width = eigen_modes.shape
    sites = ys * zs
    depth = parts * colours * sites
    row_size = parts * colours * zs
    edge = -(-(2 * row_size + 8) // 16) * 16
    lanes = -(-(depth + 2 * row_size) // 128) * 128
    across_x, across_y, groups = (lax.axis_size(a) for a in ("gx", "gy", "ma"))
    rows = groups * width // (across_x * across_y)
    inner_depth = (planes - 2) * depth
    raw = eigen_modes.transpose(0, 1, 2, 4, 3, 5)

    def shape(*dims, dtype=bf16):
        return pltpu.VMEM(dims, dtype)

    field_shape = shape(planes, depth, width)
    turned_shape = shape(width, planes * depth)
    total_shape = shape(groups, width, parts * width, dtype=f32)
    link_shape = shape(planes, 8, lanes, dtype=f32)
    total = pltpu.VMEM(total_shape.shape, f32)
    step_flops = 2 * planes * depth * depth * width
    project_flops = 2 * groups * width * planes * depth * parts * width

    raw_others = [shifted(raw, "ma", -step) for step in range(1, groups)]
    raw_links_x, raw_links_y = (a.transpose(0, 1, 2, 3, 5, 4) for a in (links_first, links_second))
    inputs = [raw, raw_links_x, raw_links_y]
    first_plane, last_plane, *inputs, past_maps = call(
        edges_kernel,
        (
            shape(parts, ys, colours, zs, width), shape(parts, ys + colours, colours, zs, width),
            *(shape(*a.shape) for a in inputs),
            shape(map_rows(parts, colours, planes, ys, zs)[-1], 2 * lanes, dtype=f32),
            shape(map_rows(parts, colours, 1, ys, zs)[-1], 2 * lanes, dtype=f32),
        ),
        0,
        inputs,
        [pltpu.SemaphoreType.DMA((5,))],
        [pltpu.HBM] * len(inputs),
    )
    low = shifted(last_plane, "gx", 1)
    high = shifted(first_plane, "gx", -1)
    field, ends, ahead_x, back_x, ahead_y, back_y = call(
        prepare_kernel,
        (field_shape, shape(planes, edge, width), link_shape, link_shape, link_shape, link_shape),
        0,
        inputs,
    )
    near = shifted(ends, "gy", 1)
    if across_y != 2:
        ahead_row = lax.broadcasted_iota(jnp.int32, ends.shape, 1) < row_size
        near = jnp.where(ahead_row, shifted(ends, "gy", -1), near)

    plan = steps()
    top = ("gx", bits("gx")[-1])
    pieces = across_x * across_y // 4
    kept_shape = shape(parts, pieces, rows, width, dtype=f32)

    def inner(*refs):
        inner_kernel(sites, *refs)

    def first(*refs):
        first_kernel(sites, *refs)

    def move_y(*refs):
        move_y_kernel(sites, zs, *refs)

    right, own = call(
        inner, (shape(inner_depth, parts * width), turned_shape), 2 * step_flops, [field, ahead_x, back_x]
    )
    turned = [call(turn_kernel, (field_shape, turned_shape), step_flops // 4, [r]) for r in raw_others]
    fields = jnp.stack([t[0] for t in turned])
    others = jnp.stack([t[1] for t in turned])
    begun_first = call(begin_first_kernel, total_shape, project_flops, [own, others, right])
    kept_first, own_first, sent_first, right_edge = call(
        first,
        (kept_shape, kept_shape, shape(2, parts, pieces, rows, width), shape(2 * depth, parts * width)),
        project_flops,
        [field, high, low, ahead_x, back_x, past_maps, own, others, begun_first],
        [total],
    )
    near, right_edge = lax.optimization_barrier((near, right_edge))
    near_rows = near[:, : 2 * row_size]
    far = jnp.stack([shifted(near_rows, "ma", -step) for step in range(1, groups)])
    lefts = call(
        move_y, shape(groups, width, planes * depth), 2 * step_flops,
        [field, fields, near, far, ahead_y, back_y],
        [pltpu.VMEM((groups,) + field_shape.shape, bf16)],
    )
    begun_second = call(begin_second_kernel, total_shape, 8 * project_flops, [lefts, right])
    sent_shape = shape(parts, pieces, rows, width)
    kept_second, own_second, sent_second, sent_own = call(
        second_kernel, (kept_shape, kept_shape, sent_shape, sent_shape), project_flops,
        [lefts, right_edge, begun_second], [total],
    )
    came_first = exchange(sent_first, plan[0])
    crossing = [(kept_first, came_first, 0), (kept_second, exchange(sent_second, plan[0]), None)]
    staying = [(own_first, came_first, 1), (own_second, exchange(sent_own, plan[0]), None)]
    after = kept_second
    for step in plan[1:]:
        for d, (kept, came, which) in enumerate(crossing):
            came, after = lax.optimization_barrier((came, after))
            kept, came = halve([(kept, came, which)], step)
            crossing[d], after = (kept, came, None), kept
    crossed = []
    for kept, came, _ in crossing:
        came, after = lax.optimization_barrier((came, after))
        after = call(sum_kernel, pltpu.VMEM(kept.shape, bf16), 0, [kept, came])
        crossed.append(exchange(after, (top, top)))
    for step in plan[1:]:
        kept, came, which = staying[-1]
        came, after = lax.optimization_barrier((came, after))
        kept, came = halve(staying[:-1] + [(kept, came, which)], step)
        staying, after = [(kept, came, None)], kept
    kept, came, _ = staying[0]
    totals = []
    for d, block in enumerate(crossed):

        def cross(*refs, start=d * parts):
            cross_kernel(start, *refs)

        block, after = lax.optimization_barrier((block, after))
        after = call(cross, shape(*block.shape, dtype=f32), 4 * project_flops, [kept, block])
        totals.append(after)
    came, after = lax.optimization_barrier((came, after))
    return call(
        finish_kernel, jax.ShapeDtypeStruct((2, parts, rows, width), f32), 0, [came, *totals]
    )


def solution(mesh):
    return jax.shard_map(
        local,
        mesh=mesh,
        in_specs=(
            P("cuts", "gx", "gy", None, None, "ma"),
            P("cuts", None, None, "gx", "gy", None),
            P("cuts", None, None, "gx", "gy", None),
        ),
        out_specs=P("cuts", None, ("gx", "gy"), "ma"),
        check_vma=False,
    )
```

```python
import jax
import jax.numpy as jnp
from jax import lax
from jax.experimental import pallas as pl
from jax.experimental.pallas import tpu as pltpu
from jax.sharding import PartitionSpec as P

VMEM_LIMIT = 16 * 1024 * 1024


def shifted(block, axis, distance):
    devices = range(lax.axis_size(axis))
    route = [((i - distance) % len(devices), i) for i in devices]
    return lax.ppermute(block, axis, route)


def call(body, out_shape, flops, operands, scratch=(), places=None):
    places = places or [pltpu.VMEM] * len(operands)
    return pl.pallas_call(
        body,
        out_shape=out_shape,
        in_specs=[pl.BlockSpec(memory_space=place) for place in places],
        scratch_shapes=scratch,
        cost_estimate=pl.CostEstimate(flops=flops // 2, bytes_accessed=0, transcendentals=0),
        compiler_params=pltpu.CompilerParams(vmem_limit_bytes=VMEM_LIMIT),
    )(*(pltpu.with_memory_space_constraint(a, place) for a, place in zip(operands, places)))


def dot(a, b):
    return jnp.dot(a, b, preferred_element_type=jnp.float32)


def iotas(shape):
    return (
        lax.broadcasted_iota(jnp.int32, shape, 0),
        lax.broadcasted_iota(jnp.int32, shape, 1),
    )


def place_of(x, planes):
    return planes - 2 if x == 0 else x if x == planes - 1 else x - 1


def map_rows(parts, colours, planes, ys, zs):
    match = ys
    choose = match + -(-parts * colours * colours * planes * zs // 8) * 8
    first_part = choose + 2 * parts * planes * 8
    return match, choose, first_part, first_part + 8


def write_maps(ref, parts, colours, planes, ys, zs):
    lanes = ref.shape[1] // 2
    sites = ys * zs
    depth = parts * colours * sites
    row_size = parts * colours * zs
    match, choose, first_part, _ = map_rows(parts, colours, planes, ys, zs)

    def ones(mask):
        return jnp.where(mask, 1.0, 0.0)

    def column(count):
        return lax.broadcasted_iota(jnp.int32, (count, 1), 0)

    def line(count):
        return lax.broadcasted_iota(jnp.int32, (1, count), 1)

    lane = line(lanes)
    inner = lane < depth
    past = lax.rem(jnp.maximum(lane - depth, 0), row_size)
    used = lane < depth + 2 * row_size
    part = jnp.where(inner, lax.div(lane, colours * sites), lax.div(past, colours * zs))
    colour = lax.rem(jnp.where(inner, lax.div(lane, sites), lax.div(past, zs)), colours)
    z = lax.rem(jnp.where(inner, lane, past), zs)
    y = lax.div(lax.rem(lane, sites), zs)
    ref[:ys, :lanes] = ones(column(ys) == jnp.where(inner, y, ys - 1))
    ref[:ys, lanes:] = ones(column(ys) == jnp.where(inner, y, ys) - 1)

    count = parts * colours * colours * planes * zs

    def link(index):
        x = lax.rem(lax.div(index, zs), planes)
        right = lax.rem(lax.div(index, zs * planes), colours)
        left = lax.rem(lax.div(index, zs * planes * colours), colours)
        return x, right, left, lax.div(index, zs * planes * colours * colours)

    row = column(count)
    _, right, left, _ = link(row)
    row_z = lax.rem(row, zs)
    key = jnp.where(used, colour * zs + z, -1)
    ref[match : match + count, :lanes] = ones(right * zs + row_z == key)
    ref[match : match + count, lanes:] = ones(left * zs + row_z == key)

    out = column(parts * planes * 8)
    field_part = lax.div(out, planes * 8)
    out_x = lax.rem(lax.div(out, 8), planes)
    out_part = lax.div(lax.rem(out, 8), colours)
    out_colour = lax.rem(lax.rem(out, 8), colours)
    x, right, left, source_part = link(line(count))
    source = source_part * planes + x
    wanted = jnp.where(out_part < parts, lax.rem(out_part + field_part, 2) * planes + out_x, -1)
    sign_ahead = jnp.where((field_part == 1) & (out_part == 0), -1.0, 1.0)
    sign_back = jnp.where((field_part == 0) & (out_part == 1), 1.0, -1.0)
    half = parts * planes * 8
    for start, end, sign in ((choose, left, sign_ahead), (choose + half, right, sign_back)):
        hit = source * colours + end == wanted * colours + jnp.where(wanted < 0, -1, out_colour)
        ref[start : start + half, :count] = jnp.where(hit, sign, 0.0)
    ref[first_part:, :lanes] = jnp.broadcast_to(ones(part == 0), (8, lanes))


def coefficients(links_x, links_y, maps_ref, planes):
    lanes = maps_ref.shape[1] // 2
    ys = links_x.shape[1]
    count = links_x.shape[0]
    half = 2 * planes * 8
    wide = dot(jnp.concatenate([links_x, links_y], axis=0), maps_ref[:ys].astype(jnp.bfloat16))
    match = maps_ref[ys : ys + count]
    match_ahead, match_back = match[:, :lanes], match[:, lanes:]
    choose = maps_ref[ys + count : ys + count + 2 * half, :count].astype(jnp.bfloat16)
    first_part = maps_ref[ys + count + 2 * half : ys + count + 2 * half + 1, :lanes] > 0.5
    ahead = jnp.concatenate([wide[:count, :lanes] * match_ahead, wide[count:, lanes:] * match_ahead], axis=1)
    back = jnp.concatenate([wide[:count, :lanes] * match_back, wide[count:, :lanes] * match_back], axis=1)
    out = []
    for chosen in (
        dot(choose[:half], ahead.astype(jnp.bfloat16)), dot(choose[half:], back.astype(jnp.bfloat16))
    ):
        for start in (0, lanes):
            part = chosen[:, start : start + lanes]
            rows = jnp.where(first_part, part[: half // 2], part[half // 2 :])
            out.append(rows.reshape(planes, 8, lanes))
    return out


def plane_rows(ref, ys):
    parts, _, colours, zs, width = ref.shape
    return jnp.concatenate(
        [ref[p, :ys, c].reshape(ys * zs, width) for p in range(parts) for c in range(colours)],
        axis=0,
    )


def edges_kernel(
    raw_hbm, links_x_hbm, links_y_hbm,
    first_ref, last_ref, raw_ref, links_x_ref, links_y_ref, maps_ref, past_maps_ref, arrived,
):
    parts, planes, ys, colours, zs, _ = raw_hbm.shape
    sources = (raw_hbm.at[:, planes - 1], raw_hbm.at[:, 0], links_x_hbm, links_y_hbm, raw_hbm)
    targets = (last_ref.at[:, :ys], first_ref, links_x_ref, links_y_ref, raw_ref)
    copies = [
        pltpu.make_async_copy(source, target, arrived.at[i])
        for i, (source, target) in enumerate(zip(sources, targets))
    ]
    for copy in copies:
        copy.start()
    last_ref[:, ys:] = jnp.zeros((parts, colours) + last_ref.shape[2:], last_ref.dtype)
    write_maps(maps_ref, parts, colours, planes, ys, zs)
    write_maps(past_maps_ref, parts, colours, 1, ys, zs)
    copies[2].wait()
    last_ref[:, ys:, :, :, :ys] = links_x_ref[:, :, :, planes - 1]
    for copy in copies[:2] + copies[3:]:
        copy.wait()


def site_matrix(rows_and_masks, count):
    blocks = []
    for q in range(count):
        block = None
        for rows, mask in rows_and_masks:
            term = rows[q : q + 1] * mask
            block = term if block is None else block + term
        blocks.append(block.astype(jnp.bfloat16))
    return jnp.concatenate(blocks, axis=0)


def prepare_kernel(
    raw_ref, links_x_ref, links_y_ref, maps_ref,
    rows_ref, ends_ref, ahead_x_ref, back_x_ref, ahead_y_ref, back_y_ref,
):
    planes, depth, width = rows_ref.shape
    zs = raw_ref.shape[4]
    ys = raw_ref.shape[2]
    sites = ys * zs
    row_size = depth // sites * zs
    lanes = ahead_y_ref.shape[2]
    ahead_x, ahead_y, back_x, back_y = coefficients(
        links_x_ref[...].reshape(-1, ys), links_y_ref[...].reshape(-1, ys), maps_ref, planes
    )
    ahead_x_ref[...] = ahead_x
    back_x_ref[...] = back_x
    ahead_y_ref[...] = ahead_y
    back_y_ref[...] = back_y

    row, lane = iotas((2 * row_size, depth))
    spot = row % row_size
    wanted = (spot // zs) * sites + spot % zs + jnp.where(row < row_size, 0, sites - zs)
    ends = (lane == wanted).astype(jnp.bfloat16)
    filler = jnp.zeros((8, width - 128), jnp.float32)
    spare = ends_ref.shape[1] - 2 * row_size - 8
    for x in range(planes):
        plane = plane_rows(raw_ref.at[:, x], ys)
        rows_ref[place_of(x, planes)] = plane
        tail = jnp.concatenate([back_y[x, :, lanes - 128 :], filler], axis=1)
        pieces = [dot(ends, plane), tail]
        if spare:
            pieces.append(jnp.zeros((spare, width), jnp.float32))
        ends_ref[x] = jnp.concatenate(pieces, axis=0).astype(jnp.bfloat16)


def turn_kernel(raw_ref, rows_ref, turned_ref):
    planes, depth, width = rows_ref.shape
    for x in range(planes):
        rows_ref[place_of(x, planes)] = plane_rows(raw_ref.at[:, x], raw_ref.shape[2])
    turned_ref[...] = rows_ref[...].reshape(planes * depth, width).T


def move_plane(same, count, ahead, back, above, below):
    depth = same.shape[1]
    moved = dot(site_matrix([(ahead[:, :depth], same)], count), above)
    return (moved + dot(site_matrix([(back[:, :depth], same)], count), below)).astype(jnp.bfloat16)


def same_site(sites, depth):
    site, lane = iotas((sites, depth))
    return (lane % sites == site).astype(jnp.float32)


def set_right(right_ref, place, moved):
    depth, width = moved.shape
    half = depth // 2
    start = place * depth
    real, imag = moved[:half], moved[half:]
    right_ref[start : start + half, :width] = real
    right_ref[start : start + half, width:] = imag
    right_ref[start + half : start + depth, :width] = imag
    right_ref[start + half : start + depth, width:] = -real


def inner_kernel(
    sites, rows_ref, ahead_ref, back_ref, right_ref, turned_ref, matrix_ref, ahead_part_ref, back_part_ref
):
    planes, depth, width = rows_ref.shape
    same = same_site(sites, depth)
    for x in range(1, planes - 1):
        above = rows_ref[place_of(x + 1, planes)]
        below = rows_ref[place_of(x - 1, planes)]
        moved = move_plane(same, depth // sites, ahead_ref[x], back_ref[x - 1], above, below)
        set_right(right_ref, place_of(x, planes), moved)
    turned_ref[...] = rows_ref[...].reshape(planes * depth, width).T
    x, count = planes - 1, depth // sites
    matrix_ref[...] = site_matrix([(ahead_ref[x, :, :depth], same)], count)
    ahead_part_ref[...] = dot(site_matrix([(ahead_ref[0, :, :depth], same)], count), rows_ref[place_of(1, planes)])
    below = rows_ref[place_of(x - 1, planes)]
    back_part_ref[...] = dot(site_matrix([(back_ref[x - 1, :, :depth], same)], count), below)


def begin_first_kernel(own_ref, others_ref, right_ref, total_ref):
    inner = right_ref.shape[0]
    right = right_ref[...]
    total_ref[0] = dot(own_ref[:, :inner], right)
    for k in range(others_ref.shape[0]):
        total_ref[k + 1] = dot(others_ref[k, :, :inner], right)


def begin_second_kernel(lefts_ref, right_ref, total_ref):
    inner = right_ref.shape[0]
    right = right_ref[...]
    for k in range(lefts_ref.shape[0]):
        total_ref[k] = dot(lefts_ref[k, :, :inner], right)


def bits(axis):
    return range(lax.axis_size(axis).bit_length() - 1)


def steps():
    one = [("gx", bit) for bit in bits("gx")[:-1]]
    two = [("gy", bit) for bit in bits("gy")]
    both = min(len(one), len(two))
    pairs = [pair for ends in zip(one, two) for pair in (ends, ends[::-1])]
    return pairs + [(step, step) for step in one[both:] + two[both:]]


def my_bit(axis, bit):
    return lax.bitwise_and(lax.shift_right_logical(lax.axis_index(axis), bit), 1)


def my_side(step):
    even, odd = (my_bit(*way) for way in step)
    return jnp.where(my_bit("ma", 0) == 0, even, odd)


def project(terms, begun_ref, keep_refs, send_refs, total_ref):
    for k, term in enumerate(terms):
        total_ref[k] = begun_ref[k] + term
    groups, own_modes, _ = total_ref.shape
    my_modes = lax.axis_index("ma")
    odd_core = my_bit("ma", 0)
    top = my_bit("gx", bits("gx")[-1])
    across_x, across_y = lax.axis_size("gx"), lax.axis_size("gy")
    parts, count, rows, width = keep_refs[0].shape
    plan = steps()
    mine = my_side(plan[0])

    def piece(gx, gy):
        start = (gx * across_y + gy) * rows
        group = lax.rem(start // own_modes + groups - my_modes, groups)
        begin = start % own_modes
        return total_ref[group, begin : begin + rows]

    for kind in range(2):
        half = lax.bitwise_xor(top, 1 - kind)

        def chosen(gx, gy):
            return jnp.where(half == 0, piece(gx, gy), piece(gx + across_x // 2, gy))

        def at(index):
            places = []
            for core in range(2):
                place = {"gx": 0, "gy": 0}
                for k, step in enumerate(plan):
                    axis, bit = step[core]
                    place[axis] |= (index >> (len(plan) - 1 - k) & 1) << bit
                places.append((place["gx"], place["gy"]))
            if places[0] == places[1]:
                return chosen(*places[0])
            return jnp.where(odd_core == 0, chosen(*places[0]), chosen(*places[1]))

        for index in range(count):
            low, high = at(index), at(index + count)
            keep = jnp.where(mine == 0, low, high)
            send = jnp.where(mine == 0, high, low).astype(jnp.bfloat16)
            for p in range(parts):
                keep_refs[kind][p, index] = keep[:, p * width : (p + 1) * width]
                send_refs[kind][p, index] = send[:, p * width : (p + 1) * width]


def first_kernel(
    sites, planes, high_ref, low_ref, matrix_ref, ahead_part_ref, back_part_ref, past_maps_ref, own_ref, others_ref, begun_ref,
    *refs,
):
    *refs, right_ref, total_ref = refs
    depth = matrix_ref.shape[0]
    same = same_site(sites, depth)
    _, ys, colours, zs, _ = high_ref.shape
    links = low_ref[:, ys:, :, :, :ys].reshape(-1, ys)
    lanes = past_maps_ref.shape[1] // 2
    count = links.shape[0]
    spread = past_maps_ref[:ys, :lanes].astype(jnp.bfloat16)
    match = past_maps_ref[ys : ys + count, lanes:]
    start = past_maps_ref.shape[0] - 24
    choose = past_maps_ref[start : start + 16, :count].astype(jnp.bfloat16)
    past = dot(choose, (dot(links, spread) * match).astype(jnp.bfloat16))
    past = jnp.where(past_maps_ref[start + 16 : start + 17, :lanes] > 0.5, past[:8], past[8:])
    past = site_matrix([(past[:, :depth], same)], depth // sites)
    moved = ahead_part_ref[...] + dot(past, plane_rows(low_ref, ys))
    set_right(right_ref, 0, moved.astype(jnp.bfloat16))
    moved = dot(matrix_ref[...], plane_rows(high_ref, ys)) + back_part_ref[...]
    set_right(right_ref, 1, moved.astype(jnp.bfloat16))
    inner = (planes - 2) * depth
    lefts = [own_ref[:, inner:]] + [others_ref[k, :, inner:] for k in range(others_ref.shape[0])]
    terms = [dot(left, right_ref[...]) for left in lefts]
    keep_other, keep_own, send_ref = refs
    project(terms, begun_ref, (keep_other, keep_own), (send_ref.at[0], send_ref.at[1]), total_ref)


def begin_y_kernel(sites, zs, rows_ref, others_ref, ahead_ref, back_ref, part_ref):
    planes, depth, _ = rows_ref.shape
    site, lane = iotas((sites, depth))
    to_next = jnp.where(lane % sites == site + zs, -1.0, 0.0)
    to_last = jnp.where(lane % sites == site - zs, -1.0, 0.0)
    for x in range(planes):
        ahead, back = ahead_ref[x, :, :depth], back_ref[x, :, :depth]
        matrix = site_matrix([(ahead, to_next), (back, to_last)], depth // sites)
        place = place_of(x, planes)
        part_ref[0, place] = dot(matrix, rows_ref[place])
        for k in range(others_ref.shape[0]):
            part_ref[k + 1, place] = dot(matrix, others_ref[k, place])


def move_y_kernel(sites, zs, part_ref, near_ref, far_ref, ahead_ref, turned_ref, field_ref):
    groups, planes, depth, width = part_ref.shape
    row_size = depth // sites * zs
    tail = 128
    head = ahead_ref.shape[2] - tail
    site, lane = iotas((sites, tail))
    lane = lane + head
    upper = (lane >= depth) & (lane < depth + row_size)
    lower = (lane >= depth + row_size) & (lane < depth + 2 * row_size)
    to_next = jnp.where(upper & (site == sites - zs + lane % zs), -1.0, 0.0)
    to_last = jnp.where(lower & (site == lane % zs), -1.0, 0.0)
    above = jnp.zeros((depth - head, width), jnp.bfloat16)
    below = jnp.zeros((tail - 2 * row_size - (depth - head), width), jnp.bfloat16)
    for x in range(planes):
        past = near_ref[x, 2 * row_size : 2 * row_size + 8, :tail].astype(jnp.float32)
        matrix = site_matrix([(ahead_ref[x, :, head:], to_next), (past, to_last)], depth // sites)
        place = place_of(x, planes)
        for k in range(groups):
            edge = near_ref[x, : 2 * row_size] if k == 0 else far_ref[k - 1, x]
            moved = part_ref[k, place] + dot(matrix, jnp.concatenate([above, edge, below], axis=0))
            field_ref[k, place] = moved.astype(jnp.bfloat16)
    for k in range(groups):
        turned_ref[k] = field_ref[k].reshape(planes * depth, width).T


def second_kernel(lefts_ref, right_ref, begun_ref, *refs):
    *refs, total_ref = refs
    inner = lefts_ref.shape[2] - right_ref.shape[0]
    lefts = [lefts_ref[k, :, inner:] for k in range(lefts_ref.shape[0])]
    terms = [dot(left, right_ref[...]) for left in lefts]
    project(terms, begun_ref, refs[:2], refs[2:], total_ref)


def exchange(block, step):
    axes = ("gx", "gy", "ma")
    sizes = [lax.axis_size(axis) for axis in axes]
    route = []
    for source in range(sizes[0] * sizes[1] * sizes[2]):
        where = [source // (sizes[1] * sizes[2]), source // sizes[2] % sizes[1], source % sizes[2]]
        axis, bit = step[where[2] % 2]
        where[axes.index(axis)] ^= 1 << bit
        route.append((source, (where[0] * sizes[1] + where[1]) * sizes[2] + where[2]))
    return lax.ppermute(block, axes, route)


def halve(sums, step, weight=0):
    parts = sum(kept.shape[0] for kept, _, _ in sums)
    count, rows, width = sums[0][0].shape[1:]
    dims = (parts, count // 2, rows, width)

    def merge(*refs):
        *refs, keep_ref, send_ref = refs
        mine = my_side(step)
        start = 0
        for k, (_, _, which) in enumerate(sums):
            kept_ref, came_ref = refs[2 * k : 2 * k + 2]
            came_ref = came_ref if which is None else came_ref.at[which]
            end = start + kept_ref.shape[0]
            for index in range(count // 2):
                low, high = (
                    kept_ref[:, at] + came_ref[:, at].astype(jnp.float32) for at in (index, index + count // 2)
                )
                keep_ref[start:end, index] = jnp.where(mine == 0, low, high)
                send_ref[start:end, index] = jnp.where(mine == 0, high, low).astype(send_ref.dtype)
            start = end

    operands = [a for kept, came, _ in sums for a in (kept, came)]
    keep, send = call(merge, (pltpu.VMEM(dims, jnp.float32), pltpu.VMEM(dims, jnp.bfloat16)), weight, operands)
    return keep, exchange(send, step)


def sum_kernel(kept_ref, came_ref, send_ref):
    send_ref[...] = (kept_ref[...] + came_ref[...].astype(jnp.float32)).astype(send_ref.dtype)


def cross_kernel(start, kept_ref, crossed_ref, out_ref):
    kept = kept_ref[start : start + out_ref.shape[0]]
    out_ref[...] = kept + crossed_ref[...].astype(jnp.float32)


def finish_kernel(came_ref, *refs):
    *kept_refs, out_ref = refs
    parts = out_ref.shape[1]
    for d, kept_ref in enumerate(kept_refs):
        out_ref[d] = kept_ref[:, 0] + came_ref[d * parts : (d + 1) * parts, 0].astype(jnp.float32)


def local(eigen_modes, links_first, links_second):
    f32, bf16 = jnp.float32, jnp.bfloat16
    parts, planes, ys, zs, colours, width = eigen_modes.shape
    sites = ys * zs
    depth = parts * colours * sites
    row_size = parts * colours * zs
    edge = -(-(2 * row_size + 8) // 16) * 16
    lanes = -(-(depth + 2 * row_size) // 128) * 128
    across_x, across_y, groups = (lax.axis_size(a) for a in ("gx", "gy", "ma"))
    rows = groups * width // (across_x * across_y)
    inner_depth = (planes - 2) * depth
    raw = eigen_modes.transpose(0, 1, 2, 4, 3, 5)

    def shape(*dims, dtype=bf16):
        return pltpu.VMEM(dims, dtype)

    field_shape = shape(planes, depth, width)
    turned_shape = shape(width, planes * depth)
    total_shape = shape(groups, width, parts * width, dtype=f32)
    link_shape = shape(planes, 8, lanes, dtype=f32)
    total = pltpu.VMEM(total_shape.shape, f32)
    step_flops = 2 * planes * depth * depth * width
    project_flops = 2 * groups * width * planes * depth * parts * width

    raw_others = [shifted(raw, "ma", -step) for step in range(1, groups)]
    raw_links_x, raw_links_y = (a.transpose(0, 1, 2, 3, 5, 4) for a in (links_first, links_second))
    inputs = [raw, raw_links_x, raw_links_y]
    first_plane, last_plane, *inputs, past_maps = call(
        edges_kernel,
        (
            shape(parts, ys, colours, zs, width), shape(parts, ys + colours, colours, zs, width),
            *(shape(*a.shape) for a in inputs),
            shape(map_rows(parts, colours, planes, ys, zs)[-1], 2 * lanes, dtype=f32),
            shape(map_rows(parts, colours, 1, ys, zs)[-1], 2 * lanes, dtype=f32),
        ),
        0,
        inputs,
        [pltpu.SemaphoreType.DMA((5,))],
        [pltpu.HBM] * len(inputs),
    )
    low = shifted(last_plane, "gx", 1)
    high = shifted(first_plane, "gx", -1)
    field, ends, ahead_x, back_x, ahead_y, back_y = call(
        prepare_kernel,
        (field_shape, shape(planes, edge, width), link_shape, link_shape, link_shape, link_shape),
        0,
        inputs,
    )
    near = shifted(ends, "gy", 1)
    if across_y != 2:
        ahead_row = lax.broadcasted_iota(jnp.int32, ends.shape, 1) < row_size
        near = jnp.where(ahead_row, shifted(ends, "gy", -1), near)

    plan = steps()
    top = ("gx", bits("gx")[-1])
    pieces = across_x * across_y // 4
    kept_shape = shape(parts, pieces, rows, width, dtype=f32)

    def inner(*refs):
        inner_kernel(sites, *refs)

    def first(*refs):
        first_kernel(sites, planes, *refs)

    def begin_y(*refs):
        begin_y_kernel(sites, zs, *refs)

    def move_y(*refs):
        move_y_kernel(sites, zs, *refs)

    right, own, matrix, ahead_part, back_part = call(
        inner,
        (
            shape(inner_depth, parts * width), turned_shape, shape(depth, depth),
            shape(depth, width, dtype=f32), shape(depth, width, dtype=f32),
        ),
        2 * step_flops,
        [field, ahead_x, back_x],
    )
    turned = [call(turn_kernel, (field_shape, turned_shape), step_flops // 4, [r]) for r in raw_others]
    fields = jnp.stack([t[0] for t in turned])
    others = jnp.stack([t[1] for t in turned])
    begun_first = call(begin_first_kernel, total_shape, project_flops, [own, others, right])
    part_y = call(
        begin_y, shape(groups, planes, depth, width, dtype=f32), 2 * step_flops, [field, fields, ahead_y, back_y]
    )
    part_y, begun_first = lax.optimization_barrier((part_y, begun_first))
    kept_first, own_first, sent_first, right_edge = call(
        first,
        (kept_shape, kept_shape, shape(2, parts, pieces, rows, width), shape(2 * depth, parts * width)),
        project_flops,
        [high, low, matrix, ahead_part, back_part, past_maps, own, others, begun_first],
        [total],
    )
    near, right_edge = lax.optimization_barrier((near, right_edge))
    near_rows = near[:, : 2 * row_size]
    far = jnp.stack([shifted(near_rows, "ma", -step) for step in range(1, groups)])
    lefts = call(
        move_y, shape(groups, width, planes * depth), 2 * step_flops,
        [part_y, near, far, ahead_y],
        [pltpu.VMEM((groups,) + field_shape.shape, bf16)],
    )
    begun_second = call(begin_second_kernel, total_shape, 8 * project_flops, [lefts, right])
    sent_shape = shape(parts, pieces, rows, width)
    kept_second, own_second, sent_second, sent_own = call(
        second_kernel, (kept_shape, kept_shape, sent_shape, sent_shape), project_flops,
        [lefts, right_edge, begun_second], [total],
    )
    came_first = exchange(sent_first, plan[0])
    crossing = [(kept_first, came_first, 0), (kept_second, exchange(sent_second, plan[0]), None)]
    staying = [(own_first, came_first, 1), (own_second, exchange(sent_own, plan[0]), None)]
    after = kept_second
    for step in plan[1:]:
        for d, (kept, came, which) in enumerate(crossing):
            came, after = lax.optimization_barrier((came, after))
            kept, came = halve([(kept, came, which)], step)
            crossing[d], after = (kept, came, None), kept
    crossed = []
    for kept, came, _ in crossing:
        came, after = lax.optimization_barrier((came, after))
        after = call(sum_kernel, pltpu.VMEM(kept.shape, bf16), 0, [kept, came])
        crossed.append(exchange(after, (top, top)))
    for step in plan[1:]:
        kept, came, which = staying[-1]
        came, after = lax.optimization_barrier((came, after))
        kept, came = halve(staying[:-1] + [(kept, came, which)], step)
        staying, after = [(kept, came, None)], kept
    kept, came, _ = staying[0]
    totals = []
    for d, block in enumerate(crossed):

        def cross(*refs, start=d * parts):
            cross_kernel(start, *refs)

        block, after = lax.optimization_barrier((block, after))
        after = call(cross, shape(*block.shape, dtype=f32), 4 * project_flops, [kept, block])
        totals.append(after)
    came, after = lax.optimization_barrier((came, after))
    return call(
        finish_kernel, jax.ShapeDtypeStruct((2, parts, rows, width), f32), 0, [came, *totals]
    )


def solution(mesh):
    return jax.shard_map(
        local,
        mesh=mesh,
        in_specs=(
            P("cuts", "gx", "gy", None, None, "ma"),
            P("cuts", None, None, "gx", "gy", None),
            P("cuts", None, None, "gx", "gy", None),
        ),
        out_specs=P("cuts", None, ("gx", "gy"), "ma"),
        check_vma=False,
    )
```

```python
import jax
import jax.numpy as jnp
from jax import lax
from jax.experimental import pallas as pl
from jax.experimental.pallas import tpu as pltpu
from jax.sharding import PartitionSpec as P

VMEM_LIMIT = 16 * 1024 * 1024


def shifted(block, axis, distance):
    devices = range(lax.axis_size(axis))
    route = [((i - distance) % len(devices), i) for i in devices]
    return lax.ppermute(block, axis, route)


def call(body, out_shape, flops, operands, scratch=(), places=None):
    places = places or [pltpu.VMEM] * len(operands)
    return pl.pallas_call(
        body,
        out_shape=out_shape,
        in_specs=[pl.BlockSpec(memory_space=place) for place in places],
        scratch_shapes=scratch,
        cost_estimate=pl.CostEstimate(flops=flops // 2, bytes_accessed=0, transcendentals=0),
        compiler_params=pltpu.CompilerParams(vmem_limit_bytes=VMEM_LIMIT),
    )(*(pltpu.with_memory_space_constraint(a, place) for a, place in zip(operands, places)))


def dot(a, b):
    return jnp.dot(a, b, preferred_element_type=jnp.float32)


def iotas(shape):
    return (
        lax.broadcasted_iota(jnp.int32, shape, 0),
        lax.broadcasted_iota(jnp.int32, shape, 1),
    )


def place_of(x, planes):
    return planes - 2 if x == 0 else x if x == planes - 1 else x - 1


def map_rows(parts, colours, planes, ys, zs):
    match = ys
    choose = match + -(-parts * colours * colours * planes * zs // 8) * 8
    first_part = choose + 2 * parts * planes * 8
    return match, choose, first_part, first_part + 8


def write_maps(ref, parts, colours, planes, ys, zs):
    lanes = ref.shape[1] // 2
    sites = ys * zs
    depth = parts * colours * sites
    row_size = parts * colours * zs
    match, choose, first_part, _ = map_rows(parts, colours, planes, ys, zs)

    def ones(mask):
        return jnp.where(mask, 1.0, 0.0)

    def column(count):
        return lax.broadcasted_iota(jnp.int32, (count, 1), 0)

    def line(count):
        return lax.broadcasted_iota(jnp.int32, (1, count), 1)

    lane = line(lanes)
    inner = lane < depth
    past = lax.rem(jnp.maximum(lane - depth, 0), row_size)
    used = lane < depth + 2 * row_size
    part = jnp.where(inner, lax.div(lane, colours * sites), lax.div(past, colours * zs))
    colour = lax.rem(jnp.where(inner, lax.div(lane, sites), lax.div(past, zs)), colours)
    z = lax.rem(jnp.where(inner, lane, past), zs)
    y = lax.div(lax.rem(lane, sites), zs)
    ref[:ys, :lanes] = ones(column(ys) == jnp.where(inner, y, ys - 1))
    ref[:ys, lanes:] = ones(column(ys) == jnp.where(inner, y, ys) - 1)

    count = parts * colours * colours * planes * zs

    def link(index):
        x = lax.rem(lax.div(index, zs), planes)
        right = lax.rem(lax.div(index, zs * planes), colours)
        left = lax.rem(lax.div(index, zs * planes * colours), colours)
        return x, right, left, lax.div(index, zs * planes * colours * colours)

    row = column(count)
    _, right, left, _ = link(row)
    row_z = lax.rem(row, zs)
    key = jnp.where(used, colour * zs + z, -1)
    ref[match : match + count, :lanes] = ones(right * zs + row_z == key)
    ref[match : match + count, lanes:] = ones(left * zs + row_z == key)

    out = column(parts * planes * 8)
    field_part = lax.div(out, planes * 8)
    out_x = lax.rem(lax.div(out, 8), planes)
    out_part = lax.div(lax.rem(out, 8), colours)
    out_colour = lax.rem(lax.rem(out, 8), colours)
    x, right, left, source_part = link(line(count))
    source = source_part * planes + x
    wanted = jnp.where(out_part < parts, lax.rem(out_part + field_part, 2) * planes + out_x, -1)
    sign_ahead = jnp.where((field_part == 1) & (out_part == 0), -1.0, 1.0)
    sign_back = jnp.where((field_part == 0) & (out_part == 1), 1.0, -1.0)
    half = parts * planes * 8
    for start, end, sign in ((choose, left, sign_ahead), (choose + half, right, sign_back)):
        hit = source * colours + end == wanted * colours + jnp.where(wanted < 0, -1, out_colour)
        ref[start : start + half, :count] = jnp.where(hit, sign, 0.0)
    ref[first_part:, :lanes] = jnp.broadcast_to(ones(part == 0), (8, lanes))


def coefficients(links_x, links_y, maps_ref, planes):
    lanes = maps_ref.shape[1] // 2
    ys = links_x.shape[1]
    count = links_x.shape[0]
    half = 2 * planes * 8
    wide = dot(jnp.concatenate([links_x, links_y], axis=0), maps_ref[:ys].astype(jnp.bfloat16))
    match = maps_ref[ys : ys + count]
    match_ahead, match_back = match[:, :lanes], match[:, lanes:]
    choose = maps_ref[ys + count : ys + count + 2 * half, :count].astype(jnp.bfloat16)
    first_part = maps_ref[ys + count + 2 * half : ys + count + 2 * half + 1, :lanes] > 0.5
    ahead = jnp.concatenate([wide[:count, :lanes] * match_ahead, wide[count:, lanes:] * match_ahead], axis=1)
    back = jnp.concatenate([wide[:count, :lanes] * match_back, wide[count:, :lanes] * match_back], axis=1)
    out = []
    for chosen in (
        dot(choose[:half], ahead.astype(jnp.bfloat16)), dot(choose[half:], back.astype(jnp.bfloat16))
    ):
        for start in (0, lanes):
            part = chosen[:, start : start + lanes]
            rows = jnp.where(first_part, part[: half // 2], part[half // 2 :])
            out.append(rows.reshape(planes, 8, lanes))
    return out


def plane_rows(ref, ys):
    parts, _, colours, zs, width = ref.shape
    return jnp.concatenate(
        [ref[p, :ys, c].reshape(ys * zs, width) for p in range(parts) for c in range(colours)],
        axis=0,
    )


def edges_kernel(
    raw_hbm, links_x_hbm, links_y_hbm,
    first_ref, last_ref, raw_ref, links_x_ref, links_y_ref, maps_ref, past_maps_ref, arrived,
):
    parts, planes, ys, colours, zs, _ = raw_hbm.shape
    sources = (raw_hbm.at[:, planes - 1], raw_hbm.at[:, 0], links_x_hbm, links_y_hbm, raw_hbm)
    targets = (last_ref.at[:, :ys], first_ref, links_x_ref, links_y_ref, raw_ref)
    copies = [
        pltpu.make_async_copy(source, target, arrived.at[i])
        for i, (source, target) in enumerate(zip(sources, targets))
    ]
    for copy in copies:
        copy.start()
    last_ref[:, ys:] = jnp.zeros((parts, colours) + last_ref.shape[2:], last_ref.dtype)
    write_maps(maps_ref, parts, colours, planes, ys, zs)
    write_maps(past_maps_ref, parts, colours, 1, ys, zs)
    copies[2].wait()
    last_ref[:, ys:, :, :, :ys] = links_x_ref[:, :, :, planes - 1]
    for copy in copies[:2] + copies[3:]:
        copy.wait()


def site_matrix(rows_and_masks, count):
    blocks = []
    for q in range(count):
        block = None
        for rows, mask in rows_and_masks:
            term = rows[q : q + 1] * mask
            block = term if block is None else block + term
        blocks.append(block.astype(jnp.bfloat16))
    return jnp.concatenate(blocks, axis=0)


def prepare_kernel(
    raw_ref, links_x_ref, links_y_ref, maps_ref,
    rows_ref, ends_ref, ahead_x_ref, back_x_ref, ahead_y_ref, back_y_ref,
):
    planes, depth, width = rows_ref.shape
    zs = raw_ref.shape[4]
    ys = raw_ref.shape[2]
    sites = ys * zs
    row_size = depth // sites * zs
    lanes = ahead_y_ref.shape[2]
    ahead_x, ahead_y, back_x, back_y = coefficients(
        links_x_ref[...].reshape(-1, ys), links_y_ref[...].reshape(-1, ys), maps_ref, planes
    )
    ahead_x_ref[...] = ahead_x
    back_x_ref[...] = back_x
    ahead_y_ref[...] = ahead_y
    back_y_ref[...] = back_y

    row, lane = iotas((2 * row_size, depth))
    spot = row % row_size
    wanted = (spot // zs) * sites + spot % zs + jnp.where(row < row_size, 0, sites - zs)
    ends = (lane == wanted).astype(jnp.bfloat16)
    filler = jnp.zeros((8, width - 128), jnp.float32)
    spare = ends_ref.shape[1] - 2 * row_size - 8
    for x in range(planes):
        plane = plane_rows(raw_ref.at[:, x], ys)
        rows_ref[place_of(x, planes)] = plane
        tail = jnp.concatenate([back_y[x, :, lanes - 128 :], filler], axis=1)
        pieces = [dot(ends, plane), tail]
        if spare:
            pieces.append(jnp.zeros((spare, width), jnp.float32))
        ends_ref[x] = jnp.concatenate(pieces, axis=0).astype(jnp.bfloat16)


def turn_kernel(raw_ref, rows_ref, turned_ref):
    planes, depth, width = rows_ref.shape
    for x in range(planes):
        rows_ref[place_of(x, planes)] = plane_rows(raw_ref.at[:, x], raw_ref.shape[2])
    turned_ref[...] = rows_ref[...].reshape(planes * depth, width).T


def move_plane(same, count, ahead, back, above, below):
    depth = same.shape[1]
    moved = dot(site_matrix([(ahead[:, :depth], same)], count), above)
    return (moved + dot(site_matrix([(back[:, :depth], same)], count), below)).astype(jnp.bfloat16)


def same_site(sites, depth):
    site, lane = iotas((sites, depth))
    return (lane % sites == site).astype(jnp.float32)


def set_right(right_ref, place, moved):
    depth, width = moved.shape
    half = depth // 2
    start = place * depth
    real, imag = moved[:half], moved[half:]
    right_ref[start : start + half, :width] = real
    right_ref[start : start + half, width:] = imag
    right_ref[start + half : start + depth, :width] = imag
    right_ref[start + half : start + depth, width:] = -real


def inner_kernel(
    sites, rows_ref, ahead_ref, back_ref, right_ref, turned_ref, matrix_ref, ahead_part_ref, back_part_ref
):
    planes, depth, width = rows_ref.shape
    same = same_site(sites, depth)
    for x in range(1, planes - 1):
        above = rows_ref[place_of(x + 1, planes)]
        below = rows_ref[place_of(x - 1, planes)]
        moved = move_plane(same, depth // sites, ahead_ref[x], back_ref[x - 1], above, below)
        set_right(right_ref, place_of(x, planes), moved)
    turned_ref[...] = rows_ref[...].reshape(planes * depth, width).T
    x, count = planes - 1, depth // sites
    matrix_ref[...] = site_matrix([(ahead_ref[x, :, :depth], same)], count)
    ahead_part_ref[...] = dot(site_matrix([(ahead_ref[0, :, :depth], same)], count), rows_ref[place_of(1, planes)])
    below = rows_ref[place_of(x - 1, planes)]
    back_part_ref[...] = dot(site_matrix([(back_ref[x - 1, :, :depth], same)], count), below)


def begin_first_kernel(own_ref, others_ref, right_ref, total_ref):
    inner = right_ref.shape[0]
    right = right_ref[...]
    total_ref[0] = dot(own_ref[:, :inner], right)
    for k in range(others_ref.shape[0]):
        total_ref[k + 1] = dot(others_ref[k, :, :inner], right)


def begin_second_kernel(lefts_ref, right_ref, total_ref):
    inner = right_ref.shape[0]
    right = right_ref[...]
    for k in range(lefts_ref.shape[0]):
        total_ref[k] = dot(lefts_ref[k, :, :inner], right)


def bits(axis):
    return range(lax.axis_size(axis).bit_length() - 1)


def steps():
    one = [("gx", bit) for bit in bits("gx")[:-1]]
    two = [("gy", bit) for bit in bits("gy")]
    both = min(len(one), len(two))
    pairs = [pair for ends in zip(one, two) for pair in (ends, ends[::-1])]
    return pairs + [(step, step) for step in one[both:] + two[both:]]


def my_bit(axis, bit):
    return lax.bitwise_and(lax.shift_right_logical(lax.axis_index(axis), bit), 1)


def my_side(step):
    even, odd = (my_bit(*way) for way in step)
    return jnp.where(my_bit("ma", 0) == 0, even, odd)


def project(terms, begun_ref, keep_refs, send_refs, total_ref):
    groups, blocks, rows, _ = total_ref.shape
    parts, count, _, width = keep_refs[0].shape
    for k, term in enumerate(terms):
        total_ref[k] = (begun_ref[k] + term).reshape(blocks, rows, parts * width)
    my_modes = lax.axis_index("ma")
    odd_core = my_bit("ma", 0)
    top = my_bit("gx", bits("gx")[-1])
    across_x, across_y = lax.axis_size("gx"), lax.axis_size("gy")
    plan = steps()
    mine = my_side(plan[0])

    def at(side, index):
        owners = []
        for core in range(2):
            place = {"gx": 0, "gy": 0}
            for k, step in enumerate(plan):
                axis, bit = step[core]
                digit = side if k == 0 else index >> (len(plan) - 1 - k) & 1
                place[axis] += digit * (1 << bit)
            owners.append(place["gx"] * across_y + place["gy"])
        return jnp.where(odd_core == 0, owners[0], owners[1])

    for kind in range(2):
        half = lax.bitwise_xor(top, 1 - kind)
        for index in range(count):
            for ref, side in ((keep_refs[kind], mine), (send_refs[kind], 1 - mine)):
                owner = half * (across_x // 2 * across_y) + at(side, index)
                group = lax.rem(lax.div(owner, blocks) + groups - my_modes, groups)
                block = total_ref[group, lax.rem(owner, blocks)].astype(ref.dtype)
                for p in range(parts):
                    ref[p, index] = block[:, p * width : (p + 1) * width]


def first_kernel(
    sites, planes, high_ref, low_ref, matrix_ref, ahead_part_ref, back_part_ref, past_maps_ref, own_ref, others_ref, begun_ref,
    *refs,
):
    *refs, right_ref, total_ref = refs
    depth = matrix_ref.shape[0]
    same = same_site(sites, depth)
    _, ys, colours, zs, _ = high_ref.shape
    links = low_ref[:, ys:, :, :, :ys].reshape(-1, ys)
    lanes = past_maps_ref.shape[1] // 2
    count = links.shape[0]
    spread = past_maps_ref[:ys, :lanes].astype(jnp.bfloat16)
    match = past_maps_ref[ys : ys + count, lanes:]
    start = past_maps_ref.shape[0] - 24
    choose = past_maps_ref[start : start + 16, :count].astype(jnp.bfloat16)
    past = dot(choose, (dot(links, spread) * match).astype(jnp.bfloat16))
    past = jnp.where(past_maps_ref[start + 16 : start + 17, :lanes] > 0.5, past[:8], past[8:])
    past = site_matrix([(past[:, :depth], same)], depth // sites)
    moved = ahead_part_ref[...] + dot(past, plane_rows(low_ref, ys))
    set_right(right_ref, 0, moved.astype(jnp.bfloat16))
    moved = dot(matrix_ref[...], plane_rows(high_ref, ys)) + back_part_ref[...]
    set_right(right_ref, 1, moved.astype(jnp.bfloat16))
    inner = (planes - 2) * depth
    lefts = [own_ref[:, inner:]] + [others_ref[k, :, inner:] for k in range(others_ref.shape[0])]
    terms = [dot(left, right_ref[...]) for left in lefts]
    keep_other, keep_own, send_ref = refs
    project(terms, begun_ref, (keep_other, keep_own), (send_ref.at[0], send_ref.at[1]), total_ref)


def begin_y_kernel(sites, zs, rows_ref, others_ref, ahead_ref, back_ref, part_ref):
    planes, depth, _ = rows_ref.shape
    site, lane = iotas((sites, depth))
    to_next = jnp.where(lane % sites == site + zs, -1.0, 0.0)
    to_last = jnp.where(lane % sites == site - zs, -1.0, 0.0)
    for x in range(planes):
        ahead, back = ahead_ref[x, :, :depth], back_ref[x, :, :depth]
        matrix = site_matrix([(ahead, to_next), (back, to_last)], depth // sites)
        place = place_of(x, planes)
        part_ref[0, place] = dot(matrix, rows_ref[place])
        for k in range(others_ref.shape[0]):
            part_ref[k + 1, place] = dot(matrix, others_ref[k, place])


def move_y_kernel(sites, zs, part_ref, near_ref, far_ref, ahead_ref, turned_ref, field_ref):
    groups, planes, depth, width = part_ref.shape
    row_size = depth // sites * zs
    tail = 128
    head = ahead_ref.shape[2] - tail
    site, lane = iotas((sites, tail))
    lane = lane + head
    upper = (lane >= depth) & (lane < depth + row_size)
    lower = (lane >= depth + row_size) & (lane < depth + 2 * row_size)
    to_next = jnp.where(upper & (site == sites - zs + lane % zs), -1.0, 0.0)
    to_last = jnp.where(lower & (site == lane % zs), -1.0, 0.0)
    above = jnp.zeros((depth - head, width), jnp.bfloat16)
    below = jnp.zeros((tail - 2 * row_size - (depth - head), width), jnp.bfloat16)
    for x in range(planes):
        past = near_ref[x, 2 * row_size : 2 * row_size + 8, :tail].astype(jnp.float32)
        matrix = site_matrix([(ahead_ref[x, :, head:], to_next), (past, to_last)], depth // sites)
        place = place_of(x, planes)
        for k in range(groups):
            edge = near_ref[x, : 2 * row_size] if k == 0 else far_ref[k - 1, x]
            moved = part_ref[k, place] + dot(matrix, jnp.concatenate([above, edge, below], axis=0))
            field_ref[k, place] = moved.astype(jnp.bfloat16)
    for k in range(groups):
        turned_ref[k] = field_ref[k].reshape(planes * depth, width).T


def second_kernel(lefts_ref, right_ref, begun_ref, *refs):
    *refs, total_ref = refs
    inner = lefts_ref.shape[2] - right_ref.shape[0]
    lefts = [lefts_ref[k, :, inner:] for k in range(lefts_ref.shape[0])]
    terms = [dot(left, right_ref[...]) for left in lefts]
    project(terms, begun_ref, refs[:2], refs[2:], total_ref)


def exchange(block, step):
    axes = ("gx", "gy", "ma")
    sizes = [lax.axis_size(axis) for axis in axes]
    route = []
    for source in range(sizes[0] * sizes[1] * sizes[2]):
        where = [source // (sizes[1] * sizes[2]), source // sizes[2] % sizes[1], source % sizes[2]]
        axis, bit = step[where[2] % 2]
        where[axes.index(axis)] ^= 1 << bit
        route.append((source, (where[0] * sizes[1] + where[1]) * sizes[2] + where[2]))
    return lax.ppermute(block, axes, route)


def halve(sums, step, weight=0):
    parts = sum(kept.shape[0] for kept, _, _ in sums)
    count, rows, width = sums[0][0].shape[1:]
    dims = (parts, count // 2, rows, width)

    def merge(*refs):
        *refs, keep_ref, send_ref = refs
        mine = my_side(step)
        start = 0
        for k, (_, _, which) in enumerate(sums):
            kept_ref, came_ref = refs[2 * k : 2 * k + 2]
            came_ref = came_ref if which is None else came_ref.at[which]
            end = start + kept_ref.shape[0]
            for index in range(count // 2):
                low, high = (
                    kept_ref[:, at] + came_ref[:, at].astype(jnp.float32) for at in (index, index + count // 2)
                )
                keep_ref[start:end, index] = jnp.where(mine == 0, low, high)
                send_ref[start:end, index] = jnp.where(mine == 0, high, low).astype(send_ref.dtype)
            start = end

    operands = [a for kept, came, _ in sums for a in (kept, came)]
    keep, send = call(merge, (pltpu.VMEM(dims, jnp.float32), pltpu.VMEM(dims, jnp.bfloat16)), weight, operands)
    return keep, exchange(send, step)


def sum_kernel(kept_ref, came_ref, send_ref):
    send_ref[...] = (kept_ref[...] + came_ref[...].astype(jnp.float32)).astype(send_ref.dtype)


def cross_kernel(start, kept_ref, crossed_ref, out_ref):
    kept = kept_ref[start : start + out_ref.shape[0]]
    out_ref[...] = kept + crossed_ref[...].astype(jnp.float32)


def finish_kernel(came_ref, *refs):
    *kept_refs, out_ref = refs
    parts = out_ref.shape[1]
    for d, kept_ref in enumerate(kept_refs):
        out_ref[d] = kept_ref[:, 0] + came_ref[d * parts : (d + 1) * parts, 0].astype(jnp.float32)


def local(eigen_modes, links_first, links_second):
    f32, bf16 = jnp.float32, jnp.bfloat16
    parts, planes, ys, zs, colours, width = eigen_modes.shape
    sites = ys * zs
    depth = parts * colours * sites
    row_size = parts * colours * zs
    edge = -(-(2 * row_size + 8) // 16) * 16
    lanes = -(-(depth + 2 * row_size) // 128) * 128
    across_x, across_y, groups = (lax.axis_size(a) for a in ("gx", "gy", "ma"))
    rows = groups * width // (across_x * across_y)
    inner_depth = (planes - 2) * depth
    raw = eigen_modes.transpose(0, 1, 2, 4, 3, 5)

    def shape(*dims, dtype=bf16):
        return pltpu.VMEM(dims, dtype)

    field_shape = shape(planes, depth, width)
    turned_shape = shape(width, planes * depth)
    total_shape = shape(groups, width, parts * width, dtype=f32)
    link_shape = shape(planes, 8, lanes, dtype=f32)
    total = pltpu.VMEM((groups, width // rows, rows, parts * width), f32)
    step_flops = 2 * planes * depth * depth * width
    project_flops = 2 * groups * width * planes * depth * parts * width

    raw_others = [shifted(raw, "ma", -step) for step in range(1, groups)]
    raw_links_x, raw_links_y = (a.transpose(0, 1, 2, 3, 5, 4) for a in (links_first, links_second))
    inputs = [raw, raw_links_x, raw_links_y]
    first_plane, last_plane, *inputs, past_maps = call(
        edges_kernel,
        (
            shape(parts, ys, colours, zs, width), shape(parts, ys + colours, colours, zs, width),
            *(shape(*a.shape) for a in inputs),
            shape(map_rows(parts, colours, planes, ys, zs)[-1], 2 * lanes, dtype=f32),
            shape(map_rows(parts, colours, 1, ys, zs)[-1], 2 * lanes, dtype=f32),
        ),
        0,
        inputs,
        [pltpu.SemaphoreType.DMA((5,))],
        [pltpu.HBM] * len(inputs),
    )
    low = shifted(last_plane, "gx", 1)
    high = shifted(first_plane, "gx", -1)
    field, ends, ahead_x, back_x, ahead_y, back_y = call(
        prepare_kernel,
        (field_shape, shape(planes, edge, width), link_shape, link_shape, link_shape, link_shape),
        0,
        inputs,
    )
    near = shifted(ends, "gy", 1)
    if across_y != 2:
        ahead_row = lax.broadcasted_iota(jnp.int32, ends.shape, 1) < row_size
        near = jnp.where(ahead_row, shifted(ends, "gy", -1), near)

    plan = steps()
    top = ("gx", bits("gx")[-1])
    pieces = across_x * across_y // 4
    kept_shape = shape(parts, pieces, rows, width, dtype=f32)

    def inner(*refs):
        inner_kernel(sites, *refs)

    def first(*refs):
        first_kernel(sites, planes, *refs)

    def begin_y(*refs):
        begin_y_kernel(sites, zs, *refs)

    def move_y(*refs):
        move_y_kernel(sites, zs, *refs)

    right, own, matrix, ahead_part, back_part = call(
        inner,
        (
            shape(inner_depth, parts * width), turned_shape, shape(depth, depth),
            shape(depth, width, dtype=f32), shape(depth, width, dtype=f32),
        ),
        2 * step_flops,
        [field, ahead_x, back_x],
    )
    turned = [call(turn_kernel, (field_shape, turned_shape), step_flops // 4, [r]) for r in raw_others]
    fields = jnp.stack([t[0] for t in turned])
    others = jnp.stack([t[1] for t in turned])
    begun_first = call(begin_first_kernel, total_shape, project_flops, [own, others, right])
    part_y = call(
        begin_y, shape(groups, planes, depth, width, dtype=f32), 2 * step_flops, [field, fields, ahead_y, back_y]
    )
    part_y, begun_first = lax.optimization_barrier((part_y, begun_first))
    kept_first, own_first, sent_first, right_edge = call(
        first,
        (kept_shape, kept_shape, shape(2, parts, pieces, rows, width), shape(2 * depth, parts * width)),
        project_flops,
        [high, low, matrix, ahead_part, back_part, past_maps, own, others, begun_first],
        [total],
    )
    near, right_edge = lax.optimization_barrier((near, right_edge))
    near_rows = near[:, : 2 * row_size]
    far = jnp.stack([shifted(near_rows, "ma", -step) for step in range(1, groups)])
    lefts = call(
        move_y, shape(groups, width, planes * depth), 2 * step_flops,
        [part_y, near, far, ahead_y],
        [pltpu.VMEM((groups,) + field_shape.shape, bf16)],
    )
    begun_second = call(begin_second_kernel, total_shape, 8 * project_flops, [lefts, right])
    sent_shape = shape(parts, pieces, rows, width)
    kept_second, own_second, sent_second, sent_own = call(
        second_kernel, (kept_shape, kept_shape, sent_shape, sent_shape), project_flops,
        [lefts, right_edge, begun_second], [total],
    )
    came_first = exchange(sent_first, plan[0])
    crossing = [(kept_first, came_first, 0), (kept_second, exchange(sent_second, plan[0]), None)]
    staying = [(own_first, came_first, 1), (own_second, exchange(sent_own, plan[0]), None)]
    after = kept_second
    for step in plan[1:]:
        for d, (kept, came, which) in enumerate(crossing):
            came, after = lax.optimization_barrier((came, after))
            kept, came = halve([(kept, came, which)], step)
            crossing[d], after = (kept, came, None), kept
    crossed = []
    for kept, came, _ in crossing:
        came, after = lax.optimization_barrier((came, after))
        after = call(sum_kernel, pltpu.VMEM(kept.shape, bf16), 0, [kept, came])
        crossed.append(exchange(after, (top, top)))
    for step in plan[1:]:
        kept, came, which = staying[-1]
        came, after = lax.optimization_barrier((came, after))
        kept, came = halve(staying[:-1] + [(kept, came, which)], step)
        staying, after = [(kept, came, None)], kept
    kept, came, _ = staying[0]
    totals = []
    for d, block in enumerate(crossed):

        def cross(*refs, start=d * parts):
            cross_kernel(start, *refs)

        block, after = lax.optimization_barrier((block, after))
        after = call(cross, shape(*block.shape, dtype=f32), 4 * project_flops, [kept, block])
        totals.append(after)
    came, after = lax.optimization_barrier((came, after))
    return call(
        finish_kernel, jax.ShapeDtypeStruct((2, parts, rows, width), f32), 0, [came, *totals]
    )


def solution(mesh):
    return jax.shard_map(
        local,
        mesh=mesh,
        in_specs=(
            P("cuts", "gx", "gy", None, None, "ma"),
            P("cuts", None, None, "gx", "gy", None),
            P("cuts", None, None, "gx", "gy", None),
        ),
        out_specs=P("cuts", None, ("gx", "gy"), "ma"),
        check_vma=False,
    )
```

```python
import jax
import jax.numpy as jnp
from jax import lax
from jax.experimental import pallas as pl
from jax.experimental.pallas import tpu as pltpu
from jax.sharding import PartitionSpec as P

VMEM_LIMIT = 16 * 1024 * 1024


def shifted(block, axis, distance):
    devices = range(lax.axis_size(axis))
    route = [((i - distance) % len(devices), i) for i in devices]
    return lax.ppermute(block, axis, route)


def call(body, out_shape, flops, operands, scratch=(), places=None):
    places = places or [pltpu.VMEM] * len(operands)
    return pl.pallas_call(
        body,
        out_shape=out_shape,
        in_specs=[pl.BlockSpec(memory_space=place) for place in places],
        scratch_shapes=scratch,
        cost_estimate=pl.CostEstimate(flops=flops // 2, bytes_accessed=0, transcendentals=0),
        compiler_params=pltpu.CompilerParams(vmem_limit_bytes=VMEM_LIMIT),
    )(*(pltpu.with_memory_space_constraint(a, place) for a, place in zip(operands, places)))


def dot(a, b):
    return jnp.dot(a, b, preferred_element_type=jnp.float32)


def iotas(shape):
    return (
        lax.broadcasted_iota(jnp.int32, shape, 0),
        lax.broadcasted_iota(jnp.int32, shape, 1),
    )


def place_of(x, planes):
    return planes - 2 if x == 0 else x if x == planes - 1 else x - 1


def map_rows(parts, colours, planes, ys, zs):
    match = ys
    choose = match + -(-parts * colours * colours * planes * zs // 8) * 8
    first_part = choose + 2 * parts * planes * 8
    return match, choose, first_part, first_part + 8


def write_maps(ref, parts, colours, planes, ys, zs):
    lanes = ref.shape[1] // 2
    sites = ys * zs
    depth = parts * colours * sites
    row_size = parts * colours * zs
    match, choose, first_part, _ = map_rows(parts, colours, planes, ys, zs)

    def ones(mask):
        return jnp.where(mask, 1.0, 0.0)

    def column(count):
        return lax.broadcasted_iota(jnp.int32, (count, 1), 0)

    def line(count):
        return lax.broadcasted_iota(jnp.int32, (1, count), 1)

    lane = line(lanes)
    inner = lane < depth
    past = lax.rem(jnp.maximum(lane - depth, 0), row_size)
    used = lane < depth + 2 * row_size
    part = jnp.where(inner, lax.div(lane, colours * sites), lax.div(past, colours * zs))
    colour = lax.rem(jnp.where(inner, lax.div(lane, sites), lax.div(past, zs)), colours)
    z = lax.rem(jnp.where(inner, lane, past), zs)
    y = lax.div(lax.rem(lane, sites), zs)
    ref[:ys, :lanes] = ones(column(ys) == jnp.where(inner, y, ys - 1))
    ref[:ys, lanes:] = ones(column(ys) == jnp.where(inner, y, ys) - 1)

    count = parts * colours * colours * planes * zs

    def link(index):
        x = lax.rem(lax.div(index, zs), planes)
        right = lax.rem(lax.div(index, zs * planes), colours)
        left = lax.rem(lax.div(index, zs * planes * colours), colours)
        return x, right, left, lax.div(index, zs * planes * colours * colours)

    row = column(count)
    _, right, left, _ = link(row)
    row_z = lax.rem(row, zs)
    key = jnp.where(used, colour * zs + z, -1)
    ref[match : match + count, :lanes] = ones(right * zs + row_z == key)
    ref[match : match + count, lanes:] = ones(left * zs + row_z == key)

    out = column(parts * planes * 8)
    field_part = lax.div(out, planes * 8)
    out_x = lax.rem(lax.div(out, 8), planes)
    out_part = lax.div(lax.rem(out, 8), colours)
    out_colour = lax.rem(lax.rem(out, 8), colours)
    x, right, left, source_part = link(line(count))
    source = source_part * planes + x
    wanted = jnp.where(out_part < parts, lax.rem(out_part + field_part, 2) * planes + out_x, -1)
    sign_ahead = jnp.where((field_part == 1) & (out_part == 0), -1.0, 1.0)
    sign_back = jnp.where((field_part == 0) & (out_part == 1), 1.0, -1.0)
    half = parts * planes * 8
    for start, end, sign in ((choose, left, sign_ahead), (choose + half, right, sign_back)):
        hit = source * colours + end == wanted * colours + jnp.where(wanted < 0, -1, out_colour)
        ref[start : start + half, :count] = jnp.where(hit, sign, 0.0)
    ref[first_part:, :lanes] = jnp.broadcast_to(ones(part == 0), (8, lanes))


def coefficients(links_x, links_y, maps_ref, planes):
    lanes = maps_ref.shape[1] // 2
    ys = links_x.shape[1]
    count = links_x.shape[0]
    half = 2 * planes * 8
    wide = dot(jnp.concatenate([links_x, links_y], axis=0), maps_ref[:ys].astype(jnp.bfloat16))
    match = maps_ref[ys : ys + count]
    match_ahead, match_back = match[:, :lanes], match[:, lanes:]
    choose = maps_ref[ys + count : ys + count + 2 * half, :count].astype(jnp.bfloat16)
    first_part = maps_ref[ys + count + 2 * half : ys + count + 2 * half + 1, :lanes] > 0.5
    ahead = jnp.concatenate([wide[:count, :lanes] * match_ahead, wide[count:, lanes:] * match_ahead], axis=1)
    back = jnp.concatenate([wide[:count, :lanes] * match_back, wide[count:, :lanes] * match_back], axis=1)
    out = []
    for chosen in (
        dot(choose[:half], ahead.astype(jnp.bfloat16)), dot(choose[half:], back.astype(jnp.bfloat16))
    ):
        for start in (0, lanes):
            part = chosen[:, start : start + lanes]
            rows = jnp.where(first_part, part[: half // 2], part[half // 2 :])
            out.append(rows.reshape(planes, 8, lanes))
    return out


def plane_rows(ref, ys):
    parts, _, colours, zs, width = ref.shape
    return jnp.concatenate(
        [ref[p, :ys, c].reshape(ys * zs, width) for p in range(parts) for c in range(colours)],
        axis=0,
    )


def edges_kernel(
    raw_hbm, links_x_hbm, links_y_hbm,
    first_ref, last_ref, raw_ref, links_x_ref, links_y_ref, maps_ref, past_maps_ref, arrived,
):
    parts, planes, ys, colours, zs, _ = raw_hbm.shape
    sources = (raw_hbm.at[:, planes - 1], raw_hbm.at[:, 0], links_x_hbm, links_y_hbm, raw_hbm)
    targets = (last_ref.at[:, :ys], first_ref, links_x_ref, links_y_ref, raw_ref)
    copies = [
        pltpu.make_async_copy(source, target, arrived.at[i])
        for i, (source, target) in enumerate(zip(sources, targets))
    ]
    for copy in copies:
        copy.start()
    last_ref[:, ys:] = jnp.zeros((parts, colours) + last_ref.shape[2:], last_ref.dtype)
    write_maps(maps_ref, parts, colours, planes, ys, zs)
    write_maps(past_maps_ref, parts, colours, 1, ys, zs)
    copies[2].wait()
    last_ref[:, ys:, :, :, :ys] = links_x_ref[:, :, :, planes - 1]
    for copy in copies[:2] + copies[3:]:
        copy.wait()


def site_matrix(rows_and_masks, count):
    blocks = []
    for q in range(count):
        block = None
        for rows, mask in rows_and_masks:
            term = rows[q : q + 1] * mask
            block = term if block is None else block + term
        blocks.append(block.astype(jnp.bfloat16))
    return jnp.concatenate(blocks, axis=0)


def prepare_kernel(
    raw_ref, links_x_ref, links_y_ref, maps_ref,
    rows_ref, ends_ref, ahead_x_ref, back_x_ref, ahead_y_ref, back_y_ref,
):
    planes, depth, width = rows_ref.shape
    zs = raw_ref.shape[4]
    ys = raw_ref.shape[2]
    sites = ys * zs
    row_size = depth // sites * zs
    lanes = ahead_y_ref.shape[2]
    ahead_x, ahead_y, back_x, back_y = coefficients(
        links_x_ref[...].reshape(-1, ys), links_y_ref[...].reshape(-1, ys), maps_ref, planes
    )
    ahead_x_ref[...] = ahead_x
    back_x_ref[...] = back_x
    ahead_y_ref[...] = ahead_y
    back_y_ref[...] = back_y

    row, lane = iotas((2 * row_size, depth))
    spot = row % row_size
    wanted = (spot // zs) * sites + spot % zs + jnp.where(row < row_size, 0, sites - zs)
    ends = (lane == wanted).astype(jnp.bfloat16)
    filler = jnp.zeros((8, width - 128), jnp.float32)
    spare = ends_ref.shape[1] - 2 * row_size - 8
    for x in range(planes):
        plane = plane_rows(raw_ref.at[:, x], ys)
        rows_ref[place_of(x, planes)] = plane
        tail = jnp.concatenate([back_y[x, :, lanes - 128 :], filler], axis=1)
        pieces = [dot(ends, plane), tail]
        if spare:
            pieces.append(jnp.zeros((spare, width), jnp.float32))
        ends_ref[x] = jnp.concatenate(pieces, axis=0).astype(jnp.bfloat16)


def turn_kernel(raw_ref, rows_ref, turned_ref):
    planes, depth, width = rows_ref.shape
    for x in range(planes):
        rows_ref[place_of(x, planes)] = plane_rows(raw_ref.at[:, x], raw_ref.shape[2])
    turned_ref[...] = rows_ref[...].reshape(planes * depth, width).T


def move_plane(same, count, ahead, back, above, below):
    depth = same.shape[1]
    moved = dot(site_matrix([(ahead[:, :depth], same)], count), above)
    return (moved + dot(site_matrix([(back[:, :depth], same)], count), below)).astype(jnp.bfloat16)


def same_site(sites, depth):
    site, lane = iotas((sites, depth))
    return (lane % sites == site).astype(jnp.float32)


def set_right(right_ref, place, moved):
    depth, width = moved.shape
    half = depth // 2
    start = place * depth
    real, imag = moved[:half], moved[half:]
    right_ref[start : start + half, :width] = real
    right_ref[start : start + half, width:] = imag
    right_ref[start + half : start + depth, :width] = imag
    right_ref[start + half : start + depth, width:] = -real


def inner_kernel(
    sites, rows_ref, ahead_ref, back_ref, right_ref, turned_ref, matrix_ref, ahead_part_ref, back_part_ref
):
    planes, depth, width = rows_ref.shape
    same = same_site(sites, depth)
    for x in range(1, planes - 1):
        above = rows_ref[place_of(x + 1, planes)]
        below = rows_ref[place_of(x - 1, planes)]
        moved = move_plane(same, depth // sites, ahead_ref[x], back_ref[x - 1], above, below)
        set_right(right_ref, place_of(x, planes), moved)
    turned_ref[...] = rows_ref[...].reshape(planes * depth, width).T
    x, count = planes - 1, depth // sites
    matrix_ref[...] = site_matrix([(ahead_ref[x, :, :depth], same)], count)
    ahead_part_ref[...] = dot(site_matrix([(ahead_ref[0, :, :depth], same)], count), rows_ref[place_of(1, planes)])
    below = rows_ref[place_of(x - 1, planes)]
    back_part_ref[...] = dot(site_matrix([(back_ref[x - 1, :, :depth], same)], count), below)


def begin_first_kernel(own_ref, others_ref, right_ref, total_ref):
    inner = right_ref.shape[0]
    right = right_ref[...]
    total_ref[0] = dot(own_ref[:, :inner], right)
    for k in range(others_ref.shape[0]):
        total_ref[k + 1] = dot(others_ref[k, :, :inner], right)


def bits(axis):
    return range(lax.axis_size(axis).bit_length() - 1)


def steps():
    one = [("gx", bit) for bit in bits("gx")[:-1]]
    two = [("gy", bit) for bit in bits("gy")]
    both = min(len(one), len(two))
    pairs = [pair for ends in zip(one, two) for pair in (ends, ends[::-1])]
    return pairs + [(step, step) for step in one[both:] + two[both:]]


def my_bit(axis, bit):
    return lax.bitwise_and(lax.shift_right_logical(lax.axis_index(axis), bit), 1)


def my_side(step):
    even, odd = (my_bit(*way) for way in step)
    return jnp.where(my_bit("ma", 0) == 0, even, odd)


def half_of(kind):
    half = lax.bitwise_xor(my_bit("gx", bits("gx")[-1]), 1 - kind)
    return lax.bitwise_xor(half, lax.axis_index("ma"))


def share(total, keep_ref, send_ref, total_ref):
    blocks, rows, double = total_ref.shape
    parts, count, _, width = keep_ref.shape
    total_ref[...] = total.reshape(blocks, rows, double)
    odd_core = my_bit("ma", 0)
    across_y = lax.axis_size("gy")
    plan = steps()
    mine = my_side(plan[0])

    def at(side, index):
        owners = []
        for core in range(2):
            place = {"gx": 0, "gy": 0}
            for k, step in enumerate(plan):
                axis, bit = step[core]
                digit = side if k == 0 else index >> (len(plan) - 1 - k) & 1
                place[axis] += digit * (1 << bit)
            owners.append(place["gx"] * across_y + place["gy"])
        return jnp.where(odd_core == 0, owners[0], owners[1])

    for index in range(count):
        for ref, side in ((keep_ref, mine), (send_ref, 1 - mine)):
            block = total_ref[at(side, index)].astype(ref.dtype)
            for p in range(parts):
                ref[p, index] = block[:, p * width : (p + 1) * width]


def first_share(kind, own_ref, others_ref, begun_ref, right, keep_ref, send_ref, total_ref):
    half = half_of(kind)
    inner = own_ref.shape[1] - right.shape[0]
    left = jnp.where(half == 0, own_ref[:, inner:], others_ref[0, :, inner:])
    share(begun_ref[half] + dot(left, right), keep_ref, send_ref, total_ref)


def first_kernel(
    sites, high_ref, low_ref, matrix_ref, ahead_part_ref, back_part_ref, past_maps_ref, own_ref, others_ref, begun_ref,
    *refs,
):
    keep_ref, send_ref, right_ref, total_ref = refs
    depth = matrix_ref.shape[0]
    same = same_site(sites, depth)
    _, ys, colours, zs, _ = high_ref.shape
    links = low_ref[:, ys:, :, :, :ys].reshape(-1, ys)
    lanes = past_maps_ref.shape[1] // 2
    count = links.shape[0]
    spread = past_maps_ref[:ys, :lanes].astype(jnp.bfloat16)
    match = past_maps_ref[ys : ys + count, lanes:]
    start = past_maps_ref.shape[0] - 24
    choose = past_maps_ref[start : start + 16, :count].astype(jnp.bfloat16)
    past = dot(choose, (dot(links, spread) * match).astype(jnp.bfloat16))
    past = jnp.where(past_maps_ref[start + 16 : start + 17, :lanes] > 0.5, past[:8], past[8:])
    past = site_matrix([(past[:, :depth], same)], depth // sites)
    moved = ahead_part_ref[...] + dot(past, plane_rows(low_ref, ys))
    set_right(right_ref, 0, moved.astype(jnp.bfloat16))
    moved = dot(matrix_ref[...], plane_rows(high_ref, ys)) + back_part_ref[...]
    set_right(right_ref, 1, moved.astype(jnp.bfloat16))
    first_share(0, own_ref, others_ref, begun_ref, right_ref[...], keep_ref, send_ref, total_ref)


def first_own_kernel(own_ref, others_ref, begun_ref, right_ref, keep_ref, send_ref, total_ref):
    first_share(1, own_ref, others_ref, begun_ref, right_ref[...], keep_ref, send_ref, total_ref)


def begin_y_kernel(sites, zs, rows_ref, others_ref, ahead_ref, back_ref, part_ref):
    planes, depth, _ = rows_ref.shape
    site, lane = iotas((sites, depth))
    to_next = jnp.where(lane % sites == site + zs, -1.0, 0.0)
    to_last = jnp.where(lane % sites == site - zs, -1.0, 0.0)
    for x in range(planes):
        ahead, back = ahead_ref[x, :, :depth], back_ref[x, :, :depth]
        matrix = site_matrix([(ahead, to_next), (back, to_last)], depth // sites)
        place = place_of(x, planes)
        part_ref[0, place] = dot(matrix, rows_ref[place])
        for k in range(others_ref.shape[0]):
            part_ref[k + 1, place] = dot(matrix, others_ref[k, place])


def move_y_kernel(sites, zs, part_ref, near_ref, far_ref, ahead_ref, turned_ref, field_ref):
    groups, planes, depth, width = part_ref.shape
    row_size = depth // sites * zs
    tail = 128
    head = ahead_ref.shape[2] - tail
    site, lane = iotas((sites, tail))
    lane = lane + head
    upper = (lane >= depth) & (lane < depth + row_size)
    lower = (lane >= depth + row_size) & (lane < depth + 2 * row_size)
    to_next = jnp.where(upper & (site == sites - zs + lane % zs), -1.0, 0.0)
    to_last = jnp.where(lower & (site == lane % zs), -1.0, 0.0)
    above = jnp.zeros((depth - head, width), jnp.bfloat16)
    below = jnp.zeros((tail - 2 * row_size - (depth - head), width), jnp.bfloat16)
    for x in range(planes):
        past = near_ref[x, 2 * row_size : 2 * row_size + 8, :tail].astype(jnp.float32)
        matrix = site_matrix([(ahead_ref[x, :, head:], to_next), (past, to_last)], depth // sites)
        place = place_of(x, planes)
        for k in range(groups):
            edge = near_ref[x, : 2 * row_size] if k == 0 else far_ref[k - 1, x]
            moved = part_ref[k, place] + dot(matrix, jnp.concatenate([above, edge, below], axis=0))
            field_ref[k, place] = moved.astype(jnp.bfloat16)
    for k in range(groups):
        turned_ref[k] = field_ref[k].reshape(planes * depth, width).T


def second_share(kind, lefts_ref, right_ref, edge_ref, keep_ref, send_ref, total_ref):
    half = half_of(kind)
    inner = right_ref.shape[0]
    total = dot(lefts_ref[half, :, :inner], right_ref[...]) + dot(lefts_ref[half, :, inner:], edge_ref[...])
    share(total, keep_ref, send_ref, total_ref)


def second_kernel(lefts_ref, right_ref, edge_ref, keep_ref, send_ref, total_ref):
    second_share(0, lefts_ref, right_ref, edge_ref, keep_ref, send_ref, total_ref)


def second_own_kernel(lefts_ref, right_ref, edge_ref, first_ref, keep_ref, send_ref, total_ref):
    parts = first_ref.shape[0]
    send_ref[:parts] = first_ref[...]
    second_share(1, lefts_ref, right_ref, edge_ref, keep_ref, send_ref.at[parts:], total_ref)


def exchange(block, step):
    axes = ("gx", "gy", "ma")
    sizes = [lax.axis_size(axis) for axis in axes]
    route = []
    for source in range(sizes[0] * sizes[1] * sizes[2]):
        where = [source // (sizes[1] * sizes[2]), source // sizes[2] % sizes[1], source % sizes[2]]
        axis, bit = step[where[2] % 2]
        where[axes.index(axis)] ^= 1 << bit
        route.append((source, (where[0] * sizes[1] + where[1]) * sizes[2] + where[2]))
    return lax.ppermute(block, axes, route)


def halve(sums, step, weight=0):
    parts = sum(kept.shape[0] for kept, _, _ in sums)
    count, rows, width = sums[0][0].shape[1:]
    dims = (parts, count // 2, rows, width)

    def merge(*refs):
        *refs, keep_ref, send_ref = refs
        mine = my_side(step)
        start = 0
        for k, (_, _, which) in enumerate(sums):
            kept_ref, came_ref = refs[2 * k : 2 * k + 2]
            came_ref = came_ref if which is None else came_ref.at[which]
            end = start + kept_ref.shape[0]
            for index in range(count // 2):
                low, high = (
                    kept_ref[:, at] + came_ref[:, at].astype(jnp.float32) for at in (index, index + count // 2)
                )
                keep_ref[start:end, index] = jnp.where(mine == 0, low, high)
                send_ref[start:end, index] = jnp.where(mine == 0, high, low).astype(send_ref.dtype)
            start = end

    operands = [a for kept, came, _ in sums for a in (kept, came)]
    keep, send = call(merge, (pltpu.VMEM(dims, jnp.float32), pltpu.VMEM(dims, jnp.bfloat16)), weight, operands)
    return keep, exchange(send, step)


def sum_kernel(kept_ref, came_ref, send_ref):
    send_ref[...] = (kept_ref[...] + came_ref[...].astype(jnp.float32)).astype(send_ref.dtype)


def cross_kernel(start, kept_ref, crossed_ref, out_ref):
    kept = kept_ref[start : start + out_ref.shape[0]]
    out_ref[...] = kept + crossed_ref[...].astype(jnp.float32)


def finish_kernel(came_ref, *refs):
    *kept_refs, out_ref = refs
    parts = out_ref.shape[1]
    for d, kept_ref in enumerate(kept_refs):
        out_ref[d] = kept_ref[:, 0] + came_ref[d * parts : (d + 1) * parts, 0].astype(jnp.float32)


def local(eigen_modes, links_first, links_second):
    f32, bf16 = jnp.float32, jnp.bfloat16
    parts, planes, ys, zs, colours, width = eigen_modes.shape
    sites = ys * zs
    depth = parts * colours * sites
    row_size = parts * colours * zs
    edge = -(-(2 * row_size + 8) // 16) * 16
    lanes = -(-(depth + 2 * row_size) // 128) * 128
    across_x, across_y, groups = (lax.axis_size(a) for a in ("gx", "gy", "ma"))
    rows = groups * width // (across_x * across_y)
    inner_depth = (planes - 2) * depth
    raw = eigen_modes.transpose(0, 1, 2, 4, 3, 5)

    def shape(*dims, dtype=bf16):
        return pltpu.VMEM(dims, dtype)

    field_shape = shape(planes, depth, width)
    turned_shape = shape(width, planes * depth)
    total_shape = shape(groups, width, parts * width, dtype=f32)
    link_shape = shape(planes, 8, lanes, dtype=f32)
    total = pltpu.VMEM((width // rows, rows, parts * width), f32)
    step_flops = 2 * planes * depth * depth * width
    project_flops = 2 * groups * width * planes * depth * parts * width

    raw_others = [shifted(raw, "ma", -step) for step in range(1, groups)]
    raw_links_x, raw_links_y = (a.transpose(0, 1, 2, 3, 5, 4) for a in (links_first, links_second))
    inputs = [raw, raw_links_x, raw_links_y]
    first_plane, last_plane, *inputs, past_maps = call(
        edges_kernel,
        (
            shape(parts, ys, colours, zs, width), shape(parts, ys + colours, colours, zs, width),
            *(shape(*a.shape) for a in inputs),
            shape(map_rows(parts, colours, planes, ys, zs)[-1], 2 * lanes, dtype=f32),
            shape(map_rows(parts, colours, 1, ys, zs)[-1], 2 * lanes, dtype=f32),
        ),
        0,
        inputs,
        [pltpu.SemaphoreType.DMA((5,))],
        [pltpu.HBM] * len(inputs),
    )
    low = shifted(last_plane, "gx", 1)
    high = shifted(first_plane, "gx", -1)
    field, ends, ahead_x, back_x, ahead_y, back_y = call(
        prepare_kernel,
        (field_shape, shape(planes, edge, width), link_shape, link_shape, link_shape, link_shape),
        0,
        inputs,
    )
    near = shifted(ends, "gy", 1)
    if across_y != 2:
        ahead_row = lax.broadcasted_iota(jnp.int32, ends.shape, 1) < row_size
        near = jnp.where(ahead_row, shifted(ends, "gy", -1), near)

    plan = steps()
    top = ("gx", bits("gx")[-1])
    pieces = across_x * across_y // 4
    kept_shape = shape(parts, pieces, rows, width, dtype=f32)
    sent_shape = shape(parts, pieces, rows, width)

    def inner(*refs):
        inner_kernel(sites, *refs)

    def first(*refs):
        first_kernel(sites, *refs)

    def begin_y(*refs):
        begin_y_kernel(sites, zs, *refs)

    def move_y(*refs):
        move_y_kernel(sites, zs, *refs)

    right, own, matrix, ahead_part, back_part = call(
        inner,
        (
            shape(inner_depth, parts * width), turned_shape, shape(depth, depth),
            shape(depth, width, dtype=f32), shape(depth, width, dtype=f32),
        ),
        2 * step_flops,
        [field, ahead_x, back_x],
    )
    turned = [call(turn_kernel, (field_shape, turned_shape), step_flops // 4, [r]) for r in raw_others]
    fields = jnp.stack([t[0] for t in turned])
    others = jnp.stack([t[1] for t in turned])
    begun_first = call(begin_first_kernel, total_shape, project_flops, [own, others, right])
    part_y = call(
        begin_y, shape(groups, planes, depth, width, dtype=f32), 2 * step_flops, [field, fields, ahead_y, back_y]
    )
    part_y, begun_first = lax.optimization_barrier((part_y, begun_first))
    kept_first, sent_first, right_edge = call(
        first,
        (kept_shape, sent_shape, shape(2 * depth, parts * width)),
        project_flops,
        [high, low, matrix, ahead_part, back_part, past_maps, own, others, begun_first],
        [total],
    )
    came_first = exchange(sent_first, plan[0])
    near, right_edge = lax.optimization_barrier((near, right_edge))
    near_rows = near[:, : 2 * row_size]
    far = jnp.stack([shifted(near_rows, "ma", -step) for step in range(1, groups)])
    lefts = call(
        move_y, shape(groups, width, planes * depth), 2 * step_flops,
        [part_y, near, far, ahead_y],
        [pltpu.VMEM((groups,) + field_shape.shape, bf16)],
    )
    kept_second, sent_second = call(
        second_kernel, (kept_shape, sent_shape), 8 * project_flops, [lefts, right, right_edge], [total]
    )
    came_second = exchange(sent_second, plan[0])
    crossing = [(kept_first, came_first), (kept_second, came_second)]
    after = kept_second
    staying = None
    for step in plan[1:]:
        for d, (kept, came) in enumerate(crossing):
            came, after = lax.optimization_barrier((came, after))
            crossing[d] = halve([(kept, came, None)], step)
            after = crossing[d][0]
            if staying is None:
                own_first, sent_own = call(
                    first_own_kernel, (kept_shape, sent_shape), 0, [own, others, begun_first, right_edge], [total]
                )
                right_edge, after = lax.optimization_barrier((right_edge, after))
                own_second, sent_own = call(
                    second_own_kernel, (kept_shape, shape(2 * parts, pieces, rows, width)), 0,
                    [lefts, right, right_edge, sent_own], [total],
                )
                came_own = exchange(sent_own, plan[0])
                staying = [(own_first, came_own, slice(0, parts)), (own_second, came_own, slice(parts, 2 * parts))]
    crossed = []
    for kept, came in crossing:
        came, after = lax.optimization_barrier((came, after))
        after = call(sum_kernel, pltpu.VMEM(kept.shape, bf16), 8 * project_flops, [kept, came])
        crossed.append(exchange(after, (top, top)))
    for step in plan[1:]:
        kept, came, which = staying[0]
        came, after = lax.optimization_barrier((came, after))
        sums = [(kept, came, which)] + [(k, came, w) for k, _, w in staying[1:]]
        kept, came = halve(sums, step)
        staying, after = [(kept, came, None)], kept
    kept, came, _ = staying[0]
    totals = []
    for d, block in enumerate(crossed):

        def cross(*refs, start=d * parts):
            cross_kernel(start, *refs)

        block, after = lax.optimization_barrier((block, after))
        after = call(cross, shape(*block.shape, dtype=f32), 4 * project_flops, [kept, block])
        totals.append(after)
    came, after = lax.optimization_barrier((came, after))
    return call(
        finish_kernel, jax.ShapeDtypeStruct((2, parts, rows, width), f32), 0, [came, *totals]
    )


def solution(mesh):
    return jax.shard_map(
        local,
        mesh=mesh,
        in_specs=(
            P("cuts", "gx", "gy", None, None, "ma"),
            P("cuts", None, None, "gx", "gy", None),
            P("cuts", None, None, "gx", "gy", None),
        ),
        out_specs=P("cuts", None, ("gx", "gy"), "ma"),
        check_vma=False,
    )
```

```python
import jax
import jax.numpy as jnp
from jax import lax
from jax.experimental import pallas as pl
from jax.experimental.pallas import tpu as pltpu
from jax.sharding import PartitionSpec as P

VMEM_LIMIT = 16 * 1024 * 1024


def shifted(block, axis, distance):
    devices = range(lax.axis_size(axis))
    route = [((i - distance) % len(devices), i) for i in devices]
    return lax.ppermute(block, axis, route)


def call(body, out_shape, flops, operands, scratch=(), places=None):
    places = places or [pltpu.VMEM] * len(operands)
    return pl.pallas_call(
        body,
        out_shape=out_shape,
        in_specs=[pl.BlockSpec(memory_space=place) for place in places],
        scratch_shapes=scratch,
        cost_estimate=pl.CostEstimate(flops=flops // 2, bytes_accessed=0, transcendentals=0),
        compiler_params=pltpu.CompilerParams(vmem_limit_bytes=VMEM_LIMIT),
    )(*(pltpu.with_memory_space_constraint(a, place) for a, place in zip(operands, places)))


def dot(a, b):
    return jnp.dot(a, b, preferred_element_type=jnp.float32)


def iotas(shape):
    return (
        lax.broadcasted_iota(jnp.int32, shape, 0),
        lax.broadcasted_iota(jnp.int32, shape, 1),
    )


def place_of(x, planes):
    return planes - 2 if x == 0 else x if x == planes - 1 else x - 1


def map_rows(parts, colours, planes, ys, zs):
    match = ys
    choose = match + -(-parts * colours * colours * planes * zs // 8) * 8
    first_part = choose + 2 * parts * planes * 8
    return match, choose, first_part, first_part + 8


def write_maps(ref, parts, colours, planes, ys, zs):
    lanes = ref.shape[1] // 2
    sites = ys * zs
    depth = parts * colours * sites
    row_size = parts * colours * zs
    match, choose, first_part, _ = map_rows(parts, colours, planes, ys, zs)

    def ones(mask):
        return jnp.where(mask, 1.0, 0.0)

    def column(count):
        return lax.broadcasted_iota(jnp.int32, (count, 1), 0)

    def line(count):
        return lax.broadcasted_iota(jnp.int32, (1, count), 1)

    lane = line(lanes)
    inner = lane < depth
    past = lax.rem(jnp.maximum(lane - depth, 0), row_size)
    used = lane < depth + 2 * row_size
    part = jnp.where(inner, lax.div(lane, colours * sites), lax.div(past, colours * zs))
    colour = lax.rem(jnp.where(inner, lax.div(lane, sites), lax.div(past, zs)), colours)
    z = lax.rem(jnp.where(inner, lane, past), zs)
    y = lax.div(lax.rem(lane, sites), zs)
    ref[:ys, :lanes] = ones(column(ys) == jnp.where(inner, y, ys - 1))
    ref[:ys, lanes:] = ones(column(ys) == jnp.where(inner, y, ys) - 1)

    count = parts * colours * colours * planes * zs

    def link(index):
        x = lax.rem(lax.div(index, zs), planes)
        right = lax.rem(lax.div(index, zs * planes), colours)
        left = lax.rem(lax.div(index, zs * planes * colours), colours)
        return x, right, left, lax.div(index, zs * planes * colours * colours)

    row = column(count)
    _, right, left, _ = link(row)
    row_z = lax.rem(row, zs)
    key = jnp.where(used, colour * zs + z, -1)
    ref[match : match + count, :lanes] = ones(right * zs + row_z == key)
    ref[match : match + count, lanes:] = ones(left * zs + row_z == key)

    out = column(parts * planes * 8)
    field_part = lax.div(out, planes * 8)
    out_x = lax.rem(lax.div(out, 8), planes)
    out_part = lax.div(lax.rem(out, 8), colours)
    out_colour = lax.rem(lax.rem(out, 8), colours)
    x, right, left, source_part = link(line(count))
    source = source_part * planes + x
    wanted = jnp.where(out_part < parts, lax.rem(out_part + field_part, 2) * planes + out_x, -1)
    sign_ahead = jnp.where((field_part == 1) & (out_part == 0), -1.0, 1.0)
    sign_back = jnp.where((field_part == 0) & (out_part == 1), 1.0, -1.0)
    half = parts * planes * 8
    for start, end, sign in ((choose, left, sign_ahead), (choose + half, right, sign_back)):
        hit = source * colours + end == wanted * colours + jnp.where(wanted < 0, -1, out_colour)
        ref[start : start + half, :count] = jnp.where(hit, sign, 0.0)
    ref[first_part:, :lanes] = jnp.broadcast_to(ones(part == 0), (8, lanes))


def coefficients(links_x, links_y, maps_ref, planes):
    lanes = maps_ref.shape[1] // 2
    ys = links_x.shape[1]
    count = links_x.shape[0]
    half = 2 * planes * 8
    wide = dot(jnp.concatenate([links_x, links_y], axis=0), maps_ref[:ys].astype(jnp.bfloat16))
    match = maps_ref[ys : ys + count]
    match_ahead, match_back = match[:, :lanes], match[:, lanes:]
    choose = maps_ref[ys + count : ys + count + 2 * half, :count].astype(jnp.bfloat16)
    first_part = maps_ref[ys + count + 2 * half : ys + count + 2 * half + 1, :lanes] > 0.5
    ahead = jnp.concatenate([wide[:count, :lanes] * match_ahead, wide[count:, lanes:] * match_ahead], axis=1)
    back = jnp.concatenate([wide[:count, :lanes] * match_back, wide[count:, :lanes] * match_back], axis=1)
    out = []
    for chosen in (
        dot(choose[:half], ahead.astype(jnp.bfloat16)), dot(choose[half:], back.astype(jnp.bfloat16))
    ):
        for start in (0, lanes):
            part = chosen[:, start : start + lanes]
            rows = jnp.where(first_part, part[: half // 2], part[half // 2 :])
            out.append(rows.reshape(planes, 8, lanes))
    return out


def plane_rows(ref, ys):
    parts, _, colours, zs, width = ref.shape
    return jnp.concatenate(
        [ref[p, :ys, c].reshape(ys * zs, width) for p in range(parts) for c in range(colours)],
        axis=0,
    )


def edges_kernel(
    raw_hbm, links_x_hbm, links_y_hbm,
    first_ref, last_ref, raw_ref, links_x_ref, links_y_ref, maps_ref, past_maps_ref, arrived,
):
    parts, planes, ys, colours, zs, _ = raw_hbm.shape
    sources = (raw_hbm.at[:, planes - 1], raw_hbm.at[:, 0], links_x_hbm, links_y_hbm, raw_hbm)
    targets = (last_ref.at[:, :ys], first_ref, links_x_ref, links_y_ref, raw_ref)
    copies = [
        pltpu.make_async_copy(source, target, arrived.at[i])
        for i, (source, target) in enumerate(zip(sources, targets))
    ]
    for copy in copies:
        copy.start()
    last_ref[:, ys:] = jnp.zeros((parts, colours) + last_ref.shape[2:], last_ref.dtype)
    write_maps(maps_ref, parts, colours, planes, ys, zs)
    write_maps(past_maps_ref, parts, colours, 1, ys, zs)
    copies[2].wait()
    last_ref[:, ys:, :, :, :ys] = links_x_ref[:, :, :, planes - 1]
    for copy in copies[:2] + copies[3:]:
        copy.wait()


def site_matrix(rows_and_masks, count):
    blocks = []
    for q in range(count):
        block = None
        for rows, mask in rows_and_masks:
            term = rows[q : q + 1] * mask
            block = term if block is None else block + term
        blocks.append(block.astype(jnp.bfloat16))
    return jnp.concatenate(blocks, axis=0)


def prepare_kernel(
    raw_ref, links_x_ref, links_y_ref, maps_ref,
    rows_ref, ends_ref, ahead_x_ref, back_x_ref, ahead_y_ref, back_y_ref,
):
    planes, depth, width = rows_ref.shape
    zs = raw_ref.shape[4]
    ys = raw_ref.shape[2]
    sites = ys * zs
    row_size = depth // sites * zs
    lanes = ahead_y_ref.shape[2]
    ahead_x, ahead_y, back_x, back_y = coefficients(
        links_x_ref[...].reshape(-1, ys), links_y_ref[...].reshape(-1, ys), maps_ref, planes
    )
    ahead_x_ref[...] = ahead_x
    back_x_ref[...] = back_x
    ahead_y_ref[...] = ahead_y
    back_y_ref[...] = back_y

    row, lane = iotas((2 * row_size, depth))
    spot = row % row_size
    wanted = (spot // zs) * sites + spot % zs + jnp.where(row < row_size, 0, sites - zs)
    ends = (lane == wanted).astype(jnp.bfloat16)
    filler = jnp.zeros((8, width - 128), jnp.float32)
    spare = ends_ref.shape[1] - 2 * row_size - 8
    for x in range(planes):
        plane = plane_rows(raw_ref.at[:, x], ys)
        rows_ref[place_of(x, planes)] = plane
        tail = jnp.concatenate([back_y[x, :, lanes - 128 :], filler], axis=1)
        pieces = [dot(ends, plane), tail]
        if spare:
            pieces.append(jnp.zeros((spare, width), jnp.float32))
        ends_ref[x] = jnp.concatenate(pieces, axis=0).astype(jnp.bfloat16)


def turn_kernel(raw_ref, rows_ref, turned_ref):
    planes, depth, width = rows_ref.shape
    for x in range(planes):
        rows_ref[place_of(x, planes)] = plane_rows(raw_ref.at[:, x], raw_ref.shape[2])
    turned_ref[...] = rows_ref[...].reshape(planes * depth, width).T


def move_plane(same, count, ahead, back, above, below):
    depth = same.shape[1]
    moved = dot(site_matrix([(ahead[:, :depth], same)], count), above)
    return (moved + dot(site_matrix([(back[:, :depth], same)], count), below)).astype(jnp.bfloat16)


def same_site(sites, depth):
    site, lane = iotas((sites, depth))
    return (lane % sites == site).astype(jnp.float32)


def set_right(right_ref, place, moved):
    depth, width = moved.shape
    half = depth // 2
    start = place * depth
    real, imag = moved[:half], moved[half:]
    right_ref[start : start + half, :width] = real
    right_ref[start : start + half, width:] = imag
    right_ref[start + half : start + depth, :width] = imag
    right_ref[start + half : start + depth, width:] = -real


def inner_kernel(
    sites, rows_ref, ahead_ref, back_ref, right_ref, turned_ref, matrix_ref, ahead_part_ref, back_part_ref
):
    planes, depth, width = rows_ref.shape
    same = same_site(sites, depth)
    for x in range(1, planes - 1):
        above = rows_ref[place_of(x + 1, planes)]
        below = rows_ref[place_of(x - 1, planes)]
        moved = move_plane(same, depth // sites, ahead_ref[x], back_ref[x - 1], above, below)
        set_right(right_ref, place_of(x, planes), moved)
    turned_ref[...] = rows_ref[...].reshape(planes * depth, width).T
    x, count = planes - 1, depth // sites
    matrix_ref[...] = site_matrix([(ahead_ref[x, :, :depth], same)], count)
    ahead_part_ref[...] = dot(site_matrix([(ahead_ref[0, :, :depth], same)], count), rows_ref[place_of(1, planes)])
    below = rows_ref[place_of(x - 1, planes)]
    back_part_ref[...] = dot(site_matrix([(back_ref[x - 1, :, :depth], same)], count), below)


def begin_first_kernel(own_ref, others_ref, right_ref, total_ref):
    inner = right_ref.shape[0]
    right = right_ref[...]
    total_ref[0] = dot(own_ref[:, :inner], right)
    for k in range(others_ref.shape[0]):
        total_ref[k + 1] = dot(others_ref[k, :, :inner], right)


def bits(axis):
    return range(lax.axis_size(axis).bit_length() - 1)


def steps():
    one = [("gx", bit) for bit in bits("gx")[:-1]]
    two = [("gy", bit) for bit in bits("gy")]
    both = min(len(one), len(two))
    pairs = [pair for ends in zip(one, two) for pair in (ends, ends[::-1])]
    return pairs + [(step, step) for step in one[both:] + two[both:]]


def my_bit(axis, bit):
    return lax.bitwise_and(lax.shift_right_logical(lax.axis_index(axis), bit), 1)


def my_side(step):
    even, odd = (my_bit(*way) for way in step)
    return jnp.where(my_bit("ma", 0) == 0, even, odd)


def half_of(kind):
    half = lax.bitwise_xor(my_bit("gx", bits("gx")[-1]), 1 - kind)
    return lax.bitwise_xor(half, lax.axis_index("ma"))


def share(total, keep_ref, send_ref, total_ref):
    blocks, rows, double = total_ref.shape
    parts, count, _, width = keep_ref.shape
    total_ref[...] = total.reshape(blocks, rows, double)
    odd_core = my_bit("ma", 0)
    across_y = lax.axis_size("gy")
    plan = steps()
    mine = my_side(plan[0])

    def at(side, index):
        owners = []
        for core in range(2):
            place = {"gx": 0, "gy": 0}
            for k, step in enumerate(plan):
                axis, bit = step[core]
                digit = side if k == 0 else index >> (len(plan) - 1 - k) & 1
                place[axis] += digit * (1 << bit)
            owners.append(place["gx"] * across_y + place["gy"])
        return jnp.where(odd_core == 0, owners[0], owners[1])

    for index in range(count):
        for ref, side in ((keep_ref, mine), (send_ref, 1 - mine)):
            block = total_ref[at(side, index)].astype(ref.dtype)
            for p in range(parts):
                ref[p, index] = block[:, p * width : (p + 1) * width]


def first_share(kind, own_ref, others_ref, begun_ref, right, keep_ref, send_ref, total_ref):
    half = half_of(kind)
    inner = own_ref.shape[1] - right.shape[0]
    left = jnp.where(half == 0, own_ref[:, inner:], others_ref[0, :, inner:])
    share(begun_ref[half] + dot(left, right), keep_ref, send_ref, total_ref)


def first_kernel(
    sites, high_ref, low_ref, matrix_ref, ahead_part_ref, back_part_ref, past_maps_ref, own_ref, others_ref, begun_ref,
    *refs,
):
    keep_ref, send_ref, right_ref, total_ref = refs
    depth = matrix_ref.shape[0]
    same = same_site(sites, depth)
    _, ys, colours, zs, _ = high_ref.shape
    links = low_ref[:, ys:, :, :, :ys].reshape(-1, ys)
    lanes = past_maps_ref.shape[1] // 2
    count = links.shape[0]
    spread = past_maps_ref[:ys, :lanes].astype(jnp.bfloat16)
    match = past_maps_ref[ys : ys + count, lanes:]
    start = past_maps_ref.shape[0] - 24
    choose = past_maps_ref[start : start + 16, :count].astype(jnp.bfloat16)
    past = dot(choose, (dot(links, spread) * match).astype(jnp.bfloat16))
    past = jnp.where(past_maps_ref[start + 16 : start + 17, :lanes] > 0.5, past[:8], past[8:])
    past = site_matrix([(past[:, :depth], same)], depth // sites)
    moved = ahead_part_ref[...] + dot(past, plane_rows(low_ref, ys))
    set_right(right_ref, 0, moved.astype(jnp.bfloat16))
    moved = dot(matrix_ref[...], plane_rows(high_ref, ys)) + back_part_ref[...]
    set_right(right_ref, 1, moved.astype(jnp.bfloat16))
    first_share(0, own_ref, others_ref, begun_ref, right_ref[...], keep_ref, send_ref, total_ref)


def first_own_kernel(own_ref, others_ref, begun_ref, right_ref, keep_ref, send_ref, total_ref):
    first_share(1, own_ref, others_ref, begun_ref, right_ref[...], keep_ref, send_ref, total_ref)


def begin_y_kernel(sites, zs, rows_ref, others_ref, ahead_ref, back_ref, part_ref):
    planes, depth, _ = rows_ref.shape
    site, lane = iotas((sites, depth))
    to_next = jnp.where(lane % sites == site + zs, -1.0, 0.0)
    to_last = jnp.where(lane % sites == site - zs, -1.0, 0.0)
    for x in range(planes):
        ahead, back = ahead_ref[x, :, :depth], back_ref[x, :, :depth]
        matrix = site_matrix([(ahead, to_next), (back, to_last)], depth // sites)
        place = place_of(x, planes)
        part_ref[0, place] = dot(matrix, rows_ref[place])
        for k in range(others_ref.shape[0]):
            part_ref[k + 1, place] = dot(matrix, others_ref[k, place])


def move_y_kernel(sites, zs, part_ref, near_ref, far_ref, ahead_ref, turned_ref, field_ref):
    groups, planes, depth, width = part_ref.shape
    row_size = depth // sites * zs
    tail = 128
    head = ahead_ref.shape[2] - tail
    site, lane = iotas((sites, tail))
    lane = lane + head
    upper = (lane >= depth) & (lane < depth + row_size)
    lower = (lane >= depth + row_size) & (lane < depth + 2 * row_size)
    to_next = jnp.where(upper & (site == sites - zs + lane % zs), -1.0, 0.0)
    to_last = jnp.where(lower & (site == lane % zs), -1.0, 0.0)
    above = jnp.zeros((depth - head, width), jnp.bfloat16)
    below = jnp.zeros((tail - 2 * row_size - (depth - head), width), jnp.bfloat16)
    for x in range(planes):
        past = near_ref[x, 2 * row_size : 2 * row_size + 8, :tail].astype(jnp.float32)
        matrix = site_matrix([(ahead_ref[x, :, head:], to_next), (past, to_last)], depth // sites)
        place = place_of(x, planes)
        for k in range(groups):
            edge = near_ref[x, : 2 * row_size] if k == 0 else far_ref[k - 1, x]
            moved = part_ref[k, place] + dot(matrix, jnp.concatenate([above, edge, below], axis=0))
            field_ref[k, place] = moved.astype(jnp.bfloat16)
    for k in range(groups):
        turned_ref[k] = field_ref[k].reshape(planes * depth, width).T


def second_share(kind, lefts_ref, right_ref, edge_ref, keep_ref, send_ref, total_ref):
    half = half_of(kind)
    inner = right_ref.shape[0]
    total = dot(lefts_ref[half, :, :inner], right_ref[...]) + dot(lefts_ref[half, :, inner:], edge_ref[...])
    share(total, keep_ref, send_ref, total_ref)


def second_kernel(lefts_ref, right_ref, edge_ref, keep_ref, send_ref, total_ref):
    second_share(0, lefts_ref, right_ref, edge_ref, keep_ref, send_ref, total_ref)


def second_own_kernel(lefts_ref, right_ref, edge_ref, first_ref, keep_ref, send_ref, total_ref):
    parts = first_ref.shape[0]
    send_ref[:parts] = first_ref[...]
    second_share(1, lefts_ref, right_ref, edge_ref, keep_ref, send_ref.at[parts:], total_ref)


def exchange(block, step):
    axes = ("gx", "gy", "ma")
    sizes = [lax.axis_size(axis) for axis in axes]
    route = []
    for source in range(sizes[0] * sizes[1] * sizes[2]):
        where = [source // (sizes[1] * sizes[2]), source // sizes[2] % sizes[1], source % sizes[2]]
        axis, bit = step[where[2] % 2]
        where[axes.index(axis)] ^= 1 << bit
        route.append((source, (where[0] * sizes[1] + where[1]) * sizes[2] + where[2]))
    return lax.ppermute(block, axes, route)


def halve(sums, step, weight=0):
    parts = sum(kept.shape[0] for kept, _, _ in sums)
    count, rows, width = sums[0][0].shape[1:]
    dims = (parts, count // 2, rows, width)

    def merge(*refs):
        *refs, keep_ref, send_ref = refs
        mine = my_side(step)
        start = 0
        for k, (_, _, which) in enumerate(sums):
            kept_ref, came_ref = refs[2 * k : 2 * k + 2]
            came_ref = came_ref if which is None else came_ref.at[which]
            end = start + kept_ref.shape[0]
            for index in range(count // 2):
                low, high = (
                    kept_ref[:, at] + came_ref[:, at].astype(jnp.float32) for at in (index, index + count // 2)
                )
                keep_ref[start:end, index] = jnp.where(mine == 0, low, high)
                send_ref[start:end, index] = jnp.where(mine == 0, high, low).astype(send_ref.dtype)
            start = end

    operands = [a for kept, came, _ in sums for a in (kept, came)]
    keep, send = call(merge, (pltpu.VMEM(dims, jnp.float32), pltpu.VMEM(dims, jnp.bfloat16)), weight, operands)
    return keep, exchange(send, step)


def sum_kernel(kept_ref, came_ref, send_ref):
    send_ref[...] = (kept_ref[...] + came_ref[...].astype(jnp.float32)).astype(send_ref.dtype)


def cross_kernel(start, kept_ref, crossed_ref, out_ref):
    kept = kept_ref[start : start + out_ref.shape[0]]
    out_ref[...] = kept + crossed_ref[...].astype(jnp.float32)


def finish_kernel(came_ref, *refs):
    *kept_refs, out_ref = refs
    parts = out_ref.shape[1]
    for d, kept_ref in enumerate(kept_refs):
        out_ref[d] = kept_ref[:, 0] + came_ref[d * parts : (d + 1) * parts, 0].astype(jnp.float32)


def local(eigen_modes, links_first, links_second):
    f32, bf16 = jnp.float32, jnp.bfloat16
    parts, planes, ys, zs, colours, width = eigen_modes.shape
    sites = ys * zs
    depth = parts * colours * sites
    row_size = parts * colours * zs
    edge = -(-(2 * row_size + 8) // 16) * 16
    lanes = -(-(depth + 2 * row_size) // 128) * 128
    across_x, across_y, groups = (lax.axis_size(a) for a in ("gx", "gy", "ma"))
    rows = groups * width // (across_x * across_y)
    inner_depth = (planes - 2) * depth
    raw = eigen_modes.transpose(0, 1, 2, 4, 3, 5)

    def shape(*dims, dtype=bf16):
        return pltpu.VMEM(dims, dtype)

    field_shape = shape(planes, depth, width)
    turned_shape = shape(width, planes * depth)
    total_shape = shape(groups, width, parts * width, dtype=f32)
    link_shape = shape(planes, 8, lanes, dtype=f32)
    total = pltpu.VMEM((width // rows, rows, parts * width), f32)
    step_flops = 2 * planes * depth * depth * width
    project_flops = 2 * groups * width * planes * depth * parts * width

    raw_others = [shifted(raw, "ma", -step) for step in range(1, groups)]
    raw_links_x, raw_links_y = (a.transpose(0, 1, 2, 3, 5, 4) for a in (links_first, links_second))
    inputs = [raw, raw_links_x, raw_links_y]
    first_plane, last_plane, *inputs, past_maps = call(
        edges_kernel,
        (
            shape(parts, ys, colours, zs, width), shape(parts, ys + colours, colours, zs, width),
            *(shape(*a.shape) for a in inputs),
            shape(map_rows(parts, colours, planes, ys, zs)[-1], 2 * lanes, dtype=f32),
            shape(map_rows(parts, colours, 1, ys, zs)[-1], 2 * lanes, dtype=f32),
        ),
        0,
        inputs,
        [pltpu.SemaphoreType.DMA((5,))],
        [pltpu.HBM] * len(inputs),
    )
    low = shifted(last_plane, "gx", 1)
    high = shifted(first_plane, "gx", -1)
    field, ends, ahead_x, back_x, ahead_y, back_y = call(
        prepare_kernel,
        (field_shape, shape(planes, edge, width), link_shape, link_shape, link_shape, link_shape),
        0,
        inputs,
    )
    near = shifted(ends, "gy", 1)
    if across_y != 2:
        ahead_row = lax.broadcasted_iota(jnp.int32, ends.shape, 1) < row_size
        near = jnp.where(ahead_row, shifted(ends, "gy", -1), near)

    plan = steps()
    top = ("gx", bits("gx")[-1])
    pieces = across_x * across_y // 4
    kept_shape = shape(parts, pieces, rows, width, dtype=f32)
    sent_shape = shape(parts, pieces, rows, width)

    def inner(*refs):
        inner_kernel(sites, *refs)

    def first(*refs):
        first_kernel(sites, *refs)

    def begin_y(*refs):
        begin_y_kernel(sites, zs, *refs)

    def move_y(*refs):
        move_y_kernel(sites, zs, *refs)

    right, own, matrix, ahead_part, back_part = call(
        inner,
        (
            shape(inner_depth, parts * width), turned_shape, shape(depth, depth),
            shape(depth, width, dtype=f32), shape(depth, width, dtype=f32),
        ),
        2 * step_flops,
        [field, ahead_x, back_x],
    )
    turned = [call(turn_kernel, (field_shape, turned_shape), step_flops // 4, [r]) for r in raw_others]
    fields = jnp.stack([t[0] for t in turned])
    others = jnp.stack([t[1] for t in turned])
    begun_first = call(begin_first_kernel, total_shape, project_flops, [own, others, right])
    part_y = call(
        begin_y, shape(groups, planes, depth, width, dtype=f32), 2 * step_flops, [field, fields, ahead_y, back_y]
    )
    part_y, begun_first = lax.optimization_barrier((part_y, begun_first))
    kept_first, sent_first, right_edge = call(
        first,
        (kept_shape, sent_shape, shape(2 * depth, parts * width)),
        project_flops,
        [high, low, matrix, ahead_part, back_part, past_maps, own, others, begun_first],
        [total],
    )
    came_first = exchange(sent_first, plan[0])
    near, right_edge = lax.optimization_barrier((near, right_edge))
    near_rows = near[:, : 2 * row_size]
    far = jnp.stack([shifted(near_rows, "ma", -step) for step in range(1, groups)])
    lefts = call(
        move_y, shape(groups, width, planes * depth), 2 * step_flops,
        [part_y, near, far, ahead_y],
        [pltpu.VMEM((groups,) + field_shape.shape, bf16)],
    )
    kept_second, sent_second = call(
        second_kernel, (kept_shape, sent_shape), 8 * project_flops, [lefts, right, right_edge], [total]
    )
    came_second = exchange(sent_second, plan[0])
    right_edge, kept_second = lax.optimization_barrier((right_edge, kept_second))
    own_first, sent_own = call(
        first_own_kernel, (kept_shape, sent_shape), 0, [own, others, begun_first, right_edge], [total]
    )
    own_second, sent_own = call(
        second_own_kernel, (kept_shape, shape(2 * parts, pieces, rows, width)), 0,
        [lefts, right, right_edge, sent_own], [total],
    )
    came_own = exchange(sent_own, plan[0])
    staying = [(own_first, came_own, slice(0, parts)), (own_second, came_own, slice(parts, 2 * parts))]
    crossing = [(kept_first, came_first), (kept_second, came_second)]
    after = own_second
    for step in plan[1:]:
        for d, (kept, came) in enumerate(crossing):
            came, after = lax.optimization_barrier((came, after))
            crossing[d] = halve([(kept, came, None)], step, 4 * project_flops if d else 0)
            after = crossing[d][0]
    crossed = []
    for kept, came in crossing:
        came, after = lax.optimization_barrier((came, after))
        after = call(sum_kernel, pltpu.VMEM(kept.shape, bf16), 0, [kept, came])
        crossed.append(exchange(after, (top, top)))
    for step in plan[1:]:
        kept, came, which = staying[0]
        came, after = lax.optimization_barrier((came, after))
        sums = [(kept, came, which)] + [(k, came, w) for k, _, w in staying[1:]]
        kept, came = halve(sums, step)
        staying, after = [(kept, came, None)], kept
    kept, came, _ = staying[0]
    totals = []
    for d, block in enumerate(crossed):

        def cross(*refs, start=d * parts):
            cross_kernel(start, *refs)

        block, after = lax.optimization_barrier((block, after))
        after = call(cross, shape(*block.shape, dtype=f32), 4 * project_flops, [kept, block])
        totals.append(after)
    came, after = lax.optimization_barrier((came, after))
    return call(
        finish_kernel, jax.ShapeDtypeStruct((2, parts, rows, width), f32), 0, [came, *totals]
    )


def solution(mesh):
    return jax.shard_map(
        local,
        mesh=mesh,
        in_specs=(
            P("cuts", "gx", "gy", None, None, "ma"),
            P("cuts", None, None, "gx", "gy", None),
            P("cuts", None, None, "gx", "gy", None),
        ),
        out_specs=P("cuts", None, ("gx", "gy"), "ma"),
        check_vma=False,
    )
```

```python
import jax
import jax.numpy as jnp
from jax import lax
from jax.experimental import pallas as pl
from jax.experimental.pallas import tpu as pltpu
from jax.sharding import PartitionSpec as P

VMEM_LIMIT = 16 * 1024 * 1024


def shifted(block, axis, distance):
    devices = range(lax.axis_size(axis))
    route = [((i - distance) % len(devices), i) for i in devices]
    return lax.ppermute(block, axis, route)


def call(body, out_shape, flops, operands, scratch=(), places=None):
    places = places or [pltpu.VMEM] * len(operands)
    return pl.pallas_call(
        body,
        out_shape=out_shape,
        in_specs=[pl.BlockSpec(memory_space=place) for place in places],
        scratch_shapes=scratch,
        cost_estimate=pl.CostEstimate(flops=flops // 2, bytes_accessed=0, transcendentals=0),
        compiler_params=pltpu.CompilerParams(vmem_limit_bytes=VMEM_LIMIT),
    )(*(pltpu.with_memory_space_constraint(a, place) for a, place in zip(operands, places)))


def dot(a, b):
    return jnp.dot(a, b, preferred_element_type=jnp.float32)


def iotas(shape):
    return (
        lax.broadcasted_iota(jnp.int32, shape, 0),
        lax.broadcasted_iota(jnp.int32, shape, 1),
    )


def place_of(x, planes):
    return planes - 2 if x == 0 else x if x == planes - 1 else x - 1


def map_rows(parts, colours, planes, ys, zs):
    match = ys
    choose = match + -(-parts * colours * colours * planes * zs // 8) * 8
    first_part = choose + 2 * parts * planes * 8
    return match, choose, first_part, first_part + 8


def write_maps(ref, parts, colours, planes, ys, zs):
    lanes = ref.shape[1] // 2
    sites = ys * zs
    depth = parts * colours * sites
    row_size = parts * colours * zs
    match, choose, first_part, _ = map_rows(parts, colours, planes, ys, zs)

    def ones(mask):
        return jnp.where(mask, 1.0, 0.0)

    def column(count):
        return lax.broadcasted_iota(jnp.int32, (count, 1), 0)

    def line(count):
        return lax.broadcasted_iota(jnp.int32, (1, count), 1)

    lane = line(lanes)
    inner = lane < depth
    past = lax.rem(jnp.maximum(lane - depth, 0), row_size)
    used = lane < depth + 2 * row_size
    part = jnp.where(inner, lax.div(lane, colours * sites), lax.div(past, colours * zs))
    colour = lax.rem(jnp.where(inner, lax.div(lane, sites), lax.div(past, zs)), colours)
    z = lax.rem(jnp.where(inner, lane, past), zs)
    y = lax.div(lax.rem(lane, sites), zs)
    ref[:ys, :lanes] = ones(column(ys) == jnp.where(inner, y, ys - 1))
    ref[:ys, lanes:] = ones(column(ys) == jnp.where(inner, y, ys) - 1)

    count = parts * colours * colours * planes * zs

    def link(index):
        x = lax.rem(lax.div(index, zs), planes)
        right = lax.rem(lax.div(index, zs * planes), colours)
        left = lax.rem(lax.div(index, zs * planes * colours), colours)
        return x, right, left, lax.div(index, zs * planes * colours * colours)

    row = column(count)
    _, right, left, _ = link(row)
    row_z = lax.rem(row, zs)
    key = jnp.where(used, colour * zs + z, -1)
    ref[match : match + count, :lanes] = ones(right * zs + row_z == key)
    ref[match : match + count, lanes:] = ones(left * zs + row_z == key)

    out = column(parts * planes * 8)
    field_part = lax.div(out, planes * 8)
    out_x = lax.rem(lax.div(out, 8), planes)
    out_part = lax.div(lax.rem(out, 8), colours)
    out_colour = lax.rem(lax.rem(out, 8), colours)
    x, right, left, source_part = link(line(count))
    source = source_part * planes + x
    wanted = jnp.where(out_part < parts, lax.rem(out_part + field_part, 2) * planes + out_x, -1)
    sign_ahead = jnp.where((field_part == 1) & (out_part == 0), -1.0, 1.0)
    sign_back = jnp.where((field_part == 0) & (out_part == 1), 1.0, -1.0)
    half = parts * planes * 8
    for start, end, sign in ((choose, left, sign_ahead), (choose + half, right, sign_back)):
        hit = source * colours + end == wanted * colours + jnp.where(wanted < 0, -1, out_colour)
        ref[start : start + half, :count] = jnp.where(hit, sign, 0.0)
    ref[first_part:, :lanes] = jnp.broadcast_to(ones(part == 0), (8, lanes))


def coefficients(links_x, links_y, maps_ref, planes):
    lanes = maps_ref.shape[1] // 2
    ys = links_x.shape[1]
    count = links_x.shape[0]
    half = 2 * planes * 8
    wide = dot(jnp.concatenate([links_x, links_y], axis=0), maps_ref[:ys].astype(jnp.bfloat16))
    match = maps_ref[ys : ys + count]
    match_ahead, match_back = match[:, :lanes], match[:, lanes:]
    choose = maps_ref[ys + count : ys + count + 2 * half, :count].astype(jnp.bfloat16)
    first_part = maps_ref[ys + count + 2 * half : ys + count + 2 * half + 1, :lanes] > 0.5
    ahead = jnp.concatenate([wide[:count, :lanes] * match_ahead, wide[count:, lanes:] * match_ahead], axis=1)
    back = jnp.concatenate([wide[:count, :lanes] * match_back, wide[count:, :lanes] * match_back], axis=1)
    out = []
    for chosen in (
        dot(choose[:half], ahead.astype(jnp.bfloat16)), dot(choose[half:], back.astype(jnp.bfloat16))
    ):
        for start in (0, lanes):
            part = chosen[:, start : start + lanes]
            rows = jnp.where(first_part, part[: half // 2], part[half // 2 :])
            out.append(rows.reshape(planes, 8, lanes))
    return out


def plane_rows(ref, ys):
    parts, _, colours, zs, width = ref.shape
    return jnp.concatenate(
        [ref[p, :ys, c].reshape(ys * zs, width) for p in range(parts) for c in range(colours)],
        axis=0,
    )


def edges_kernel(
    raw_hbm, links_x_hbm, links_y_hbm,
    first_ref, last_ref, raw_ref, links_x_ref, links_y_ref, maps_ref, past_maps_ref, arrived,
):
    parts, planes, ys, colours, zs, _ = raw_hbm.shape
    sources = (raw_hbm.at[:, planes - 1], raw_hbm.at[:, 0], links_x_hbm, links_y_hbm, raw_hbm)
    targets = (last_ref.at[:, :ys], first_ref, links_x_ref, links_y_ref, raw_ref)
    copies = [
        pltpu.make_async_copy(source, target, arrived.at[i])
        for i, (source, target) in enumerate(zip(sources, targets))
    ]
    for copy in copies:
        copy.start()
    last_ref[:, ys:] = jnp.zeros((parts, colours) + last_ref.shape[2:], last_ref.dtype)
    write_maps(maps_ref, parts, colours, planes, ys, zs)
    write_maps(past_maps_ref, parts, colours, 1, ys, zs)
    copies[2].wait()
    last_ref[:, ys:, :, :, :ys] = links_x_ref[:, :, :, planes - 1]
    for copy in copies[:2] + copies[3:]:
        copy.wait()


def site_matrix(rows_and_masks, count):
    blocks = []
    for q in range(count):
        block = None
        for rows, mask in rows_and_masks:
            term = rows[q : q + 1] * mask
            block = term if block is None else block + term
        blocks.append(block.astype(jnp.bfloat16))
    return jnp.concatenate(blocks, axis=0)


def prepare_kernel(
    raw_ref, links_x_ref, links_y_ref, maps_ref,
    rows_ref, ends_ref, ahead_x_ref, back_x_ref, ahead_y_ref, back_y_ref,
):
    planes, depth, width = rows_ref.shape
    zs = raw_ref.shape[4]
    ys = raw_ref.shape[2]
    sites = ys * zs
    row_size = depth // sites * zs
    lanes = ahead_y_ref.shape[2]
    ahead_x, ahead_y, back_x, back_y = coefficients(
        links_x_ref[...].reshape(-1, ys), links_y_ref[...].reshape(-1, ys), maps_ref, planes
    )
    ahead_x_ref[...] = ahead_x
    back_x_ref[...] = back_x
    ahead_y_ref[...] = ahead_y
    back_y_ref[...] = back_y

    row, lane = iotas((2 * row_size, depth))
    spot = row % row_size
    wanted = (spot // zs) * sites + spot % zs + jnp.where(row < row_size, 0, sites - zs)
    ends = (lane == wanted).astype(jnp.bfloat16)
    filler = jnp.zeros((8, width - 128), jnp.float32)
    spare = ends_ref.shape[1] - 2 * row_size - 8
    for x in range(planes):
        plane = plane_rows(raw_ref.at[:, x], ys)
        rows_ref[place_of(x, planes)] = plane
        tail = jnp.concatenate([back_y[x, :, lanes - 128 :], filler], axis=1)
        pieces = [dot(ends, plane), tail]
        if spare:
            pieces.append(jnp.zeros((spare, width), jnp.float32))
        ends_ref[x] = jnp.concatenate(pieces, axis=0).astype(jnp.bfloat16)


def turn_kernel(raw_ref, rows_ref, turned_ref):
    planes, depth, width = rows_ref.shape
    for x in range(planes):
        rows_ref[place_of(x, planes)] = plane_rows(raw_ref.at[:, x], raw_ref.shape[2])
    turned_ref[...] = rows_ref[...].reshape(planes * depth, width).T


def move_plane(same, count, ahead, back, above, below):
    depth = same.shape[1]
    moved = dot(site_matrix([(ahead[:, :depth], same)], count), above)
    return (moved + dot(site_matrix([(back[:, :depth], same)], count), below)).astype(jnp.bfloat16)


def same_site(sites, depth):
    site, lane = iotas((sites, depth))
    return (lane % sites == site).astype(jnp.float32)


def set_right(right_ref, place, moved):
    depth, width = moved.shape
    half = depth // 2
    start = place * depth
    real, imag = moved[:half], moved[half:]
    right_ref[start : start + half, :width] = real
    right_ref[start : start + half, width:] = imag
    right_ref[start + half : start + depth, :width] = imag
    right_ref[start + half : start + depth, width:] = -real


def inner_kernel(
    sites, rows_ref, ahead_ref, back_ref, right_ref, turned_ref, matrix_ref, ahead_part_ref, back_part_ref
):
    planes, depth, width = rows_ref.shape
    same = same_site(sites, depth)
    for x in range(1, planes - 1):
        above = rows_ref[place_of(x + 1, planes)]
        below = rows_ref[place_of(x - 1, planes)]
        moved = move_plane(same, depth // sites, ahead_ref[x], back_ref[x - 1], above, below)
        set_right(right_ref, place_of(x, planes), moved)
    turned_ref[...] = rows_ref[...].reshape(planes * depth, width).T
    x, count = planes - 1, depth // sites
    matrix_ref[...] = site_matrix([(ahead_ref[x, :, :depth], same)], count)
    ahead_part_ref[...] = dot(site_matrix([(ahead_ref[0, :, :depth], same)], count), rows_ref[place_of(1, planes)])
    below = rows_ref[place_of(x - 1, planes)]
    back_part_ref[...] = dot(site_matrix([(back_ref[x - 1, :, :depth], same)], count), below)


def begin_first_kernel(own_ref, others_ref, right_ref, total_ref):
    inner = right_ref.shape[0]
    right = right_ref[...]
    total_ref[0] = dot(own_ref[:, :inner], right)
    for k in range(others_ref.shape[0]):
        total_ref[k + 1] = dot(others_ref[k, :, :inner], right)


def bits(axis):
    return range(lax.axis_size(axis).bit_length() - 1)


def steps():
    one = [("gx", bit) for bit in bits("gx")[:-1]]
    two = [("gy", bit) for bit in bits("gy")]
    both = min(len(one), len(two))
    pairs = [pair for ends in zip(one, two) for pair in (ends, ends[::-1])]
    return pairs + [(step, step) for step in one[both:] + two[both:]]


def my_bit(axis, bit):
    return lax.bitwise_and(lax.shift_right_logical(lax.axis_index(axis), bit), 1)


def my_side(step):
    even, odd = (my_bit(*way) for way in step)
    return jnp.where(my_bit("ma", 0) == 0, even, odd)


def half_of(kind):
    half = lax.bitwise_xor(my_bit("gx", bits("gx")[-1]), 1 - kind)
    return lax.bitwise_xor(half, lax.axis_index("ma"))


def share(total, keep_ref, send_ref, total_ref):
    blocks, rows, double = total_ref.shape
    parts, count, _, width = keep_ref.shape
    total_ref[...] = total.reshape(blocks, rows, double)
    odd_core = my_bit("ma", 0)
    across_y = lax.axis_size("gy")
    plan = steps()
    mine = my_side(plan[0])

    def at(side, index):
        owners = []
        for core in range(2):
            place = {"gx": 0, "gy": 0}
            for k, step in enumerate(plan):
                axis, bit = step[core]
                digit = side if k == 0 else index >> (len(plan) - 1 - k) & 1
                place[axis] += digit * (1 << bit)
            owners.append(place["gx"] * across_y + place["gy"])
        return jnp.where(odd_core == 0, owners[0], owners[1])

    for index in range(count):
        for ref, side in ((keep_ref, mine), (send_ref, 1 - mine)):
            block = total_ref[at(side, index)].astype(ref.dtype)
            for p in range(parts):
                ref[p, index] = block[:, p * width : (p + 1) * width]


def first_share(kind, own_ref, others_ref, begun_ref, right, keep_ref, send_ref, total_ref):
    half = half_of(kind)
    inner = own_ref.shape[1] - right.shape[0]
    left = jnp.where(half == 0, own_ref[:, inner:], others_ref[0, :, inner:])
    share(begun_ref[half] + dot(left, right), keep_ref, send_ref, total_ref)


def first_kernel(
    sites, high_ref, low_ref, matrix_ref, ahead_part_ref, back_part_ref, past_maps_ref, own_ref, others_ref, begun_ref,
    *refs,
):
    keep_ref, send_ref, right_ref, total_ref = refs
    depth = matrix_ref.shape[0]
    same = same_site(sites, depth)
    _, ys, colours, zs, _ = high_ref.shape
    links = low_ref[:, ys:, :, :, :ys].reshape(-1, ys)
    lanes = past_maps_ref.shape[1] // 2
    count = links.shape[0]
    spread = past_maps_ref[:ys, :lanes].astype(jnp.bfloat16)
    match = past_maps_ref[ys : ys + count, lanes:]
    start = past_maps_ref.shape[0] - 24
    choose = past_maps_ref[start : start + 16, :count].astype(jnp.bfloat16)
    past = dot(choose, (dot(links, spread) * match).astype(jnp.bfloat16))
    past = jnp.where(past_maps_ref[start + 16 : start + 17, :lanes] > 0.5, past[:8], past[8:])
    past = site_matrix([(past[:, :depth], same)], depth // sites)
    moved = ahead_part_ref[...] + dot(past, plane_rows(low_ref, ys))
    set_right(right_ref, 0, moved.astype(jnp.bfloat16))
    moved = dot(matrix_ref[...], plane_rows(high_ref, ys)) + back_part_ref[...]
    set_right(right_ref, 1, moved.astype(jnp.bfloat16))
    first_share(0, own_ref, others_ref, begun_ref, right_ref[...], keep_ref, send_ref, total_ref)


def first_own_kernel(own_ref, others_ref, begun_ref, right_ref, keep_ref, send_ref, total_ref):
    first_share(1, own_ref, others_ref, begun_ref, right_ref[...], keep_ref, send_ref, total_ref)


def begin_y_kernel(sites, zs, rows_ref, others_ref, ahead_ref, back_ref, part_ref):
    planes, depth, _ = rows_ref.shape
    site, lane = iotas((sites, depth))
    to_next = jnp.where(lane % sites == site + zs, -1.0, 0.0)
    to_last = jnp.where(lane % sites == site - zs, -1.0, 0.0)
    for x in range(planes):
        ahead, back = ahead_ref[x, :, :depth], back_ref[x, :, :depth]
        matrix = site_matrix([(ahead, to_next), (back, to_last)], depth // sites)
        place = place_of(x, planes)
        part_ref[0, place] = dot(matrix, rows_ref[place])
        for k in range(others_ref.shape[0]):
            part_ref[k + 1, place] = dot(matrix, others_ref[k, place])


def move_y(kind, sites, zs, part_ref, near_ref, far_ref, ahead_ref, turned_ref, field_ref):
    _, planes, depth, width = part_ref.shape
    half = half_of(kind)
    row_size = depth // sites * zs
    tail = 128
    head = ahead_ref.shape[2] - tail
    site, lane = iotas((sites, tail))
    lane = lane + head
    upper = (lane >= depth) & (lane < depth + row_size)
    lower = (lane >= depth + row_size) & (lane < depth + 2 * row_size)
    to_next = jnp.where(upper & (site == sites - zs + lane % zs), -1.0, 0.0)
    to_last = jnp.where(lower & (site == lane % zs), -1.0, 0.0)
    above = jnp.zeros((depth - head, width), jnp.bfloat16)
    below = jnp.zeros((tail - 2 * row_size - (depth - head), width), jnp.bfloat16)
    for x in range(planes):
        past = near_ref[x, 2 * row_size : 2 * row_size + 8, :tail].astype(jnp.float32)
        matrix = site_matrix([(ahead_ref[x, :, head:], to_next), (past, to_last)], depth // sites)
        place = place_of(x, planes)
        edge = jnp.where(half == 0, near_ref[x, : 2 * row_size], far_ref[0, x])
        moved = part_ref[half, place] + dot(matrix, jnp.concatenate([above, edge, below], axis=0))
        field_ref[place] = moved.astype(jnp.bfloat16)
    turned_ref[...] = field_ref[...].reshape(planes * depth, width).T


def second_share(left_ref, right_ref, edge_ref, keep_ref, send_ref, total_ref):
    inner = right_ref.shape[0]
    total = dot(left_ref[:, :inner], right_ref[...]) + dot(left_ref[:, inner:], edge_ref[...])
    share(total, keep_ref, send_ref, total_ref)


def second_own_kernel(left_ref, right_ref, edge_ref, first_ref, keep_ref, send_ref, total_ref):
    parts = first_ref.shape[0]
    send_ref[:parts] = first_ref[...]
    second_share(left_ref, right_ref, edge_ref, keep_ref, send_ref.at[parts:], total_ref)


def exchange(block, step):
    axes = ("gx", "gy", "ma")
    sizes = [lax.axis_size(axis) for axis in axes]
    route = []
    for source in range(sizes[0] * sizes[1] * sizes[2]):
        where = [source // (sizes[1] * sizes[2]), source // sizes[2] % sizes[1], source % sizes[2]]
        axis, bit = step[where[2] % 2]
        where[axes.index(axis)] ^= 1 << bit
        route.append((source, (where[0] * sizes[1] + where[1]) * sizes[2] + where[2]))
    return lax.ppermute(block, axes, route)


def halve(sums, step, weight=0):
    parts = sum(kept.shape[0] for kept, _, _ in sums)
    count, rows, width = sums[0][0].shape[1:]
    dims = (parts, count // 2, rows, width)

    def merge(*refs):
        *refs, keep_ref, send_ref = refs
        mine = my_side(step)
        start = 0
        for k, (_, _, which) in enumerate(sums):
            kept_ref, came_ref = refs[2 * k : 2 * k + 2]
            came_ref = came_ref if which is None else came_ref.at[which]
            end = start + kept_ref.shape[0]
            for index in range(count // 2):
                low, high = (
                    kept_ref[:, at] + came_ref[:, at].astype(jnp.float32) for at in (index, index + count // 2)
                )
                keep_ref[start:end, index] = jnp.where(mine == 0, low, high)
                send_ref[start:end, index] = jnp.where(mine == 0, high, low).astype(send_ref.dtype)
            start = end

    operands = [a for kept, came, _ in sums for a in (kept, came)]
    keep, send = call(merge, (pltpu.VMEM(dims, jnp.float32), pltpu.VMEM(dims, jnp.bfloat16)), weight, operands)
    return keep, exchange(send, step)


def sum_kernel(kept_ref, came_ref, send_ref):
    send_ref[...] = (kept_ref[...] + came_ref[...].astype(jnp.float32)).astype(send_ref.dtype)


def cross_kernel(start, kept_ref, crossed_ref, out_ref):
    kept = kept_ref[start : start + out_ref.shape[0]]
    out_ref[...] = kept + crossed_ref[...].astype(jnp.float32)


def finish_kernel(came_ref, *refs):
    *kept_refs, out_ref = refs
    parts = out_ref.shape[1]
    for d, kept_ref in enumerate(kept_refs):
        out_ref[d] = kept_ref[:, 0] + came_ref[d * parts : (d + 1) * parts, 0].astype(jnp.float32)


def local(eigen_modes, links_first, links_second):
    f32, bf16 = jnp.float32, jnp.bfloat16
    parts, planes, ys, zs, colours, width = eigen_modes.shape
    sites = ys * zs
    depth = parts * colours * sites
    row_size = parts * colours * zs
    edge = -(-(2 * row_size + 8) // 16) * 16
    lanes = -(-(depth + 2 * row_size) // 128) * 128
    across_x, across_y, groups = (lax.axis_size(a) for a in ("gx", "gy", "ma"))
    rows = groups * width // (across_x * across_y)
    inner_depth = (planes - 2) * depth
    raw = eigen_modes.transpose(0, 1, 2, 4, 3, 5)

    def shape(*dims, dtype=bf16):
        return pltpu.VMEM(dims, dtype)

    field_shape = shape(planes, depth, width)
    turned_shape = shape(width, planes * depth)
    total_shape = shape(groups, width, parts * width, dtype=f32)
    link_shape = shape(planes, 8, lanes, dtype=f32)
    total = pltpu.VMEM((width // rows, rows, parts * width), f32)
    step_flops = 2 * planes * depth * depth * width
    project_flops = 2 * groups * width * planes * depth * parts * width

    raw_others = [shifted(raw, "ma", -step) for step in range(1, groups)]
    raw_links_x, raw_links_y = (a.transpose(0, 1, 2, 3, 5, 4) for a in (links_first, links_second))
    inputs = [raw, raw_links_x, raw_links_y]
    first_plane, last_plane, *inputs, past_maps = call(
        edges_kernel,
        (
            shape(parts, ys, colours, zs, width), shape(parts, ys + colours, colours, zs, width),
            *(shape(*a.shape) for a in inputs),
            shape(map_rows(parts, colours, planes, ys, zs)[-1], 2 * lanes, dtype=f32),
            shape(map_rows(parts, colours, 1, ys, zs)[-1], 2 * lanes, dtype=f32),
        ),
        0,
        inputs,
        [pltpu.SemaphoreType.DMA((5,))],
        [pltpu.HBM] * len(inputs),
    )
    low = shifted(last_plane, "gx", 1)
    high = shifted(first_plane, "gx", -1)
    field, ends, ahead_x, back_x, ahead_y, back_y = call(
        prepare_kernel,
        (field_shape, shape(planes, edge, width), link_shape, link_shape, link_shape, link_shape),
        0,
        inputs,
    )
    near = shifted(ends, "gy", 1)
    if across_y != 2:
        ahead_row = lax.broadcasted_iota(jnp.int32, ends.shape, 1) < row_size
        near = jnp.where(ahead_row, shifted(ends, "gy", -1), near)

    plan = steps()
    top = ("gx", bits("gx")[-1])
    pieces = across_x * across_y // 4
    kept_shape = shape(parts, pieces, rows, width, dtype=f32)
    sent_shape = shape(parts, pieces, rows, width)

    def inner(*refs):
        inner_kernel(sites, *refs)

    def first(*refs):
        first_kernel(sites, *refs)

    def begin_y(*refs):
        begin_y_kernel(sites, zs, *refs)

    def move_cross(*refs):
        move_y(0, sites, zs, *refs)

    def move_own(*refs):
        move_y(1, sites, zs, *refs)

    right, own, matrix, ahead_part, back_part = call(
        inner,
        (
            shape(inner_depth, parts * width), turned_shape, shape(depth, depth),
            shape(depth, width, dtype=f32), shape(depth, width, dtype=f32),
        ),
        2 * step_flops,
        [field, ahead_x, back_x],
    )
    turned = [call(turn_kernel, (field_shape, turned_shape), step_flops // 4, [r]) for r in raw_others]
    fields = jnp.stack([t[0] for t in turned])
    others = jnp.stack([t[1] for t in turned])
    begun_first = call(begin_first_kernel, total_shape, project_flops, [own, others, right])
    part_y = call(
        begin_y, shape(groups, planes, depth, width, dtype=f32), 2 * step_flops, [field, fields, ahead_y, back_y]
    )
    part_y, begun_first = lax.optimization_barrier((part_y, begun_first))
    kept_first, sent_first, right_edge = call(
        first,
        (kept_shape, sent_shape, shape(2 * depth, parts * width)),
        project_flops,
        [high, low, matrix, ahead_part, back_part, past_maps, own, others, begun_first],
        [total],
    )
    came_first = exchange(sent_first, plan[0])
    near, right_edge = lax.optimization_barrier((near, right_edge))
    near_rows = near[:, : 2 * row_size]
    far = jnp.stack([shifted(near_rows, "ma", -step) for step in range(1, groups)])
    move_operands = [part_y, near, far, ahead_y]
    move_scratch = [pltpu.VMEM(field_shape.shape, bf16)]
    left = call(move_cross, turned_shape, step_flops, move_operands, move_scratch)
    kept_second, sent_second = call(
        second_share, (kept_shape, sent_shape), 8 * project_flops, [left, right, right_edge], [total]
    )
    came_second = exchange(sent_second, plan[0])
    right_edge, part_y, kept_second = lax.optimization_barrier((right_edge, part_y, kept_second))
    left = call(move_own, turned_shape, 0, [part_y] + move_operands[1:], move_scratch)
    own_first, sent_own = call(
        first_own_kernel, (kept_shape, sent_shape), 0, [own, others, begun_first, right_edge], [total]
    )
    own_second, sent_own = call(
        second_own_kernel, (kept_shape, shape(2 * parts, pieces, rows, width)), 0,
        [left, right, right_edge, sent_own], [total],
    )
    came_own = exchange(sent_own, plan[0])
    staying = [(own_first, came_own, slice(0, parts)), (own_second, came_own, slice(parts, 2 * parts))]
    crossing = [(kept_first, came_first), (kept_second, came_second)]
    after = own_second
    for step in plan[1:]:
        for d, (kept, came) in enumerate(crossing):
            came, after = lax.optimization_barrier((came, after))
            crossing[d] = halve([(kept, came, None)], step, 4 * project_flops if d else 0)
            after = crossing[d][0]
    crossed = []
    for kept, came in crossing:
        came, after = lax.optimization_barrier((came, after))
        after = call(sum_kernel, pltpu.VMEM(kept.shape, bf16), 0, [kept, came])
        crossed.append(exchange(after, (top, top)))
    for step in plan[1:]:
        kept, came, which = staying[0]
        came, after = lax.optimization_barrier((came, after))
        sums = [(kept, came, which)] + [(k, came, w) for k, _, w in staying[1:]]
        kept, came = halve(sums, step)
        staying, after = [(kept, came, None)], kept
    kept, came, _ = staying[0]
    totals = []
    for d, block in enumerate(crossed):

        def cross(*refs, start=d * parts):
            cross_kernel(start, *refs)

        block, after = lax.optimization_barrier((block, after))
        after = call(cross, shape(*block.shape, dtype=f32), 4 * project_flops, [kept, block])
        totals.append(after)
    came, after = lax.optimization_barrier((came, after))
    return call(
        finish_kernel, jax.ShapeDtypeStruct((2, parts, rows, width), f32), 0, [came, *totals]
    )


def solution(mesh):
    return jax.shard_map(
        local,
        mesh=mesh,
        in_specs=(
            P("cuts", "gx", "gy", None, None, "ma"),
            P("cuts", None, None, "gx", "gy", None),
            P("cuts", None, None, "gx", "gy", None),
        ),
        out_specs=P("cuts", None, ("gx", "gy"), "ma"),
        check_vma=False,
    )
```

```python
import jax
import jax.numpy as jnp
from jax import lax
from jax.experimental import pallas as pl
from jax.experimental.pallas import tpu as pltpu
from jax.sharding import PartitionSpec as P

VMEM_LIMIT = 16 * 1024 * 1024


def shifted(block, axis, distance):
    devices = range(lax.axis_size(axis))
    route = [((i - distance) % len(devices), i) for i in devices]
    return lax.ppermute(block, axis, route)


def call(body, out_shape, flops, operands, scratch=(), places=None):
    places = places or [pltpu.VMEM] * len(operands)
    return pl.pallas_call(
        body,
        out_shape=out_shape,
        in_specs=[pl.BlockSpec(memory_space=place) for place in places],
        scratch_shapes=scratch,
        cost_estimate=pl.CostEstimate(flops=flops // 2, bytes_accessed=0, transcendentals=0),
        compiler_params=pltpu.CompilerParams(vmem_limit_bytes=VMEM_LIMIT),
    )(*(pltpu.with_memory_space_constraint(a, place) for a, place in zip(operands, places)))


def dot(a, b):
    return jnp.dot(a, b, preferred_element_type=jnp.float32)


def iotas(shape):
    return (
        lax.broadcasted_iota(jnp.int32, shape, 0),
        lax.broadcasted_iota(jnp.int32, shape, 1),
    )


def place_of(x, planes):
    return planes - 2 if x == 0 else x if x == planes - 1 else x - 1


def map_rows(parts, colours, planes, ys, zs):
    match = ys
    choose = match + -(-parts * colours * colours * planes * zs // 8) * 8
    first_part = choose + 2 * parts * planes * 8
    return match, choose, first_part, first_part + 8


def write_maps(ref, parts, colours, planes, ys, zs):
    lanes = ref.shape[1] // 2
    sites = ys * zs
    depth = parts * colours * sites
    row_size = parts * colours * zs
    match, choose, first_part, _ = map_rows(parts, colours, planes, ys, zs)

    def ones(mask):
        return jnp.where(mask, 1.0, 0.0)

    def column(count):
        return lax.broadcasted_iota(jnp.int32, (count, 1), 0)

    def line(count):
        return lax.broadcasted_iota(jnp.int32, (1, count), 1)

    lane = line(lanes)
    inner = lane < depth
    past = lax.rem(jnp.maximum(lane - depth, 0), row_size)
    used = lane < depth + 2 * row_size
    part = jnp.where(inner, lax.div(lane, colours * sites), lax.div(past, colours * zs))
    colour = lax.rem(jnp.where(inner, lax.div(lane, sites), lax.div(past, zs)), colours)
    z = lax.rem(jnp.where(inner, lane, past), zs)
    y = lax.div(lax.rem(lane, sites), zs)
    ref[:ys, :lanes] = ones(column(ys) == jnp.where(inner, y, ys - 1))
    ref[:ys, lanes:] = ones(column(ys) == jnp.where(inner, y, ys) - 1)

    count = parts * colours * colours * planes * zs

    def link(index):
        x = lax.rem(lax.div(index, zs), planes)
        right = lax.rem(lax.div(index, zs * planes), colours)
        left = lax.rem(lax.div(index, zs * planes * colours), colours)
        return x, right, left, lax.div(index, zs * planes * colours * colours)

    row = column(count)
    _, right, left, _ = link(row)
    row_z = lax.rem(row, zs)
    key = jnp.where(used, colour * zs + z, -1)
    ref[match : match + count, :lanes] = ones(right * zs + row_z == key)
    ref[match : match + count, lanes:] = ones(left * zs + row_z == key)

    out = column(parts * planes * 8)
    field_part = lax.div(out, planes * 8)
    out_x = lax.rem(lax.div(out, 8), planes)
    out_part = lax.div(lax.rem(out, 8), colours)
    out_colour = lax.rem(lax.rem(out, 8), colours)
    x, right, left, source_part = link(line(count))
    source = source_part * planes + x
    wanted = jnp.where(out_part < parts, lax.rem(out_part + field_part, 2) * planes + out_x, -1)
    sign_ahead = jnp.where((field_part == 1) & (out_part == 0), -1.0, 1.0)
    sign_back = jnp.where((field_part == 0) & (out_part == 1), 1.0, -1.0)
    half = parts * planes * 8
    for start, end, sign in ((choose, left, sign_ahead), (choose + half, right, sign_back)):
        hit = source * colours + end == wanted * colours + jnp.where(wanted < 0, -1, out_colour)
        ref[start : start + half, :count] = jnp.where(hit, sign, 0.0)
    ref[first_part:, :lanes] = jnp.broadcast_to(ones(part == 0), (8, lanes))


def coefficients(links_x, links_y, maps_ref, planes):
    lanes = maps_ref.shape[1] // 2
    ys = links_x.shape[1]
    count = links_x.shape[0]
    half = 2 * planes * 8
    wide = dot(jnp.concatenate([links_x, links_y], axis=0), maps_ref[:ys].astype(jnp.bfloat16))
    match = maps_ref[ys : ys + count]
    match_ahead, match_back = match[:, :lanes], match[:, lanes:]
    choose = maps_ref[ys + count : ys + count + 2 * half, :count].astype(jnp.bfloat16)
    first_part = maps_ref[ys + count + 2 * half : ys + count + 2 * half + 1, :lanes] > 0.5
    ahead = jnp.concatenate([wide[:count, :lanes] * match_ahead, wide[count:, lanes:] * match_ahead], axis=1)
    back = jnp.concatenate([wide[:count, :lanes] * match_back, wide[count:, :lanes] * match_back], axis=1)
    out = []
    for chosen in (
        dot(choose[:half], ahead.astype(jnp.bfloat16)), dot(choose[half:], back.astype(jnp.bfloat16))
    ):
        for start in (0, lanes):
            part = chosen[:, start : start + lanes]
            rows = jnp.where(first_part, part[: half // 2], part[half // 2 :])
            out.append(rows.reshape(planes, 8, lanes))
    return out


def plane_rows(ref, ys):
    parts, _, colours, zs, width = ref.shape
    return jnp.concatenate(
        [ref[p, :ys, c].reshape(ys * zs, width) for p in range(parts) for c in range(colours)],
        axis=0,
    )


def edges_kernel(
    raw_hbm, links_x_hbm, links_y_hbm,
    first_ref, last_ref, raw_ref, links_x_ref, links_y_ref, maps_ref, past_maps_ref, arrived,
):
    parts, planes, ys, colours, zs, _ = raw_hbm.shape
    sources = (raw_hbm.at[:, planes - 1], raw_hbm.at[:, 0], links_x_hbm, links_y_hbm, raw_hbm)
    targets = (last_ref.at[:, :ys], first_ref, links_x_ref, links_y_ref, raw_ref)
    copies = [
        pltpu.make_async_copy(source, target, arrived.at[i])
        for i, (source, target) in enumerate(zip(sources, targets))
    ]
    for copy in copies:
        copy.start()
    last_ref[:, ys:] = jnp.zeros((parts, colours) + last_ref.shape[2:], last_ref.dtype)
    write_maps(maps_ref, parts, colours, planes, ys, zs)
    write_maps(past_maps_ref, parts, colours, 1, ys, zs)
    copies[2].wait()
    last_ref[:, ys:, :, :, :ys] = links_x_ref[:, :, :, planes - 1]
    for copy in copies[:2] + copies[3:]:
        copy.wait()


def site_matrix(rows_and_masks, count):
    blocks = []
    for q in range(count):
        block = None
        for rows, mask in rows_and_masks:
            term = rows[q : q + 1] * mask
            block = term if block is None else block + term
        blocks.append(block.astype(jnp.bfloat16))
    return jnp.concatenate(blocks, axis=0)


def prepare_kernel(
    raw_ref, links_x_ref, links_y_ref, maps_ref,
    rows_ref, ends_ref, ahead_x_ref, back_x_ref, ahead_y_ref, back_y_ref,
):
    planes, depth, width = rows_ref.shape
    zs = raw_ref.shape[4]
    ys = raw_ref.shape[2]
    sites = ys * zs
    row_size = depth // sites * zs
    lanes = ahead_y_ref.shape[2]
    ahead_x, ahead_y, back_x, back_y = coefficients(
        links_x_ref[...].reshape(-1, ys), links_y_ref[...].reshape(-1, ys), maps_ref, planes
    )
    ahead_x_ref[...] = ahead_x
    back_x_ref[...] = back_x
    ahead_y_ref[...] = ahead_y
    back_y_ref[...] = back_y

    row, lane = iotas((2 * row_size, depth))
    spot = row % row_size
    wanted = (spot // zs) * sites + spot % zs + jnp.where(row < row_size, 0, sites - zs)
    ends = (lane == wanted).astype(jnp.bfloat16)
    filler = jnp.zeros((8, width - 128), jnp.float32)
    spare = ends_ref.shape[1] - 2 * row_size - 8
    for x in range(planes):
        plane = plane_rows(raw_ref.at[:, x], ys)
        rows_ref[place_of(x, planes)] = plane
        tail = jnp.concatenate([back_y[x, :, lanes - 128 :], filler], axis=1)
        pieces = [dot(ends, plane), tail]
        if spare:
            pieces.append(jnp.zeros((spare, width), jnp.float32))
        ends_ref[x] = jnp.concatenate(pieces, axis=0).astype(jnp.bfloat16)


def turn_kernel(raw_ref, rows_ref, turned_ref):
    planes, depth, width = rows_ref.shape
    for x in range(planes):
        rows_ref[place_of(x, planes)] = plane_rows(raw_ref.at[:, x], raw_ref.shape[2])
    turned_ref[...] = rows_ref[...].reshape(planes * depth, width).T


def move_plane(same, count, ahead, back, above, below):
    depth = same.shape[1]
    moved = dot(site_matrix([(ahead[:, :depth], same)], count), above)
    return (moved + dot(site_matrix([(back[:, :depth], same)], count), below)).astype(jnp.bfloat16)


def same_site(sites, depth):
    site, lane = iotas((sites, depth))
    return (lane % sites == site).astype(jnp.float32)


def set_right(right_ref, place, moved):
    depth, width = moved.shape
    half = depth // 2
    start = place * depth
    real, imag = moved[:half], moved[half:]
    right_ref[start : start + half, :width] = real
    right_ref[start : start + half, width:] = imag
    right_ref[start + half : start + depth, :width] = imag
    right_ref[start + half : start + depth, width:] = -real


def inner_kernel(
    sites, rows_ref, ahead_ref, back_ref, right_ref, turned_ref, matrix_ref, ahead_part_ref, back_part_ref
):
    planes, depth, width = rows_ref.shape
    same = same_site(sites, depth)
    for x in range(1, planes - 1):
        above = rows_ref[place_of(x + 1, planes)]
        below = rows_ref[place_of(x - 1, planes)]
        moved = move_plane(same, depth // sites, ahead_ref[x], back_ref[x - 1], above, below)
        set_right(right_ref, place_of(x, planes), moved)
    turned_ref[...] = rows_ref[...].reshape(planes * depth, width).T
    x, count = planes - 1, depth // sites
    matrix_ref[...] = site_matrix([(ahead_ref[x, :, :depth], same)], count)
    ahead_part_ref[...] = dot(site_matrix([(ahead_ref[0, :, :depth], same)], count), rows_ref[place_of(1, planes)])
    below = rows_ref[place_of(x - 1, planes)]
    back_part_ref[...] = dot(site_matrix([(back_ref[x - 1, :, :depth], same)], count), below)


def begin_first_kernel(own_ref, others_ref, right_ref, total_ref):
    inner = right_ref.shape[0]
    right = right_ref[...]
    total_ref[0] = dot(own_ref[:, :inner], right)
    for k in range(others_ref.shape[0]):
        total_ref[k + 1] = dot(others_ref[k, :, :inner], right)


def bits(axis):
    return range(lax.axis_size(axis).bit_length() - 1)


def steps():
    one = [("gx", bit) for bit in bits("gx")[:-1]]
    two = [("gy", bit) for bit in bits("gy")]
    both = min(len(one), len(two))
    pairs = [pair for ends in zip(one, two) for pair in (ends, ends[::-1])]
    return pairs + [(step, step) for step in one[both:] + two[both:]]


def my_bit(axis, bit):
    return lax.bitwise_and(lax.shift_right_logical(lax.axis_index(axis), bit), 1)


def my_side(step):
    even, odd = (my_bit(*way) for way in step)
    return jnp.where(my_bit("ma", 0) == 0, even, odd)


def half_of(kind):
    half = lax.bitwise_xor(my_bit("gx", bits("gx")[-1]), 1 - kind)
    return lax.bitwise_xor(half, lax.axis_index("ma"))


def share(total, keep_ref, send_ref, total_ref):
    blocks, rows, double = total_ref.shape
    parts, count, _, width = keep_ref.shape
    total_ref[...] = total.reshape(blocks, rows, double)
    odd_core = my_bit("ma", 0)
    across_y = lax.axis_size("gy")
    plan = steps()
    mine = my_side(plan[0])

    def at(side, index):
        owners = []
        for core in range(2):
            place = {"gx": 0, "gy": 0}
            for k, step in enumerate(plan):
                axis, bit = step[core]
                digit = side if k == 0 else index >> (len(plan) - 1 - k) & 1
                place[axis] += digit * (1 << bit)
            owners.append(place["gx"] * across_y + place["gy"])
        return jnp.where(odd_core == 0, owners[0], owners[1])

    for index in range(count):
        for ref, side in ((keep_ref, mine), (send_ref, 1 - mine)):
            block = total_ref[at(side, index)].astype(ref.dtype)
            for p in range(parts):
                ref[p, index] = block[:, p * width : (p + 1) * width]


def first_share(kind, own_ref, others_ref, begun_ref, right, keep_ref, send_ref, total_ref):
    half = half_of(kind)
    inner = own_ref.shape[1] - right.shape[0]
    left = jnp.where(half == 0, own_ref[:, inner:], others_ref[0, :, inner:])
    share(begun_ref[half] + dot(left, right), keep_ref, send_ref, total_ref)


def first_kernel(
    sites, high_ref, low_ref, matrix_ref, ahead_part_ref, back_part_ref, past_maps_ref, own_ref, others_ref, begun_ref,
    *refs,
):
    keep_ref, send_ref, right_ref, total_ref = refs
    depth = matrix_ref.shape[0]
    same = same_site(sites, depth)
    _, ys, colours, zs, _ = high_ref.shape
    links = low_ref[:, ys:, :, :, :ys].reshape(-1, ys)
    lanes = past_maps_ref.shape[1] // 2
    count = links.shape[0]
    spread = past_maps_ref[:ys, :lanes].astype(jnp.bfloat16)
    match = past_maps_ref[ys : ys + count, lanes:]
    start = past_maps_ref.shape[0] - 24
    choose = past_maps_ref[start : start + 16, :count].astype(jnp.bfloat16)
    past = dot(choose, (dot(links, spread) * match).astype(jnp.bfloat16))
    past = jnp.where(past_maps_ref[start + 16 : start + 17, :lanes] > 0.5, past[:8], past[8:])
    past = site_matrix([(past[:, :depth], same)], depth // sites)
    moved = ahead_part_ref[...] + dot(past, plane_rows(low_ref, ys))
    set_right(right_ref, 0, moved.astype(jnp.bfloat16))
    moved = dot(matrix_ref[...], plane_rows(high_ref, ys)) + back_part_ref[...]
    set_right(right_ref, 1, moved.astype(jnp.bfloat16))
    first_share(0, own_ref, others_ref, begun_ref, right_ref[...], keep_ref, send_ref, total_ref)


def first_own_kernel(own_ref, others_ref, begun_ref, right_ref, keep_ref, send_ref, total_ref):
    first_share(1, own_ref, others_ref, begun_ref, right_ref[...], keep_ref, send_ref, total_ref)


def begin_y_kernel(sites, zs, rows_ref, others_ref, ahead_ref, back_ref, part_ref):
    planes, depth, _ = rows_ref.shape
    site, lane = iotas((sites, depth))
    to_next = jnp.where(lane % sites == site + zs, -1.0, 0.0)
    to_last = jnp.where(lane % sites == site - zs, -1.0, 0.0)
    for x in range(planes):
        ahead, back = ahead_ref[x, :, :depth], back_ref[x, :, :depth]
        matrix = site_matrix([(ahead, to_next), (back, to_last)], depth // sites)
        place = place_of(x, planes)
        part_ref[0, place] = dot(matrix, rows_ref[place])
        for k in range(others_ref.shape[0]):
            part_ref[k + 1, place] = dot(matrix, others_ref[k, place])


def move_y(kind, sites, zs, part_ref, near_ref, far_ref, ahead_ref, turned_ref, field_ref):
    _, planes, depth, width = part_ref.shape
    half = half_of(kind)
    row_size = depth // sites * zs
    tail = 128
    head = ahead_ref.shape[2] - tail
    site, lane = iotas((sites, tail))
    lane = lane + head
    upper = (lane >= depth) & (lane < depth + row_size)
    lower = (lane >= depth + row_size) & (lane < depth + 2 * row_size)
    to_next = jnp.where(upper & (site == sites - zs + lane % zs), -1.0, 0.0)
    to_last = jnp.where(lower & (site == lane % zs), -1.0, 0.0)
    above = jnp.zeros((depth - head, width), jnp.bfloat16)
    below = jnp.zeros((tail - 2 * row_size - (depth - head), width), jnp.bfloat16)
    for x in range(planes):
        past = near_ref[x, 2 * row_size : 2 * row_size + 8, :tail].astype(jnp.float32)
        matrix = site_matrix([(ahead_ref[x, :, head:], to_next), (past, to_last)], depth // sites)
        place = place_of(x, planes)
        edge = jnp.where(half == 0, near_ref[x, : 2 * row_size], far_ref[0, x])
        moved = part_ref[half, place] + dot(matrix, jnp.concatenate([above, edge, below], axis=0))
        field_ref[place] = moved.astype(jnp.bfloat16)
    turned_ref[...] = field_ref[...].reshape(planes * depth, width).T


def second_share(left_ref, right_ref, edge_ref, keep_ref, send_ref, total_ref):
    inner = right_ref.shape[0]
    total = dot(left_ref[:, :inner], right_ref[...]) + dot(left_ref[:, inner:], edge_ref[...])
    share(total, keep_ref, send_ref, total_ref)


def second_own_kernel(left_ref, right_ref, edge_ref, first_ref, keep_ref, send_ref, total_ref):
    parts = first_ref.shape[0]
    send_ref[:parts] = first_ref[...]
    second_share(left_ref, right_ref, edge_ref, keep_ref, send_ref.at[parts:], total_ref)


def exchange(block, step):
    axes = ("gx", "gy", "ma")
    sizes = [lax.axis_size(axis) for axis in axes]
    route = []
    for source in range(sizes[0] * sizes[1] * sizes[2]):
        where = [source // (sizes[1] * sizes[2]), source // sizes[2] % sizes[1], source % sizes[2]]
        axis, bit = step[where[2] % 2]
        where[axes.index(axis)] ^= 1 << bit
        route.append((source, (where[0] * sizes[1] + where[1]) * sizes[2] + where[2]))
    return lax.ppermute(block, axes, route)


def halve(sums, step, weight=0):
    parts = sum(kept.shape[0] for kept, _, _ in sums)
    count, rows, width = sums[0][0].shape[1:]
    dims = (parts, count // 2, rows, width)

    def merge(*refs):
        *refs, keep_ref, send_ref = refs
        mine = my_side(step)
        start = 0
        for k, (_, _, which) in enumerate(sums):
            kept_ref, came_ref = refs[2 * k : 2 * k + 2]
            came_ref = came_ref if which is None else came_ref.at[which]
            end = start + kept_ref.shape[0]
            for index in range(count // 2):
                low, high = (
                    kept_ref[:, at] + came_ref[:, at].astype(jnp.float32) for at in (index, index + count // 2)
                )
                keep_ref[start:end, index] = jnp.where(mine == 0, low, high)
                send_ref[start:end, index] = jnp.where(mine == 0, high, low).astype(send_ref.dtype)
            start = end

    operands = [a for kept, came, _ in sums for a in (kept, came)]
    keep, send = call(merge, (pltpu.VMEM(dims, jnp.float32), pltpu.VMEM(dims, jnp.bfloat16)), weight, operands)
    return keep, exchange(send, step)


def sum_kernel(kept_ref, came_ref, send_ref):
    send_ref[...] = (kept_ref[...] + came_ref[...].astype(jnp.float32)).astype(send_ref.dtype)


def cross_kernel(start, kept_ref, crossed_ref, out_ref):
    kept = kept_ref[start : start + out_ref.shape[0]]
    out_ref[...] = kept + crossed_ref[...].astype(jnp.float32)


def finish_kernel(came_ref, *refs):
    *kept_refs, out_ref = refs
    parts = out_ref.shape[1]
    for d, kept_ref in enumerate(kept_refs):
        out_ref[d] = kept_ref[:, 0] + came_ref[d * parts : (d + 1) * parts, 0].astype(jnp.float32)


def local(eigen_modes, links_first, links_second):
    f32, bf16 = jnp.float32, jnp.bfloat16
    parts, planes, ys, zs, colours, width = eigen_modes.shape
    sites = ys * zs
    depth = parts * colours * sites
    row_size = parts * colours * zs
    edge = -(-(2 * row_size + 8) // 16) * 16
    lanes = -(-(depth + 2 * row_size) // 128) * 128
    across_x, across_y, groups = (lax.axis_size(a) for a in ("gx", "gy", "ma"))
    rows = groups * width // (across_x * across_y)
    inner_depth = (planes - 2) * depth
    raw = eigen_modes.transpose(0, 1, 2, 4, 3, 5)

    def shape(*dims, dtype=bf16):
        return pltpu.VMEM(dims, dtype)

    field_shape = shape(planes, depth, width)
    turned_shape = shape(width, planes * depth)
    total_shape = shape(groups, width, parts * width, dtype=f32)
    link_shape = shape(planes, 8, lanes, dtype=f32)
    total = pltpu.VMEM((width // rows, rows, parts * width), f32)
    step_flops = 2 * planes * depth * depth * width
    project_flops = 2 * groups * width * planes * depth * parts * width

    raw_others = [shifted(raw, "ma", -step) for step in range(1, groups)]
    raw_links_x, raw_links_y = (a.transpose(0, 1, 2, 3, 5, 4) for a in (links_first, links_second))
    inputs = [raw, raw_links_x, raw_links_y]
    first_plane, last_plane, *inputs, past_maps = call(
        edges_kernel,
        (
            shape(parts, ys, colours, zs, width), shape(parts, ys + colours, colours, zs, width),
            *(shape(*a.shape) for a in inputs),
            shape(map_rows(parts, colours, planes, ys, zs)[-1], 2 * lanes, dtype=f32),
            shape(map_rows(parts, colours, 1, ys, zs)[-1], 2 * lanes, dtype=f32),
        ),
        0,
        inputs,
        [pltpu.SemaphoreType.DMA((5,))],
        [pltpu.HBM] * len(inputs),
    )
    low = shifted(last_plane, "gx", 1)
    high = shifted(first_plane, "gx", -1)
    field, ends, ahead_x, back_x, ahead_y, back_y = call(
        prepare_kernel,
        (field_shape, shape(planes, edge, width), link_shape, link_shape, link_shape, link_shape),
        0,
        inputs,
    )
    near = shifted(ends, "gy", 1)
    if across_y != 2:
        ahead_row = lax.broadcasted_iota(jnp.int32, ends.shape, 1) < row_size
        near = jnp.where(ahead_row, shifted(ends, "gy", -1), near)

    plan = steps()
    top = ("gx", bits("gx")[-1])
    pieces = across_x * across_y // 4
    kept_shape = shape(parts, pieces, rows, width, dtype=f32)
    sent_shape = shape(parts, pieces, rows, width)

    def inner(*refs):
        inner_kernel(sites, *refs)

    def first(*refs):
        first_kernel(sites, *refs)

    def begin_y(*refs):
        begin_y_kernel(sites, zs, *refs)

    def move_cross(*refs):
        move_y(0, sites, zs, *refs)

    def move_own(*refs):
        move_y(1, sites, zs, *refs)

    right, own, matrix, ahead_part, back_part = call(
        inner,
        (
            shape(inner_depth, parts * width), turned_shape, shape(depth, depth),
            shape(depth, width, dtype=f32), shape(depth, width, dtype=f32),
        ),
        2 * step_flops,
        [field, ahead_x, back_x],
    )
    turned = [call(turn_kernel, (field_shape, turned_shape), step_flops // 4, [r]) for r in raw_others]
    fields = jnp.stack([t[0] for t in turned])
    others = jnp.stack([t[1] for t in turned])
    begun_first = call(begin_first_kernel, total_shape, project_flops, [own, others, right])
    part_y = call(
        begin_y, shape(groups, planes, depth, width, dtype=f32), 2 * step_flops, [field, fields, ahead_y, back_y]
    )
    part_y, begun_first = lax.optimization_barrier((part_y, begun_first))
    kept_first, sent_first, right_edge = call(
        first,
        (kept_shape, sent_shape, shape(2 * depth, parts * width)),
        project_flops,
        [high, low, matrix, ahead_part, back_part, past_maps, own, others, begun_first],
        [total],
    )
    came_first = exchange(sent_first, plan[0])
    near, right_edge = lax.optimization_barrier((near, right_edge))
    near_rows = near[:, : 2 * row_size]
    far = jnp.stack([shifted(near_rows, "ma", -step) for step in range(1, groups)])
    move_operands = [part_y, near, far, ahead_y]
    move_scratch = [pltpu.VMEM(field_shape.shape, bf16)]
    left = call(move_cross, turned_shape, step_flops, move_operands, move_scratch)
    kept_second, sent_second = call(
        second_share, (kept_shape, sent_shape), 8 * project_flops, [left, right, right_edge], [total]
    )
    came_second = exchange(sent_second, plan[0])
    right_edge, part_y, kept_second = lax.optimization_barrier((right_edge, part_y, kept_second))
    left = call(move_own, turned_shape, 0, [part_y] + move_operands[1:], move_scratch)
    own_first, sent_own = call(
        first_own_kernel, (kept_shape, sent_shape), 0, [own, others, begun_first, right_edge], [total]
    )
    own_second, sent_own = call(
        second_own_kernel, (kept_shape, shape(2 * parts, pieces, rows, width)), 0,
        [left, right, right_edge, sent_own], [total],
    )
    crossing = [(kept_first, came_first), (kept_second, came_second)]
    after = own_second
    staying = None
    for step in plan[1:]:
        for d, (kept, came) in enumerate(crossing):
            came, after = lax.optimization_barrier((came, after))
            crossing[d] = halve([(kept, came, None)], step)
            after = crossing[d][0]
            if staying is None:
                sent_own, after = lax.optimization_barrier((sent_own, after))
                came_own = exchange(sent_own, plan[0])
                staying = [
                    (own_first, came_own, slice(0, parts)), (own_second, came_own, slice(parts, 2 * parts))
                ]
    crossed = []
    for kept, came in crossing:
        came, after = lax.optimization_barrier((came, after))
        after = call(sum_kernel, pltpu.VMEM(kept.shape, bf16), 8 * project_flops, [kept, came])
        crossed.append(exchange(after, (top, top)))
    for step in plan[1:]:
        kept, came, which = staying[0]
        came, after = lax.optimization_barrier((came, after))
        sums = [(kept, came, which)] + [(k, came, w) for k, _, w in staying[1:]]
        kept, came = halve(sums, step)
        staying, after = [(kept, came, None)], kept
    kept, came, _ = staying[0]
    totals = []
    for d, block in enumerate(crossed):

        def cross(*refs, start=d * parts):
            cross_kernel(start, *refs)

        block, after = lax.optimization_barrier((block, after))
        after = call(cross, shape(*block.shape, dtype=f32), 4 * project_flops, [kept, block])
        totals.append(after)
    came, after = lax.optimization_barrier((came, after))
    return call(
        finish_kernel, jax.ShapeDtypeStruct((2, parts, rows, width), f32), 0, [came, *totals]
    )


def solution(mesh):
    return jax.shard_map(
        local,
        mesh=mesh,
        in_specs=(
            P("cuts", "gx", "gy", None, None, "ma"),
            P("cuts", None, None, "gx", "gy", None),
            P("cuts", None, None, "gx", "gy", None),
        ),
        out_specs=P("cuts", None, ("gx", "gy"), "ma"),
        check_vma=False,
    )
```

```python
import jax
import jax.numpy as jnp
from jax import lax
from jax.experimental import pallas as pl
from jax.experimental.pallas import tpu as pltpu
from jax.sharding import PartitionSpec as P

VMEM_LIMIT = 16 * 1024 * 1024


def shifted(block, axis, distance):
    devices = range(lax.axis_size(axis))
    route = [((i - distance) % len(devices), i) for i in devices]
    return lax.ppermute(block, axis, route)


def call(body, out_shape, flops, operands, scratch=(), places=None):
    places = places or [pltpu.VMEM] * len(operands)
    return pl.pallas_call(
        body,
        out_shape=out_shape,
        in_specs=[pl.BlockSpec(memory_space=place) for place in places],
        scratch_shapes=scratch,
        cost_estimate=pl.CostEstimate(flops=flops // 2, bytes_accessed=0, transcendentals=0),
        compiler_params=pltpu.CompilerParams(vmem_limit_bytes=VMEM_LIMIT),
    )(*(pltpu.with_memory_space_constraint(a, place) for a, place in zip(operands, places)))


def dot(a, b):
    return jnp.dot(a, b, preferred_element_type=jnp.float32)


def iotas(shape):
    return (
        lax.broadcasted_iota(jnp.int32, shape, 0),
        lax.broadcasted_iota(jnp.int32, shape, 1),
    )


def place_of(x, planes):
    return planes - 2 if x == 0 else x if x == planes - 1 else x - 1


def map_rows(parts, colours, planes, ys, zs):
    match = ys
    choose = match + -(-parts * colours * colours * planes * zs // 8) * 8
    first_part = choose + 2 * parts * planes * 8
    return match, choose, first_part, first_part + 8


def write_maps(ref, parts, colours, planes, ys, zs):
    lanes = ref.shape[1] // 2
    sites = ys * zs
    depth = parts * colours * sites
    row_size = parts * colours * zs
    match, choose, first_part, _ = map_rows(parts, colours, planes, ys, zs)

    def ones(mask):
        return jnp.where(mask, 1.0, 0.0)

    def column(count):
        return lax.broadcasted_iota(jnp.int32, (count, 1), 0)

    def line(count):
        return lax.broadcasted_iota(jnp.int32, (1, count), 1)

    lane = line(lanes)
    inner = lane < depth
    past = lax.rem(jnp.maximum(lane - depth, 0), row_size)
    used = lane < depth + 2 * row_size
    part = jnp.where(inner, lax.div(lane, colours * sites), lax.div(past, colours * zs))
    colour = lax.rem(jnp.where(inner, lax.div(lane, sites), lax.div(past, zs)), colours)
    z = lax.rem(jnp.where(inner, lane, past), zs)
    y = lax.div(lax.rem(lane, sites), zs)
    ref[:ys, :lanes] = ones(column(ys) == jnp.where(inner, y, ys - 1))
    ref[:ys, lanes:] = ones(column(ys) == jnp.where(inner, y, ys) - 1)

    count = parts * colours * colours * planes * zs

    def link(index):
        x = lax.rem(lax.div(index, zs), planes)
        right = lax.rem(lax.div(index, zs * planes), colours)
        left = lax.rem(lax.div(index, zs * planes * colours), colours)
        return x, right, left, lax.div(index, zs * planes * colours * colours)

    row = column(count)
    _, right, left, _ = link(row)
    row_z = lax.rem(row, zs)
    key = jnp.where(used, colour * zs + z, -1)
    ref[match : match + count, :lanes] = ones(right * zs + row_z == key)
    ref[match : match + count, lanes:] = ones(left * zs + row_z == key)

    out = column(parts * planes * 8)
    field_part = lax.div(out, planes * 8)
    out_x = lax.rem(lax.div(out, 8), planes)
    out_part = lax.div(lax.rem(out, 8), colours)
    out_colour = lax.rem(lax.rem(out, 8), colours)
    x, right, left, source_part = link(line(count))
    source = source_part * planes + x
    wanted = jnp.where(out_part < parts, lax.rem(out_part + field_part, 2) * planes + out_x, -1)
    sign_ahead = jnp.where((field_part == 1) & (out_part == 0), -1.0, 1.0)
    sign_back = jnp.where((field_part == 0) & (out_part == 1), 1.0, -1.0)
    half = parts * planes * 8
    for start, end, sign in ((choose, left, sign_ahead), (choose + half, right, sign_back)):
        hit = source * colours + end == wanted * colours + jnp.where(wanted < 0, -1, out_colour)
        ref[start : start + half, :count] = jnp.where(hit, sign, 0.0)
    ref[first_part:, :lanes] = jnp.broadcast_to(ones(part == 0), (8, lanes))


def coefficients(links_x, links_y, maps_ref, planes):
    lanes = maps_ref.shape[1] // 2
    ys = links_x.shape[1]
    count = links_x.shape[0]
    half = 2 * planes * 8
    wide = dot(jnp.concatenate([links_x, links_y], axis=0), maps_ref[:ys].astype(jnp.bfloat16))
    match = maps_ref[ys : ys + count]
    match_ahead, match_back = match[:, :lanes], match[:, lanes:]
    choose = maps_ref[ys + count : ys + count + 2 * half, :count].astype(jnp.bfloat16)
    first_part = maps_ref[ys + count + 2 * half : ys + count + 2 * half + 1, :lanes] > 0.5
    ahead = jnp.concatenate([wide[:count, :lanes] * match_ahead, wide[count:, lanes:] * match_ahead], axis=1)
    back = jnp.concatenate([wide[:count, :lanes] * match_back, wide[count:, :lanes] * match_back], axis=1)
    out = []
    for chosen in (
        dot(choose[:half], ahead.astype(jnp.bfloat16)), dot(choose[half:], back.astype(jnp.bfloat16))
    ):
        for start in (0, lanes):
            part = chosen[:, start : start + lanes]
            rows = jnp.where(first_part, part[: half // 2], part[half // 2 :])
            out.append(rows.reshape(planes, 8, lanes))
    return out


def plane_rows(ref, ys):
    parts, _, colours, zs, width = ref.shape
    return jnp.concatenate(
        [ref[p, :ys, c].reshape(ys * zs, width) for p in range(parts) for c in range(colours)],
        axis=0,
    )


def edges_kernel(
    raw_hbm, links_x_hbm, links_y_hbm,
    first_ref, last_ref, links_x_ref, links_y_ref, maps_ref, past_maps_ref, arrived,
):
    parts, planes, ys, colours, zs, _ = raw_hbm.shape
    sources = (raw_hbm.at[:, planes - 1], raw_hbm.at[:, 0], links_x_hbm, links_y_hbm)
    targets = (last_ref.at[:, :ys], first_ref, links_x_ref, links_y_ref)
    copies = [
        pltpu.make_async_copy(source, target, arrived.at[i])
        for i, (source, target) in enumerate(zip(sources, targets))
    ]
    for copy in copies:
        copy.start()
    last_ref[:, ys:] = jnp.zeros((parts, colours) + last_ref.shape[2:], last_ref.dtype)
    write_maps(maps_ref, parts, colours, planes, ys, zs)
    write_maps(past_maps_ref, parts, colours, 1, ys, zs)
    copies[2].wait()
    last_ref[:, ys:, :, :, :ys] = links_x_ref[:, :, :, planes - 1]
    for copy in copies[:2] + copies[3:]:
        copy.wait()


def site_matrix(rows_and_masks, count):
    blocks = []
    for q in range(count):
        block = None
        for rows, mask in rows_and_masks:
            term = rows[q : q + 1] * mask
            block = term if block is None else block + term
        blocks.append(block.astype(jnp.bfloat16))
    return jnp.concatenate(blocks, axis=0)


def prepare_kernel(
    raw_hbm, links_x_ref, links_y_ref, maps_ref,
    rows_ref, ends_ref, ahead_x_ref, back_x_ref, ahead_y_ref, back_y_ref, raw_ref, arrived,
):
    copy = pltpu.make_async_copy(raw_hbm, raw_ref, arrived)
    copy.start()
    planes, depth, width = rows_ref.shape
    zs = raw_ref.shape[4]
    ys = raw_ref.shape[2]
    sites = ys * zs
    row_size = depth // sites * zs
    lanes = ahead_y_ref.shape[2]
    ahead_x, ahead_y, back_x, back_y = coefficients(
        links_x_ref[...].reshape(-1, ys), links_y_ref[...].reshape(-1, ys), maps_ref, planes
    )
    ahead_x_ref[...] = ahead_x
    back_x_ref[...] = back_x
    ahead_y_ref[...] = ahead_y
    back_y_ref[...] = back_y

    row, lane = iotas((2 * row_size, depth))
    spot = row % row_size
    wanted = (spot // zs) * sites + spot % zs + jnp.where(row < row_size, 0, sites - zs)
    ends = (lane == wanted).astype(jnp.bfloat16)
    filler = jnp.zeros((8, width - 128), jnp.float32)
    spare = ends_ref.shape[1] - 2 * row_size - 8
    copy.wait()
    for x in range(planes):
        plane = plane_rows(raw_ref.at[:, x], ys)
        rows_ref[place_of(x, planes)] = plane
        tail = jnp.concatenate([back_y[x, :, lanes - 128 :], filler], axis=1)
        pieces = [dot(ends, plane), tail]
        if spare:
            pieces.append(jnp.zeros((spare, width), jnp.float32))
        ends_ref[x] = jnp.concatenate(pieces, axis=0).astype(jnp.bfloat16)


def turn_kernel(raw_ref, rows_ref, turned_ref):
    planes, depth, width = rows_ref.shape
    for x in range(planes):
        rows_ref[place_of(x, planes)] = plane_rows(raw_ref.at[:, x], raw_ref.shape[2])
    turned_ref[...] = rows_ref[...].reshape(planes * depth, width).T


def move_plane(same, count, ahead, back, above, below):
    depth = same.shape[1]
    moved = dot(site_matrix([(ahead[:, :depth], same)], count), above)
    return (moved + dot(site_matrix([(back[:, :depth], same)], count), below)).astype(jnp.bfloat16)


def same_site(sites, depth):
    site, lane = iotas((sites, depth))
    return (lane % sites == site).astype(jnp.float32)


def set_right(right_ref, place, moved):
    depth, width = moved.shape
    half = depth // 2
    start = place * depth
    real, imag = moved[:half], moved[half:]
    right_ref[start : start + half, :width] = real
    right_ref[start : start + half, width:] = imag
    right_ref[start + half : start + depth, :width] = imag
    right_ref[start + half : start + depth, width:] = -real


def inner_kernel(
    sites, rows_ref, ahead_ref, back_ref, right_ref, turned_ref, matrix_ref, ahead_part_ref, back_part_ref
):
    planes, depth, width = rows_ref.shape
    same = same_site(sites, depth)
    for x in range(1, planes - 1):
        above = rows_ref[place_of(x + 1, planes)]
        below = rows_ref[place_of(x - 1, planes)]
        moved = move_plane(same, depth // sites, ahead_ref[x], back_ref[x - 1], above, below)
        set_right(right_ref, place_of(x, planes), moved)
    turned_ref[...] = rows_ref[...].reshape(planes * depth, width).T
    x, count = planes - 1, depth // sites
    matrix_ref[...] = site_matrix([(ahead_ref[x, :, :depth], same)], count)
    ahead_part_ref[...] = dot(site_matrix([(ahead_ref[0, :, :depth], same)], count), rows_ref[place_of(1, planes)])
    below = rows_ref[place_of(x - 1, planes)]
    back_part_ref[...] = dot(site_matrix([(back_ref[x - 1, :, :depth], same)], count), below)


def begin_first_kernel(own_ref, others_ref, right_ref, total_ref):
    inner = right_ref.shape[0]
    right = right_ref[...]
    total_ref[0] = dot(own_ref[:, :inner], right)
    for k in range(others_ref.shape[0]):
        total_ref[k + 1] = dot(others_ref[k, :, :inner], right)


def bits(axis):
    return range(lax.axis_size(axis).bit_length() - 1)


def steps():
    one = [("gx", bit) for bit in bits("gx")[:-1]]
    two = [("gy", bit) for bit in bits("gy")]
    both = min(len(one), len(two))
    pairs = [pair for ends in zip(one, two) for pair in (ends, ends[::-1])]
    return pairs + [(step, step) for step in one[both:] + two[both:]]


def my_bit(axis, bit):
    return lax.bitwise_and(lax.shift_right_logical(lax.axis_index(axis), bit), 1)


def my_side(step):
    even, odd = (my_bit(*way) for way in step)
    return jnp.where(my_bit("ma", 0) == 0, even, odd)


def half_of(kind):
    half = lax.bitwise_xor(my_bit("gx", bits("gx")[-1]), 1 - kind)
    return lax.bitwise_xor(half, lax.axis_index("ma"))


def share(total, keep_ref, send_ref, total_ref):
    blocks, rows, double = total_ref.shape
    parts, count, _, width = keep_ref.shape
    total_ref[...] = total.reshape(blocks, rows, double)
    odd_core = my_bit("ma", 0)
    across_y = lax.axis_size("gy")
    plan = steps()
    mine = my_side(plan[0])

    def at(side, index):
        owners = []
        for core in range(2):
            place = {"gx": 0, "gy": 0}
            for k, step in enumerate(plan):
                axis, bit = step[core]
                digit = side if k == 0 else index >> (len(plan) - 1 - k) & 1
                place[axis] += digit * (1 << bit)
            owners.append(place["gx"] * across_y + place["gy"])
        return jnp.where(odd_core == 0, owners[0], owners[1])

    for index in range(count):
        for ref, side in ((keep_ref, mine), (send_ref, 1 - mine)):
            block = total_ref[at(side, index)].astype(ref.dtype)
            for p in range(parts):
                ref[p, index] = block[:, p * width : (p + 1) * width]


def first_share(kind, own_ref, others_ref, begun_ref, right, keep_ref, send_ref, total_ref):
    half = half_of(kind)
    inner = own_ref.shape[1] - right.shape[0]
    left = jnp.where(half == 0, own_ref[:, inner:], others_ref[0, :, inner:])
    share(begun_ref[half] + dot(left, right), keep_ref, send_ref, total_ref)


def first_kernel(
    sites, high_ref, low_ref, matrix_ref, ahead_part_ref, back_part_ref, past_maps_ref, own_ref, others_ref, begun_ref,
    *refs,
):
    keep_ref, send_ref, right_ref, total_ref = refs
    depth = matrix_ref.shape[0]
    same = same_site(sites, depth)
    _, ys, colours, zs, _ = high_ref.shape
    links = low_ref[:, ys:, :, :, :ys].reshape(-1, ys)
    lanes = past_maps_ref.shape[1] // 2
    count = links.shape[0]
    spread = past_maps_ref[:ys, :lanes].astype(jnp.bfloat16)
    match = past_maps_ref[ys : ys + count, lanes:]
    start = past_maps_ref.shape[0] - 24
    choose = past_maps_ref[start : start + 16, :count].astype(jnp.bfloat16)
    past = dot(choose, (dot(links, spread) * match).astype(jnp.bfloat16))
    past = jnp.where(past_maps_ref[start + 16 : start + 17, :lanes] > 0.5, past[:8], past[8:])
    past = site_matrix([(past[:, :depth], same)], depth // sites)
    moved = ahead_part_ref[...] + dot(past, plane_rows(low_ref, ys))
    set_right(right_ref, 0, moved.astype(jnp.bfloat16))
    moved = dot(matrix_ref[...], plane_rows(high_ref, ys)) + back_part_ref[...]
    set_right(right_ref, 1, moved.astype(jnp.bfloat16))
    first_share(0, own_ref, others_ref, begun_ref, right_ref[...], keep_ref, send_ref, total_ref)


def first_own_kernel(own_ref, others_ref, begun_ref, right_ref, keep_ref, send_ref, total_ref):
    first_share(1, own_ref, others_ref, begun_ref, right_ref[...], keep_ref, send_ref, total_ref)


def begin_y_kernel(sites, zs, rows_ref, others_ref, ahead_ref, back_ref, part_ref):
    planes, depth, _ = rows_ref.shape
    site, lane = iotas((sites, depth))
    to_next = jnp.where(lane % sites == site + zs, -1.0, 0.0)
    to_last = jnp.where(lane % sites == site - zs, -1.0, 0.0)
    for x in range(planes):
        ahead, back = ahead_ref[x, :, :depth], back_ref[x, :, :depth]
        matrix = site_matrix([(ahead, to_next), (back, to_last)], depth // sites)
        place = place_of(x, planes)
        part_ref[0, place] = dot(matrix, rows_ref[place])
        for k in range(others_ref.shape[0]):
            part_ref[k + 1, place] = dot(matrix, others_ref[k, place])


def move_y_kernel(sites, zs, part_ref, near_ref, far_ref, ahead_ref, turned_ref, field_ref):
    groups, planes, depth, width = part_ref.shape
    row_size = depth // sites * zs
    tail = 128
    head = ahead_ref.shape[2] - tail
    site, lane = iotas((sites, tail))
    lane = lane + head
    upper = (lane >= depth) & (lane < depth + row_size)
    lower = (lane >= depth + row_size) & (lane < depth + 2 * row_size)
    to_next = jnp.where(upper & (site == sites - zs + lane % zs), -1.0, 0.0)
    to_last = jnp.where(lower & (site == lane % zs), -1.0, 0.0)
    above = jnp.zeros((depth - head, width), jnp.bfloat16)
    below = jnp.zeros((tail - 2 * row_size - (depth - head), width), jnp.bfloat16)
    for x in range(planes):
        past = near_ref[x, 2 * row_size : 2 * row_size + 8, :tail].astype(jnp.float32)
        matrix = site_matrix([(ahead_ref[x, :, head:], to_next), (past, to_last)], depth // sites)
        place = place_of(x, planes)
        for k in range(groups):
            edge = near_ref[x, : 2 * row_size] if k == 0 else far_ref[k - 1, x]
            moved = part_ref[k, place] + dot(matrix, jnp.concatenate([above, edge, below], axis=0))
            field_ref[k, place] = moved.astype(jnp.bfloat16)
    for k in range(groups):
        turned_ref[k] = field_ref[k].reshape(planes * depth, width).T


def second_share(kind, lefts_ref, right_ref, edge_ref, keep_ref, send_ref, total_ref):
    half = half_of(kind)
    inner = right_ref.shape[0]
    total = dot(lefts_ref[half, :, :inner], right_ref[...]) + dot(lefts_ref[half, :, inner:], edge_ref[...])
    share(total, keep_ref, send_ref, total_ref)


def second_kernel(lefts_ref, right_ref, edge_ref, keep_ref, send_ref, total_ref):
    second_share(0, lefts_ref, right_ref, edge_ref, keep_ref, send_ref, total_ref)


def second_own_kernel(lefts_ref, right_ref, edge_ref, first_ref, keep_ref, send_ref, total_ref):
    parts = first_ref.shape[0]
    send_ref[:parts] = first_ref[...]
    second_share(1, lefts_ref, right_ref, edge_ref, keep_ref, send_ref.at[parts:], total_ref)


def exchange(block, step):
    axes = ("gx", "gy", "ma")
    sizes = [lax.axis_size(axis) for axis in axes]
    route = []
    for source in range(sizes[0] * sizes[1] * sizes[2]):
        where = [source // (sizes[1] * sizes[2]), source // sizes[2] % sizes[1], source % sizes[2]]
        axis, bit = step[where[2] % 2]
        where[axes.index(axis)] ^= 1 << bit
        route.append((source, (where[0] * sizes[1] + where[1]) * sizes[2] + where[2]))
    return lax.ppermute(block, axes, route)


def halve(sums, step, weight=0):
    parts = sum(kept.shape[0] for kept, _, _ in sums)
    count, rows, width = sums[0][0].shape[1:]
    dims = (parts, count // 2, rows, width)

    def merge(*refs):
        *refs, keep_ref, send_ref = refs
        mine = my_side(step)
        start = 0
        for k, (_, _, which) in enumerate(sums):
            kept_ref, came_ref = refs[2 * k : 2 * k + 2]
            came_ref = came_ref if which is None else came_ref.at[which]
            end = start + kept_ref.shape[0]
            for index in range(count // 2):
                low, high = (
                    kept_ref[:, at] + came_ref[:, at].astype(jnp.float32) for at in (index, index + count // 2)
                )
                keep_ref[start:end, index] = jnp.where(mine == 0, low, high)
                send_ref[start:end, index] = jnp.where(mine == 0, high, low).astype(send_ref.dtype)
            start = end

    operands = [a for kept, came, _ in sums for a in (kept, came)]
    keep, send = call(merge, (pltpu.VMEM(dims, jnp.float32), pltpu.VMEM(dims, jnp.bfloat16)), weight, operands)
    return keep, exchange(send, step)


def sum_kernel(kept_ref, came_ref, send_ref):
    send_ref[...] = (kept_ref[...] + came_ref[...].astype(jnp.float32)).astype(send_ref.dtype)


def cross_kernel(start, kept_ref, crossed_ref, out_ref):
    kept = kept_ref[start : start + out_ref.shape[0]]
    out_ref[...] = kept + crossed_ref[...].astype(jnp.float32)


def finish_kernel(came_ref, *refs):
    *kept_refs, out_ref = refs
    parts = out_ref.shape[1]
    for d, kept_ref in enumerate(kept_refs):
        out_ref[d] = kept_ref[:, 0] + came_ref[d * parts : (d + 1) * parts, 0].astype(jnp.float32)


def local(eigen_modes, links_first, links_second):
    f32, bf16 = jnp.float32, jnp.bfloat16
    parts, planes, ys, zs, colours, width = eigen_modes.shape
    sites = ys * zs
    depth = parts * colours * sites
    row_size = parts * colours * zs
    edge = -(-(2 * row_size + 8) // 16) * 16
    lanes = -(-(depth + 2 * row_size) // 128) * 128
    across_x, across_y, groups = (lax.axis_size(a) for a in ("gx", "gy", "ma"))
    rows = groups * width // (across_x * across_y)
    inner_depth = (planes - 2) * depth
    raw = eigen_modes.transpose(0, 1, 2, 4, 3, 5)

    def shape(*dims, dtype=bf16):
        return pltpu.VMEM(dims, dtype)

    field_shape = shape(planes, depth, width)
    turned_shape = shape(width, planes * depth)
    total_shape = shape(groups, width, parts * width, dtype=f32)
    link_shape = shape(planes, 8, lanes, dtype=f32)
    total = pltpu.VMEM((width // rows, rows, parts * width), f32)
    step_flops = 2 * planes * depth * depth * width
    project_flops = 2 * groups * width * planes * depth * parts * width

    raw_others = [shifted(raw, "ma", -step) for step in range(1, groups)]
    raw_links_x, raw_links_y = (a.transpose(0, 1, 2, 3, 5, 4) for a in (links_first, links_second))
    inputs = [raw, raw_links_x, raw_links_y]
    first_plane, last_plane, *inputs, past_maps = call(
        edges_kernel,
        (
            shape(parts, ys, colours, zs, width), shape(parts, ys + colours, colours, zs, width),
            *(shape(*a.shape) for a in inputs[1:]),
            shape(map_rows(parts, colours, planes, ys, zs)[-1], 2 * lanes, dtype=f32),
            shape(map_rows(parts, colours, 1, ys, zs)[-1], 2 * lanes, dtype=f32),
        ),
        0,
        inputs,
        [pltpu.SemaphoreType.DMA((4,))],
        [pltpu.HBM] * len(inputs),
    )
    low = shifted(last_plane, "gx", 1)
    high = shifted(first_plane, "gx", -1)
    field, ends, ahead_x, back_x, ahead_y, back_y = call(
        prepare_kernel,
        (field_shape, shape(planes, edge, width), link_shape, link_shape, link_shape, link_shape),
        0,
        [raw] + inputs,
        [pltpu.VMEM(raw.shape, bf16), pltpu.SemaphoreType.DMA],
        [pltpu.HBM] + [pltpu.VMEM] * len(inputs),
    )
    near = shifted(ends, "gy", 1)
    if across_y != 2:
        ahead_row = lax.broadcasted_iota(jnp.int32, ends.shape, 1) < row_size
        near = jnp.where(ahead_row, shifted(ends, "gy", -1), near)

    plan = steps()
    top = ("gx", bits("gx")[-1])
    pieces = across_x * across_y // 4
    kept_shape = shape(parts, pieces, rows, width, dtype=f32)
    sent_shape = shape(parts, pieces, rows, width)

    def inner(*refs):
        inner_kernel(sites, *refs)

    def first(*refs):
        first_kernel(sites, *refs)

    def begin_y(*refs):
        begin_y_kernel(sites, zs, *refs)

    def move_y(*refs):
        move_y_kernel(sites, zs, *refs)

    right, own, matrix, ahead_part, back_part = call(
        inner,
        (
            shape(inner_depth, parts * width), turned_shape, shape(depth, depth),
            shape(depth, width, dtype=f32), shape(depth, width, dtype=f32),
        ),
        2 * step_flops,
        [field, ahead_x, back_x],
    )
    turned = [call(turn_kernel, (field_shape, turned_shape), step_flops // 4, [r]) for r in raw_others]
    fields = jnp.stack([t[0] for t in turned])
    others = jnp.stack([t[1] for t in turned])
    begun_first = call(begin_first_kernel, total_shape, project_flops, [own, others, right])
    part_y = call(
        begin_y, shape(groups, planes, depth, width, dtype=f32), 2 * step_flops, [field, fields, ahead_y, back_y]
    )
    part_y, begun_first = lax.optimization_barrier((part_y, begun_first))
    kept_first, sent_first, right_edge = call(
        first,
        (kept_shape, sent_shape, shape(2 * depth, parts * width)),
        project_flops,
        [high, low, matrix, ahead_part, back_part, past_maps, own, others, begun_first],
        [total],
    )
    came_first = exchange(sent_first, plan[0])
    near, right_edge = lax.optimization_barrier((near, right_edge))
    near_rows = near[:, : 2 * row_size]
    far = jnp.stack([shifted(near_rows, "ma", -step) for step in range(1, groups)])
    lefts = call(
        move_y, shape(groups, width, planes * depth), 2 * step_flops,
        [part_y, near, far, ahead_y],
        [pltpu.VMEM((groups,) + field_shape.shape, bf16)],
    )
    kept_second, sent_second = call(
        second_kernel, (kept_shape, sent_shape), 8 * project_flops, [lefts, right, right_edge], [total]
    )
    came_second = exchange(sent_second, plan[0])
    right_edge, kept_second = lax.optimization_barrier((right_edge, kept_second))
    own_first, sent_own = call(
        first_own_kernel, (kept_shape, sent_shape), 0, [own, others, begun_first, right_edge], [total]
    )
    own_second, sent_own = call(
        second_own_kernel, (kept_shape, shape(2 * parts, pieces, rows, width)), 0,
        [lefts, right, right_edge, sent_own], [total],
    )
    came_own = exchange(sent_own, plan[0])
    staying = [(own_first, came_own, slice(0, parts)), (own_second, came_own, slice(parts, 2 * parts))]
    crossing = [(kept_first, came_first), (kept_second, came_second)]
    after = own_second
    for step in plan[1:]:
        for d, (kept, came) in enumerate(crossing):
            came, after = lax.optimization_barrier((came, after))
            crossing[d] = halve([(kept, came, None)], step, 4 * project_flops if d else 0)
            after = crossing[d][0]
    crossed = []
    for kept, came in crossing:
        came, after = lax.optimization_barrier((came, after))
        after = call(sum_kernel, pltpu.VMEM(kept.shape, bf16), 0, [kept, came])
        crossed.append(exchange(after, (top, top)))
    for step in plan[1:]:
        kept, came, which = staying[0]
        came, after = lax.optimization_barrier((came, after))
        sums = [(kept, came, which)] + [(k, came, w) for k, _, w in staying[1:]]
        kept, came = halve(sums, step)
        staying, after = [(kept, came, None)], kept
    kept, came, _ = staying[0]
    totals = []
    for d, block in enumerate(crossed):

        def cross(*refs, start=d * parts):
            cross_kernel(start, *refs)

        block, after = lax.optimization_barrier((block, after))
        after = call(cross, shape(*block.shape, dtype=f32), 4 * project_flops, [kept, block])
        totals.append(after)
    came, after = lax.optimization_barrier((came, after))
    return call(
        finish_kernel, jax.ShapeDtypeStruct((2, parts, rows, width), f32), 0, [came, *totals]
    )


def solution(mesh):
    return jax.shard_map(
        local,
        mesh=mesh,
        in_specs=(
            P("cuts", "gx", "gy", None, None, "ma"),
            P("cuts", None, None, "gx", "gy", None),
            P("cuts", None, None, "gx", "gy", None),
        ),
        out_specs=P("cuts", None, ("gx", "gy"), "ma"),
        check_vma=False,
    )
```

```python
import jax
import jax.numpy as jnp
from jax import lax
from jax.experimental import pallas as pl
from jax.experimental.pallas import tpu as pltpu
from jax.sharding import PartitionSpec as P

VMEM_LIMIT = 16 * 1024 * 1024


def shifted(block, axis, distance):
    devices = range(lax.axis_size(axis))
    route = [((i - distance) % len(devices), i) for i in devices]
    return lax.ppermute(block, axis, route)


def call(body, out_shape, flops, operands, scratch=(), places=None):
    places = places or [pltpu.VMEM] * len(operands)
    return pl.pallas_call(
        body,
        out_shape=out_shape,
        in_specs=[pl.BlockSpec(memory_space=place) for place in places],
        scratch_shapes=scratch,
        cost_estimate=pl.CostEstimate(flops=flops // 2, bytes_accessed=0, transcendentals=0),
        compiler_params=pltpu.CompilerParams(vmem_limit_bytes=VMEM_LIMIT),
    )(*(pltpu.with_memory_space_constraint(a, place) for a, place in zip(operands, places)))


def dot(a, b):
    return jnp.dot(a, b, preferred_element_type=jnp.float32)


def iotas(shape):
    return (
        lax.broadcasted_iota(jnp.int32, shape, 0),
        lax.broadcasted_iota(jnp.int32, shape, 1),
    )


def place_of(x, planes):
    return planes - 2 if x == 0 else x if x == planes - 1 else x - 1


def map_rows(parts, colours, planes, ys, zs):
    match = ys
    choose = match + -(-parts * colours * colours * planes * zs // 8) * 8
    first_part = choose + 2 * parts * planes * 8
    return match, choose, first_part, first_part + 8


def write_maps(ref, parts, colours, planes, ys, zs):
    lanes = ref.shape[1] // 2
    sites = ys * zs
    depth = parts * colours * sites
    row_size = parts * colours * zs
    match, choose, first_part, _ = map_rows(parts, colours, planes, ys, zs)

    def ones(mask):
        return jnp.where(mask, 1.0, 0.0)

    def column(count):
        return lax.broadcasted_iota(jnp.int32, (count, 1), 0)

    def line(count):
        return lax.broadcasted_iota(jnp.int32, (1, count), 1)

    lane = line(lanes)
    inner = lane < depth
    past = lax.rem(jnp.maximum(lane - depth, 0), row_size)
    used = lane < depth + 2 * row_size
    part = jnp.where(inner, lax.div(lane, colours * sites), lax.div(past, colours * zs))
    colour = lax.rem(jnp.where(inner, lax.div(lane, sites), lax.div(past, zs)), colours)
    z = lax.rem(jnp.where(inner, lane, past), zs)
    y = lax.div(lax.rem(lane, sites), zs)
    ref[:ys, :lanes] = ones(column(ys) == jnp.where(inner, y, ys - 1))
    ref[:ys, lanes:] = ones(column(ys) == jnp.where(inner, y, ys) - 1)

    count = parts * colours * colours * planes * zs

    def link(index):
        x = lax.rem(lax.div(index, zs), planes)
        right = lax.rem(lax.div(index, zs * planes), colours)
        left = lax.rem(lax.div(index, zs * planes * colours), colours)
        return x, right, left, lax.div(index, zs * planes * colours * colours)

    row = column(count)
    _, right, left, _ = link(row)
    row_z = lax.rem(row, zs)
    key = jnp.where(used, colour * zs + z, -1)
    ref[match : match + count, :lanes] = ones(right * zs + row_z == key)
    ref[match : match + count, lanes:] = ones(left * zs + row_z == key)

    out = column(parts * planes * 8)
    field_part = lax.div(out, planes * 8)
    out_x = lax.rem(lax.div(out, 8), planes)
    out_part = lax.div(lax.rem(out, 8), colours)
    out_colour = lax.rem(lax.rem(out, 8), colours)
    x, right, left, source_part = link(line(count))
    source = source_part * planes + x
    wanted = jnp.where(out_part < parts, lax.rem(out_part + field_part, 2) * planes + out_x, -1)
    sign_ahead = jnp.where((field_part == 1) & (out_part == 0), -1.0, 1.0)
    sign_back = jnp.where((field_part == 0) & (out_part == 1), 1.0, -1.0)
    half = parts * planes * 8
    for start, end, sign in ((choose, left, sign_ahead), (choose + half, right, sign_back)):
        hit = source * colours + end == wanted * colours + jnp.where(wanted < 0, -1, out_colour)
        ref[start : start + half, :count] = jnp.where(hit, sign, 0.0)
    ref[first_part:, :lanes] = jnp.broadcast_to(ones(part == 0), (8, lanes))


def coefficients(links_x, links_y, maps_ref, planes):
    lanes = maps_ref.shape[1] // 2
    ys = links_x.shape[1]
    count = links_x.shape[0]
    half = 2 * planes * 8
    wide = dot(jnp.concatenate([links_x, links_y], axis=0), maps_ref[:ys].astype(jnp.bfloat16))
    match = maps_ref[ys : ys + count]
    match_ahead, match_back = match[:, :lanes], match[:, lanes:]
    choose = maps_ref[ys + count : ys + count + 2 * half, :count].astype(jnp.bfloat16)
    first_part = maps_ref[ys + count + 2 * half : ys + count + 2 * half + 1, :lanes] > 0.5
    ahead = jnp.concatenate([wide[:count, :lanes] * match_ahead, wide[count:, lanes:] * match_ahead], axis=1)
    back = jnp.concatenate([wide[:count, :lanes] * match_back, wide[count:, :lanes] * match_back], axis=1)
    out = []
    for chosen in (
        dot(choose[:half], ahead.astype(jnp.bfloat16)), dot(choose[half:], back.astype(jnp.bfloat16))
    ):
        for start in (0, lanes):
            part = chosen[:, start : start + lanes]
            rows = jnp.where(first_part, part[: half // 2], part[half // 2 :])
            out.append(rows.reshape(planes, 8, lanes))
    return out


def plane_rows(ref, ys):
    parts, _, colours, zs, width = ref.shape
    return jnp.concatenate(
        [ref[p, :ys, c].reshape(ys * zs, width) for p in range(parts) for c in range(colours)],
        axis=0,
    )


def edges_kernel(
    raw_hbm, links_x_hbm, links_y_hbm,
    first_ref, last_ref, raw_ref, links_x_ref, links_y_ref, maps_ref, past_maps_ref, arrived,
):
    parts, planes, ys, colours, zs, _ = raw_hbm.shape
    sources = (raw_hbm.at[:, planes - 1], raw_hbm.at[:, 0], links_x_hbm, links_y_hbm, raw_hbm)
    targets = (last_ref.at[:, :ys], first_ref, links_x_ref, links_y_ref, raw_ref)
    copies = [
        pltpu.make_async_copy(source, target, arrived.at[i])
        for i, (source, target) in enumerate(zip(sources, targets))
    ]
    for copy in copies:
        copy.start()
    last_ref[:, ys:] = jnp.zeros((parts, colours) + last_ref.shape[2:], last_ref.dtype)
    write_maps(maps_ref, parts, colours, planes, ys, zs)
    write_maps(past_maps_ref, parts, colours, 1, ys, zs)
    copies[2].wait()
    last_ref[:, ys:, :, :, :ys] = links_x_ref[:, :, :, planes - 1]
    for copy in copies[:2] + copies[3:]:
        copy.wait()


def site_matrix(rows_and_masks, count):
    blocks = []
    for q in range(count):
        block = None
        for rows, mask in rows_and_masks:
            term = rows[q : q + 1] * mask
            block = term if block is None else block + term
        blocks.append(block.astype(jnp.bfloat16))
    return jnp.concatenate(blocks, axis=0)


def prepare_kernel(
    raw_ref, links_x_ref, links_y_ref, maps_ref,
    rows_ref, ends_ref, ahead_x_ref, back_x_ref, ahead_y_ref, back_y_ref,
):
    planes, depth, width = rows_ref.shape
    zs = raw_ref.shape[4]
    ys = raw_ref.shape[2]
    sites = ys * zs
    row_size = depth // sites * zs
    lanes = ahead_y_ref.shape[2]
    ahead_x, ahead_y, back_x, back_y = coefficients(
        links_x_ref[...].reshape(-1, ys), links_y_ref[...].reshape(-1, ys), maps_ref, planes
    )
    ahead_x_ref[...] = ahead_x
    back_x_ref[...] = back_x
    ahead_y_ref[...] = ahead_y
    back_y_ref[...] = back_y

    row, lane = iotas((2 * row_size, depth))
    spot = row % row_size
    wanted = (spot // zs) * sites + spot % zs + jnp.where(row < row_size, 0, sites - zs)
    ends = (lane == wanted).astype(jnp.bfloat16)
    filler = jnp.zeros((8, width - 128), jnp.float32)
    spare = ends_ref.shape[1] - 2 * row_size - 8
    for x in range(planes):
        plane = plane_rows(raw_ref.at[:, x], ys)
        rows_ref[place_of(x, planes)] = plane
        tail = jnp.concatenate([back_y[x, :, lanes - 128 :], filler], axis=1)
        pieces = [dot(ends, plane), tail]
        if spare:
            pieces.append(jnp.zeros((spare, width), jnp.float32))
        ends_ref[x] = jnp.concatenate(pieces, axis=0).astype(jnp.bfloat16)


def turn_kernel(raw_ref, rows_ref, turned_ref):
    planes, depth, width = rows_ref.shape
    for x in range(planes):
        rows_ref[place_of(x, planes)] = plane_rows(raw_ref.at[:, x], raw_ref.shape[2])
    turned_ref[...] = rows_ref[...].reshape(planes * depth, width).T


def move_plane(same, count, ahead, back, above, below):
    depth = same.shape[1]
    moved = dot(site_matrix([(ahead[:, :depth], same)], count), above)
    return (moved + dot(site_matrix([(back[:, :depth], same)], count), below)).astype(jnp.bfloat16)


def same_site(sites, depth):
    site, lane = iotas((sites, depth))
    return (lane % sites == site).astype(jnp.float32)


def set_right(right_ref, place, moved):
    depth, width = moved.shape
    half = depth // 2
    start = place * depth
    real, imag = moved[:half], moved[half:]
    right_ref[start : start + half, :width] = real
    right_ref[start : start + half, width:] = imag
    right_ref[start + half : start + depth, :width] = imag
    right_ref[start + half : start + depth, width:] = -real


def inner_kernel(
    sites, rows_ref, ahead_ref, back_ref, right_ref, turned_ref, matrix_ref, ahead_part_ref, back_part_ref
):
    planes, depth, width = rows_ref.shape
    same = same_site(sites, depth)
    for x in range(1, planes - 1):
        above = rows_ref[place_of(x + 1, planes)]
        below = rows_ref[place_of(x - 1, planes)]
        moved = move_plane(same, depth // sites, ahead_ref[x], back_ref[x - 1], above, below)
        set_right(right_ref, place_of(x, planes), moved)
    turned_ref[...] = rows_ref[...].reshape(planes * depth, width).T
    x, count = planes - 1, depth // sites
    matrix_ref[...] = site_matrix([(ahead_ref[x, :, :depth], same)], count)
    ahead_part_ref[...] = dot(site_matrix([(ahead_ref[0, :, :depth], same)], count), rows_ref[place_of(1, planes)])
    below = rows_ref[place_of(x - 1, planes)]
    back_part_ref[...] = dot(site_matrix([(back_ref[x - 1, :, :depth], same)], count), below)


def begin_first_kernel(own_ref, others_ref, right_ref, total_ref):
    inner = right_ref.shape[0]
    right = right_ref[...]
    total_ref[0] = dot(own_ref[:, :inner], right)
    for k in range(others_ref.shape[0]):
        total_ref[k + 1] = dot(others_ref[k, :, :inner], right)


def bits(axis):
    return range(lax.axis_size(axis).bit_length() - 1)


def steps(turns=True):
    one = [("gx", bit) for bit in bits("gx")[:-1]]
    two = [("gy", bit) for bit in bits("gy")]
    if not turns:
        return [(step, step) for step in two + one]
    both = min(len(one), len(two))
    pairs = [pair for ends in zip(one, two) for pair in (ends, ends[::-1])]
    return pairs + [(step, step) for step in one[both:] + two[both:]]


def my_bit(axis, bit):
    return lax.bitwise_and(lax.shift_right_logical(lax.axis_index(axis), bit), 1)


def my_side(step):
    even, odd = (my_bit(*way) for way in step)
    return jnp.where(my_bit("ma", 0) == 0, even, odd)


def half_of(kind):
    half = lax.bitwise_xor(my_bit("gx", bits("gx")[-1]), 1 - kind)
    return lax.bitwise_xor(half, lax.axis_index("ma"))


def share(plan, total, keep_ref, send_ref, total_ref):
    blocks, rows, double = total_ref.shape
    parts, count, _, width = keep_ref.shape
    total_ref[...] = total.reshape(blocks, rows, double)
    odd_core = my_bit("ma", 0)
    across_y = lax.axis_size("gy")
    mine = my_side(plan[0])

    def at(side, index):
        owners = []
        for core in range(2):
            place = {"gx": 0, "gy": 0}
            for k, step in enumerate(plan):
                axis, bit = step[core]
                digit = side if k == 0 else index >> (len(plan) - 1 - k) & 1
                place[axis] += digit * (1 << bit)
            owners.append(place["gx"] * across_y + place["gy"])
        return jnp.where(odd_core == 0, owners[0], owners[1])

    for index in range(count):
        for ref, side in ((keep_ref, mine), (send_ref, 1 - mine)):
            block = total_ref[at(side, index)].astype(ref.dtype)
            for p in range(parts):
                ref[p, index] = block[:, p * width : (p + 1) * width]


def first_share(kind, own_ref, others_ref, begun_ref, right, keep_ref, send_ref, total_ref):
    half = half_of(kind)
    inner = own_ref.shape[1] - right.shape[0]
    left = jnp.where(half == 0, own_ref[:, inner:], others_ref[0, :, inner:])
    share(steps(kind == 1), begun_ref[half] + dot(left, right), keep_ref, send_ref, total_ref)


def first_kernel(
    sites, high_ref, low_ref, matrix_ref, ahead_part_ref, back_part_ref, past_maps_ref, own_ref, others_ref, begun_ref,
    *refs,
):
    keep_ref, send_ref, right_ref, total_ref = refs
    depth = matrix_ref.shape[0]
    same = same_site(sites, depth)
    _, ys, colours, zs, _ = high_ref.shape
    links = low_ref[:, ys:, :, :, :ys].reshape(-1, ys)
    lanes = past_maps_ref.shape[1] // 2
    count = links.shape[0]
    spread = past_maps_ref[:ys, :lanes].astype(jnp.bfloat16)
    match = past_maps_ref[ys : ys + count, lanes:]
    start = past_maps_ref.shape[0] - 24
    choose = past_maps_ref[start : start + 16, :count].astype(jnp.bfloat16)
    past = dot(choose, (dot(links, spread) * match).astype(jnp.bfloat16))
    past = jnp.where(past_maps_ref[start + 16 : start + 17, :lanes] > 0.5, past[:8], past[8:])
    past = site_matrix([(past[:, :depth], same)], depth // sites)
    moved = ahead_part_ref[...] + dot(past, plane_rows(low_ref, ys))
    set_right(right_ref, 0, moved.astype(jnp.bfloat16))
    moved = dot(matrix_ref[...], plane_rows(high_ref, ys)) + back_part_ref[...]
    set_right(right_ref, 1, moved.astype(jnp.bfloat16))
    first_share(0, own_ref, others_ref, begun_ref, right_ref[...], keep_ref, send_ref, total_ref)


def first_own_kernel(own_ref, others_ref, begun_ref, right_ref, keep_ref, send_ref, total_ref):
    first_share(1, own_ref, others_ref, begun_ref, right_ref[...], keep_ref, send_ref, total_ref)


def begin_y_kernel(sites, zs, rows_ref, others_ref, ahead_ref, back_ref, part_ref):
    planes, depth, _ = rows_ref.shape
    site, lane = iotas((sites, depth))
    to_next = jnp.where(lane % sites == site + zs, -1.0, 0.0)
    to_last = jnp.where(lane % sites == site - zs, -1.0, 0.0)
    for x in range(planes):
        ahead, back = ahead_ref[x, :, :depth], back_ref[x, :, :depth]
        matrix = site_matrix([(ahead, to_next), (back, to_last)], depth // sites)
        place = place_of(x, planes)
        part_ref[0, place] = dot(matrix, rows_ref[place])
        for k in range(others_ref.shape[0]):
            part_ref[k + 1, place] = dot(matrix, others_ref[k, place])


def move_y_kernel(sites, zs, part_ref, near_ref, far_ref, ahead_ref, turned_ref, field_ref):
    groups, planes, depth, width = part_ref.shape
    row_size = depth // sites * zs
    tail = 128
    head = ahead_ref.shape[2] - tail
    site, lane = iotas((sites, tail))
    lane = lane + head
    upper = (lane >= depth) & (lane < depth + row_size)
    lower = (lane >= depth + row_size) & (lane < depth + 2 * row_size)
    to_next = jnp.where(upper & (site == sites - zs + lane % zs), -1.0, 0.0)
    to_last = jnp.where(lower & (site == lane % zs), -1.0, 0.0)
    above = jnp.zeros((depth - head, width), jnp.bfloat16)
    below = jnp.zeros((tail - 2 * row_size - (depth - head), width), jnp.bfloat16)
    for x in range(planes):
        past = near_ref[x, 2 * row_size : 2 * row_size + 8, :tail].astype(jnp.float32)
        matrix = site_matrix([(ahead_ref[x, :, head:], to_next), (past, to_last)], depth // sites)
        place = place_of(x, planes)
        for k in range(groups):
            edge = near_ref[x, : 2 * row_size] if k == 0 else far_ref[k - 1, x]
            moved = part_ref[k, place] + dot(matrix, jnp.concatenate([above, edge, below], axis=0))
            field_ref[k, place] = moved.astype(jnp.bfloat16)
    for k in range(groups):
        turned_ref[k] = field_ref[k].reshape(planes * depth, width).T


def second_share(kind, lefts_ref, right_ref, edge_ref, keep_ref, send_ref, total_ref):
    half = half_of(kind)
    inner = right_ref.shape[0]
    total = dot(lefts_ref[half, :, :inner], right_ref[...]) + dot(lefts_ref[half, :, inner:], edge_ref[...])
    share(steps(), total, keep_ref, send_ref, total_ref)


def second_kernel(lefts_ref, right_ref, edge_ref, keep_ref, send_ref, total_ref):
    second_share(0, lefts_ref, right_ref, edge_ref, keep_ref, send_ref, total_ref)


def second_own_kernel(lefts_ref, right_ref, edge_ref, first_ref, keep_ref, send_ref, total_ref):
    parts = first_ref.shape[0]
    send_ref[:parts] = first_ref[...]
    second_share(1, lefts_ref, right_ref, edge_ref, keep_ref, send_ref.at[parts:], total_ref)


def exchange(block, step):
    axes = ("gx", "gy", "ma")
    sizes = [lax.axis_size(axis) for axis in axes]
    route = []
    for source in range(sizes[0] * sizes[1] * sizes[2]):
        where = [source // (sizes[1] * sizes[2]), source // sizes[2] % sizes[1], source % sizes[2]]
        axis, bit = step[where[2] % 2]
        where[axes.index(axis)] ^= 1 << bit
        route.append((source, (where[0] * sizes[1] + where[1]) * sizes[2] + where[2]))
    return lax.ppermute(block, axes, route)


def halve(sums, step, weight=0):
    parts = sum(kept.shape[0] for kept, _, _ in sums)
    count, rows, width = sums[0][0].shape[1:]
    dims = (parts, count // 2, rows, width)

    def merge(*refs):
        *refs, keep_ref, send_ref = refs
        mine = my_side(step)
        start = 0
        for k, (_, _, which) in enumerate(sums):
            kept_ref, came_ref = refs[2 * k : 2 * k + 2]
            came_ref = came_ref if which is None else came_ref.at[which]
            end = start + kept_ref.shape[0]
            for index in range(count // 2):
                low, high = (
                    kept_ref[:, at] + came_ref[:, at].astype(jnp.float32) for at in (index, index + count // 2)
                )
                keep_ref[start:end, index] = jnp.where(mine == 0, low, high)
                send_ref[start:end, index] = jnp.where(mine == 0, high, low).astype(send_ref.dtype)
            start = end

    operands = [a for kept, came, _ in sums for a in (kept, came)]
    keep, send = call(merge, (pltpu.VMEM(dims, jnp.float32), pltpu.VMEM(dims, jnp.bfloat16)), weight, operands)
    return keep, exchange(send, step)


def sum_kernel(kept_ref, came_ref, send_ref):
    send_ref[...] = (kept_ref[...] + came_ref[...].astype(jnp.float32)).astype(send_ref.dtype)


def cross_kernel(start, kept_ref, crossed_ref, out_ref):
    kept = kept_ref[start : start + out_ref.shape[0]]
    out_ref[...] = kept + crossed_ref[...].astype(jnp.float32)


def finish_kernel(came_ref, *refs):
    *kept_refs, out_ref = refs
    parts = out_ref.shape[1]
    for d, kept_ref in enumerate(kept_refs):
        out_ref[d] = kept_ref[:, 0] + came_ref[d * parts : (d + 1) * parts, 0].astype(jnp.float32)


def local(eigen_modes, links_first, links_second):
    f32, bf16 = jnp.float32, jnp.bfloat16
    parts, planes, ys, zs, colours, width = eigen_modes.shape
    sites = ys * zs
    depth = parts * colours * sites
    row_size = parts * colours * zs
    edge = -(-(2 * row_size + 8) // 16) * 16
    lanes = -(-(depth + 2 * row_size) // 128) * 128
    across_x, across_y, groups = (lax.axis_size(a) for a in ("gx", "gy", "ma"))
    rows = groups * width // (across_x * across_y)
    inner_depth = (planes - 2) * depth
    raw = eigen_modes.transpose(0, 1, 2, 4, 3, 5)

    def shape(*dims, dtype=bf16):
        return pltpu.VMEM(dims, dtype)

    field_shape = shape(planes, depth, width)
    turned_shape = shape(width, planes * depth)
    total_shape = shape(groups, width, parts * width, dtype=f32)
    link_shape = shape(planes, 8, lanes, dtype=f32)
    total = pltpu.VMEM((width // rows, rows, parts * width), f32)
    step_flops = 2 * planes * depth * depth * width
    project_flops = 2 * groups * width * planes * depth * parts * width

    raw_others = [shifted(raw, "ma", -step) for step in range(1, groups)]
    raw_links_x, raw_links_y = (a.transpose(0, 1, 2, 3, 5, 4) for a in (links_first, links_second))
    inputs = [raw, raw_links_x, raw_links_y]
    first_plane, last_plane, *inputs, past_maps = call(
        edges_kernel,
        (
            shape(parts, ys, colours, zs, width), shape(parts, ys + colours, colours, zs, width),
            *(shape(*a.shape) for a in inputs),
            shape(map_rows(parts, colours, planes, ys, zs)[-1], 2 * lanes, dtype=f32),
            shape(map_rows(parts, colours, 1, ys, zs)[-1], 2 * lanes, dtype=f32),
        ),
        0,
        inputs,
        [pltpu.SemaphoreType.DMA((5,))],
        [pltpu.HBM] * len(inputs),
    )
    low = shifted(last_plane, "gx", 1)
    high = shifted(first_plane, "gx", -1)
    field, ends, ahead_x, back_x, ahead_y, back_y = call(
        prepare_kernel,
        (field_shape, shape(planes, edge, width), link_shape, link_shape, link_shape, link_shape),
        0,
        inputs,
    )
    near = shifted(ends, "gy", 1)
    if across_y != 2:
        ahead_row = lax.broadcasted_iota(jnp.int32, ends.shape, 1) < row_size
        near = jnp.where(ahead_row, shifted(ends, "gy", -1), near)

    plan = steps()
    top = ("gx", bits("gx")[-1])
    pieces = across_x * across_y // 4
    kept_shape = shape(parts, pieces, rows, width, dtype=f32)
    sent_shape = shape(parts, pieces, rows, width)

    def inner(*refs):
        inner_kernel(sites, *refs)

    def first(*refs):
        first_kernel(sites, *refs)

    def begin_y(*refs):
        begin_y_kernel(sites, zs, *refs)

    def move_y(*refs):
        move_y_kernel(sites, zs, *refs)

    right, own, matrix, ahead_part, back_part = call(
        inner,
        (
            shape(inner_depth, parts * width), turned_shape, shape(depth, depth),
            shape(depth, width, dtype=f32), shape(depth, width, dtype=f32),
        ),
        2 * step_flops,
        [field, ahead_x, back_x],
    )
    turned = [call(turn_kernel, (field_shape, turned_shape), step_flops // 4, [r]) for r in raw_others]
    fields = jnp.stack([t[0] for t in turned])
    others = jnp.stack([t[1] for t in turned])
    begun_first = call(begin_first_kernel, total_shape, project_flops, [own, others, right])
    part_y = call(
        begin_y, shape(groups, planes, depth, width, dtype=f32), 2 * step_flops, [field, fields, ahead_y, back_y]
    )
    part_y, begun_first = lax.optimization_barrier((part_y, begun_first))
    kept_first, sent_first, right_edge = call(
        first,
        (kept_shape, sent_shape, shape(2 * depth, parts * width)),
        project_flops,
        [high, low, matrix, ahead_part, back_part, past_maps, own, others, begun_first],
        [total],
    )
    plan_first = steps(False)
    came_first = exchange(sent_first, plan_first[0])
    near, right_edge = lax.optimization_barrier((near, right_edge))
    near_rows = near[:, : 2 * row_size]
    far = jnp.stack([shifted(near_rows, "ma", -step) for step in range(1, groups)])
    lefts = call(
        move_y, shape(groups, width, planes * depth), 2 * step_flops,
        [part_y, near, far, ahead_y],
        [pltpu.VMEM((groups,) + field_shape.shape, bf16)],
    )
    kept_second, sent_second = call(
        second_kernel, (kept_shape, sent_shape), 8 * project_flops, [lefts, right, right_edge], [total]
    )
    came_second = exchange(sent_second, plan[0])
    right_edge, kept_second = lax.optimization_barrier((right_edge, kept_second))
    own_first, sent_own = call(
        first_own_kernel, (kept_shape, sent_shape), 0, [own, others, begun_first, right_edge], [total]
    )
    own_second, sent_own = call(
        second_own_kernel, (kept_shape, shape(2 * parts, pieces, rows, width)), 0,
        [lefts, right, right_edge, sent_own], [total],
    )
    came_own = exchange(sent_own, plan[0])
    staying = [(own_first, came_own, slice(0, parts)), (own_second, came_own, slice(parts, 2 * parts))]
    crossing = [(kept_first, came_first), (kept_second, came_second)]
    after = own_second
    for turn in zip(plan_first[1:], plan[1:]):
        for d, (kept, came) in enumerate(crossing):
            came, after = lax.optimization_barrier((came, after))
            crossing[d] = halve([(kept, came, None)], turn[d], 4 * project_flops if d else 0)
            after = crossing[d][0]
    crossed = []
    for kept, came in crossing:
        came, after = lax.optimization_barrier((came, after))
        after = call(sum_kernel, pltpu.VMEM(kept.shape, bf16), 0, [kept, came])
        crossed.append(exchange(after, (top, top)))
    for step in plan[1:]:
        kept, came, which = staying[0]
        came, after = lax.optimization_barrier((came, after))
        sums = [(kept, came, which)] + [(k, came, w) for k, _, w in staying[1:]]
        kept, came = halve(sums, step)
        staying, after = [(kept, came, None)], kept
    kept, came, _ = staying[0]
    totals = []
    for d, block in enumerate(crossed):

        def cross(*refs, start=d * parts):
            cross_kernel(start, *refs)

        block, after = lax.optimization_barrier((block, after))
        after = call(cross, shape(*block.shape, dtype=f32), 4 * project_flops, [kept, block])
        totals.append(after)
    came, after = lax.optimization_barrier((came, after))
    return call(
        finish_kernel, jax.ShapeDtypeStruct((2, parts, rows, width), f32), 0, [came, *totals]
    )


def solution(mesh):
    return jax.shard_map(
        local,
        mesh=mesh,
        in_specs=(
            P("cuts", "gx", "gy", None, None, "ma"),
            P("cuts", None, None, "gx", "gy", None),
            P("cuts", None, None, "gx", "gy", None),
        ),
        out_specs=P("cuts", None, ("gx", "gy"), "ma"),
        check_vma=False,
    )
```

```python
import jax
import jax.numpy as jnp
from jax import lax
from jax.experimental import pallas as pl
from jax.experimental.pallas import tpu as pltpu
from jax.sharding import PartitionSpec as P

VMEM_LIMIT = 16 * 1024 * 1024


def shifted(block, axis, distance):
    devices = range(lax.axis_size(axis))
    route = [((i - distance) % len(devices), i) for i in devices]
    return lax.ppermute(block, axis, route)


def call(body, out_shape, flops, operands, scratch=(), places=None):
    places = places or [pltpu.VMEM] * len(operands)
    return pl.pallas_call(
        body,
        out_shape=out_shape,
        in_specs=[pl.BlockSpec(memory_space=place) for place in places],
        scratch_shapes=scratch,
        cost_estimate=pl.CostEstimate(flops=flops // 2, bytes_accessed=0, transcendentals=0),
        compiler_params=pltpu.CompilerParams(vmem_limit_bytes=VMEM_LIMIT),
    )(*(pltpu.with_memory_space_constraint(a, place) for a, place in zip(operands, places)))


def dot(a, b):
    return jnp.dot(a, b, preferred_element_type=jnp.float32)


def iotas(shape):
    return (
        lax.broadcasted_iota(jnp.int32, shape, 0),
        lax.broadcasted_iota(jnp.int32, shape, 1),
    )


def place_of(x, planes):
    return planes - 2 if x == 0 else x if x == planes - 1 else x - 1


def map_rows(parts, colours, planes, ys, zs):
    match = ys
    choose = match + -(-parts * colours * colours * planes * zs // 8) * 8
    first_part = choose + 2 * parts * planes * 8
    return match, choose, first_part, first_part + 8


def write_maps(ref, parts, colours, planes, ys, zs):
    lanes = ref.shape[1] // 2
    sites = ys * zs
    depth = parts * colours * sites
    row_size = parts * colours * zs
    match, choose, first_part, _ = map_rows(parts, colours, planes, ys, zs)

    def ones(mask):
        return jnp.where(mask, 1.0, 0.0)

    def column(count):
        return lax.broadcasted_iota(jnp.int32, (count, 1), 0)

    def line(count):
        return lax.broadcasted_iota(jnp.int32, (1, count), 1)

    lane = line(lanes)
    inner = lane < depth
    past = lax.rem(jnp.maximum(lane - depth, 0), row_size)
    used = lane < depth + 2 * row_size
    part = jnp.where(inner, lax.div(lane, colours * sites), lax.div(past, colours * zs))
    colour = lax.rem(jnp.where(inner, lax.div(lane, sites), lax.div(past, zs)), colours)
    z = lax.rem(jnp.where(inner, lane, past), zs)
    y = lax.div(lax.rem(lane, sites), zs)
    ref[:ys, :lanes] = ones(column(ys) == jnp.where(inner, y, ys - 1))
    ref[:ys, lanes:] = ones(column(ys) == jnp.where(inner, y, ys) - 1)

    count = parts * colours * colours * planes * zs

    def link(index):
        x = lax.rem(lax.div(index, zs), planes)
        right = lax.rem(lax.div(index, zs * planes), colours)
        left = lax.rem(lax.div(index, zs * planes * colours), colours)
        return x, right, left, lax.div(index, zs * planes * colours * colours)

    row = column(count)
    _, right, left, _ = link(row)
    row_z = lax.rem(row, zs)
    key = jnp.where(used, colour * zs + z, -1)
    ref[match : match + count, :lanes] = ones(right * zs + row_z == key)
    ref[match : match + count, lanes:] = ones(left * zs + row_z == key)

    out = column(parts * planes * 8)
    field_part = lax.div(out, planes * 8)
    out_x = lax.rem(lax.div(out, 8), planes)
    out_part = lax.div(lax.rem(out, 8), colours)
    out_colour = lax.rem(lax.rem(out, 8), colours)
    x, right, left, source_part = link(line(count))
    source = source_part * planes + x
    wanted = jnp.where(out_part < parts, lax.rem(out_part + field_part, 2) * planes + out_x, -1)
    sign_ahead = jnp.where((field_part == 1) & (out_part == 0), -1.0, 1.0)
    sign_back = jnp.where((field_part == 0) & (out_part == 1), 1.0, -1.0)
    half = parts * planes * 8
    for start, end, sign in ((choose, left, sign_ahead), (choose + half, right, sign_back)):
        hit = source * colours + end == wanted * colours + jnp.where(wanted < 0, -1, out_colour)
        ref[start : start + half, :count] = jnp.where(hit, sign, 0.0)
    ref[first_part:, :lanes] = jnp.broadcast_to(ones(part == 0), (8, lanes))


def coefficients(links_x, links_y, maps_ref, planes):
    lanes = maps_ref.shape[1] // 2
    ys = links_x.shape[1]
    count = links_x.shape[0]
    half = 2 * planes * 8
    wide = dot(jnp.concatenate([links_x, links_y], axis=0), maps_ref[:ys].astype(jnp.bfloat16))
    match = maps_ref[ys : ys + count]
    match_ahead, match_back = match[:, :lanes], match[:, lanes:]
    choose = maps_ref[ys + count : ys + count + 2 * half, :count].astype(jnp.bfloat16)
    first_part = maps_ref[ys + count + 2 * half : ys + count + 2 * half + 1, :lanes] > 0.5
    ahead = jnp.concatenate([wide[:count, :lanes] * match_ahead, wide[count:, lanes:] * match_ahead], axis=1)
    back = jnp.concatenate([wide[:count, :lanes] * match_back, wide[count:, :lanes] * match_back], axis=1)
    out = []
    for chosen in (
        dot(choose[:half], ahead.astype(jnp.bfloat16)), dot(choose[half:], back.astype(jnp.bfloat16))
    ):
        for start in (0, lanes):
            part = chosen[:, start : start + lanes]
            rows = jnp.where(first_part, part[: half // 2], part[half // 2 :])
            out.append(rows.reshape(planes, 8, lanes))
    return out


def plane_rows(ref, ys):
    parts, _, colours, zs, width = ref.shape
    return jnp.concatenate(
        [ref[p, :ys, c].reshape(ys * zs, width) for p in range(parts) for c in range(colours)],
        axis=0,
    )


def edges_kernel(
    raw_hbm, links_x_hbm, links_y_hbm,
    first_ref, last_ref, raw_ref, links_x_ref, links_y_ref, maps_ref, past_maps_ref, arrived,
):
    parts, planes, ys, colours, zs, _ = raw_hbm.shape
    sources = (raw_hbm.at[:, planes - 1], raw_hbm.at[:, 0], links_x_hbm, links_y_hbm, raw_hbm)
    targets = (last_ref.at[:, :ys], first_ref, links_x_ref, links_y_ref, raw_ref)
    copies = [
        pltpu.make_async_copy(source, target, arrived.at[i])
        for i, (source, target) in enumerate(zip(sources, targets))
    ]
    for copy in copies:
        copy.start()
    last_ref[:, ys:] = jnp.zeros((parts, colours) + last_ref.shape[2:], last_ref.dtype)
    write_maps(maps_ref, parts, colours, planes, ys, zs)
    write_maps(past_maps_ref, parts, colours, 1, ys, zs)
    copies[2].wait()
    last_ref[:, ys:, :, :, :ys] = links_x_ref[:, :, :, planes - 1]
    for copy in copies[:2] + copies[3:]:
        copy.wait()


def site_matrix(rows_and_masks, count):
    blocks = []
    for q in range(count):
        block = None
        for rows, mask in rows_and_masks:
            term = rows[q : q + 1] * mask
            block = term if block is None else block + term
        blocks.append(block.astype(jnp.bfloat16))
    return jnp.concatenate(blocks, axis=0)


def prepare_kernel(
    raw_ref, links_x_ref, links_y_ref, maps_ref,
    rows_ref, ends_ref, ahead_x_ref, back_x_ref, ahead_y_ref, back_y_ref,
):
    planes, depth, width = rows_ref.shape
    zs = raw_ref.shape[4]
    ys = raw_ref.shape[2]
    sites = ys * zs
    row_size = depth // sites * zs
    lanes = ahead_y_ref.shape[2]
    ahead_x, ahead_y, back_x, back_y = coefficients(
        links_x_ref[...].reshape(-1, ys), links_y_ref[...].reshape(-1, ys), maps_ref, planes
    )
    ahead_x_ref[...] = ahead_x
    back_x_ref[...] = back_x
    ahead_y_ref[...] = ahead_y
    back_y_ref[...] = back_y

    row, lane = iotas((2 * row_size, depth))
    spot = row % row_size
    wanted = (spot // zs) * sites + spot % zs + jnp.where(row < row_size, 0, sites - zs)
    ends = (lane == wanted).astype(jnp.bfloat16)
    filler = jnp.zeros((8, width - 128), jnp.float32)
    spare = ends_ref.shape[1] - 2 * row_size - 8
    for x in range(planes):
        plane = plane_rows(raw_ref.at[:, x], ys)
        rows_ref[place_of(x, planes)] = plane
        tail = jnp.concatenate([back_y[x, :, lanes - 128 :], filler], axis=1)
        pieces = [dot(ends, plane), tail]
        if spare:
            pieces.append(jnp.zeros((spare, width), jnp.float32))
        ends_ref[x] = jnp.concatenate(pieces, axis=0).astype(jnp.bfloat16)


def turn_kernel(raw_ref, rows_ref, turned_ref):
    planes, depth, width = rows_ref.shape
    for x in range(planes):
        rows_ref[place_of(x, planes)] = plane_rows(raw_ref.at[:, x], raw_ref.shape[2])
    turned_ref[...] = rows_ref[...].reshape(planes * depth, width).T


def move_plane(same, count, ahead, back, above, below):
    depth = same.shape[1]
    moved = dot(site_matrix([(ahead[:, :depth], same)], count), above)
    return (moved + dot(site_matrix([(back[:, :depth], same)], count), below)).astype(jnp.bfloat16)


def same_site(sites, depth):
    site, lane = iotas((sites, depth))
    return (lane % sites == site).astype(jnp.float32)


def set_right(right_ref, place, moved):
    depth, width = moved.shape
    half = depth // 2
    start = place * depth
    real, imag = moved[:half], moved[half:]
    right_ref[start : start + half, :width] = real
    right_ref[start : start + half, width:] = imag
    right_ref[start + half : start + depth, :width] = imag
    right_ref[start + half : start + depth, width:] = -real


def inner_kernel(
    sites, rows_ref, ahead_ref, back_ref, right_ref, turned_ref, matrix_ref, ahead_part_ref, back_part_ref
):
    planes, depth, width = rows_ref.shape
    same = same_site(sites, depth)
    for x in range(1, planes - 1):
        above = rows_ref[place_of(x + 1, planes)]
        below = rows_ref[place_of(x - 1, planes)]
        moved = move_plane(same, depth // sites, ahead_ref[x], back_ref[x - 1], above, below)
        set_right(right_ref, place_of(x, planes), moved)
    turned_ref[...] = rows_ref[...].reshape(planes * depth, width).T
    x, count = planes - 1, depth // sites
    matrix_ref[...] = site_matrix([(ahead_ref[x, :, :depth], same)], count)
    ahead_part_ref[...] = dot(site_matrix([(ahead_ref[0, :, :depth], same)], count), rows_ref[place_of(1, planes)])
    below = rows_ref[place_of(x - 1, planes)]
    back_part_ref[...] = dot(site_matrix([(back_ref[x - 1, :, :depth], same)], count), below)


def begin_first_kernel(own_ref, others_ref, right_ref, total_ref):
    inner = right_ref.shape[0]
    right = right_ref[...]
    total_ref[0] = dot(own_ref[:, :inner], right)
    for k in range(others_ref.shape[0]):
        total_ref[k + 1] = dot(others_ref[k, :, :inner], right)


def bits(axis):
    return range(lax.axis_size(axis).bit_length() - 1)


def steps():
    one = [("gx", bit) for bit in bits("gx")[:-1]]
    two = [("gy", bit) for bit in bits("gy")]
    both = min(len(one), len(two))
    pairs = [pair for ends in zip(one, two) for pair in (ends, ends[::-1])]
    return pairs + [(step, step) for step in one[both:] + two[both:]]


def my_bit(axis, bit):
    return lax.bitwise_and(lax.shift_right_logical(lax.axis_index(axis), bit), 1)


def my_side(step):
    even, odd = (my_bit(*way) for way in step)
    return jnp.where(my_bit("ma", 0) == 0, even, odd)


def half_of(kind):
    half = lax.bitwise_xor(my_bit("gx", bits("gx")[-1]), 1 - kind)
    return lax.bitwise_xor(half, lax.axis_index("ma"))


def share(total, keep_ref, send_ref, total_ref):
    blocks, rows, double = total_ref.shape
    parts, count, _, width = keep_ref.shape
    total_ref[...] = total.reshape(blocks, rows, double)
    odd_core = my_bit("ma", 0)
    across_y = lax.axis_size("gy")
    plan = steps()
    mine = my_side(plan[0])

    def at(side, index):
        owners = []
        for core in range(2):
            place = {"gx": 0, "gy": 0}
            for k, step in enumerate(plan):
                axis, bit = step[core]
                digit = side if k == 0 else index >> (len(plan) - 1 - k) & 1
                place[axis] += digit * (1 << bit)
            owners.append(place["gx"] * across_y + place["gy"])
        return jnp.where(odd_core == 0, owners[0], owners[1])

    for index in range(count):
        for ref, side in ((keep_ref, mine), (send_ref, 1 - mine)):
            block = total_ref[at(side, index)].astype(ref.dtype)
            for p in range(parts):
                ref[p, index] = block[:, p * width : (p + 1) * width]


def first_share(kind, own_ref, others_ref, begun_ref, right, keep_ref, send_ref, total_ref):
    half = half_of(kind)
    inner = own_ref.shape[1] - right.shape[0]
    left = jnp.where(half == 0, own_ref[:, inner:], others_ref[0, :, inner:])
    share(begun_ref[half] + dot(left, right), keep_ref, send_ref, total_ref)


def first_kernel(
    sites, high_ref, low_ref, matrix_ref, ahead_part_ref, back_part_ref, past_maps_ref, own_ref, others_ref, begun_ref,
    *refs,
):
    keep_ref, send_ref, right_ref, total_ref = refs
    depth = matrix_ref.shape[0]
    same = same_site(sites, depth)
    _, ys, colours, zs, _ = high_ref.shape
    links = low_ref[:, ys:, :, :, :ys].reshape(-1, ys)
    lanes = past_maps_ref.shape[1] // 2
    count = links.shape[0]
    spread = past_maps_ref[:ys, :lanes].astype(jnp.bfloat16)
    match = past_maps_ref[ys : ys + count, lanes:]
    start = past_maps_ref.shape[0] - 24
    choose = past_maps_ref[start : start + 16, :count].astype(jnp.bfloat16)
    past = dot(choose, (dot(links, spread) * match).astype(jnp.bfloat16))
    past = jnp.where(past_maps_ref[start + 16 : start + 17, :lanes] > 0.5, past[:8], past[8:])
    past = site_matrix([(past[:, :depth], same)], depth // sites)
    moved = ahead_part_ref[...] + dot(past, plane_rows(low_ref, ys))
    set_right(right_ref, 0, moved.astype(jnp.bfloat16))
    moved = dot(matrix_ref[...], plane_rows(high_ref, ys)) + back_part_ref[...]
    set_right(right_ref, 1, moved.astype(jnp.bfloat16))
    first_share(0, own_ref, others_ref, begun_ref, right_ref[...], keep_ref, send_ref, total_ref)


def first_own_kernel(own_ref, others_ref, begun_ref, right_ref, keep_ref, send_ref, total_ref):
    first_share(1, own_ref, others_ref, begun_ref, right_ref[...], keep_ref, send_ref, total_ref)


def begin_y_kernel(sites, zs, rows_ref, others_ref, ahead_ref, back_ref, part_ref):
    planes, depth, _ = rows_ref.shape
    site, lane = iotas((sites, depth))
    to_next = jnp.where(lane % sites == site + zs, -1.0, 0.0)
    to_last = jnp.where(lane % sites == site - zs, -1.0, 0.0)
    for x in range(planes):
        ahead, back = ahead_ref[x, :, :depth], back_ref[x, :, :depth]
        matrix = site_matrix([(ahead, to_next), (back, to_last)], depth // sites)
        place = place_of(x, planes)
        part_ref[0, place] = dot(matrix, rows_ref[place])
        for k in range(others_ref.shape[0]):
            part_ref[k + 1, place] = dot(matrix, others_ref[k, place])


def move_y_kernel(sites, zs, part_ref, near_ref, far_ref, ahead_ref, turned_ref, field_ref):
    groups, planes, depth, width = part_ref.shape
    row_size = depth // sites * zs
    tail = 128
    head = ahead_ref.shape[2] - tail
    site, lane = iotas((sites, tail))
    lane = lane + head
    upper = (lane >= depth) & (lane < depth + row_size)
    lower = (lane >= depth + row_size) & (lane < depth + 2 * row_size)
    to_next = jnp.where(upper & (site == sites - zs + lane % zs), -1.0, 0.0)
    to_last = jnp.where(lower & (site == lane % zs), -1.0, 0.0)
    above = jnp.zeros((depth - head, width), jnp.float32)
    below = jnp.zeros((tail - 2 * row_size - (depth - head), width), jnp.float32)
    for x in range(planes):
        near = near_ref[x].astype(jnp.float32)
        past = near[2 * row_size : 2 * row_size + 8, :tail]
        matrix = site_matrix([(ahead_ref[x, :, head:], to_next), (past, to_last)], depth // sites)
        place = place_of(x, planes)
        for k in range(groups):
            edge = near[: 2 * row_size] if k == 0 else far_ref[k - 1, x].astype(jnp.float32)
            column = jnp.concatenate([above, edge, below], axis=0).astype(jnp.bfloat16)
            field_ref[k, place] = (part_ref[k, place] + dot(matrix, column)).astype(jnp.bfloat16)
    for k in range(groups):
        turned_ref[k] = field_ref[k].reshape(planes * depth, width).T


def second_share(kind, lefts_ref, right_ref, edge_ref, keep_ref, send_ref, total_ref):
    half = half_of(kind)
    inner = right_ref.shape[0]
    total = dot(lefts_ref[half, :, :inner], right_ref[...]) + dot(lefts_ref[half, :, inner:], edge_ref[...])
    share(total, keep_ref, send_ref, total_ref)


def second_kernel(lefts_ref, right_ref, edge_ref, keep_ref, send_ref, total_ref):
    second_share(0, lefts_ref, right_ref, edge_ref, keep_ref, send_ref, total_ref)


def second_own_kernel(lefts_ref, right_ref, edge_ref, first_ref, keep_ref, send_ref, total_ref):
    parts = first_ref.shape[0]
    send_ref[:parts] = first_ref[...]
    second_share(1, lefts_ref, right_ref, edge_ref, keep_ref, send_ref.at[parts:], total_ref)


def exchange(block, step):
    axes = ("gx", "gy", "ma")
    sizes = [lax.axis_size(axis) for axis in axes]
    route = []
    for source in range(sizes[0] * sizes[1] * sizes[2]):
        where = [source // (sizes[1] * sizes[2]), source // sizes[2] % sizes[1], source % sizes[2]]
        axis, bit = step[where[2] % 2]
        where[axes.index(axis)] ^= 1 << bit
        route.append((source, (where[0] * sizes[1] + where[1]) * sizes[2] + where[2]))
    return lax.ppermute(block, axes, route)


def halve(sums, step, weight=0):
    parts = sum(kept.shape[0] for kept, _, _ in sums)
    count, rows, width = sums[0][0].shape[1:]
    dims = (parts, count // 2, rows, width)

    def merge(*refs):
        *refs, keep_ref, send_ref = refs
        mine = my_side(step)
        start = 0
        for k, (_, _, which) in enumerate(sums):
            kept_ref, came_ref = refs[2 * k : 2 * k + 2]
            came_ref = came_ref if which is None else came_ref.at[which]
            end = start + kept_ref.shape[0]
            for index in range(count // 2):
                low, high = (
                    kept_ref[:, at] + came_ref[:, at].astype(jnp.float32) for at in (index, index + count // 2)
                )
                keep_ref[start:end, index] = jnp.where(mine == 0, low, high)
                send_ref[start:end, index] = jnp.where(mine == 0, high, low).astype(send_ref.dtype)
            start = end

    operands = [a for kept, came, _ in sums for a in (kept, came)]
    keep, send = call(merge, (pltpu.VMEM(dims, jnp.float32), pltpu.VMEM(dims, jnp.bfloat16)), weight, operands)
    return keep, exchange(send, step)


def sum_kernel(kept_ref, came_ref, send_ref):
    send_ref[...] = (kept_ref[...] + came_ref[...].astype(jnp.float32)).astype(send_ref.dtype)


def cross_kernel(start, kept_ref, crossed_ref, out_ref):
    kept = kept_ref[start : start + out_ref.shape[0]]
    out_ref[...] = kept + crossed_ref[...].astype(jnp.float32)


def finish_kernel(came_ref, *refs):
    *kept_refs, out_ref = refs
    parts = out_ref.shape[1]
    for d, kept_ref in enumerate(kept_refs):
        out_ref[d] = kept_ref[:, 0] + came_ref[d * parts : (d + 1) * parts, 0].astype(jnp.float32)


def local(eigen_modes, links_first, links_second):
    f32, bf16 = jnp.float32, jnp.bfloat16
    parts, planes, ys, zs, colours, width = eigen_modes.shape
    sites = ys * zs
    depth = parts * colours * sites
    row_size = parts * colours * zs
    edge = -(-(2 * row_size + 8) // 16) * 16
    lanes = -(-(depth + 2 * row_size) // 128) * 128
    across_x, across_y, groups = (lax.axis_size(a) for a in ("gx", "gy", "ma"))
    rows = groups * width // (across_x * across_y)
    inner_depth = (planes - 2) * depth
    raw = eigen_modes.transpose(0, 1, 2, 4, 3, 5)

    def shape(*dims, dtype=bf16):
        return pltpu.VMEM(dims, dtype)

    field_shape = shape(planes, depth, width)
    turned_shape = shape(width, planes * depth)
    total_shape = shape(groups, width, parts * width, dtype=f32)
    link_shape = shape(planes, 8, lanes, dtype=f32)
    total = pltpu.VMEM((width // rows, rows, parts * width), f32)
    step_flops = 2 * planes * depth * depth * width
    project_flops = 2 * groups * width * planes * depth * parts * width

    raw_others = [shifted(raw, "ma", -step) for step in range(1, groups)]
    raw_links_x, raw_links_y = (a.transpose(0, 1, 2, 3, 5, 4) for a in (links_first, links_second))
    inputs = [raw, raw_links_x, raw_links_y]
    first_plane, last_plane, *inputs, past_maps = call(
        edges_kernel,
        (
            shape(parts, ys, colours, zs, width), shape(parts, ys + colours, colours, zs, width),
            *(shape(*a.shape) for a in inputs),
            shape(map_rows(parts, colours, planes, ys, zs)[-1], 2 * lanes, dtype=f32),
            shape(map_rows(parts, colours, 1, ys, zs)[-1], 2 * lanes, dtype=f32),
        ),
        0,
        inputs,
        [pltpu.SemaphoreType.DMA((5,))],
        [pltpu.HBM] * len(inputs),
    )
    low = shifted(last_plane, "gx", 1)
    high = shifted(first_plane, "gx", -1)
    field, ends, ahead_x, back_x, ahead_y, back_y = call(
        prepare_kernel,
        (field_shape, shape(planes, edge, width), link_shape, link_shape, link_shape, link_shape),
        0,
        inputs,
    )
    near = shifted(ends, "gy", 1)
    if across_y != 2:
        ahead_row = lax.broadcasted_iota(jnp.int32, ends.shape, 1) < row_size
        near = jnp.where(ahead_row, shifted(ends, "gy", -1), near)

    plan = steps()
    top = ("gx", bits("gx")[-1])
    pieces = across_x * across_y // 4
    kept_shape = shape(parts, pieces, rows, width, dtype=f32)
    sent_shape = shape(parts, pieces, rows, width)

    def inner(*refs):
        inner_kernel(sites, *refs)

    def first(*refs):
        first_kernel(sites, *refs)

    def begin_y(*refs):
        begin_y_kernel(sites, zs, *refs)

    def move_y(*refs):
        move_y_kernel(sites, zs, *refs)

    right, own, matrix, ahead_part, back_part = call(
        inner,
        (
            shape(inner_depth, parts * width), turned_shape, shape(depth, depth),
            shape(depth, width, dtype=f32), shape(depth, width, dtype=f32),
        ),
        2 * step_flops,
        [field, ahead_x, back_x],
    )
    turned = [call(turn_kernel, (field_shape, turned_shape), step_flops // 4, [r]) for r in raw_others]
    fields = jnp.stack([t[0] for t in turned])
    others = jnp.stack([t[1] for t in turned])
    begun_first = call(begin_first_kernel, total_shape, project_flops, [own, others, right])
    part_y = call(
        begin_y, shape(groups, planes, depth, width, dtype=f32), 2 * step_flops, [field, fields, ahead_y, back_y]
    )
    part_y, begun_first = lax.optimization_barrier((part_y, begun_first))
    kept_first, sent_first, right_edge = call(
        first,
        (kept_shape, sent_shape, shape(2 * depth, parts * width)),
        project_flops,
        [high, low, matrix, ahead_part, back_part, past_maps, own, others, begun_first],
        [total],
    )
    came_first = exchange(sent_first, plan[0])
    near, right_edge = lax.optimization_barrier((near, right_edge))
    near_rows = near[:, : 2 * row_size]
    far = jnp.stack([shifted(near_rows, "ma", -step) for step in range(1, groups)])
    lefts = call(
        move_y, shape(groups, width, planes * depth), 2 * step_flops,
        [part_y, near, far, ahead_y],
        [pltpu.VMEM((groups,) + field_shape.shape, bf16)],
    )
    kept_second, sent_second = call(
        second_kernel, (kept_shape, sent_shape), 8 * project_flops, [lefts, right, right_edge], [total]
    )
    came_second = exchange(sent_second, plan[0])
    right_edge, kept_second = lax.optimization_barrier((right_edge, kept_second))
    own_first, sent_own = call(
        first_own_kernel, (kept_shape, sent_shape), 0, [own, others, begun_first, right_edge], [total]
    )
    own_second, sent_own = call(
        second_own_kernel, (kept_shape, shape(2 * parts, pieces, rows, width)), 0,
        [lefts, right, right_edge, sent_own], [total],
    )
    came_own = exchange(sent_own, plan[0])
    staying = [(own_first, came_own, slice(0, parts)), (own_second, came_own, slice(parts, 2 * parts))]
    crossing = [(kept_first, came_first), (kept_second, came_second)]
    after = own_second
    for step in plan[1:]:
        for d, (kept, came) in enumerate(crossing):
            came, after = lax.optimization_barrier((came, after))
            crossing[d] = halve([(kept, came, None)], step, 4 * project_flops if d else 0)
            after = crossing[d][0]
    crossed = []
    for kept, came in crossing:
        came, after = lax.optimization_barrier((came, after))
        after = call(sum_kernel, pltpu.VMEM(kept.shape, bf16), 0, [kept, came])
        crossed.append(exchange(after, (top, top)))
    for step in plan[1:]:
        kept, came, which = staying[0]
        came, after = lax.optimization_barrier((came, after))
        sums = [(kept, came, which)] + [(k, came, w) for k, _, w in staying[1:]]
        kept, came = halve(sums, step)
        staying, after = [(kept, came, None)], kept
    kept, came, _ = staying[0]
    totals = []
    for d, block in enumerate(crossed):

        def cross(*refs, start=d * parts):
            cross_kernel(start, *refs)

        block, after = lax.optimization_barrier((block, after))
        after = call(cross, shape(*block.shape, dtype=f32), 4 * project_flops, [kept, block])
        totals.append(after)
    came, after = lax.optimization_barrier((came, after))
    return call(
        finish_kernel, jax.ShapeDtypeStruct((2, parts, rows, width), f32), 0, [came, *totals]
    )


def solution(mesh):
    return jax.shard_map(
        local,
        mesh=mesh,
        in_specs=(
            P("cuts", "gx", "gy", None, None, "ma"),
            P("cuts", None, None, "gx", "gy", None),
            P("cuts", None, None, "gx", "gy", None),
        ),
        out_specs=P("cuts", None, ("gx", "gy"), "ma"),
        check_vma=False,
    )
```

```python
import jax
import jax.numpy as jnp
from jax import lax
from jax.experimental import pallas as pl
from jax.experimental.pallas import tpu as pltpu
from jax.sharding import PartitionSpec as P

VMEM_LIMIT = 16 * 1024 * 1024


def shifted(block, axis, distance):
    devices = range(lax.axis_size(axis))
    route = [((i - distance) % len(devices), i) for i in devices]
    return lax.ppermute(block, axis, route)


def call(body, out_shape, flops, operands, scratch=(), places=None):
    places = places or [pltpu.VMEM] * len(operands)
    return pl.pallas_call(
        body,
        out_shape=out_shape,
        in_specs=[pl.BlockSpec(memory_space=place) for place in places],
        scratch_shapes=scratch,
        cost_estimate=pl.CostEstimate(flops=flops // 2, bytes_accessed=0, transcendentals=0),
        compiler_params=pltpu.CompilerParams(vmem_limit_bytes=VMEM_LIMIT),
    )(*(pltpu.with_memory_space_constraint(a, place) for a, place in zip(operands, places)))


def dot(a, b):
    return jnp.dot(a, b, preferred_element_type=jnp.float32)


def iotas(shape):
    return (
        lax.broadcasted_iota(jnp.int32, shape, 0),
        lax.broadcasted_iota(jnp.int32, shape, 1),
    )


def place_of(x, planes):
    return planes - 2 if x == 0 else x if x == planes - 1 else x - 1


def map_rows(parts, colours, planes, ys, zs):
    match = ys
    choose = match + -(-parts * colours * colours * planes * zs // 8) * 8
    first_part = choose + 2 * parts * planes * 8
    return match, choose, first_part, first_part + 8


def write_maps(ref, parts, colours, planes, ys, zs):
    lanes = ref.shape[1] // 2
    sites = ys * zs
    depth = parts * colours * sites
    row_size = parts * colours * zs
    match, choose, first_part, _ = map_rows(parts, colours, planes, ys, zs)

    def ones(mask):
        return jnp.where(mask, 1.0, 0.0)

    def column(count):
        return lax.broadcasted_iota(jnp.int32, (count, 1), 0)

    def line(count):
        return lax.broadcasted_iota(jnp.int32, (1, count), 1)

    lane = line(lanes)
    inner = lane < depth
    past = lax.rem(jnp.maximum(lane - depth, 0), row_size)
    used = lane < depth + 2 * row_size
    part = jnp.where(inner, lax.div(lane, colours * sites), lax.div(past, colours * zs))
    colour = lax.rem(jnp.where(inner, lax.div(lane, sites), lax.div(past, zs)), colours)
    z = lax.rem(jnp.where(inner, lane, past), zs)
    y = lax.div(lax.rem(lane, sites), zs)
    ref[:ys, :lanes] = ones(column(ys) == jnp.where(inner, y, ys - 1))
    ref[:ys, lanes:] = ones(column(ys) == jnp.where(inner, y, ys) - 1)

    count = parts * colours * colours * planes * zs

    def link(index):
        x = lax.rem(lax.div(index, zs), planes)
        right = lax.rem(lax.div(index, zs * planes), colours)
        left = lax.rem(lax.div(index, zs * planes * colours), colours)
        return x, right, left, lax.div(index, zs * planes * colours * colours)

    row = column(count)
    _, right, left, _ = link(row)
    row_z = lax.rem(row, zs)
    key = jnp.where(used, colour * zs + z, -1)
    ref[match : match + count, :lanes] = ones(right * zs + row_z == key)
    ref[match : match + count, lanes:] = ones(left * zs + row_z == key)

    out = column(parts * planes * 8)
    field_part = lax.div(out, planes * 8)
    out_x = lax.rem(lax.div(out, 8), planes)
    out_part = lax.div(lax.rem(out, 8), colours)
    out_colour = lax.rem(lax.rem(out, 8), colours)
    x, right, left, source_part = link(line(count))
    source = source_part * planes + x
    wanted = jnp.where(out_part < parts, lax.rem(out_part + field_part, 2) * planes + out_x, -1)
    sign_ahead = jnp.where((field_part == 1) & (out_part == 0), -1.0, 1.0)
    sign_back = jnp.where((field_part == 0) & (out_part == 1), 1.0, -1.0)
    half = parts * planes * 8
    for start, end, sign in ((choose, left, sign_ahead), (choose + half, right, sign_back)):
        hit = source * colours + end == wanted * colours + jnp.where(wanted < 0, -1, out_colour)
        ref[start : start + half, :count] = jnp.where(hit, sign, 0.0)
    ref[first_part:, :lanes] = jnp.broadcast_to(ones(part == 0), (8, lanes))


def coefficients(links_x, links_y, maps_ref, planes):
    lanes = maps_ref.shape[1] // 2
    ys = links_x.shape[1]
    count = links_x.shape[0]
    half = 2 * planes * 8
    wide = dot(jnp.concatenate([links_x, links_y], axis=0), maps_ref[:ys].astype(jnp.bfloat16))
    match = maps_ref[ys : ys + count]
    match_ahead, match_back = match[:, :lanes], match[:, lanes:]
    choose = maps_ref[ys + count : ys + count + 2 * half, :count].astype(jnp.bfloat16)
    first_part = maps_ref[ys + count + 2 * half : ys + count + 2 * half + 1, :lanes] > 0.5
    ahead = jnp.concatenate([wide[:count, :lanes] * match_ahead, wide[count:, lanes:] * match_ahead], axis=1)
    back = jnp.concatenate([wide[:count, :lanes] * match_back, wide[count:, :lanes] * match_back], axis=1)
    out = []
    for chosen in (
        dot(choose[:half], ahead.astype(jnp.bfloat16)), dot(choose[half:], back.astype(jnp.bfloat16))
    ):
        for start in (0, lanes):
            part = chosen[:, start : start + lanes]
            rows = jnp.where(first_part, part[: half // 2], part[half // 2 :])
            out.append(rows.reshape(planes, 8, lanes))
    return out


def plane_rows(ref, ys):
    parts, _, colours, zs, width = ref.shape
    return jnp.concatenate(
        [ref[p, :ys, c].reshape(ys * zs, width) for p in range(parts) for c in range(colours)],
        axis=0,
    )


def edges_kernel(
    raw_hbm, links_x_hbm, links_y_hbm,
    first_ref, last_ref, raw_ref, links_x_ref, links_y_ref, maps_ref, past_maps_ref, arrived,
):
    parts, planes, ys, colours, zs, _ = raw_hbm.shape
    sources = (raw_hbm.at[:, planes - 1], raw_hbm.at[:, 0], links_x_hbm, links_y_hbm, raw_hbm)
    targets = (last_ref.at[:, :ys], first_ref, links_x_ref, links_y_ref, raw_ref)
    copies = [
        pltpu.make_async_copy(source, target, arrived.at[i])
        for i, (source, target) in enumerate(zip(sources, targets))
    ]
    for copy in copies:
        copy.start()
    last_ref[:, ys:] = jnp.zeros((parts, colours) + last_ref.shape[2:], last_ref.dtype)
    write_maps(maps_ref, parts, colours, planes, ys, zs)
    write_maps(past_maps_ref, parts, colours, 1, ys, zs)
    copies[2].wait()
    last_ref[:, ys:, :, :, :ys] = links_x_ref[:, :, :, planes - 1]
    for copy in copies[:2] + copies[3:]:
        copy.wait()


def site_matrix(rows_and_masks, count):
    blocks = []
    for q in range(count):
        block = None
        for rows, mask in rows_and_masks:
            term = rows[q : q + 1] * mask
            block = term if block is None else block + term
        blocks.append(block.astype(jnp.bfloat16))
    return jnp.concatenate(blocks, axis=0)


def prepare_kernel(
    raw_ref, links_x_ref, links_y_ref, maps_ref,
    rows_ref, ends_ref, ahead_x_ref, back_x_ref, ahead_y_ref, back_y_ref,
):
    planes, depth, width = rows_ref.shape
    zs = raw_ref.shape[4]
    ys = raw_ref.shape[2]
    sites = ys * zs
    row_size = depth // sites * zs
    lanes = ahead_y_ref.shape[2]
    ahead_x, ahead_y, back_x, back_y = coefficients(
        links_x_ref[...].reshape(-1, ys), links_y_ref[...].reshape(-1, ys), maps_ref, planes
    )
    ahead_x_ref[...] = ahead_x
    back_x_ref[...] = back_x
    ahead_y_ref[...] = ahead_y
    back_y_ref[...] = back_y

    row, lane = iotas((2 * row_size, depth))
    spot = row % row_size
    wanted = (spot // zs) * sites + spot % zs + jnp.where(row < row_size, 0, sites - zs)
    ends = (lane == wanted).astype(jnp.bfloat16)
    filler = jnp.zeros((8, width - 128), jnp.float32)
    spare = ends_ref.shape[1] - 2 * row_size - 8
    for x in range(planes):
        plane = plane_rows(raw_ref.at[:, x], ys)
        rows_ref[place_of(x, planes)] = plane
        tail = jnp.concatenate([back_y[x, :, lanes - 128 :], filler], axis=1)
        pieces = [dot(ends, plane), tail]
        if spare:
            pieces.append(jnp.zeros((spare, width), jnp.float32))
        ends_ref[x] = jnp.concatenate(pieces, axis=0).astype(jnp.bfloat16)


def turn_kernel(raw_ref, rows_ref, turned_ref):
    planes, depth, width = rows_ref.shape
    for x in range(planes):
        rows_ref[place_of(x, planes)] = plane_rows(raw_ref.at[:, x], raw_ref.shape[2])
    turned_ref[...] = rows_ref[...].reshape(planes * depth, width).T


def move_plane(same, count, ahead, back, above, below):
    depth = same.shape[1]
    moved = dot(site_matrix([(ahead[:, :depth], same)], count), above)
    return (moved + dot(site_matrix([(back[:, :depth], same)], count), below)).astype(jnp.bfloat16)


def same_site(sites, depth):
    site, lane = iotas((sites, depth))
    return (lane % sites == site).astype(jnp.float32)


def set_right(right_ref, place, moved):
    depth, width = moved.shape
    half = depth // 2
    start = place * depth
    real, imag = moved[:half], moved[half:]
    right_ref[start : start + half, :width] = real
    right_ref[start : start + half, width:] = imag
    right_ref[start + half : start + depth, :width] = imag
    right_ref[start + half : start + depth, width:] = -real


def inner_kernel(
    sites, rows_ref, ahead_ref, back_ref, right_ref, turned_ref, matrix_ref, ahead_part_ref, back_part_ref
):
    planes, depth, width = rows_ref.shape
    same = same_site(sites, depth)
    for x in range(1, planes - 1):
        above = rows_ref[place_of(x + 1, planes)]
        below = rows_ref[place_of(x - 1, planes)]
        moved = move_plane(same, depth // sites, ahead_ref[x], back_ref[x - 1], above, below)
        set_right(right_ref, place_of(x, planes), moved)
    turned_ref[...] = rows_ref[...].reshape(planes * depth, width).T
    x, count = planes - 1, depth // sites
    matrix_ref[...] = site_matrix([(ahead_ref[x, :, :depth], same)], count)
    ahead_part_ref[...] = dot(site_matrix([(ahead_ref[0, :, :depth], same)], count), rows_ref[place_of(1, planes)])
    below = rows_ref[place_of(x - 1, planes)]
    back_part_ref[...] = dot(site_matrix([(back_ref[x - 1, :, :depth], same)], count), below)


def begin_first_kernel(own_ref, others_ref, right_ref, total_ref):
    inner = right_ref.shape[0]
    right = right_ref[...]
    total_ref[0] = dot(own_ref[:, :inner], right)
    for k in range(others_ref.shape[0]):
        total_ref[k + 1] = dot(others_ref[k, :, :inner], right)


def bits(axis):
    return range(lax.axis_size(axis).bit_length() - 1)


def steps():
    one = [("gx", bit) for bit in bits("gx")[:-1]]
    two = [("gy", bit) for bit in bits("gy")]
    both = min(len(one), len(two))
    pairs = [pair for ends in zip(two, one) for pair in (ends, ends[::-1])]
    return pairs + [(step, step) for step in one[both:] + two[both:]]


def my_bit(axis, bit):
    return lax.bitwise_and(lax.shift_right_logical(lax.axis_index(axis), bit), 1)


def my_side(step):
    even, odd = (my_bit(*way) for way in step)
    return jnp.where(my_bit("ma", 0) == 0, even, odd)


def half_of(kind):
    half = lax.bitwise_xor(my_bit("gx", bits("gx")[-1]), 1 - kind)
    return lax.bitwise_xor(half, lax.axis_index("ma"))


def share(total, keep_ref, send_ref, total_ref):
    blocks, rows, double = total_ref.shape
    parts, count, _, width = keep_ref.shape
    total_ref[...] = total.reshape(blocks, rows, double)
    odd_core = my_bit("ma", 0)
    across_y = lax.axis_size("gy")
    plan = steps()
    mine = my_side(plan[0])

    def at(side, index):
        owners = []
        for core in range(2):
            place = {"gx": 0, "gy": 0}
            for k, step in enumerate(plan):
                axis, bit = step[core]
                digit = side if k == 0 else index >> (len(plan) - 1 - k) & 1
                place[axis] += digit * (1 << bit)
            owners.append(place["gx"] * across_y + place["gy"])
        return jnp.where(odd_core == 0, owners[0], owners[1])

    for index in range(count):
        for ref, side in ((keep_ref, mine), (send_ref, 1 - mine)):
            block = total_ref[at(side, index)].astype(ref.dtype)
            for p in range(parts):
                ref[p, index] = block[:, p * width : (p + 1) * width]


def first_share(kind, own_ref, others_ref, begun_ref, right, keep_ref, send_ref, total_ref):
    half = half_of(kind)
    inner = own_ref.shape[1] - right.shape[0]
    left = jnp.where(half == 0, own_ref[:, inner:], others_ref[0, :, inner:])
    share(begun_ref[half] + dot(left, right), keep_ref, send_ref, total_ref)


def first_kernel(
    sites, high_ref, low_ref, matrix_ref, ahead_part_ref, back_part_ref, past_maps_ref, own_ref, others_ref, begun_ref,
    *refs,
):
    keep_ref, send_ref, right_ref, total_ref = refs
    depth = matrix_ref.shape[0]
    same = same_site(sites, depth)
    _, ys, colours, zs, _ = high_ref.shape
    links = low_ref[:, ys:, :, :, :ys].reshape(-1, ys)
    lanes = past_maps_ref.shape[1] // 2
    count = links.shape[0]
    spread = past_maps_ref[:ys, :lanes].astype(jnp.bfloat16)
    match = past_maps_ref[ys : ys + count, lanes:]
    start = past_maps_ref.shape[0] - 24
    choose = past_maps_ref[start : start + 16, :count].astype(jnp.bfloat16)
    past = dot(choose, (dot(links, spread) * match).astype(jnp.bfloat16))
    past = jnp.where(past_maps_ref[start + 16 : start + 17, :lanes] > 0.5, past[:8], past[8:])
    past = site_matrix([(past[:, :depth], same)], depth // sites)
    moved = ahead_part_ref[...] + dot(past, plane_rows(low_ref, ys))
    set_right(right_ref, 0, moved.astype(jnp.bfloat16))
    moved = dot(matrix_ref[...], plane_rows(high_ref, ys)) + back_part_ref[...]
    set_right(right_ref, 1, moved.astype(jnp.bfloat16))
    first_share(0, own_ref, others_ref, begun_ref, right_ref[...], keep_ref, send_ref, total_ref)


def first_own_kernel(own_ref, others_ref, begun_ref, right_ref, keep_ref, send_ref, total_ref):
    first_share(1, own_ref, others_ref, begun_ref, right_ref[...], keep_ref, send_ref, total_ref)


def begin_y_kernel(sites, zs, rows_ref, others_ref, ahead_ref, back_ref, part_ref):
    planes, depth, _ = rows_ref.shape
    site, lane = iotas((sites, depth))
    to_next = jnp.where(lane % sites == site + zs, -1.0, 0.0)
    to_last = jnp.where(lane % sites == site - zs, -1.0, 0.0)
    for x in range(planes):
        ahead, back = ahead_ref[x, :, :depth], back_ref[x, :, :depth]
        matrix = site_matrix([(ahead, to_next), (back, to_last)], depth // sites)
        place = place_of(x, planes)
        part_ref[0, place] = dot(matrix, rows_ref[place])
        for k in range(others_ref.shape[0]):
            part_ref[k + 1, place] = dot(matrix, others_ref[k, place])


def move_y_kernel(sites, zs, part_ref, near_ref, far_ref, ahead_ref, turned_ref, field_ref):
    groups, planes, depth, width = part_ref.shape
    row_size = depth // sites * zs
    tail = 128
    head = ahead_ref.shape[2] - tail
    site, lane = iotas((sites, tail))
    lane = lane + head
    upper = (lane >= depth) & (lane < depth + row_size)
    lower = (lane >= depth + row_size) & (lane < depth + 2 * row_size)
    to_next = jnp.where(upper & (site == sites - zs + lane % zs), -1.0, 0.0)
    to_last = jnp.where(lower & (site == lane % zs), -1.0, 0.0)
    above = jnp.zeros((depth - head, width), jnp.float32)
    below = jnp.zeros((tail - 2 * row_size - (depth - head), width), jnp.float32)
    for x in range(planes):
        near = near_ref[x].astype(jnp.float32)
        past = near[2 * row_size : 2 * row_size + 8, :tail]
        matrix = site_matrix([(ahead_ref[x, :, head:], to_next), (past, to_last)], depth // sites)
        place = place_of(x, planes)
        for k in range(groups):
            edge = near[: 2 * row_size] if k == 0 else far_ref[k - 1, x].astype(jnp.float32)
            column = jnp.concatenate([above, edge, below], axis=0).astype(jnp.bfloat16)
            field_ref[k, place] = (part_ref[k, place] + dot(matrix, column)).astype(jnp.bfloat16)
    for k in range(groups):
        turned_ref[k] = field_ref[k].reshape(planes * depth, width).T


def second_share(kind, lefts_ref, right_ref, edge_ref, keep_ref, send_ref, total_ref):
    half = half_of(kind)
    inner = right_ref.shape[0]
    total = dot(lefts_ref[half, :, :inner], right_ref[...]) + dot(lefts_ref[half, :, inner:], edge_ref[...])
    share(total, keep_ref, send_ref, total_ref)


def second_kernel(lefts_ref, right_ref, edge_ref, keep_ref, send_ref, total_ref):
    second_share(0, lefts_ref, right_ref, edge_ref, keep_ref, send_ref, total_ref)


def second_own_kernel(lefts_ref, right_ref, edge_ref, first_ref, keep_ref, send_ref, total_ref):
    parts = first_ref.shape[0]
    send_ref[:parts] = first_ref[...]
    second_share(1, lefts_ref, right_ref, edge_ref, keep_ref, send_ref.at[parts:], total_ref)


def exchange(block, step):
    axes = ("gx", "gy", "ma")
    sizes = [lax.axis_size(axis) for axis in axes]
    route = []
    for source in range(sizes[0] * sizes[1] * sizes[2]):
        where = [source // (sizes[1] * sizes[2]), source // sizes[2] % sizes[1], source % sizes[2]]
        axis, bit = step[where[2] % 2]
        where[axes.index(axis)] ^= 1 << bit
        route.append((source, (where[0] * sizes[1] + where[1]) * sizes[2] + where[2]))
    return lax.ppermute(block, axes, route)


def halve(sums, step, weight=0):
    parts = sum(kept.shape[0] for kept, _, _ in sums)
    count, rows, width = sums[0][0].shape[1:]
    dims = (parts, count // 2, rows, width)

    def merge(*refs):
        *refs, keep_ref, send_ref = refs
        mine = my_side(step)
        start = 0
        for k, (_, _, which) in enumerate(sums):
            kept_ref, came_ref = refs[2 * k : 2 * k + 2]
            came_ref = came_ref if which is None else came_ref.at[which]
            end = start + kept_ref.shape[0]
            for index in range(count // 2):
                low, high = (
                    kept_ref[:, at] + came_ref[:, at].astype(jnp.float32) for at in (index, index + count // 2)
                )
                keep_ref[start:end, index] = jnp.where(mine == 0, low, high)
                send_ref[start:end, index] = jnp.where(mine == 0, high, low).astype(send_ref.dtype)
            start = end

    operands = [a for kept, came, _ in sums for a in (kept, came)]
    keep, send = call(merge, (pltpu.VMEM(dims, jnp.float32), pltpu.VMEM(dims, jnp.bfloat16)), weight, operands)
    return keep, exchange(send, step)


def sum_kernel(kept_ref, came_ref, send_ref):
    send_ref[...] = (kept_ref[...] + came_ref[...].astype(jnp.float32)).astype(send_ref.dtype)


def cross_kernel(start, kept_ref, crossed_ref, out_ref):
    kept = kept_ref[start : start + out_ref.shape[0]]
    out_ref[...] = kept + crossed_ref[...].astype(jnp.float32)


def finish_kernel(came_ref, *refs):
    *kept_refs, out_ref = refs
    parts = out_ref.shape[1]
    for d, kept_ref in enumerate(kept_refs):
        out_ref[d] = kept_ref[:, 0] + came_ref[d * parts : (d + 1) * parts, 0].astype(jnp.float32)


def local(eigen_modes, links_first, links_second):
    f32, bf16 = jnp.float32, jnp.bfloat16
    parts, planes, ys, zs, colours, width = eigen_modes.shape
    sites = ys * zs
    depth = parts * colours * sites
    row_size = parts * colours * zs
    edge = -(-(2 * row_size + 8) // 16) * 16
    lanes = -(-(depth + 2 * row_size) // 128) * 128
    across_x, across_y, groups = (lax.axis_size(a) for a in ("gx", "gy", "ma"))
    rows = groups * width // (across_x * across_y)
    inner_depth = (planes - 2) * depth
    raw = eigen_modes.transpose(0, 1, 2, 4, 3, 5)

    def shape(*dims, dtype=bf16):
        return pltpu.VMEM(dims, dtype)

    field_shape = shape(planes, depth, width)
    turned_shape = shape(width, planes * depth)
    total_shape = shape(groups, width, parts * width, dtype=f32)
    link_shape = shape(planes, 8, lanes, dtype=f32)
    total = pltpu.VMEM((width // rows, rows, parts * width), f32)
    step_flops = 2 * planes * depth * depth * width
    project_flops = 2 * groups * width * planes * depth * parts * width

    raw_others = [shifted(raw, "ma", -step) for step in range(1, groups)]
    raw_links_x, raw_links_y = (a.transpose(0, 1, 2, 3, 5, 4) for a in (links_first, links_second))
    inputs = [raw, raw_links_x, raw_links_y]
    first_plane, last_plane, *inputs, past_maps = call(
        edges_kernel,
        (
            shape(parts, ys, colours, zs, width), shape(parts, ys + colours, colours, zs, width),
            *(shape(*a.shape) for a in inputs),
            shape(map_rows(parts, colours, planes, ys, zs)[-1], 2 * lanes, dtype=f32),
            shape(map_rows(parts, colours, 1, ys, zs)[-1], 2 * lanes, dtype=f32),
        ),
        0,
        inputs,
        [pltpu.SemaphoreType.DMA((5,))],
        [pltpu.HBM] * len(inputs),
    )
    low = shifted(last_plane, "gx", 1)
    high = shifted(first_plane, "gx", -1)
    field, ends, ahead_x, back_x, ahead_y, back_y = call(
        prepare_kernel,
        (field_shape, shape(planes, edge, width), link_shape, link_shape, link_shape, link_shape),
        0,
        inputs,
    )
    near = shifted(ends, "gy", 1)
    if across_y != 2:
        ahead_row = lax.broadcasted_iota(jnp.int32, ends.shape, 1) < row_size
        near = jnp.where(ahead_row, shifted(ends, "gy", -1), near)

    plan = steps()
    top = ("gx", bits("gx")[-1])
    pieces = across_x * across_y // 4
    kept_shape = shape(parts, pieces, rows, width, dtype=f32)
    sent_shape = shape(parts, pieces, rows, width)

    def inner(*refs):
        inner_kernel(sites, *refs)

    def first(*refs):
        first_kernel(sites, *refs)

    def begin_y(*refs):
        begin_y_kernel(sites, zs, *refs)

    def move_y(*refs):
        move_y_kernel(sites, zs, *refs)

    right, own, matrix, ahead_part, back_part = call(
        inner,
        (
            shape(inner_depth, parts * width), turned_shape, shape(depth, depth),
            shape(depth, width, dtype=f32), shape(depth, width, dtype=f32),
        ),
        2 * step_flops,
        [field, ahead_x, back_x],
    )
    turned = [call(turn_kernel, (field_shape, turned_shape), step_flops // 4, [r]) for r in raw_others]
    fields = jnp.stack([t[0] for t in turned])
    others = jnp.stack([t[1] for t in turned])
    begun_first = call(begin_first_kernel, total_shape, project_flops, [own, others, right])
    part_y = call(
        begin_y, shape(groups, planes, depth, width, dtype=f32), 2 * step_flops, [field, fields, ahead_y, back_y]
    )
    part_y, begun_first = lax.optimization_barrier((part_y, begun_first))
    kept_first, sent_first, right_edge = call(
        first,
        (kept_shape, sent_shape, shape(2 * depth, parts * width)),
        project_flops,
        [high, low, matrix, ahead_part, back_part, past_maps, own, others, begun_first],
        [total],
    )
    came_first = exchange(sent_first, plan[0])
    near, right_edge = lax.optimization_barrier((near, right_edge))
    near_rows = near[:, : 2 * row_size]
    far = jnp.stack([shifted(near_rows, "ma", -step) for step in range(1, groups)])
    lefts = call(
        move_y, shape(groups, width, planes * depth), 2 * step_flops,
        [part_y, near, far, ahead_y],
        [pltpu.VMEM((groups,) + field_shape.shape, bf16)],
    )
    kept_second, sent_second = call(
        second_kernel, (kept_shape, sent_shape), 8 * project_flops, [lefts, right, right_edge], [total]
    )
    came_second = exchange(sent_second, plan[0])
    right_edge, kept_second = lax.optimization_barrier((right_edge, kept_second))
    own_first, sent_own = call(
        first_own_kernel, (kept_shape, sent_shape), 0, [own, others, begun_first, right_edge], [total]
    )
    own_second, sent_own = call(
        second_own_kernel, (kept_shape, shape(2 * parts, pieces, rows, width)), 0,
        [lefts, right, right_edge, sent_own], [total],
    )
    came_own = exchange(sent_own, plan[0])
    staying = [(own_first, came_own, slice(0, parts)), (own_second, came_own, slice(parts, 2 * parts))]
    crossing = [(kept_first, came_first), (kept_second, came_second)]
    after = own_second
    for step in plan[1:]:
        for d, (kept, came) in enumerate(crossing):
            came, after = lax.optimization_barrier((came, after))
            crossing[d] = halve([(kept, came, None)], step, 4 * project_flops if d else 0)
            after = crossing[d][0]
    crossed = []
    for kept, came in crossing:
        came, after = lax.optimization_barrier((came, after))
        after = call(sum_kernel, pltpu.VMEM(kept.shape, bf16), 0, [kept, came])
        crossed.append(exchange(after, (top, top)))
    for step in plan[1:]:
        kept, came, which = staying[0]
        came, after = lax.optimization_barrier((came, after))
        sums = [(kept, came, which)] + [(k, came, w) for k, _, w in staying[1:]]
        kept, came = halve(sums, step)
        staying, after = [(kept, came, None)], kept
    kept, came, _ = staying[0]
    totals = []
    for d, block in enumerate(crossed):

        def cross(*refs, start=d * parts):
            cross_kernel(start, *refs)

        block, after = lax.optimization_barrier((block, after))
        after = call(cross, shape(*block.shape, dtype=f32), 4 * project_flops, [kept, block])
        totals.append(after)
    came, after = lax.optimization_barrier((came, after))
    return call(
        finish_kernel, jax.ShapeDtypeStruct((2, parts, rows, width), f32), 0, [came, *totals]
    )


def solution(mesh):
    return jax.shard_map(
        local,
        mesh=mesh,
        in_specs=(
            P("cuts", "gx", "gy", None, None, "ma"),
            P("cuts", None, None, "gx", "gy", None),
            P("cuts", None, None, "gx", "gy", None),
        ),
        out_specs=P("cuts", None, ("gx", "gy"), "ma"),
        check_vma=False,
    )
```

```python
import jax
import jax.numpy as jnp
from jax import lax
from jax.experimental import pallas as pl
from jax.experimental.pallas import tpu as pltpu
from jax.sharding import PartitionSpec as P

VMEM_LIMIT = 16 * 1024 * 1024


def shifted(block, axis, distance):
    devices = range(lax.axis_size(axis))
    route = [((i - distance) % len(devices), i) for i in devices]
    return lax.ppermute(block, axis, route)


def call(body, out_shape, flops, operands, scratch=(), places=None):
    places = places or [pltpu.VMEM] * len(operands)
    return pl.pallas_call(
        body,
        out_shape=out_shape,
        in_specs=[pl.BlockSpec(memory_space=place) for place in places],
        scratch_shapes=scratch,
        cost_estimate=pl.CostEstimate(flops=flops // 2, bytes_accessed=0, transcendentals=0),
        compiler_params=pltpu.CompilerParams(vmem_limit_bytes=VMEM_LIMIT),
    )(*(pltpu.with_memory_space_constraint(a, place) for a, place in zip(operands, places)))


def dot(a, b):
    return jnp.dot(a, b, preferred_element_type=jnp.float32)


def iotas(shape):
    return (
        lax.broadcasted_iota(jnp.int32, shape, 0),
        lax.broadcasted_iota(jnp.int32, shape, 1),
    )


def place_of(x, planes):
    return planes - 2 if x == 0 else x if x == planes - 1 else x - 1


def map_rows(parts, colours, planes, ys, zs):
    match = ys
    choose = match + -(-parts * colours * colours * planes * zs // 8) * 8
    first_part = choose + 2 * parts * planes * 8
    return match, choose, first_part, first_part + 8


def write_maps(ref, parts, colours, planes, ys, zs):
    lanes = ref.shape[1] // 2
    sites = ys * zs
    depth = parts * colours * sites
    row_size = parts * colours * zs
    match, choose, first_part, _ = map_rows(parts, colours, planes, ys, zs)

    def ones(mask):
        return jnp.where(mask, 1.0, 0.0)

    def column(count):
        return lax.broadcasted_iota(jnp.int32, (count, 1), 0)

    def line(count):
        return lax.broadcasted_iota(jnp.int32, (1, count), 1)

    lane = line(lanes)
    inner = lane < depth
    past = lax.rem(jnp.maximum(lane - depth, 0), row_size)
    used = lane < depth + 2 * row_size
    part = jnp.where(inner, lax.div(lane, colours * sites), lax.div(past, colours * zs))
    colour = lax.rem(jnp.where(inner, lax.div(lane, sites), lax.div(past, zs)), colours)
    z = lax.rem(jnp.where(inner, lane, past), zs)
    y = lax.div(lax.rem(lane, sites), zs)
    ref[:ys, :lanes] = ones(column(ys) == jnp.where(inner, y, ys - 1))
    ref[:ys, lanes:] = ones(column(ys) == jnp.where(inner, y, ys) - 1)

    count = parts * colours * colours * planes * zs

    def link(index):
        x = lax.rem(lax.div(index, zs), planes)
        right = lax.rem(lax.div(index, zs * planes), colours)
        left = lax.rem(lax.div(index, zs * planes * colours), colours)
        return x, right, left, lax.div(index, zs * planes * colours * colours)

    row = column(count)
    _, right, left, _ = link(row)
    row_z = lax.rem(row, zs)
    key = jnp.where(used, colour * zs + z, -1)
    ref[match : match + count, :lanes] = ones(right * zs + row_z == key)
    ref[match : match + count, lanes:] = ones(left * zs + row_z == key)

    out = column(parts * planes * 8)
    field_part = lax.div(out, planes * 8)
    out_x = lax.rem(lax.div(out, 8), planes)
    out_part = lax.div(lax.rem(out, 8), colours)
    out_colour = lax.rem(lax.rem(out, 8), colours)
    x, right, left, source_part = link(line(count))
    source = source_part * planes + x
    wanted = jnp.where(out_part < parts, lax.rem(out_part + field_part, 2) * planes + out_x, -1)
    sign_ahead = jnp.where((field_part == 1) & (out_part == 0), -1.0, 1.0)
    sign_back = jnp.where((field_part == 0) & (out_part == 1), 1.0, -1.0)
    half = parts * planes * 8
    for start, end, sign in ((choose, left, sign_ahead), (choose + half, right, sign_back)):
        hit = source * colours + end == wanted * colours + jnp.where(wanted < 0, -1, out_colour)
        ref[start : start + half, :count] = jnp.where(hit, sign, 0.0)
    ref[first_part:, :lanes] = jnp.broadcast_to(ones(part == 0), (8, lanes))


def coefficients(links_x, links_y, maps_ref, planes):
    lanes = maps_ref.shape[1] // 2
    ys = links_x.shape[1]
    count = links_x.shape[0]
    half = 2 * planes * 8
    wide = dot(jnp.concatenate([links_x, links_y], axis=0), maps_ref[:ys].astype(jnp.bfloat16))
    match = maps_ref[ys : ys + count]
    match_ahead, match_back = match[:, :lanes], match[:, lanes:]
    choose = maps_ref[ys + count : ys + count + 2 * half, :count].astype(jnp.bfloat16)
    first_part = maps_ref[ys + count + 2 * half : ys + count + 2 * half + 1, :lanes] > 0.5
    ahead = jnp.concatenate([wide[:count, :lanes] * match_ahead, wide[count:, lanes:] * match_ahead], axis=1)
    back = jnp.concatenate([wide[:count, :lanes] * match_back, wide[count:, :lanes] * match_back], axis=1)
    out = []
    for chosen in (
        dot(choose[:half], ahead.astype(jnp.bfloat16)), dot(choose[half:], back.astype(jnp.bfloat16))
    ):
        for start in (0, lanes):
            part = chosen[:, start : start + lanes]
            rows = jnp.where(first_part, part[: half // 2], part[half // 2 :])
            out.append(rows.reshape(planes, 8, lanes))
    return out


def plane_rows(ref, ys):
    parts, _, colours, zs, width = ref.shape
    return jnp.concatenate(
        [ref[p, :ys, c].reshape(ys * zs, width) for p in range(parts) for c in range(colours)],
        axis=0,
    )


def edges_kernel(
    raw_hbm, links_x_hbm, links_y_hbm,
    first_ref, last_ref, raw_ref, links_x_ref, links_y_ref, maps_ref, past_maps_ref, arrived,
):
    parts, planes, ys, colours, zs, _ = raw_hbm.shape
    sources = (raw_hbm.at[:, planes - 1], raw_hbm.at[:, 0], links_x_hbm, links_y_hbm, raw_hbm)
    targets = (last_ref.at[:, :ys], first_ref, links_x_ref, links_y_ref, raw_ref)
    copies = [
        pltpu.make_async_copy(source, target, arrived.at[i])
        for i, (source, target) in enumerate(zip(sources, targets))
    ]
    for copy in copies:
        copy.start()
    last_ref[:, ys:] = jnp.zeros((parts, colours) + last_ref.shape[2:], last_ref.dtype)
    write_maps(maps_ref, parts, colours, planes, ys, zs)
    write_maps(past_maps_ref, parts, colours, 1, ys, zs)
    copies[2].wait()
    last_ref[:, ys:, :, :, :ys] = links_x_ref[:, :, :, planes - 1]
    for copy in copies[:2] + copies[3:]:
        copy.wait()


def site_matrix(rows_and_masks, count):
    blocks = []
    for q in range(count):
        block = None
        for rows, mask in rows_and_masks:
            term = rows[q : q + 1] * mask
            block = term if block is None else block + term
        blocks.append(block.astype(jnp.bfloat16))
    return jnp.concatenate(blocks, axis=0)


def prepare_kernel(
    raw_ref, links_x_ref, links_y_ref, maps_ref,
    rows_ref, ends_ref, ahead_x_ref, back_x_ref, ahead_y_ref, back_y_ref,
):
    planes, depth, width = rows_ref.shape
    zs = raw_ref.shape[4]
    ys = raw_ref.shape[2]
    sites = ys * zs
    row_size = depth // sites * zs
    lanes = ahead_y_ref.shape[2]
    ahead_x, ahead_y, back_x, back_y = coefficients(
        links_x_ref[...].reshape(-1, ys), links_y_ref[...].reshape(-1, ys), maps_ref, planes
    )
    ahead_x_ref[...] = ahead_x
    back_x_ref[...] = back_x
    ahead_y_ref[...] = ahead_y
    back_y_ref[...] = back_y

    row, lane = iotas((2 * row_size, depth))
    spot = row % row_size
    wanted = (spot // zs) * sites + spot % zs + jnp.where(row < row_size, 0, sites - zs)
    ends = (lane == wanted).astype(jnp.bfloat16)
    filler = jnp.zeros((8, width - 128), jnp.float32)
    spare = ends_ref.shape[1] - 2 * row_size - 8
    for x in range(planes):
        plane = plane_rows(raw_ref.at[:, x], ys)
        rows_ref[place_of(x, planes)] = plane
        tail = jnp.concatenate([back_y[x, :, lanes - 128 :], filler], axis=1)
        pieces = [dot(ends, plane), tail]
        if spare:
            pieces.append(jnp.zeros((spare, width), jnp.float32))
        ends_ref[x] = jnp.concatenate(pieces, axis=0).astype(jnp.bfloat16)


def turn_kernel(raw_ref, rows_ref, turned_ref):
    planes, depth, width = rows_ref.shape
    for x in range(planes):
        rows_ref[place_of(x, planes)] = plane_rows(raw_ref.at[:, x], raw_ref.shape[2])
    turned_ref[...] = rows_ref[...].reshape(planes * depth, width).T


def move_plane(same, count, ahead, back, above, below):
    depth = same.shape[1]
    moved = dot(site_matrix([(ahead[:, :depth], same)], count), above)
    return (moved + dot(site_matrix([(back[:, :depth], same)], count), below)).astype(jnp.bfloat16)


def same_site(sites, depth):
    site, lane = iotas((sites, depth))
    return (lane % sites == site).astype(jnp.float32)


def set_right(right_ref, place, moved):
    depth, width = moved.shape
    half = depth // 2
    start = place * depth
    real, imag = moved[:half], moved[half:]
    right_ref[start : start + half, :width] = real
    right_ref[start : start + half, width:] = imag
    right_ref[start + half : start + depth, :width] = imag
    right_ref[start + half : start + depth, width:] = -real


def inner_kernel(
    sites, rows_ref, ahead_ref, back_ref, right_ref, turned_ref, matrix_ref, ahead_part_ref, back_part_ref
):
    planes, depth, width = rows_ref.shape
    same = same_site(sites, depth)
    for x in range(1, planes - 1):
        above = rows_ref[place_of(x + 1, planes)]
        below = rows_ref[place_of(x - 1, planes)]
        moved = move_plane(same, depth // sites, ahead_ref[x], back_ref[x - 1], above, below)
        set_right(right_ref, place_of(x, planes), moved)
    turned_ref[...] = rows_ref[...].reshape(planes * depth, width).T
    x, count = planes - 1, depth // sites
    matrix_ref[...] = site_matrix([(ahead_ref[x, :, :depth], same)], count)
    ahead_part_ref[...] = dot(site_matrix([(ahead_ref[0, :, :depth], same)], count), rows_ref[place_of(1, planes)])
    below = rows_ref[place_of(x - 1, planes)]
    back_part_ref[...] = dot(site_matrix([(back_ref[x - 1, :, :depth], same)], count), below)


def begin_first_kernel(own_ref, others_ref, right_ref, total_ref):
    inner = right_ref.shape[0]
    right = right_ref[...]
    total_ref[0] = dot(own_ref[:, :inner], right)
    for k in range(others_ref.shape[0]):
        total_ref[k + 1] = dot(others_ref[k, :, :inner], right)


def bits(axis):
    return range(lax.axis_size(axis).bit_length() - 1)


def steps():
    one = [("gx", bit) for bit in bits("gx")[:-1]]
    two = [("gy", bit) for bit in bits("gy")]
    both = min(len(one), len(two))
    pairs = [pair for ends in zip(one, two) for pair in (ends, ends[::-1])]
    return pairs + [(step, step) for step in one[both:] + two[both:]]


def my_bit(axis, bit):
    return lax.bitwise_and(lax.shift_right_logical(lax.axis_index(axis), bit), 1)


def my_side(step):
    even, odd = (my_bit(*way) for way in step)
    return jnp.where(my_bit("ma", 0) == 0, even, odd)


def half_of(kind):
    half = lax.bitwise_xor(my_bit("gx", bits("gx")[-1]), 1 - kind)
    return lax.bitwise_xor(half, lax.axis_index("ma"))


def share(total, keep_ref, send_ref, total_ref):
    blocks, rows, double = total_ref.shape
    parts, count, _, width = keep_ref.shape
    total_ref[...] = total.reshape(blocks, rows, double)
    odd_core = my_bit("ma", 0)
    across_y = lax.axis_size("gy")
    plan = steps()
    mine = my_side(plan[0])

    def at(side, index):
        owners = []
        for core in range(2):
            place = {"gx": 0, "gy": 0}
            for k, step in enumerate(plan):
                axis, bit = step[core]
                digit = side if k == 0 else index >> (len(plan) - 1 - k) & 1
                place[axis] += digit * (1 << bit)
            owners.append(place["gx"] * across_y + place["gy"])
        return jnp.where(odd_core == 0, owners[0], owners[1])

    for index in range(count):
        for ref, side in ((keep_ref, mine), (send_ref, 1 - mine)):
            block = total_ref[at(side, index)].astype(ref.dtype)
            for p in range(parts):
                ref[p, index] = block[:, p * width : (p + 1) * width]


def first_share(kind, own_ref, others_ref, begun_ref, right, keep_ref, send_ref, total_ref):
    half = half_of(kind)
    inner = own_ref.shape[1] - right.shape[0]
    left = jnp.where(half == 0, own_ref[:, inner:], others_ref[0, :, inner:])
    share(begun_ref[half] + dot(left, right), keep_ref, send_ref, total_ref)


def first_kernel(
    sites, high_ref, low_ref, matrix_ref, ahead_part_ref, back_part_ref, past_maps_ref, own_ref, others_ref, begun_ref,
    *refs,
):
    keep_ref, send_ref, right_ref, total_ref = refs
    depth = matrix_ref.shape[0]
    same = same_site(sites, depth)
    _, ys, colours, zs, _ = high_ref.shape
    links = low_ref[:, ys:, :, :, :ys].reshape(-1, ys)
    lanes = past_maps_ref.shape[1] // 2
    count = links.shape[0]
    spread = past_maps_ref[:ys, :lanes].astype(jnp.bfloat16)
    match = past_maps_ref[ys : ys + count, lanes:]
    start = past_maps_ref.shape[0] - 24
    choose = past_maps_ref[start : start + 16, :count].astype(jnp.bfloat16)
    past = dot(choose, (dot(links, spread) * match).astype(jnp.bfloat16))
    past = jnp.where(past_maps_ref[start + 16 : start + 17, :lanes] > 0.5, past[:8], past[8:])
    past = site_matrix([(past[:, :depth], same)], depth // sites)
    moved = ahead_part_ref[...] + dot(past, plane_rows(low_ref, ys))
    set_right(right_ref, 0, moved.astype(jnp.bfloat16))
    moved = dot(matrix_ref[...], plane_rows(high_ref, ys)) + back_part_ref[...]
    set_right(right_ref, 1, moved.astype(jnp.bfloat16))
    first_share(0, own_ref, others_ref, begun_ref, right_ref[...], keep_ref, send_ref, total_ref)


def first_own_kernel(own_ref, others_ref, begun_ref, right_ref, keep_ref, send_ref, total_ref):
    first_share(1, own_ref, others_ref, begun_ref, right_ref[...], keep_ref, send_ref, total_ref)


def begin_y_kernel(sites, zs, rows_ref, others_ref, ahead_ref, back_ref, part_ref):
    planes, depth, _ = rows_ref.shape
    site, lane = iotas((sites, depth))
    to_next = jnp.where(lane % sites == site + zs, -1.0, 0.0)
    to_last = jnp.where(lane % sites == site - zs, -1.0, 0.0)
    for x in range(planes):
        ahead, back = ahead_ref[x, :, :depth], back_ref[x, :, :depth]
        matrix = site_matrix([(ahead, to_next), (back, to_last)], depth // sites)
        place = place_of(x, planes)
        part_ref[0, place] = dot(matrix, rows_ref[place])
        for k in range(others_ref.shape[0]):
            part_ref[k + 1, place] = dot(matrix, others_ref[k, place])


def move_y_kernel(sites, zs, part_ref, near_ref, far_ref, ahead_ref, turned_ref, field_ref):
    groups, planes, depth, width = part_ref.shape
    row_size = depth // sites * zs
    tail = 128
    head = ahead_ref.shape[2] - tail
    site, lane = iotas((sites, tail))
    lane = lane + head
    upper = (lane >= depth) & (lane < depth + row_size)
    lower = (lane >= depth + row_size) & (lane < depth + 2 * row_size)
    to_next = jnp.where(upper & (site == sites - zs + lane % zs), -1.0, 0.0)
    to_last = jnp.where(lower & (site == lane % zs), -1.0, 0.0)
    above = jnp.zeros((depth - head, width), jnp.float32)
    below = jnp.zeros((tail - 2 * row_size - (depth - head), width), jnp.float32)
    for x in range(planes):
        near = near_ref[x].astype(jnp.float32)
        past = near[2 * row_size : 2 * row_size + 8, :tail]
        matrix = site_matrix([(ahead_ref[x, :, head:], to_next), (past, to_last)], depth // sites)
        place = place_of(x, planes)
        for k in range(groups):
            edge = near[: 2 * row_size] if k == 0 else far_ref[k - 1, x].astype(jnp.float32)
            column = jnp.concatenate([above, edge, below], axis=0).astype(jnp.bfloat16)
            field_ref[k, place] = (part_ref[k, place] + dot(matrix, column)).astype(jnp.bfloat16)
    for k in range(groups):
        turned_ref[k] = field_ref[k].reshape(planes * depth, width).T


def second_share(kind, lefts_ref, right_ref, edge_ref, keep_ref, send_ref, total_ref):
    half = half_of(kind)
    inner = right_ref.shape[0]
    total = dot(lefts_ref[half, :, :inner], right_ref[...]) + dot(lefts_ref[half, :, inner:], edge_ref[...])
    share(total, keep_ref, send_ref, total_ref)


def second_kernel(lefts_ref, right_ref, edge_ref, keep_ref, send_ref, total_ref):
    second_share(0, lefts_ref, right_ref, edge_ref, keep_ref, send_ref, total_ref)


def second_own_kernel(lefts_ref, right_ref, edge_ref, first_ref, keep_ref, send_ref, total_ref):
    parts = first_ref.shape[0]
    send_ref[:parts] = first_ref[...]
    second_share(1, lefts_ref, right_ref, edge_ref, keep_ref, send_ref.at[parts:], total_ref)


def exchange(block, step):
    axes = ("gx", "gy", "ma")
    sizes = [lax.axis_size(axis) for axis in axes]
    route = []
    for source in range(sizes[0] * sizes[1] * sizes[2]):
        where = [source // (sizes[1] * sizes[2]), source // sizes[2] % sizes[1], source % sizes[2]]
        axis, bit = step[where[2] % 2]
        where[axes.index(axis)] ^= 1 << bit
        route.append((source, (where[0] * sizes[1] + where[1]) * sizes[2] + where[2]))
    return lax.ppermute(block, axes, route)


def halve(sums, step, weight=0):
    parts = sum(kept.shape[0] for kept, _, _ in sums)
    count, rows, width = sums[0][0].shape[1:]
    dims = (parts, count // 2, rows, width)

    def merge(*refs):
        *refs, keep_ref, send_ref = refs
        mine = my_side(step)
        start = 0
        for k, (_, _, which) in enumerate(sums):
            kept_ref, came_ref = refs[2 * k : 2 * k + 2]
            came_ref = came_ref if which is None else came_ref.at[which]
            end = start + kept_ref.shape[0]
            for index in range(count // 2):
                low, high = (
                    kept_ref[:, at] + came_ref[:, at].astype(jnp.float32) for at in (index, index + count // 2)
                )
                keep_ref[start:end, index] = jnp.where(mine == 0, low, high)
                send_ref[start:end, index] = jnp.where(mine == 0, high, low).astype(send_ref.dtype)
            start = end

    operands = [a for kept, came, _ in sums for a in (kept, came)]
    keep, send = call(merge, (pltpu.VMEM(dims, jnp.float32), pltpu.VMEM(dims, jnp.bfloat16)), weight, operands)
    return keep, exchange(send, step)


def sum_kernel(kept_ref, came_ref, send_ref):
    send_ref[...] = (kept_ref[...] + came_ref[...].astype(jnp.float32)).astype(send_ref.dtype)


def cross_kernel(start, kept_ref, crossed_ref, out_ref):
    kept = kept_ref[start : start + out_ref.shape[0]]
    out_ref[...] = kept + crossed_ref[...].astype(jnp.float32)


def finish_kernel(came_ref, *refs):
    *kept_refs, out_ref = refs
    parts = out_ref.shape[1]
    for d, kept_ref in enumerate(kept_refs):
        out_ref[d] = kept_ref[:, 0] + came_ref[d * parts : (d + 1) * parts, 0].astype(jnp.float32)


def local(eigen_modes, links_first, links_second):
    f32, bf16 = jnp.float32, jnp.bfloat16
    parts, planes, ys, zs, colours, width = eigen_modes.shape
    sites = ys * zs
    depth = parts * colours * sites
    row_size = parts * colours * zs
    edge = -(-(2 * row_size + 8) // 16) * 16
    lanes = -(-(depth + 2 * row_size) // 128) * 128
    across_x, across_y, groups = (lax.axis_size(a) for a in ("gx", "gy", "ma"))
    rows = groups * width // (across_x * across_y)
    inner_depth = (planes - 2) * depth
    raw = eigen_modes.transpose(0, 1, 2, 4, 3, 5)

    def shape(*dims, dtype=bf16):
        return pltpu.VMEM(dims, dtype)

    field_shape = shape(planes, depth, width)
    turned_shape = shape(width, planes * depth)
    total_shape = shape(groups, width, parts * width, dtype=f32)
    link_shape = shape(planes, 8, lanes, dtype=f32)
    total = pltpu.VMEM((width // rows, rows, parts * width), f32)
    step_flops = 2 * planes * depth * depth * width
    project_flops = 2 * groups * width * planes * depth * parts * width

    raw_others = [shifted(raw, "ma", -step) for step in range(1, groups)]
    raw_links_x, raw_links_y = (a.transpose(0, 1, 2, 3, 5, 4) for a in (links_first, links_second))
    inputs = [raw, raw_links_x, raw_links_y]
    first_plane, last_plane, *inputs, past_maps = call(
        edges_kernel,
        (
            shape(parts, ys, colours, zs, width), shape(parts, ys + colours, colours, zs, width),
            *(shape(*a.shape) for a in inputs),
            shape(map_rows(parts, colours, planes, ys, zs)[-1], 2 * lanes, dtype=f32),
            shape(map_rows(parts, colours, 1, ys, zs)[-1], 2 * lanes, dtype=f32),
        ),
        0,
        inputs,
        [pltpu.SemaphoreType.DMA((5,))],
        [pltpu.HBM] * len(inputs),
    )
    low = shifted(last_plane, "gx", 1)
    high = shifted(first_plane, "gx", -1)
    field, ends, ahead_x, back_x, ahead_y, back_y = call(
        prepare_kernel,
        (field_shape, shape(planes, edge, width), link_shape, link_shape, link_shape, link_shape),
        0,
        inputs,
    )
    near = shifted(ends, "gy", 1)
    if across_y != 2:
        ahead_row = lax.broadcasted_iota(jnp.int32, ends.shape, 1) < row_size
        near = jnp.where(ahead_row, shifted(ends, "gy", -1), near)

    plan = steps()
    top = ("gx", bits("gx")[-1])
    pieces = across_x * across_y // 4
    kept_shape = shape(parts, pieces, rows, width, dtype=f32)
    sent_shape = shape(parts, pieces, rows, width)

    def inner(*refs):
        inner_kernel(sites, *refs)

    def first(*refs):
        first_kernel(sites, *refs)

    def begin_y(*refs):
        begin_y_kernel(sites, zs, *refs)

    def move_y(*refs):
        move_y_kernel(sites, zs, *refs)

    right, own, matrix, ahead_part, back_part = call(
        inner,
        (
            shape(inner_depth, parts * width), turned_shape, shape(depth, depth),
            shape(depth, width, dtype=f32), shape(depth, width, dtype=f32),
        ),
        2 * step_flops,
        [field, ahead_x, back_x],
    )
    turned = [call(turn_kernel, (field_shape, turned_shape), step_flops // 4, [r]) for r in raw_others]
    fields = jnp.stack([t[0] for t in turned])
    others = jnp.stack([t[1] for t in turned])
    begun_first = call(begin_first_kernel, total_shape, project_flops, [own, others, right])
    part_y = call(
        begin_y, shape(groups, planes, depth, width, dtype=f32), 2 * step_flops, [field, fields, ahead_y, back_y]
    )
    part_y, begun_first = lax.optimization_barrier((part_y, begun_first))
    kept_first, sent_first, right_edge = call(
        first,
        (kept_shape, sent_shape, shape(2 * depth, parts * width)),
        project_flops,
        [high, low, matrix, ahead_part, back_part, past_maps, own, others, begun_first],
        [total],
    )
    came_first = exchange(sent_first, plan[0])
    near, right_edge = lax.optimization_barrier((near, right_edge))
    near_rows = near[:, : 2 * row_size]
    far = jnp.stack([shifted(near_rows, "ma", -step) for step in range(1, groups)])
    lefts = call(
        move_y, shape(groups, width, planes * depth), 2 * step_flops,
        [part_y, near, far, ahead_y],
        [pltpu.VMEM((groups,) + field_shape.shape, bf16)],
    )
    kept_second, sent_second = call(
        second_kernel, (kept_shape, sent_shape), 8 * project_flops, [lefts, right, right_edge], [total]
    )
    came_second = exchange(sent_second, plan[0])
    right_edge, kept_second = lax.optimization_barrier((right_edge, kept_second))
    own_first, sent_own = call(
        first_own_kernel, (kept_shape, sent_shape), 0, [own, others, begun_first, right_edge], [total]
    )
    own_second, sent_own = call(
        second_own_kernel, (kept_shape, shape(2 * parts, pieces, rows, width)), 0,
        [lefts, right, right_edge, sent_own], [total],
    )
    crossing = [(kept_first, came_first), (kept_second, came_second)]
    after = own_second
    staying = None
    for step in plan[1:]:
        for d, (kept, came) in enumerate(crossing):
            came, after = lax.optimization_barrier((came, after))
            crossing[d] = halve([(kept, came, None)], step)
            after = crossing[d][0]
            if staying is None:
                sent_own, after = lax.optimization_barrier((sent_own, after))
                came_own = exchange(sent_own, plan[0])
                staying = [
                    (own_first, came_own, slice(0, parts)), (own_second, came_own, slice(parts, 2 * parts))
                ]
    crossed = []
    for kept, came in crossing:
        came, after = lax.optimization_barrier((came, after))
        after = call(sum_kernel, pltpu.VMEM(kept.shape, bf16), 8 * project_flops, [kept, came])
        crossed.append(exchange(after, (top, top)))
    for step in plan[1:]:
        kept, came, which = staying[0]
        came, after = lax.optimization_barrier((came, after))
        sums = [(kept, came, which)] + [(k, came, w) for k, _, w in staying[1:]]
        kept, came = halve(sums, step)
        staying, after = [(kept, came, None)], kept
    kept, came, _ = staying[0]
    totals = []
    for d, block in enumerate(crossed):

        def cross(*refs, start=d * parts):
            cross_kernel(start, *refs)

        block, after = lax.optimization_barrier((block, after))
        after = call(cross, shape(*block.shape, dtype=f32), 4 * project_flops, [kept, block])
        totals.append(after)
    came, after = lax.optimization_barrier((came, after))
    return call(
        finish_kernel, jax.ShapeDtypeStruct((2, parts, rows, width), f32), 0, [came, *totals]
    )


def solution(mesh):
    return jax.shard_map(
        local,
        mesh=mesh,
        in_specs=(
            P("cuts", "gx", "gy", None, None, "ma"),
            P("cuts", None, None, "gx", "gy", None),
            P("cuts", None, None, "gx", "gy", None),
        ),
        out_specs=P("cuts", None, ("gx", "gy"), "ma"),
        check_vma=False,
    )
```

```python
import jax
import jax.numpy as jnp
from jax import lax
from jax.experimental import pallas as pl
from jax.experimental.pallas import tpu as pltpu
from jax.sharding import PartitionSpec as P

VMEM_LIMIT = 16 * 1024 * 1024


def shifted(block, axis, distance):
    devices = range(lax.axis_size(axis))
    route = [((i - distance) % len(devices), i) for i in devices]
    return lax.ppermute(block, axis, route)


def call(body, out_shape, flops, operands, scratch=(), places=None, **more):
    places = places or [pltpu.VMEM] * len(operands)
    return pl.pallas_call(
        body,
        out_shape=out_shape,
        in_specs=[pl.BlockSpec(memory_space=place) for place in places],
        scratch_shapes=scratch,
        cost_estimate=pl.CostEstimate(flops=flops // 2, bytes_accessed=0, transcendentals=0),
        compiler_params=pltpu.CompilerParams(vmem_limit_bytes=VMEM_LIMIT),
        **more,
    )(*(pltpu.with_memory_space_constraint(a, place) for a, place in zip(operands, places)))


def dot(a, b):
    return jnp.dot(a, b, preferred_element_type=jnp.float32)


def iotas(shape):
    return (
        lax.broadcasted_iota(jnp.int32, shape, 0),
        lax.broadcasted_iota(jnp.int32, shape, 1),
    )


def place_of(x, planes):
    return planes - 2 if x == 0 else x if x == planes - 1 else x - 1


def map_rows(parts, colours, planes, ys, zs):
    match = ys
    choose = match + -(-parts * colours * colours * planes * zs // 8) * 8
    first_part = choose + 2 * parts * planes * 8
    return match, choose, first_part, first_part + 8


def write_maps(ref, parts, colours, planes, ys, zs):
    lanes = ref.shape[1] // 2
    sites = ys * zs
    depth = parts * colours * sites
    row_size = parts * colours * zs
    match, choose, first_part, _ = map_rows(parts, colours, planes, ys, zs)

    def ones(mask):
        return jnp.where(mask, 1.0, 0.0)

    def column(count):
        return lax.broadcasted_iota(jnp.int32, (count, 1), 0)

    def line(count):
        return lax.broadcasted_iota(jnp.int32, (1, count), 1)

    lane = line(lanes)
    inner = lane < depth
    past = lax.rem(jnp.maximum(lane - depth, 0), row_size)
    used = lane < depth + 2 * row_size
    part = jnp.where(inner, lax.div(lane, colours * sites), lax.div(past, colours * zs))
    colour = lax.rem(jnp.where(inner, lax.div(lane, sites), lax.div(past, zs)), colours)
    z = lax.rem(jnp.where(inner, lane, past), zs)
    y = lax.div(lax.rem(lane, sites), zs)
    ref[:ys, :lanes] = ones(column(ys) == jnp.where(inner, y, ys - 1))
    ref[:ys, lanes:] = ones(column(ys) == jnp.where(inner, y, ys) - 1)

    count = parts * colours * colours * planes * zs

    def link(index):
        x = lax.rem(lax.div(index, zs), planes)
        right = lax.rem(lax.div(index, zs * planes), colours)
        left = lax.rem(lax.div(index, zs * planes * colours), colours)
        return x, right, left, lax.div(index, zs * planes * colours * colours)

    row = column(count)
    _, right, left, _ = link(row)
    row_z = lax.rem(row, zs)
    key = jnp.where(used, colour * zs + z, -1)
    ref[match : match + count, :lanes] = ones(right * zs + row_z == key)
    ref[match : match + count, lanes:] = ones(left * zs + row_z == key)

    out = column(parts * planes * 8)
    field_part = lax.div(out, planes * 8)
    out_x = lax.rem(lax.div(out, 8), planes)
    out_part = lax.div(lax.rem(out, 8), colours)
    out_colour = lax.rem(lax.rem(out, 8), colours)
    x, right, left, source_part = link(line(count))
    source = source_part * planes + x
    wanted = jnp.where(out_part < parts, lax.rem(out_part + field_part, 2) * planes + out_x, -1)
    sign_ahead = jnp.where((field_part == 1) & (out_part == 0), -1.0, 1.0)
    sign_back = jnp.where((field_part == 0) & (out_part == 1), 1.0, -1.0)
    half = parts * planes * 8
    for start, end, sign in ((choose, left, sign_ahead), (choose + half, right, sign_back)):
        hit = source * colours + end == wanted * colours + jnp.where(wanted < 0, -1, out_colour)
        ref[start : start + half, :count] = jnp.where(hit, sign, 0.0)
    ref[first_part:, :lanes] = jnp.broadcast_to(ones(part == 0), (8, lanes))


def coefficients(links_x, links_y, maps_ref, planes):
    lanes = maps_ref.shape[1] // 2
    ys = links_x.shape[1]
    count = links_x.shape[0]
    half = 2 * planes * 8
    wide = dot(jnp.concatenate([links_x, links_y], axis=0), maps_ref[:ys].astype(jnp.bfloat16))
    match = maps_ref[ys : ys + count]
    match_ahead, match_back = match[:, :lanes], match[:, lanes:]
    choose = maps_ref[ys + count : ys + count + 2 * half, :count].astype(jnp.bfloat16)
    first_part = maps_ref[ys + count + 2 * half : ys + count + 2 * half + 1, :lanes] > 0.5
    ahead = jnp.concatenate([wide[:count, :lanes] * match_ahead, wide[count:, lanes:] * match_ahead], axis=1)
    back = jnp.concatenate([wide[:count, :lanes] * match_back, wide[count:, :lanes] * match_back], axis=1)
    out = []
    for chosen in (
        dot(choose[:half], ahead.astype(jnp.bfloat16)), dot(choose[half:], back.astype(jnp.bfloat16))
    ):
        for start in (0, lanes):
            part = chosen[:, start : start + lanes]
            rows = jnp.where(first_part, part[: half // 2], part[half // 2 :])
            out.append(rows.reshape(planes, 8, lanes))
    return out


def plane_rows(ref, ys):
    parts, _, colours, zs, width = ref.shape
    return jnp.concatenate(
        [ref[p, :ys, c].reshape(ys * zs, width) for p in range(parts) for c in range(colours)],
        axis=0,
    )


def edges_kernel(
    raw_hbm, links_x_hbm, links_y_hbm,
    first_ref, last_ref, raw_ref, links_x_ref, links_y_ref, maps_ref, past_maps_ref, arrived,
):
    parts, planes, ys, colours, zs, _ = raw_hbm.shape
    sources = (raw_hbm.at[:, planes - 1], raw_hbm.at[:, 0], links_x_hbm, links_y_hbm, raw_hbm)
    targets = (last_ref.at[:, :ys], first_ref, links_x_ref, links_y_ref, raw_ref)
    copies = [
        pltpu.make_async_copy(source, target, arrived.at[i])
        for i, (source, target) in enumerate(zip(sources, targets))
    ]
    for copy in copies:
        copy.start()
    last_ref[:, ys:] = jnp.zeros((parts, colours) + last_ref.shape[2:], last_ref.dtype)
    write_maps(maps_ref, parts, colours, planes, ys, zs)
    write_maps(past_maps_ref, parts, colours, 1, ys, zs)
    copies[2].wait()
    last_ref[:, ys:, :, :, :ys] = links_x_ref[:, :, :, planes - 1]
    for copy in copies[:2] + copies[3:]:
        copy.wait()


def site_matrix(rows_and_masks, count):
    blocks = []
    for q in range(count):
        block = None
        for rows, mask in rows_and_masks:
            term = rows[q : q + 1] * mask
            block = term if block is None else block + term
        blocks.append(block.astype(jnp.bfloat16))
    return jnp.concatenate(blocks, axis=0)


def prepare_kernel(
    raw_ref, links_x_ref, links_y_ref, maps_ref,
    rows_ref, ends_ref, ahead_x_ref, back_x_ref, ahead_y_ref, back_y_ref,
):
    planes, depth, width = rows_ref.shape
    zs = raw_ref.shape[4]
    ys = raw_ref.shape[2]
    sites = ys * zs
    row_size = depth // sites * zs
    lanes = ahead_y_ref.shape[2]
    ahead_x, ahead_y, back_x, back_y = coefficients(
        links_x_ref[...].reshape(-1, ys), links_y_ref[...].reshape(-1, ys), maps_ref, planes
    )
    ahead_x_ref[...] = ahead_x
    back_x_ref[...] = back_x
    ahead_y_ref[...] = ahead_y
    back_y_ref[...] = back_y

    row, lane = iotas((2 * row_size, depth))
    spot = row % row_size
    wanted = (spot // zs) * sites + spot % zs + jnp.where(row < row_size, 0, sites - zs)
    ends = (lane == wanted).astype(jnp.bfloat16)
    filler = jnp.zeros((8, width - 128), jnp.float32)
    spare = ends_ref.shape[1] - 2 * row_size - 8
    for x in range(planes):
        plane = plane_rows(raw_ref.at[:, x], ys)
        rows_ref[place_of(x, planes)] = plane
        tail = jnp.concatenate([back_y[x, :, lanes - 128 :], filler], axis=1)
        pieces = [dot(ends, plane), tail]
        if spare:
            pieces.append(jnp.zeros((spare, width), jnp.float32))
        ends_ref[x] = jnp.concatenate(pieces, axis=0).astype(jnp.bfloat16)


def turn_kernel(raw_ref, rows_ref, turned_ref):
    planes, depth, width = rows_ref.shape
    for x in range(planes):
        rows_ref[place_of(x, planes)] = plane_rows(raw_ref.at[:, x], raw_ref.shape[2])
    turned_ref[...] = rows_ref[...].reshape(planes * depth, width).T


def move_plane(same, count, ahead, back, above, below):
    depth = same.shape[1]
    moved = dot(site_matrix([(ahead[:, :depth], same)], count), above)
    return (moved + dot(site_matrix([(back[:, :depth], same)], count), below)).astype(jnp.bfloat16)


def same_site(sites, depth):
    site, lane = iotas((sites, depth))
    return (lane % sites == site).astype(jnp.float32)


def set_right(right_ref, place, moved):
    depth, width = moved.shape
    half = depth // 2
    start = place * depth
    real, imag = moved[:half], moved[half:]
    right_ref[start : start + half, :width] = real
    right_ref[start : start + half, width:] = imag
    right_ref[start + half : start + depth, :width] = imag
    right_ref[start + half : start + depth, width:] = -real


def inner_kernel(
    sites, rows_ref, ahead_ref, back_ref, right_ref, turned_ref, matrix_ref, ahead_part_ref, back_part_ref
):
    planes, depth, width = rows_ref.shape
    same = same_site(sites, depth)
    for x in range(1, planes - 1):
        above = rows_ref[place_of(x + 1, planes)]
        below = rows_ref[place_of(x - 1, planes)]
        moved = move_plane(same, depth // sites, ahead_ref[x], back_ref[x - 1], above, below)
        set_right(right_ref, place_of(x, planes), moved)
    turned_ref[...] = rows_ref[...].reshape(planes * depth, width).T
    x, count = planes - 1, depth // sites
    matrix_ref[...] = site_matrix([(ahead_ref[x, :, :depth], same)], count)
    ahead_part_ref[...] = dot(site_matrix([(ahead_ref[0, :, :depth], same)], count), rows_ref[place_of(1, planes)])
    below = rows_ref[place_of(x - 1, planes)]
    back_part_ref[...] = dot(site_matrix([(back_ref[x - 1, :, :depth], same)], count), below)


def begin_first_kernel(own_ref, others_ref, right_ref, total_ref):
    inner = right_ref.shape[0]
    right = right_ref[...]
    total_ref[0] = dot(own_ref[:, :inner], right)
    for k in range(others_ref.shape[0]):
        total_ref[k + 1] = dot(others_ref[k, :, :inner], right)


def bits(axis):
    return range(lax.axis_size(axis).bit_length() - 1)


def steps():
    one = [("gx", bit) for bit in bits("gx")[:-1]]
    two = [("gy", bit) for bit in bits("gy")]
    both = min(len(one), len(two))
    pairs = [pair for ends in zip(one, two) for pair in (ends, ends[::-1])]
    return pairs + [(step, step) for step in one[both:] + two[both:]]


def my_bit(axis, bit):
    return lax.bitwise_and(lax.shift_right_logical(lax.axis_index(axis), bit), 1)


def my_side(step):
    even, odd = (my_bit(*way) for way in step)
    return jnp.where(my_bit("ma", 0) == 0, even, odd)


def half_of(kind):
    half = lax.bitwise_xor(my_bit("gx", bits("gx")[-1]), 1 - kind)
    return lax.bitwise_xor(half, lax.axis_index("ma"))


def share(total, keep_ref, send_ref, total_ref):
    blocks, rows, double = total_ref.shape
    parts, count, _, width = keep_ref.shape
    total_ref[...] = total.reshape(blocks, rows, double)
    odd_core = my_bit("ma", 0)
    across_y = lax.axis_size("gy")
    plan = steps()
    mine = my_side(plan[0])

    def at(side, index):
        owners = []
        for core in range(2):
            place = {"gx": 0, "gy": 0}
            for k, step in enumerate(plan):
                axis, bit = step[core]
                digit = side if k == 0 else index >> (len(plan) - 1 - k) & 1
                place[axis] += digit * (1 << bit)
            owners.append(place["gx"] * across_y + place["gy"])
        return jnp.where(odd_core == 0, owners[0], owners[1])

    for index in range(count):
        for ref, side in ((keep_ref, mine), (send_ref, 1 - mine)):
            block = total_ref[at(side, index)].astype(ref.dtype)
            for p in range(parts):
                ref[p, index] = block[:, p * width : (p + 1) * width]


def first_share(kind, own_ref, others_ref, begun_ref, right, keep_ref, send_ref, total_ref):
    half = half_of(kind)
    inner = own_ref.shape[1] - right.shape[0]
    left = jnp.where(half == 0, own_ref[:, inner:], others_ref[0, :, inner:])
    share(begun_ref[half] + dot(left, right), keep_ref, send_ref, total_ref)


def first_kernel(
    sites, high_ref, low_ref, matrix_ref, ahead_part_ref, back_part_ref, past_maps_ref, own_ref, others_ref, begun_ref,
    *refs,
):
    keep_ref, send_ref, right_ref, total_ref = refs
    depth = matrix_ref.shape[0]
    same = same_site(sites, depth)
    _, ys, colours, zs, _ = high_ref.shape
    links = low_ref[:, ys:, :, :, :ys].reshape(-1, ys)
    lanes = past_maps_ref.shape[1] // 2
    count = links.shape[0]
    spread = past_maps_ref[:ys, :lanes].astype(jnp.bfloat16)
    match = past_maps_ref[ys : ys + count, lanes:]
    start = past_maps_ref.shape[0] - 24
    choose = past_maps_ref[start : start + 16, :count].astype(jnp.bfloat16)
    past = dot(choose, (dot(links, spread) * match).astype(jnp.bfloat16))
    past = jnp.where(past_maps_ref[start + 16 : start + 17, :lanes] > 0.5, past[:8], past[8:])
    past = site_matrix([(past[:, :depth], same)], depth // sites)
    moved = ahead_part_ref[...] + dot(past, plane_rows(low_ref, ys))
    set_right(right_ref, 0, moved.astype(jnp.bfloat16))
    moved = dot(matrix_ref[...], plane_rows(high_ref, ys)) + back_part_ref[...]
    set_right(right_ref, 1, moved.astype(jnp.bfloat16))
    first_share(0, own_ref, others_ref, begun_ref, right_ref[...], keep_ref, send_ref, total_ref)


def first_own_kernel(own_ref, others_ref, begun_ref, right_ref, keep_ref, send_ref, total_ref):
    first_share(1, own_ref, others_ref, begun_ref, right_ref[...], keep_ref, send_ref, total_ref)


def begin_y_kernel(sites, zs, rows_ref, others_ref, ahead_ref, back_ref, part_ref):
    planes, depth, _ = rows_ref.shape
    site, lane = iotas((sites, depth))
    to_next = jnp.where(lane % sites == site + zs, -1.0, 0.0)
    to_last = jnp.where(lane % sites == site - zs, -1.0, 0.0)
    for x in range(planes):
        ahead, back = ahead_ref[x, :, :depth], back_ref[x, :, :depth]
        matrix = site_matrix([(ahead, to_next), (back, to_last)], depth // sites)
        place = place_of(x, planes)
        part_ref[0, place] = dot(matrix, rows_ref[place])
        for k in range(others_ref.shape[0]):
            part_ref[k + 1, place] = dot(matrix, others_ref[k, place])


def move_y_kernel(sites, zs, part_ref, near_ref, far_ref, ahead_ref, turned_ref, field_ref):
    groups, planes, depth, width = part_ref.shape
    row_size = depth // sites * zs
    tail = 128
    head = ahead_ref.shape[2] - tail
    site, lane = iotas((sites, tail))
    lane = lane + head
    upper = (lane >= depth) & (lane < depth + row_size)
    lower = (lane >= depth + row_size) & (lane < depth + 2 * row_size)
    to_next = jnp.where(upper & (site == sites - zs + lane % zs), -1.0, 0.0)
    to_last = jnp.where(lower & (site == lane % zs), -1.0, 0.0)
    above = jnp.zeros((depth - head, width), jnp.float32)
    below = jnp.zeros((tail - 2 * row_size - (depth - head), width), jnp.float32)
    for x in range(planes):
        near = near_ref[x].astype(jnp.float32)
        past = near[2 * row_size : 2 * row_size + 8, :tail]
        matrix = site_matrix([(ahead_ref[x, :, head:], to_next), (past, to_last)], depth // sites)
        place = place_of(x, planes)
        for k in range(groups):
            edge = near[: 2 * row_size] if k == 0 else far_ref[k - 1, x].astype(jnp.float32)
            column = jnp.concatenate([above, edge, below], axis=0).astype(jnp.bfloat16)
            field_ref[k, place] = (part_ref[k, place] + dot(matrix, column)).astype(jnp.bfloat16)
    for k in range(groups):
        turned_ref[k] = field_ref[k].reshape(planes * depth, width).T


def second_share(kind, lefts_ref, right_ref, edge_ref, keep_ref, send_ref, total_ref):
    half = half_of(kind)
    inner = right_ref.shape[0]
    total = dot(lefts_ref[half, :, :inner], right_ref[...]) + dot(lefts_ref[half, :, inner:], edge_ref[...])
    share(total, keep_ref, send_ref, total_ref)


def second_kernel(lefts_ref, right_ref, edge_ref, keep_ref, send_ref, total_ref):
    second_share(0, lefts_ref, right_ref, edge_ref, keep_ref, send_ref, total_ref)


def second_own_kernel(lefts_ref, right_ref, edge_ref, first_ref, keep_ref, send_ref, total_ref):
    parts = first_ref.shape[0]
    send_ref[:parts] = first_ref[...]
    second_share(1, lefts_ref, right_ref, edge_ref, keep_ref, send_ref.at[parts:], total_ref)


def exchange(block, step):
    axes = ("gx", "gy", "ma")
    sizes = [lax.axis_size(axis) for axis in axes]
    route = []
    for source in range(sizes[0] * sizes[1] * sizes[2]):
        where = [source // (sizes[1] * sizes[2]), source // sizes[2] % sizes[1], source % sizes[2]]
        axis, bit = step[where[2] % 2]
        where[axes.index(axis)] ^= 1 << bit
        route.append((source, (where[0] * sizes[1] + where[1]) * sizes[2] + where[2]))
    return lax.ppermute(block, axes, route)


def halve(sums, step, weight=0):
    parts = sum(kept.shape[0] for kept, _, _ in sums)
    count, rows, width = sums[0][0].shape[1:]
    dims = (parts, count // 2, rows, width)

    def merge(*refs):
        *refs, keep_ref, send_ref = refs
        mine = my_side(step)
        start = 0
        for k, (_, _, which) in enumerate(sums):
            kept_ref, came_ref = refs[2 * k : 2 * k + 2]
            came_ref = came_ref if which is None else came_ref.at[which]
            end = start + kept_ref.shape[0]
            for index in range(count // 2):
                low, high = (
                    kept_ref[:, at] + came_ref[:, at].astype(jnp.float32) for at in (index, index + count // 2)
                )
                keep_ref[start:end, index] = jnp.where(mine == 0, low, high)
                send_ref[start:end, index] = jnp.where(mine == 0, high, low).astype(send_ref.dtype)
            start = end

    operands = [a for kept, came, _ in sums for a in (kept, came)]
    keep, send = call(merge, (pltpu.VMEM(dims, jnp.float32), pltpu.VMEM(dims, jnp.bfloat16)), weight, operands)
    return keep, exchange(send, step)


def sum_kernel(kept_ref, came_ref, send_ref):
    send_ref[...] = (kept_ref[...] + came_ref[...].astype(jnp.float32)).astype(send_ref.dtype)


def cross_kernel(start, kept_ref, crossed_ref, out_ref):
    kept = kept_ref[start : start + out_ref.shape[0]]
    out_ref[...] = kept + crossed_ref[...].astype(jnp.float32)


def finish_kernel(came_ref, *refs):
    *kept_refs, out_hbm, sum_ref, left = refs
    parts = sum_ref.shape[1]
    copies = []
    for d, kept_ref in enumerate(kept_refs):
        for p in range(parts):
            sum_ref[d, p] = kept_ref[p, 0] + came_ref[d * parts + p, 0].astype(jnp.float32)
            copies.append(pltpu.make_async_copy(sum_ref.at[d, p], out_hbm.at[d, p], left.at[d * parts + p]))
            copies[-1].start()
    for copy in copies:
        copy.wait()


def local(eigen_modes, links_first, links_second):
    f32, bf16 = jnp.float32, jnp.bfloat16
    parts, planes, ys, zs, colours, width = eigen_modes.shape
    sites = ys * zs
    depth = parts * colours * sites
    row_size = parts * colours * zs
    edge = -(-(2 * row_size + 8) // 16) * 16
    lanes = -(-(depth + 2 * row_size) // 128) * 128
    across_x, across_y, groups = (lax.axis_size(a) for a in ("gx", "gy", "ma"))
    rows = groups * width // (across_x * across_y)
    inner_depth = (planes - 2) * depth
    raw = eigen_modes.transpose(0, 1, 2, 4, 3, 5)

    def shape(*dims, dtype=bf16):
        return pltpu.VMEM(dims, dtype)

    field_shape = shape(planes, depth, width)
    turned_shape = shape(width, planes * depth)
    total_shape = shape(groups, width, parts * width, dtype=f32)
    link_shape = shape(planes, 8, lanes, dtype=f32)
    total = pltpu.VMEM((width // rows, rows, parts * width), f32)
    step_flops = 2 * planes * depth * depth * width
    project_flops = 2 * groups * width * planes * depth * parts * width

    raw_others = [shifted(raw, "ma", -step) for step in range(1, groups)]
    raw_links_x, raw_links_y = (a.transpose(0, 1, 2, 3, 5, 4) for a in (links_first, links_second))
    inputs = [raw, raw_links_x, raw_links_y]
    first_plane, last_plane, *inputs, past_maps = call(
        edges_kernel,
        (
            shape(parts, ys, colours, zs, width), shape(parts, ys + colours, colours, zs, width),
            *(shape(*a.shape) for a in inputs),
            shape(map_rows(parts, colours, planes, ys, zs)[-1], 2 * lanes, dtype=f32),
            shape(map_rows(parts, colours, 1, ys, zs)[-1], 2 * lanes, dtype=f32),
        ),
        0,
        inputs,
        [pltpu.SemaphoreType.DMA((5,))],
        [pltpu.HBM] * len(inputs),
    )
    low = shifted(last_plane, "gx", 1)
    high = shifted(first_plane, "gx", -1)
    field, ends, ahead_x, back_x, ahead_y, back_y = call(
        prepare_kernel,
        (field_shape, shape(planes, edge, width), link_shape, link_shape, link_shape, link_shape),
        0,
        inputs,
    )
    near = shifted(ends, "gy", 1)
    if across_y != 2:
        ahead_row = lax.broadcasted_iota(jnp.int32, ends.shape, 1) < row_size
        near = jnp.where(ahead_row, shifted(ends, "gy", -1), near)

    plan = steps()
    top = ("gx", bits("gx")[-1])
    pieces = across_x * across_y // 4
    kept_shape = shape(parts, pieces, rows, width, dtype=f32)
    sent_shape = shape(parts, pieces, rows, width)

    def inner(*refs):
        inner_kernel(sites, *refs)

    def first(*refs):
        first_kernel(sites, *refs)

    def begin_y(*refs):
        begin_y_kernel(sites, zs, *refs)

    def move_y(*refs):
        move_y_kernel(sites, zs, *refs)

    right, own, matrix, ahead_part, back_part = call(
        inner,
        (
            shape(inner_depth, parts * width), turned_shape, shape(depth, depth),
            shape(depth, width, dtype=f32), shape(depth, width, dtype=f32),
        ),
        2 * step_flops,
        [field, ahead_x, back_x],
    )
    turned = [call(turn_kernel, (field_shape, turned_shape), step_flops // 4, [r]) for r in raw_others]
    fields = jnp.stack([t[0] for t in turned])
    others = jnp.stack([t[1] for t in turned])
    begun_first = call(begin_first_kernel, total_shape, project_flops, [own, others, right])
    part_y = call(
        begin_y, shape(groups, planes, depth, width, dtype=f32), 2 * step_flops, [field, fields, ahead_y, back_y]
    )
    part_y, begun_first = lax.optimization_barrier((part_y, begun_first))
    kept_first, sent_first, right_edge = call(
        first,
        (kept_shape, sent_shape, shape(2 * depth, parts * width)),
        project_flops,
        [high, low, matrix, ahead_part, back_part, past_maps, own, others, begun_first],
        [total],
    )
    came_first = exchange(sent_first, plan[0])
    near, right_edge = lax.optimization_barrier((near, right_edge))
    near_rows = near[:, : 2 * row_size]
    far = jnp.stack([shifted(near_rows, "ma", -step) for step in range(1, groups)])
    lefts = call(
        move_y, shape(groups, width, planes * depth), 2 * step_flops,
        [part_y, near, far, ahead_y],
        [pltpu.VMEM((groups,) + field_shape.shape, bf16)],
    )
    kept_second, sent_second = call(
        second_kernel, (kept_shape, sent_shape), 8 * project_flops, [lefts, right, right_edge], [total]
    )
    came_second = exchange(sent_second, plan[0])
    right_edge, kept_second = lax.optimization_barrier((right_edge, kept_second))
    own_first, sent_own = call(
        first_own_kernel, (kept_shape, sent_shape), 0, [own, others, begun_first, right_edge], [total]
    )
    own_second, sent_own = call(
        second_own_kernel, (kept_shape, shape(2 * parts, pieces, rows, width)), 0,
        [lefts, right, right_edge, sent_own], [total],
    )
    came_own = exchange(sent_own, plan[0])
    staying = [(own_first, came_own, slice(0, parts)), (own_second, came_own, slice(parts, 2 * parts))]
    crossing = [(kept_first, came_first), (kept_second, came_second)]
    after = own_second
    for step in plan[1:]:
        for d, (kept, came) in enumerate(crossing):
            came, after = lax.optimization_barrier((came, after))
            crossing[d] = halve([(kept, came, None)], step, 4 * project_flops if d else 0)
            after = crossing[d][0]
    crossed = []
    for kept, came in crossing:
        came, after = lax.optimization_barrier((came, after))
        after = call(sum_kernel, pltpu.VMEM(kept.shape, bf16), 0, [kept, came])
        crossed.append(exchange(after, (top, top)))
    for step in plan[1:]:
        kept, came, which = staying[0]
        came, after = lax.optimization_barrier((came, after))
        sums = [(kept, came, which)] + [(k, came, w) for k, _, w in staying[1:]]
        kept, came = halve(sums, step)
        staying, after = [(kept, came, None)], kept
    kept, came, _ = staying[0]
    totals = []
    for d, block in enumerate(crossed):

        def cross(*refs, start=d * parts):
            cross_kernel(start, *refs)

        block, after = lax.optimization_barrier((block, after))
        after = call(cross, shape(*block.shape, dtype=f32), 4 * project_flops, [kept, block])
        totals.append(after)
    came, after = lax.optimization_barrier((came, after))
    result = (2, parts, rows, width)
    return call(
        finish_kernel, jax.ShapeDtypeStruct(result, f32), 0, [came, *totals],
        [pltpu.VMEM(result, f32), pltpu.SemaphoreType.DMA((2 * parts,))],
        out_specs=pl.BlockSpec(memory_space=pltpu.HBM),
    )


def solution(mesh):
    return jax.shard_map(
        local,
        mesh=mesh,
        in_specs=(
            P("cuts", "gx", "gy", None, None, "ma"),
            P("cuts", None, None, "gx", "gy", None),
            P("cuts", None, None, "gx", "gy", None),
        ),
        out_specs=P("cuts", None, ("gx", "gy"), "ma"),
        check_vma=False,
    )
```

```python
import jax
import jax.numpy as jnp
from jax import lax
from jax.experimental import pallas as pl
from jax.experimental.pallas import tpu as pltpu
from jax.sharding import PartitionSpec as P

VMEM_LIMIT = 16 * 1024 * 1024


def shifted(block, axis, distance):
    devices = range(lax.axis_size(axis))
    route = [((i - distance) % len(devices), i) for i in devices]
    return lax.ppermute(block, axis, route)


def call(body, out_shape, flops, operands, scratch=(), places=None):
    places = places or [pltpu.VMEM] * len(operands)
    return pl.pallas_call(
        body,
        out_shape=out_shape,
        in_specs=[pl.BlockSpec(memory_space=place) for place in places],
        scratch_shapes=scratch,
        cost_estimate=pl.CostEstimate(flops=flops // 2, bytes_accessed=0, transcendentals=0),
        compiler_params=pltpu.CompilerParams(vmem_limit_bytes=VMEM_LIMIT),
    )(*(pltpu.with_memory_space_constraint(a, place) for a, place in zip(operands, places)))


def dot(a, b):
    return jnp.dot(a, b, preferred_element_type=jnp.float32)


def iotas(shape):
    return (
        lax.broadcasted_iota(jnp.int32, shape, 0),
        lax.broadcasted_iota(jnp.int32, shape, 1),
    )


def place_of(x, planes):
    return planes - 2 if x == 0 else x if x == planes - 1 else x - 1


def map_rows(parts, colours, planes, ys, zs):
    match = ys
    choose = match + -(-parts * colours * colours * planes * zs // 8) * 8
    first_part = choose + 2 * parts * planes * 8
    return match, choose, first_part, first_part + 8


def write_maps(ref, parts, colours, planes, ys, zs):
    lanes = ref.shape[1] // 2
    sites = ys * zs
    depth = parts * colours * sites
    row_size = parts * colours * zs
    match, choose, first_part, _ = map_rows(parts, colours, planes, ys, zs)

    def ones(mask):
        return jnp.where(mask, 1.0, 0.0)

    def column(count):
        return lax.broadcasted_iota(jnp.int32, (count, 1), 0)

    def line(count):
        return lax.broadcasted_iota(jnp.int32, (1, count), 1)

    lane = line(lanes)
    inner = lane < depth
    past = lax.rem(jnp.maximum(lane - depth, 0), row_size)
    used = lane < depth + 2 * row_size
    part = jnp.where(inner, lax.div(lane, colours * sites), lax.div(past, colours * zs))
    colour = lax.rem(jnp.where(inner, lax.div(lane, sites), lax.div(past, zs)), colours)
    z = lax.rem(jnp.where(inner, lane, past), zs)
    y = lax.div(lax.rem(lane, sites), zs)
    ref[:ys, :lanes] = ones(column(ys) == jnp.where(inner, y, ys - 1))
    ref[:ys, lanes:] = ones(column(ys) == jnp.where(inner, y, ys) - 1)

    count = parts * colours * colours * planes * zs

    def link(index):
        x = lax.rem(lax.div(index, zs), planes)
        right = lax.rem(lax.div(index, zs * planes), colours)
        left = lax.rem(lax.div(index, zs * planes * colours), colours)
        return x, right, left, lax.div(index, zs * planes * colours * colours)

    row = column(count)
    _, right, left, _ = link(row)
    row_z = lax.rem(row, zs)
    key = jnp.where(used, colour * zs + z, -1)
    ref[match : match + count, :lanes] = ones(right * zs + row_z == key)
    ref[match : match + count, lanes:] = ones(left * zs + row_z == key)

    out = column(parts * planes * 8)
    field_part = lax.div(out, planes * 8)
    out_x = lax.rem(lax.div(out, 8), planes)
    out_part = lax.div(lax.rem(out, 8), colours)
    out_colour = lax.rem(lax.rem(out, 8), colours)
    x, right, left, source_part = link(line(count))
    source = source_part * planes + x
    wanted = jnp.where(out_part < parts, lax.rem(out_part + field_part, 2) * planes + out_x, -1)
    sign_ahead = jnp.where((field_part == 1) & (out_part == 0), -1.0, 1.0)
    sign_back = jnp.where((field_part == 0) & (out_part == 1), 1.0, -1.0)
    half = parts * planes * 8
    for start, end, sign in ((choose, left, sign_ahead), (choose + half, right, sign_back)):
        hit = source * colours + end == wanted * colours + jnp.where(wanted < 0, -1, out_colour)
        ref[start : start + half, :count] = jnp.where(hit, sign, 0.0)
    ref[first_part:, :lanes] = jnp.broadcast_to(ones(part == 0), (8, lanes))


def coefficients(links_x, links_y, maps_ref, planes):
    lanes = maps_ref.shape[1] // 2
    ys = links_x.shape[1]
    count = links_x.shape[0]
    half = 2 * planes * 8
    wide = dot(jnp.concatenate([links_x, links_y], axis=0), maps_ref[:ys].astype(jnp.bfloat16))
    match = maps_ref[ys : ys + count]
    match_ahead, match_back = match[:, :lanes], match[:, lanes:]
    choose = maps_ref[ys + count : ys + count + 2 * half, :count].astype(jnp.bfloat16)
    first_part = maps_ref[ys + count + 2 * half : ys + count + 2 * half + 1, :lanes] > 0.5
    ahead = jnp.concatenate([wide[:count, :lanes] * match_ahead, wide[count:, lanes:] * match_ahead], axis=1)
    back = jnp.concatenate([wide[:count, :lanes] * match_back, wide[count:, :lanes] * match_back], axis=1)
    out = []
    for chosen in (
        dot(choose[:half], ahead.astype(jnp.bfloat16)), dot(choose[half:], back.astype(jnp.bfloat16))
    ):
        for start in (0, lanes):
            part = chosen[:, start : start + lanes]
            rows = jnp.where(first_part, part[: half // 2], part[half // 2 :])
            out.append(rows.reshape(planes, 8, lanes))
    return out


def plane_rows(ref, ys):
    parts, _, colours, zs, width = ref.shape
    return jnp.concatenate(
        [ref[p, :ys, c].reshape(ys * zs, width) for p in range(parts) for c in range(colours)],
        axis=0,
    )


def edges_kernel(
    raw_hbm, links_x_hbm, links_y_hbm,
    first_ref, last_ref, raw_ref, links_x_ref, links_y_ref, maps_ref, past_maps_ref, arrived,
):
    parts, planes, ys, colours, zs, _ = raw_hbm.shape
    sources = (raw_hbm.at[:, planes - 1], raw_hbm.at[:, 0], links_x_hbm, links_y_hbm, raw_hbm)
    targets = (last_ref.at[:, :ys], first_ref, links_x_ref, links_y_ref, raw_ref)
    copies = [
        pltpu.make_async_copy(source, target, arrived.at[i])
        for i, (source, target) in enumerate(zip(sources, targets))
    ]
    for copy in copies:
        copy.start()
    last_ref[:, ys:] = jnp.zeros((parts, colours) + last_ref.shape[2:], last_ref.dtype)
    write_maps(maps_ref, parts, colours, planes, ys, zs)
    write_maps(past_maps_ref, parts, colours, 1, ys, zs)
    copies[2].wait()
    last_ref[:, ys:, :, :, :ys] = links_x_ref[:, :, :, planes - 1]
    for copy in copies[:2] + copies[3:]:
        copy.wait()


def site_matrix(rows_and_masks, count):
    blocks = []
    for q in range(count):
        block = None
        for rows, mask in rows_and_masks:
            term = rows[q : q + 1] * mask
            block = term if block is None else block + term
        blocks.append(block.astype(jnp.bfloat16))
    return jnp.concatenate(blocks, axis=0)


def prepare_kernel(
    raw_ref, links_x_ref, links_y_ref, maps_ref, ends_ref, ahead_x_ref, back_x_ref, ahead_y_ref, back_y_ref
):
    parts, planes, ys, colours, zs, width = raw_ref.shape
    lanes = ahead_y_ref.shape[2]
    ahead_x, ahead_y, back_x, back_y = coefficients(
        links_x_ref[...].reshape(-1, ys), links_y_ref[...].reshape(-1, ys), maps_ref, planes
    )
    ahead_x_ref[...] = ahead_x
    back_x_ref[...] = back_x
    ahead_y_ref[...] = ahead_y
    back_y_ref[...] = back_y
    filler = jnp.zeros((8, width - 128), jnp.float32)
    spare = ends_ref.shape[1] - 2 * parts * colours * zs - 8
    for x in range(planes):
        pieces = [
            raw_ref[p, x, y].astype(jnp.float32).reshape(colours * zs, width) for y in (0, ys - 1) for p in range(parts)
        ]
        pieces.append(jnp.concatenate([back_y[x, :, lanes - 128 :], filler], axis=1))
        if spare:
            pieces.append(jnp.zeros((spare, width), jnp.float32))
        ends_ref[x] = jnp.concatenate(pieces, axis=0).astype(jnp.bfloat16)


def turn_kernel(raw_ref, rows_ref, turned_ref):
    planes, depth, width = rows_ref.shape
    for x in range(planes):
        rows_ref[place_of(x, planes)] = plane_rows(raw_ref.at[:, x], raw_ref.shape[2])
    turned_ref[...] = rows_ref[...].reshape(planes * depth, width).T


def move_plane(same, count, ahead, back, above, below):
    depth = same.shape[1]
    moved = dot(site_matrix([(ahead[:, :depth], same)], count), above)
    return (moved + dot(site_matrix([(back[:, :depth], same)], count), below)).astype(jnp.bfloat16)


def same_site(sites, depth):
    site, lane = iotas((sites, depth))
    return (lane % sites == site).astype(jnp.float32)


def set_right(right_ref, place, moved):
    depth, width = moved.shape
    half = depth // 2
    start = place * depth
    real, imag = moved[:half], moved[half:]
    right_ref[start : start + half, :width] = real
    right_ref[start : start + half, width:] = imag
    right_ref[start + half : start + depth, :width] = imag
    right_ref[start + half : start + depth, width:] = -real


def inner_kernel(
    sites, raw_ref, ahead_ref, back_ref, rows_ref, right_ref, turned_ref, matrix_ref, ahead_part_ref, back_part_ref
):
    planes, depth, width = rows_ref.shape
    for x in range(planes):
        rows_ref[place_of(x, planes)] = plane_rows(raw_ref.at[:, x], raw_ref.shape[2])
    same = same_site(sites, depth)
    for x in range(1, planes - 1):
        above = rows_ref[place_of(x + 1, planes)]
        below = rows_ref[place_of(x - 1, planes)]
        moved = move_plane(same, depth // sites, ahead_ref[x], back_ref[x - 1], above, below)
        set_right(right_ref, place_of(x, planes), moved)
    turned_ref[...] = rows_ref[...].reshape(planes * depth, width).T
    x, count = planes - 1, depth // sites
    matrix_ref[...] = site_matrix([(ahead_ref[x, :, :depth], same)], count)
    ahead_part_ref[...] = dot(site_matrix([(ahead_ref[0, :, :depth], same)], count), rows_ref[place_of(1, planes)])
    below = rows_ref[place_of(x - 1, planes)]
    back_part_ref[...] = dot(site_matrix([(back_ref[x - 1, :, :depth], same)], count), below)


def begin_first_kernel(own_ref, others_ref, right_ref, total_ref):
    inner = right_ref.shape[0]
    right = right_ref[...]
    total_ref[0] = dot(own_ref[:, :inner], right)
    for k in range(others_ref.shape[0]):
        total_ref[k + 1] = dot(others_ref[k, :, :inner], right)


def bits(axis):
    return range(lax.axis_size(axis).bit_length() - 1)


def steps():
    one = [("gx", bit) for bit in bits("gx")[:-1]]
    two = [("gy", bit) for bit in bits("gy")]
    both = min(len(one), len(two))
    pairs = [pair for ends in zip(one, two) for pair in (ends, ends[::-1])]
    return pairs + [(step, step) for step in one[both:] + two[both:]]


def my_bit(axis, bit):
    return lax.bitwise_and(lax.shift_right_logical(lax.axis_index(axis), bit), 1)


def my_side(step):
    even, odd = (my_bit(*way) for way in step)
    return jnp.where(my_bit("ma", 0) == 0, even, odd)


def half_of(kind):
    half = lax.bitwise_xor(my_bit("gx", bits("gx")[-1]), 1 - kind)
    return lax.bitwise_xor(half, lax.axis_index("ma"))


def share(total, keep_ref, send_ref, total_ref):
    blocks, rows, double = total_ref.shape
    parts, count, _, width = keep_ref.shape
    total_ref[...] = total.reshape(blocks, rows, double)
    odd_core = my_bit("ma", 0)
    across_y = lax.axis_size("gy")
    plan = steps()
    mine = my_side(plan[0])

    def at(side, index):
        owners = []
        for core in range(2):
            place = {"gx": 0, "gy": 0}
            for k, step in enumerate(plan):
                axis, bit = step[core]
                digit = side if k == 0 else index >> (len(plan) - 1 - k) & 1
                place[axis] += digit * (1 << bit)
            owners.append(place["gx"] * across_y + place["gy"])
        return jnp.where(odd_core == 0, owners[0], owners[1])

    for index in range(count):
        for ref, side in ((keep_ref, mine), (send_ref, 1 - mine)):
            block = total_ref[at(side, index)].astype(ref.dtype)
            for p in range(parts):
                ref[p, index] = block[:, p * width : (p + 1) * width]


def first_share(kind, own_ref, others_ref, begun_ref, right, keep_ref, send_ref, total_ref):
    half = half_of(kind)
    inner = own_ref.shape[1] - right.shape[0]
    left = jnp.where(half == 0, own_ref[:, inner:], others_ref[0, :, inner:])
    share(begun_ref[half] + dot(left, right), keep_ref, send_ref, total_ref)


def first_kernel(
    sites, high_ref, low_ref, matrix_ref, ahead_part_ref, back_part_ref, past_maps_ref, own_ref, others_ref, begun_ref,
    *refs,
):
    keep_ref, send_ref, right_ref, total_ref = refs
    depth = matrix_ref.shape[0]
    same = same_site(sites, depth)
    _, ys, colours, zs, _ = high_ref.shape
    links = low_ref[:, ys:, :, :, :ys].reshape(-1, ys)
    lanes = past_maps_ref.shape[1] // 2
    count = links.shape[0]
    spread = past_maps_ref[:ys, :lanes].astype(jnp.bfloat16)
    match = past_maps_ref[ys : ys + count, lanes:]
    start = past_maps_ref.shape[0] - 24
    choose = past_maps_ref[start : start + 16, :count].astype(jnp.bfloat16)
    past = dot(choose, (dot(links, spread) * match).astype(jnp.bfloat16))
    past = jnp.where(past_maps_ref[start + 16 : start + 17, :lanes] > 0.5, past[:8], past[8:])
    past = site_matrix([(past[:, :depth], same)], depth // sites)
    moved = ahead_part_ref[...] + dot(past, plane_rows(low_ref, ys))
    set_right(right_ref, 0, moved.astype(jnp.bfloat16))
    moved = dot(matrix_ref[...], plane_rows(high_ref, ys)) + back_part_ref[...]
    set_right(right_ref, 1, moved.astype(jnp.bfloat16))
    first_share(0, own_ref, others_ref, begun_ref, right_ref[...], keep_ref, send_ref, total_ref)


def first_own_kernel(own_ref, others_ref, begun_ref, right_ref, keep_ref, send_ref, total_ref):
    first_share(1, own_ref, others_ref, begun_ref, right_ref[...], keep_ref, send_ref, total_ref)


def begin_y_kernel(sites, zs, rows_ref, others_ref, ahead_ref, back_ref, part_ref):
    planes, depth, _ = rows_ref.shape
    site, lane = iotas((sites, depth))
    to_next = jnp.where(lane % sites == site + zs, -1.0, 0.0)
    to_last = jnp.where(lane % sites == site - zs, -1.0, 0.0)
    for x in range(planes):
        ahead, back = ahead_ref[x, :, :depth], back_ref[x, :, :depth]
        matrix = site_matrix([(ahead, to_next), (back, to_last)], depth // sites)
        place = place_of(x, planes)
        part_ref[0, place] = dot(matrix, rows_ref[place])
        for k in range(others_ref.shape[0]):
            part_ref[k + 1, place] = dot(matrix, others_ref[k, place])


def move_y_kernel(sites, zs, part_ref, near_ref, far_ref, ahead_ref, turned_ref, field_ref):
    groups, planes, depth, width = part_ref.shape
    row_size = depth // sites * zs
    tail = 128
    head = ahead_ref.shape[2] - tail
    site, lane = iotas((sites, tail))
    lane = lane + head
    upper = (lane >= depth) & (lane < depth + row_size)
    lower = (lane >= depth + row_size) & (lane < depth + 2 * row_size)
    to_next = jnp.where(upper & (site == sites - zs + lane % zs), -1.0, 0.0)
    to_last = jnp.where(lower & (site == lane % zs), -1.0, 0.0)
    above = jnp.zeros((depth - head, width), jnp.float32)
    below = jnp.zeros((tail - 2 * row_size - (depth - head), width), jnp.float32)
    for x in range(planes):
        near = near_ref[x].astype(jnp.float32)
        past = near[2 * row_size : 2 * row_size + 8, :tail]
        matrix = site_matrix([(ahead_ref[x, :, head:], to_next), (past, to_last)], depth // sites)
        place = place_of(x, planes)
        for k in range(groups):
            edge = near[: 2 * row_size] if k == 0 else far_ref[k - 1, x].astype(jnp.float32)
            column = jnp.concatenate([above, edge, below], axis=0).astype(jnp.bfloat16)
            field_ref[k, place] = (part_ref[k, place] + dot(matrix, column)).astype(jnp.bfloat16)
    for k in range(groups):
        turned_ref[k] = field_ref[k].reshape(planes * depth, width).T


def second_share(kind, lefts_ref, right_ref, edge_ref, keep_ref, send_ref, total_ref):
    half = half_of(kind)
    inner = right_ref.shape[0]
    total = dot(lefts_ref[half, :, :inner], right_ref[...]) + dot(lefts_ref[half, :, inner:], edge_ref[...])
    share(total, keep_ref, send_ref, total_ref)


def second_kernel(lefts_ref, right_ref, edge_ref, keep_ref, send_ref, total_ref):
    second_share(0, lefts_ref, right_ref, edge_ref, keep_ref, send_ref, total_ref)


def second_own_kernel(lefts_ref, right_ref, edge_ref, first_ref, keep_ref, send_ref, total_ref):
    parts = first_ref.shape[0]
    send_ref[:parts] = first_ref[...]
    second_share(1, lefts_ref, right_ref, edge_ref, keep_ref, send_ref.at[parts:], total_ref)


def exchange(block, step):
    axes = ("gx", "gy", "ma")
    sizes = [lax.axis_size(axis) for axis in axes]
    route = []
    for source in range(sizes[0] * sizes[1] * sizes[2]):
        where = [source // (sizes[1] * sizes[2]), source // sizes[2] % sizes[1], source % sizes[2]]
        axis, bit = step[where[2] % 2]
        where[axes.index(axis)] ^= 1 << bit
        route.append((source, (where[0] * sizes[1] + where[1]) * sizes[2] + where[2]))
    return lax.ppermute(block, axes, route)


def halve(sums, step, weight=0):
    parts = sum(kept.shape[0] for kept, _, _ in sums)
    count, rows, width = sums[0][0].shape[1:]
    dims = (parts, count // 2, rows, width)

    def merge(*refs):
        *refs, keep_ref, send_ref = refs
        mine = my_side(step)
        start = 0
        for k, (_, _, which) in enumerate(sums):
            kept_ref, came_ref = refs[2 * k : 2 * k + 2]
            came_ref = came_ref if which is None else came_ref.at[which]
            end = start + kept_ref.shape[0]
            for index in range(count // 2):
                low, high = (
                    kept_ref[:, at] + came_ref[:, at].astype(jnp.float32) for at in (index, index + count // 2)
                )
                keep_ref[start:end, index] = jnp.where(mine == 0, low, high)
                send_ref[start:end, index] = jnp.where(mine == 0, high, low).astype(send_ref.dtype)
            start = end

    operands = [a for kept, came, _ in sums for a in (kept, came)]
    keep, send = call(merge, (pltpu.VMEM(dims, jnp.float32), pltpu.VMEM(dims, jnp.bfloat16)), weight, operands)
    return keep, exchange(send, step)


def sum_kernel(kept_ref, came_ref, send_ref):
    send_ref[...] = (kept_ref[...] + came_ref[...].astype(jnp.float32)).astype(send_ref.dtype)


def cross_kernel(start, kept_ref, crossed_ref, out_ref):
    kept = kept_ref[start : start + out_ref.shape[0]]
    out_ref[...] = kept + crossed_ref[...].astype(jnp.float32)


def finish_kernel(came_ref, *refs):
    *kept_refs, out_ref = refs
    parts = out_ref.shape[1]
    for d, kept_ref in enumerate(kept_refs):
        out_ref[d] = kept_ref[:, 0] + came_ref[d * parts : (d + 1) * parts, 0].astype(jnp.float32)


def local(eigen_modes, links_first, links_second):
    f32, bf16 = jnp.float32, jnp.bfloat16
    parts, planes, ys, zs, colours, width = eigen_modes.shape
    sites = ys * zs
    depth = parts * colours * sites
    row_size = parts * colours * zs
    edge = -(-(2 * row_size + 8) // 16) * 16
    lanes = -(-(depth + 2 * row_size) // 128) * 128
    across_x, across_y, groups = (lax.axis_size(a) for a in ("gx", "gy", "ma"))
    rows = groups * width // (across_x * across_y)
    inner_depth = (planes - 2) * depth
    raw = eigen_modes.transpose(0, 1, 2, 4, 3, 5)

    def shape(*dims, dtype=bf16):
        return pltpu.VMEM(dims, dtype)

    field_shape = shape(planes, depth, width)
    turned_shape = shape(width, planes * depth)
    total_shape = shape(groups, width, parts * width, dtype=f32)
    link_shape = shape(planes, 8, lanes, dtype=f32)
    total = pltpu.VMEM((width // rows, rows, parts * width), f32)
    step_flops = 2 * planes * depth * depth * width
    project_flops = 2 * groups * width * planes * depth * parts * width

    raw_others = [shifted(raw, "ma", -step) for step in range(1, groups)]
    raw_links_x, raw_links_y = (a.transpose(0, 1, 2, 3, 5, 4) for a in (links_first, links_second))
    inputs = [raw, raw_links_x, raw_links_y]
    first_plane, last_plane, *inputs, past_maps = call(
        edges_kernel,
        (
            shape(parts, ys, colours, zs, width), shape(parts, ys + colours, colours, zs, width),
            *(shape(*a.shape) for a in inputs),
            shape(map_rows(parts, colours, planes, ys, zs)[-1], 2 * lanes, dtype=f32),
            shape(map_rows(parts, colours, 1, ys, zs)[-1], 2 * lanes, dtype=f32),
        ),
        0,
        inputs,
        [pltpu.SemaphoreType.DMA((5,))],
        [pltpu.HBM] * len(inputs),
    )
    low = shifted(last_plane, "gx", 1)
    high = shifted(first_plane, "gx", -1)
    ends, ahead_x, back_x, ahead_y, back_y = call(
        prepare_kernel,
        (shape(planes, edge, width), link_shape, link_shape, link_shape, link_shape),
        0,
        inputs,
    )
    near = shifted(ends, "gy", 1)
    if across_y != 2:
        ahead_row = lax.broadcasted_iota(jnp.int32, ends.shape, 1) < row_size
        near = jnp.where(ahead_row, shifted(ends, "gy", -1), near)

    plan = steps()
    top = ("gx", bits("gx")[-1])
    pieces = across_x * across_y // 4
    kept_shape = shape(parts, pieces, rows, width, dtype=f32)
    sent_shape = shape(parts, pieces, rows, width)

    def inner(*refs):
        inner_kernel(sites, *refs)

    def first(*refs):
        first_kernel(sites, *refs)

    def begin_y(*refs):
        begin_y_kernel(sites, zs, *refs)

    def move_y(*refs):
        move_y_kernel(sites, zs, *refs)

    field, right, own, matrix, ahead_part, back_part = call(
        inner,
        (
            field_shape, shape(inner_depth, parts * width), turned_shape, shape(depth, depth),
            shape(depth, width, dtype=f32), shape(depth, width, dtype=f32),
        ),
        2 * step_flops,
        [inputs[0], ahead_x, back_x],
    )
    turned = [call(turn_kernel, (field_shape, turned_shape), step_flops // 4, [r]) for r in raw_others]
    fields = jnp.stack([t[0] for t in turned])
    others = jnp.stack([t[1] for t in turned])
    begun_first = call(begin_first_kernel, total_shape, project_flops, [own, others, right])
    part_y = call(
        begin_y, shape(groups, planes, depth, width, dtype=f32), 2 * step_flops, [field, fields, ahead_y, back_y]
    )
    part_y, begun_first = lax.optimization_barrier((part_y, begun_first))
    kept_first, sent_first, right_edge = call(
        first,
        (kept_shape, sent_shape, shape(2 * depth, parts * width)),
        project_flops,
        [high, low, matrix, ahead_part, back_part, past_maps, own, others, begun_first],
        [total],
    )
    came_first = exchange(sent_first, plan[0])
    near, right_edge = lax.optimization_barrier((near, right_edge))
    near_rows = near[:, : 2 * row_size]
    far = jnp.stack([shifted(near_rows, "ma", -step) for step in range(1, groups)])
    lefts = call(
        move_y, shape(groups, width, planes * depth), 2 * step_flops,
        [part_y, near, far, ahead_y],
        [pltpu.VMEM((groups,) + field_shape.shape, bf16)],
    )
    kept_second, sent_second = call(
        second_kernel, (kept_shape, sent_shape), 8 * project_flops, [lefts, right, right_edge], [total]
    )
    came_second = exchange(sent_second, plan[0])
    right_edge, kept_second = lax.optimization_barrier((right_edge, kept_second))
    own_first, sent_own = call(
        first_own_kernel, (kept_shape, sent_shape), 0, [own, others, begun_first, right_edge], [total]
    )
    own_second, sent_own = call(
        second_own_kernel, (kept_shape, shape(2 * parts, pieces, rows, width)), 0,
        [lefts, right, right_edge, sent_own], [total],
    )
    came_own = exchange(sent_own, plan[0])
    staying = [(own_first, came_own, slice(0, parts)), (own_second, came_own, slice(parts, 2 * parts))]
    crossing = [(kept_first, came_first), (kept_second, came_second)]
    after = own_second
    for step in plan[1:]:
        for d, (kept, came) in enumerate(crossing):
            came, after = lax.optimization_barrier((came, after))
            crossing[d] = halve([(kept, came, None)], step, 4 * project_flops if d else 0)
            after = crossing[d][0]
    crossed = []
    for kept, came in crossing:
        came, after = lax.optimization_barrier((came, after))
        after = call(sum_kernel, pltpu.VMEM(kept.shape, bf16), 0, [kept, came])
        crossed.append(exchange(after, (top, top)))
    for step in plan[1:]:
        kept, came, which = staying[0]
        came, after = lax.optimization_barrier((came, after))
        sums = [(kept, came, which)] + [(k, came, w) for k, _, w in staying[1:]]
        kept, came = halve(sums, step)
        staying, after = [(kept, came, None)], kept
    kept, came, _ = staying[0]
    totals = []
    for d, block in enumerate(crossed):

        def cross(*refs, start=d * parts):
            cross_kernel(start, *refs)

        block, after = lax.optimization_barrier((block, after))
        after = call(cross, shape(*block.shape, dtype=f32), 4 * project_flops, [kept, block])
        totals.append(after)
    came, after = lax.optimization_barrier((came, after))
    return call(
        finish_kernel, jax.ShapeDtypeStruct((2, parts, rows, width), f32), 0, [came, *totals]
    )


def solution(mesh):
    return jax.shard_map(
        local,
        mesh=mesh,
        in_specs=(
            P("cuts", "gx", "gy", None, None, "ma"),
            P("cuts", None, None, "gx", "gy", None),
            P("cuts", None, None, "gx", "gy", None),
        ),
        out_specs=P("cuts", None, ("gx", "gy"), "ma"),
        check_vma=False,
    )
```

```python
import jax
import jax.numpy as jnp
from jax import lax
from jax.experimental import pallas as pl
from jax.experimental.pallas import tpu as pltpu
from jax.sharding import PartitionSpec as P

VMEM_LIMIT = 16 * 1024 * 1024


def shifted(block, axis, distance):
    devices = range(lax.axis_size(axis))
    route = [((i - distance) % len(devices), i) for i in devices]
    return lax.ppermute(block, axis, route)


def call(body, out_shape, flops, operands, scratch=(), places=None):
    places = places or [pltpu.VMEM] * len(operands)
    return pl.pallas_call(
        body,
        out_shape=out_shape,
        in_specs=[pl.BlockSpec(memory_space=place) for place in places],
        scratch_shapes=scratch,
        cost_estimate=pl.CostEstimate(flops=flops // 2, bytes_accessed=0, transcendentals=0),
        compiler_params=pltpu.CompilerParams(vmem_limit_bytes=VMEM_LIMIT),
    )(*(pltpu.with_memory_space_constraint(a, place) for a, place in zip(operands, places)))


def dot(a, b):
    return jnp.dot(a, b, preferred_element_type=jnp.float32)


def iotas(shape):
    return (
        lax.broadcasted_iota(jnp.int32, shape, 0),
        lax.broadcasted_iota(jnp.int32, shape, 1),
    )


def place_of(x, planes):
    return planes - 2 if x == 0 else x if x == planes - 1 else x - 1


def map_rows(parts, colours, planes, ys, zs):
    match = ys
    choose = match + -(-parts * colours * colours * planes * zs // 8) * 8
    first_part = choose + 2 * parts * planes * 8
    return match, choose, first_part, first_part + 8


def write_maps(ref, parts, colours, planes, ys, zs):
    lanes = ref.shape[1] // 2
    sites = ys * zs
    depth = parts * colours * sites
    row_size = parts * colours * zs
    match, choose, first_part, _ = map_rows(parts, colours, planes, ys, zs)

    def ones(mask):
        return jnp.where(mask, 1.0, 0.0)

    def column(count):
        return lax.broadcasted_iota(jnp.int32, (count, 1), 0)

    def line(count):
        return lax.broadcasted_iota(jnp.int32, (1, count), 1)

    lane = line(lanes)
    inner = lane < depth
    past = lax.rem(jnp.maximum(lane - depth, 0), row_size)
    used = lane < depth + 2 * row_size
    part = jnp.where(inner, lax.div(lane, colours * sites), lax.div(past, colours * zs))
    colour = lax.rem(jnp.where(inner, lax.div(lane, sites), lax.div(past, zs)), colours)
    z = lax.rem(jnp.where(inner, lane, past), zs)
    y = lax.div(lax.rem(lane, sites), zs)
    ref[:ys, :lanes] = ones(column(ys) == jnp.where(inner, y, ys - 1))
    ref[:ys, lanes:] = ones(column(ys) == jnp.where(inner, y, ys) - 1)

    count = parts * colours * colours * planes * zs

    def link(index):
        x = lax.rem(lax.div(index, zs), planes)
        right = lax.rem(lax.div(index, zs * planes), colours)
        left = lax.rem(lax.div(index, zs * planes * colours), colours)
        return x, right, left, lax.div(index, zs * planes * colours * colours)

    row = column(count)
    _, right, left, _ = link(row)
    row_z = lax.rem(row, zs)
    key = jnp.where(used, colour * zs + z, -1)
    ref[match : match + count, :lanes] = ones(right * zs + row_z == key)
    ref[match : match + count, lanes:] = ones(left * zs + row_z == key)

    out = column(parts * planes * 8)
    field_part = lax.div(out, planes * 8)
    out_x = lax.rem(lax.div(out, 8), planes)
    out_part = lax.div(lax.rem(out, 8), colours)
    out_colour = lax.rem(lax.rem(out, 8), colours)
    x, right, left, source_part = link(line(count))
    source = source_part * planes + x
    wanted = jnp.where(out_part < parts, lax.rem(out_part + field_part, 2) * planes + out_x, -1)
    sign_ahead = jnp.where((field_part == 1) & (out_part == 0), -1.0, 1.0)
    sign_back = jnp.where((field_part == 0) & (out_part == 1), 1.0, -1.0)
    half = parts * planes * 8
    for start, end, sign in ((choose, left, sign_ahead), (choose + half, right, sign_back)):
        hit = source * colours + end == wanted * colours + jnp.where(wanted < 0, -1, out_colour)
        ref[start : start + half, :count] = jnp.where(hit, sign, 0.0)
    ref[first_part:, :lanes] = jnp.broadcast_to(ones(part == 0), (8, lanes))


def coefficients(links_x, links_y, maps_ref, planes):
    lanes = maps_ref.shape[1] // 2
    ys = links_x.shape[1]
    count = links_x.shape[0]
    half = 2 * planes * 8
    wide = dot(jnp.concatenate([links_x, links_y], axis=0), maps_ref[:ys].astype(jnp.bfloat16))
    match = maps_ref[ys : ys + count]
    match_ahead, match_back = match[:, :lanes], match[:, lanes:]
    choose = maps_ref[ys + count : ys + count + 2 * half, :count].astype(jnp.bfloat16)
    first_part = maps_ref[ys + count + 2 * half : ys + count + 2 * half + 1, :lanes] > 0.5
    ahead = jnp.concatenate([wide[:count, :lanes] * match_ahead, wide[count:, lanes:] * match_ahead], axis=1)
    back = jnp.concatenate([wide[:count, :lanes] * match_back, wide[count:, :lanes] * match_back], axis=1)
    out = []
    for chosen in (
        dot(choose[:half], ahead.astype(jnp.bfloat16)), dot(choose[half:], back.astype(jnp.bfloat16))
    ):
        for start in (0, lanes):
            part = chosen[:, start : start + lanes]
            rows = jnp.where(first_part, part[: half // 2], part[half // 2 :])
            out.append(rows.reshape(planes, 8, lanes))
    return out


def plane_rows(ref, ys):
    parts, _, colours, zs, width = ref.shape
    return jnp.concatenate(
        [ref[p, :ys, c].reshape(ys * zs, width) for p in range(parts) for c in range(colours)],
        axis=0,
    )


def edges_kernel(
    raw_hbm, links_x_hbm, links_y_hbm,
    first_ref, last_ref, rows_y_ref, links_x_ref, links_y_ref, maps_ref, past_maps_ref, arrived,
):
    parts, planes, ys, colours, zs, _ = raw_hbm.shape
    sources = (raw_hbm.at[:, planes - 1], raw_hbm.at[:, 0], links_x_hbm, links_y_hbm) + tuple(
        raw_hbm.at[:, :, y] for y in (0, ys - 1)
    )
    targets = (last_ref.at[:, :ys], first_ref, links_x_ref, links_y_ref, rows_y_ref.at[0], rows_y_ref.at[1])
    copies = [
        pltpu.make_async_copy(source, target, arrived.at[i])
        for i, (source, target) in enumerate(zip(sources, targets))
    ]
    for copy in copies:
        copy.start()
    last_ref[:, ys:] = jnp.zeros((parts, colours) + last_ref.shape[2:], last_ref.dtype)
    write_maps(maps_ref, parts, colours, planes, ys, zs)
    write_maps(past_maps_ref, parts, colours, 1, ys, zs)
    copies[2].wait()
    last_ref[:, ys:, :, :, :ys] = links_x_ref[:, :, :, planes - 1]
    for copy in copies[:2] + copies[3:]:
        copy.wait()


def site_matrix(rows_and_masks, count):
    blocks = []
    for q in range(count):
        block = None
        for rows, mask in rows_and_masks:
            term = rows[q : q + 1] * mask
            block = term if block is None else block + term
        blocks.append(block.astype(jnp.bfloat16))
    return jnp.concatenate(blocks, axis=0)


def prepare_kernel(
    rows_y_ref, links_x_ref, links_y_ref, maps_ref, ends_ref, ahead_x_ref, back_x_ref, ahead_y_ref, back_y_ref
):
    _, parts, planes, colours, zs, width = rows_y_ref.shape
    ys = links_x_ref.shape[5]
    lanes = ahead_y_ref.shape[2]
    ahead_x, ahead_y, back_x, back_y = coefficients(
        links_x_ref[...].reshape(-1, ys), links_y_ref[...].reshape(-1, ys), maps_ref, planes
    )
    ahead_x_ref[...] = ahead_x
    back_x_ref[...] = back_x
    ahead_y_ref[...] = ahead_y
    back_y_ref[...] = back_y
    filler = jnp.zeros((8, width - 128), jnp.float32)
    spare = ends_ref.shape[1] - 2 * parts * colours * zs - 8
    for x in range(planes):
        pieces = [
            rows_y_ref[side, p, x].astype(jnp.float32).reshape(colours * zs, width)
            for side in range(2)
            for p in range(parts)
        ]
        pieces.append(jnp.concatenate([back_y[x, :, lanes - 128 :], filler], axis=1))
        if spare:
            pieces.append(jnp.zeros((spare, width), jnp.float32))
        ends_ref[x] = jnp.concatenate(pieces, axis=0).astype(jnp.bfloat16)


def turn_kernel(raw_ref, rows_ref, turned_ref):
    planes, depth, width = rows_ref.shape
    for x in range(planes):
        rows_ref[place_of(x, planes)] = plane_rows(raw_ref.at[:, x], raw_ref.shape[2])
    turned_ref[...] = rows_ref[...].reshape(planes * depth, width).T


def move_plane(same, count, ahead, back, above, below):
    depth = same.shape[1]
    moved = dot(site_matrix([(ahead[:, :depth], same)], count), above)
    return (moved + dot(site_matrix([(back[:, :depth], same)], count), below)).astype(jnp.bfloat16)


def same_site(sites, depth):
    site, lane = iotas((sites, depth))
    return (lane % sites == site).astype(jnp.float32)


def set_right(right_ref, place, moved):
    depth, width = moved.shape
    half = depth // 2
    start = place * depth
    real, imag = moved[:half], moved[half:]
    right_ref[start : start + half, :width] = real
    right_ref[start : start + half, width:] = imag
    right_ref[start + half : start + depth, :width] = imag
    right_ref[start + half : start + depth, width:] = -real


def inner_kernel(
    sites, raw_hbm, ahead_ref, back_ref, rows_ref, right_ref, turned_ref, matrix_ref, ahead_part_ref, back_part_ref,
    raw_ref, arrived,
):
    copy = pltpu.make_async_copy(raw_hbm, raw_ref, arrived)
    copy.start()
    copy.wait()
    planes, depth, width = rows_ref.shape
    for x in range(planes):
        rows_ref[place_of(x, planes)] = plane_rows(raw_ref.at[:, x], raw_ref.shape[2])
    same = same_site(sites, depth)
    for x in range(1, planes - 1):
        above = rows_ref[place_of(x + 1, planes)]
        below = rows_ref[place_of(x - 1, planes)]
        moved = move_plane(same, depth // sites, ahead_ref[x], back_ref[x - 1], above, below)
        set_right(right_ref, place_of(x, planes), moved)
    turned_ref[...] = rows_ref[...].reshape(planes * depth, width).T
    x, count = planes - 1, depth // sites
    matrix_ref[...] = site_matrix([(ahead_ref[x, :, :depth], same)], count)
    ahead_part_ref[...] = dot(site_matrix([(ahead_ref[0, :, :depth], same)], count), rows_ref[place_of(1, planes)])
    below = rows_ref[place_of(x - 1, planes)]
    back_part_ref[...] = dot(site_matrix([(back_ref[x - 1, :, :depth], same)], count), below)


def begin_first_kernel(own_ref, others_ref, right_ref, total_ref):
    inner = right_ref.shape[0]
    right = right_ref[...]
    total_ref[0] = dot(own_ref[:, :inner], right)
    for k in range(others_ref.shape[0]):
        total_ref[k + 1] = dot(others_ref[k, :, :inner], right)


def bits(axis):
    return range(lax.axis_size(axis).bit_length() - 1)


def steps():
    one = [("gx", bit) for bit in bits("gx")[:-1]]
    two = [("gy", bit) for bit in bits("gy")]
    both = min(len(one), len(two))
    pairs = [pair for ends in zip(one, two) for pair in (ends, ends[::-1])]
    return pairs + [(step, step) for step in one[both:] + two[both:]]


def my_bit(axis, bit):
    return lax.bitwise_and(lax.shift_right_logical(lax.axis_index(axis), bit), 1)


def my_side(step):
    even, odd = (my_bit(*way) for way in step)
    return jnp.where(my_bit("ma", 0) == 0, even, odd)


def half_of(kind):
    half = lax.bitwise_xor(my_bit("gx", bits("gx")[-1]), 1 - kind)
    return lax.bitwise_xor(half, lax.axis_index("ma"))


def share(total, keep_ref, send_ref, total_ref):
    blocks, rows, double = total_ref.shape
    parts, count, _, width = keep_ref.shape
    total_ref[...] = total.reshape(blocks, rows, double)
    odd_core = my_bit("ma", 0)
    across_y = lax.axis_size("gy")
    plan = steps()
    mine = my_side(plan[0])

    def at(side, index):
        owners = []
        for core in range(2):
            place = {"gx": 0, "gy": 0}
            for k, step in enumerate(plan):
                axis, bit = step[core]
                digit = side if k == 0 else index >> (len(plan) - 1 - k) & 1
                place[axis] += digit * (1 << bit)
            owners.append(place["gx"] * across_y + place["gy"])
        return jnp.where(odd_core == 0, owners[0], owners[1])

    for index in range(count):
        for ref, side in ((keep_ref, mine), (send_ref, 1 - mine)):
            block = total_ref[at(side, index)].astype(ref.dtype)
            for p in range(parts):
                ref[p, index] = block[:, p * width : (p + 1) * width]


def first_share(kind, own_ref, others_ref, begun_ref, right, keep_ref, send_ref, total_ref):
    half = half_of(kind)
    inner = own_ref.shape[1] - right.shape[0]
    left = jnp.where(half == 0, own_ref[:, inner:], others_ref[0, :, inner:])
    share(begun_ref[half] + dot(left, right), keep_ref, send_ref, total_ref)


def first_kernel(
    sites, high_ref, low_ref, matrix_ref, ahead_part_ref, back_part_ref, past_maps_ref, own_ref, others_ref, begun_ref,
    *refs,
):
    keep_ref, send_ref, right_ref, total_ref = refs
    depth = matrix_ref.shape[0]
    same = same_site(sites, depth)
    _, ys, colours, zs, _ = high_ref.shape
    links = low_ref[:, ys:, :, :, :ys].reshape(-1, ys)
    lanes = past_maps_ref.shape[1] // 2
    count = links.shape[0]
    spread = past_maps_ref[:ys, :lanes].astype(jnp.bfloat16)
    match = past_maps_ref[ys : ys + count, lanes:]
    start = past_maps_ref.shape[0] - 24
    choose = past_maps_ref[start : start + 16, :count].astype(jnp.bfloat16)
    past = dot(choose, (dot(links, spread) * match).astype(jnp.bfloat16))
    past = jnp.where(past_maps_ref[start + 16 : start + 17, :lanes] > 0.5, past[:8], past[8:])
    past = site_matrix([(past[:, :depth], same)], depth // sites)
    moved = ahead_part_ref[...] + dot(past, plane_rows(low_ref, ys))
    set_right(right_ref, 0, moved.astype(jnp.bfloat16))
    moved = dot(matrix_ref[...], plane_rows(high_ref, ys)) + back_part_ref[...]
    set_right(right_ref, 1, moved.astype(jnp.bfloat16))
    first_share(0, own_ref, others_ref, begun_ref, right_ref[...], keep_ref, send_ref, total_ref)


def first_own_kernel(own_ref, others_ref, begun_ref, right_ref, keep_ref, send_ref, total_ref):
    first_share(1, own_ref, others_ref, begun_ref, right_ref[...], keep_ref, send_ref, total_ref)


def begin_y_kernel(sites, zs, rows_ref, others_ref, ahead_ref, back_ref, part_ref):
    planes, depth, _ = rows_ref.shape
    site, lane = iotas((sites, depth))
    to_next = jnp.where(lane % sites == site + zs, -1.0, 0.0)
    to_last = jnp.where(lane % sites == site - zs, -1.0, 0.0)
    for x in range(planes):
        ahead, back = ahead_ref[x, :, :depth], back_ref[x, :, :depth]
        matrix = site_matrix([(ahead, to_next), (back, to_last)], depth // sites)
        place = place_of(x, planes)
        part_ref[0, place] = dot(matrix, rows_ref[place])
        for k in range(others_ref.shape[0]):
            part_ref[k + 1, place] = dot(matrix, others_ref[k, place])


def move_y_kernel(sites, zs, part_ref, near_ref, far_ref, ahead_ref, turned_ref, field_ref):
    groups, planes, depth, width = part_ref.shape
    row_size = depth // sites * zs
    tail = 128
    head = ahead_ref.shape[2] - tail
    site, lane = iotas((sites, tail))
    lane = lane + head
    upper = (lane >= depth) & (lane < depth + row_size)
    lower = (lane >= depth + row_size) & (lane < depth + 2 * row_size)
    to_next = jnp.where(upper & (site == sites - zs + lane % zs), -1.0, 0.0)
    to_last = jnp.where(lower & (site == lane % zs), -1.0, 0.0)
    above = jnp.zeros((depth - head, width), jnp.float32)
    below = jnp.zeros((tail - 2 * row_size - (depth - head), width), jnp.float32)
    for x in range(planes):
        near = near_ref[x].astype(jnp.float32)
        past = near[2 * row_size : 2 * row_size + 8, :tail]
        matrix = site_matrix([(ahead_ref[x, :, head:], to_next), (past, to_last)], depth // sites)
        place = place_of(x, planes)
        for k in range(groups):
            edge = near[: 2 * row_size] if k == 0 else far_ref[k - 1, x].astype(jnp.float32)
            column = jnp.concatenate([above, edge, below], axis=0).astype(jnp.bfloat16)
            field_ref[k, place] = (part_ref[k, place] + dot(matrix, column)).astype(jnp.bfloat16)
    for k in range(groups):
        turned_ref[k] = field_ref[k].reshape(planes * depth, width).T


def second_share(kind, lefts_ref, right_ref, edge_ref, keep_ref, send_ref, total_ref):
    half = half_of(kind)
    inner = right_ref.shape[0]
    total = dot(lefts_ref[half, :, :inner], right_ref[...]) + dot(lefts_ref[half, :, inner:], edge_ref[...])
    share(total, keep_ref, send_ref, total_ref)


def second_kernel(lefts_ref, right_ref, edge_ref, keep_ref, send_ref, total_ref):
    second_share(0, lefts_ref, right_ref, edge_ref, keep_ref, send_ref, total_ref)


def second_own_kernel(lefts_ref, right_ref, edge_ref, first_ref, keep_ref, send_ref, total_ref):
    parts = first_ref.shape[0]
    send_ref[:parts] = first_ref[...]
    second_share(1, lefts_ref, right_ref, edge_ref, keep_ref, send_ref.at[parts:], total_ref)


def exchange(block, step):
    axes = ("gx", "gy", "ma")
    sizes = [lax.axis_size(axis) for axis in axes]
    route = []
    for source in range(sizes[0] * sizes[1] * sizes[2]):
        where = [source // (sizes[1] * sizes[2]), source // sizes[2] % sizes[1], source % sizes[2]]
        axis, bit = step[where[2] % 2]
        where[axes.index(axis)] ^= 1 << bit
        route.append((source, (where[0] * sizes[1] + where[1]) * sizes[2] + where[2]))
    return lax.ppermute(block, axes, route)


def halve(sums, step, weight=0):
    parts = sum(kept.shape[0] for kept, _, _ in sums)
    count, rows, width = sums[0][0].shape[1:]
    dims = (parts, count // 2, rows, width)

    def merge(*refs):
        *refs, keep_ref, send_ref = refs
        mine = my_side(step)
        start = 0
        for k, (_, _, which) in enumerate(sums):
            kept_ref, came_ref = refs[2 * k : 2 * k + 2]
            came_ref = came_ref if which is None else came_ref.at[which]
            end = start + kept_ref.shape[0]
            for index in range(count // 2):
                low, high = (
                    kept_ref[:, at] + came_ref[:, at].astype(jnp.float32) for at in (index, index + count // 2)
                )
                keep_ref[start:end, index] = jnp.where(mine == 0, low, high)
                send_ref[start:end, index] = jnp.where(mine == 0, high, low).astype(send_ref.dtype)
            start = end

    operands = [a for kept, came, _ in sums for a in (kept, came)]
    keep, send = call(merge, (pltpu.VMEM(dims, jnp.float32), pltpu.VMEM(dims, jnp.bfloat16)), weight, operands)
    return keep, exchange(send, step)


def sum_kernel(kept_ref, came_ref, send_ref):
    send_ref[...] = (kept_ref[...] + came_ref[...].astype(jnp.float32)).astype(send_ref.dtype)


def cross_kernel(start, kept_ref, crossed_ref, out_ref):
    kept = kept_ref[start : start + out_ref.shape[0]]
    out_ref[...] = kept + crossed_ref[...].astype(jnp.float32)


def finish_kernel(came_ref, *refs):
    *kept_refs, out_ref = refs
    parts = out_ref.shape[1]
    for d, kept_ref in enumerate(kept_refs):
        out_ref[d] = kept_ref[:, 0] + came_ref[d * parts : (d + 1) * parts, 0].astype(jnp.float32)


def local(eigen_modes, links_first, links_second):
    f32, bf16 = jnp.float32, jnp.bfloat16
    parts, planes, ys, zs, colours, width = eigen_modes.shape
    sites = ys * zs
    depth = parts * colours * sites
    row_size = parts * colours * zs
    edge = -(-(2 * row_size + 8) // 16) * 16
    lanes = -(-(depth + 2 * row_size) // 128) * 128
    across_x, across_y, groups = (lax.axis_size(a) for a in ("gx", "gy", "ma"))
    rows = groups * width // (across_x * across_y)
    inner_depth = (planes - 2) * depth
    raw = eigen_modes.transpose(0, 1, 2, 4, 3, 5)

    def shape(*dims, dtype=bf16):
        return pltpu.VMEM(dims, dtype)

    field_shape = shape(planes, depth, width)
    turned_shape = shape(width, planes * depth)
    total_shape = shape(groups, width, parts * width, dtype=f32)
    link_shape = shape(planes, 8, lanes, dtype=f32)
    total = pltpu.VMEM((width // rows, rows, parts * width), f32)
    step_flops = 2 * planes * depth * depth * width
    project_flops = 2 * groups * width * planes * depth * parts * width

    raw_others = [shifted(raw, "ma", -step) for step in range(1, groups)]
    raw_links_x, raw_links_y = (a.transpose(0, 1, 2, 3, 5, 4) for a in (links_first, links_second))
    inputs = [raw, raw_links_x, raw_links_y]
    first_plane, last_plane, *inputs, past_maps = call(
        edges_kernel,
        (
            shape(parts, ys, colours, zs, width), shape(parts, ys + colours, colours, zs, width),
            shape(2, parts, planes, colours, zs, width),
            *(shape(*a.shape) for a in inputs[1:]),
            shape(map_rows(parts, colours, planes, ys, zs)[-1], 2 * lanes, dtype=f32),
            shape(map_rows(parts, colours, 1, ys, zs)[-1], 2 * lanes, dtype=f32),
        ),
        0,
        inputs,
        [pltpu.SemaphoreType.DMA((6,))],
        [pltpu.HBM] * len(inputs),
    )
    low = shifted(last_plane, "gx", 1)
    high = shifted(first_plane, "gx", -1)
    ends, ahead_x, back_x, ahead_y, back_y = call(
        prepare_kernel,
        (shape(planes, edge, width), link_shape, link_shape, link_shape, link_shape),
        0,
        inputs,
    )
    near = shifted(ends, "gy", 1)
    if across_y != 2:
        ahead_row = lax.broadcasted_iota(jnp.int32, ends.shape, 1) < row_size
        near = jnp.where(ahead_row, shifted(ends, "gy", -1), near)

    plan = steps()
    top = ("gx", bits("gx")[-1])
    pieces = across_x * across_y // 4
    kept_shape = shape(parts, pieces, rows, width, dtype=f32)
    sent_shape = shape(parts, pieces, rows, width)

    def inner(*refs):
        inner_kernel(sites, *refs)

    def first(*refs):
        first_kernel(sites, *refs)

    def begin_y(*refs):
        begin_y_kernel(sites, zs, *refs)

    def move_y(*refs):
        move_y_kernel(sites, zs, *refs)

    field, right, own, matrix, ahead_part, back_part = call(
        inner,
        (
            field_shape, shape(inner_depth, parts * width), turned_shape, shape(depth, depth),
            shape(depth, width, dtype=f32), shape(depth, width, dtype=f32),
        ),
        2 * step_flops,
        [raw, ahead_x, back_x],
        [pltpu.VMEM(raw.shape, bf16), pltpu.SemaphoreType.DMA],
        [pltpu.HBM, pltpu.VMEM, pltpu.VMEM],
    )
    turned = [call(turn_kernel, (field_shape, turned_shape), step_flops // 4, [r]) for r in raw_others]
    fields = jnp.stack([t[0] for t in turned])
    others = jnp.stack([t[1] for t in turned])
    begun_first = call(begin_first_kernel, total_shape, project_flops, [own, others, right])
    part_y = call(
        begin_y, shape(groups, planes, depth, width, dtype=f32), 2 * step_flops, [field, fields, ahead_y, back_y]
    )
    part_y, begun_first = lax.optimization_barrier((part_y, begun_first))
    kept_first, sent_first, right_edge = call(
        first,
        (kept_shape, sent_shape, shape(2 * depth, parts * width)),
        project_flops,
        [high, low, matrix, ahead_part, back_part, past_maps, own, others, begun_first],
        [total],
    )
    came_first = exchange(sent_first, plan[0])
    near, right_edge = lax.optimization_barrier((near, right_edge))
    near_rows = near[:, : 2 * row_size]
    far = jnp.stack([shifted(near_rows, "ma", -step) for step in range(1, groups)])
    lefts = call(
        move_y, shape(groups, width, planes * depth), 2 * step_flops,
        [part_y, near, far, ahead_y],
        [pltpu.VMEM((groups,) + field_shape.shape, bf16)],
    )
    kept_second, sent_second = call(
        second_kernel, (kept_shape, sent_shape), 8 * project_flops, [lefts, right, right_edge], [total]
    )
    came_second = exchange(sent_second, plan[0])
    right_edge, kept_second = lax.optimization_barrier((right_edge, kept_second))
    own_first, sent_own = call(
        first_own_kernel, (kept_shape, sent_shape), 0, [own, others, begun_first, right_edge], [total]
    )
    own_second, sent_own = call(
        second_own_kernel, (kept_shape, shape(2 * parts, pieces, rows, width)), 0,
        [lefts, right, right_edge, sent_own], [total],
    )
    came_own = exchange(sent_own, plan[0])
    staying = [(own_first, came_own, slice(0, parts)), (own_second, came_own, slice(parts, 2 * parts))]
    crossing = [(kept_first, came_first), (kept_second, came_second)]
    after = own_second
    for step in plan[1:]:
        for d, (kept, came) in enumerate(crossing):
            came, after = lax.optimization_barrier((came, after))
            crossing[d] = halve([(kept, came, None)], step, 4 * project_flops if d else 0)
            after = crossing[d][0]
    crossed = []
    for kept, came in crossing:
        came, after = lax.optimization_barrier((came, after))
        after = call(sum_kernel, pltpu.VMEM(kept.shape, bf16), 0, [kept, came])
        crossed.append(exchange(after, (top, top)))
    for step in plan[1:]:
        kept, came, which = staying[0]
        came, after = lax.optimization_barrier((came, after))
        sums = [(kept, came, which)] + [(k, came, w) for k, _, w in staying[1:]]
        kept, came = halve(sums, step)
        staying, after = [(kept, came, None)], kept
    kept, came, _ = staying[0]
    totals = []
    for d, block in enumerate(crossed):

        def cross(*refs, start=d * parts):
            cross_kernel(start, *refs)

        block, after = lax.optimization_barrier((block, after))
        after = call(cross, shape(*block.shape, dtype=f32), 4 * project_flops, [kept, block])
        totals.append(after)
    came, after = lax.optimization_barrier((came, after))
    return call(
        finish_kernel, jax.ShapeDtypeStruct((2, parts, rows, width), f32), 0, [came, *totals]
    )


def solution(mesh):
    return jax.shard_map(
        local,
        mesh=mesh,
        in_specs=(
            P("cuts", "gx", "gy", None, None, "ma"),
            P("cuts", None, None, "gx", "gy", None),
            P("cuts", None, None, "gx", "gy", None),
        ),
        out_specs=P("cuts", None, ("gx", "gy"), "ma"),
        check_vma=False,
    )
```

```python
import jax
import jax.numpy as jnp
from jax import lax
from jax.experimental import pallas as pl
from jax.experimental.pallas import tpu as pltpu
from jax.sharding import PartitionSpec as P

VMEM_LIMIT = 16 * 1024 * 1024


def shifted(block, axis, distance):
    devices = range(lax.axis_size(axis))
    route = [((i - distance) % len(devices), i) for i in devices]
    return lax.ppermute(block, axis, route)


def call(body, out_shape, flops, operands, scratch=(), places=None):
    places = places or [pltpu.VMEM] * len(operands)
    return pl.pallas_call(
        body,
        out_shape=out_shape,
        in_specs=[pl.BlockSpec(memory_space=place) for place in places],
        scratch_shapes=scratch,
        cost_estimate=pl.CostEstimate(flops=flops // 2, bytes_accessed=0, transcendentals=0),
        compiler_params=pltpu.CompilerParams(vmem_limit_bytes=VMEM_LIMIT),
    )(*(pltpu.with_memory_space_constraint(a, place) for a, place in zip(operands, places)))


def dot(a, b):
    return jnp.dot(a, b, preferred_element_type=jnp.float32)


def iotas(shape):
    return (
        lax.broadcasted_iota(jnp.int32, shape, 0),
        lax.broadcasted_iota(jnp.int32, shape, 1),
    )


def place_of(x, planes):
    return planes - 2 if x == 0 else x if x == planes - 1 else x - 1


def map_rows(parts, colours, planes, ys, zs):
    match = ys
    choose = match + -(-parts * colours * colours * planes * zs // 8) * 8
    first_part = choose + 2 * parts * planes * 8
    return match, choose, first_part, first_part + 8


def write_maps(ref, parts, colours, planes, ys, zs):
    lanes = ref.shape[1] // 2
    sites = ys * zs
    depth = parts * colours * sites
    row_size = parts * colours * zs
    match, choose, first_part, _ = map_rows(parts, colours, planes, ys, zs)

    def ones(mask):
        return jnp.where(mask, 1.0, 0.0)

    def column(count):
        return lax.broadcasted_iota(jnp.int32, (count, 1), 0)

    def line(count):
        return lax.broadcasted_iota(jnp.int32, (1, count), 1)

    lane = line(lanes)
    inner = lane < depth
    past = lax.rem(jnp.maximum(lane - depth, 0), row_size)
    used = lane < depth + 2 * row_size
    part = jnp.where(inner, lax.div(lane, colours * sites), lax.div(past, colours * zs))
    colour = lax.rem(jnp.where(inner, lax.div(lane, sites), lax.div(past, zs)), colours)
    z = lax.rem(jnp.where(inner, lane, past), zs)
    y = lax.div(lax.rem(lane, sites), zs)
    ref[:ys, :lanes] = ones(column(ys) == jnp.where(inner, y, ys - 1))
    ref[:ys, lanes:] = ones(column(ys) == jnp.where(inner, y, ys) - 1)

    count = parts * colours * colours * planes * zs

    def link(index):
        x = lax.rem(lax.div(index, zs), planes)
        right = lax.rem(lax.div(index, zs * planes), colours)
        left = lax.rem(lax.div(index, zs * planes * colours), colours)
        return x, right, left, lax.div(index, zs * planes * colours * colours)

    row = column(count)
    _, right, left, _ = link(row)
    row_z = lax.rem(row, zs)
    key = jnp.where(used, colour * zs + z, -1)
    ref[match : match + count, :lanes] = ones(right * zs + row_z == key)
    ref[match : match + count, lanes:] = ones(left * zs + row_z == key)

    out = column(parts * planes * 8)
    field_part = lax.div(out, planes * 8)
    out_x = lax.rem(lax.div(out, 8), planes)
    out_part = lax.div(lax.rem(out, 8), colours)
    out_colour = lax.rem(lax.rem(out, 8), colours)
    x, right, left, source_part = link(line(count))
    source = source_part * planes + x
    wanted = jnp.where(out_part < parts, lax.rem(out_part + field_part, 2) * planes + out_x, -1)
    sign_ahead = jnp.where((field_part == 1) & (out_part == 0), -1.0, 1.0)
    sign_back = jnp.where((field_part == 0) & (out_part == 1), 1.0, -1.0)
    half = parts * planes * 8
    for start, end, sign in ((choose, left, sign_ahead), (choose + half, right, sign_back)):
        hit = source * colours + end == wanted * colours + jnp.where(wanted < 0, -1, out_colour)
        ref[start : start + half, :count] = jnp.where(hit, sign, 0.0)
    ref[first_part:, :lanes] = jnp.broadcast_to(ones(part == 0), (8, lanes))


def coefficients(links_x, links_y, maps_ref, planes):
    lanes = maps_ref.shape[1] // 2
    ys = links_x.shape[1]
    count = links_x.shape[0]
    half = 2 * planes * 8
    wide = dot(jnp.concatenate([links_x, links_y], axis=0), maps_ref[:ys].astype(jnp.bfloat16))
    match = maps_ref[ys : ys + count]
    match_ahead, match_back = match[:, :lanes], match[:, lanes:]
    choose = maps_ref[ys + count : ys + count + 2 * half, :count].astype(jnp.bfloat16)
    first_part = maps_ref[ys + count + 2 * half : ys + count + 2 * half + 1, :lanes] > 0.5
    ahead = jnp.concatenate([wide[:count, :lanes] * match_ahead, wide[count:, lanes:] * match_ahead], axis=1)
    back = jnp.concatenate([wide[:count, :lanes] * match_back, wide[count:, :lanes] * match_back], axis=1)
    out = []
    for chosen in (
        dot(choose[:half], ahead.astype(jnp.bfloat16)), dot(choose[half:], back.astype(jnp.bfloat16))
    ):
        for start in (0, lanes):
            part = chosen[:, start : start + lanes]
            rows = jnp.where(first_part, part[: half // 2], part[half // 2 :])
            out.append(rows.reshape(planes, 8, lanes))
    return out


def plane_rows(ref, ys):
    parts, _, colours, zs, width = ref.shape
    return jnp.concatenate(
        [ref[p, :ys, c].reshape(ys * zs, width) for p in range(parts) for c in range(colours)],
        axis=0,
    )


def edges_kernel(
    raw_hbm, links_x_hbm, links_y_hbm,
    first_ref, last_ref, raw_ref, links_x_ref, links_y_ref, maps_ref, past_maps_ref, arrived,
):
    parts, planes, ys, colours, zs, _ = raw_hbm.shape
    sources = (raw_hbm.at[:, planes - 1], raw_hbm.at[:, 0], links_x_hbm, links_y_hbm, raw_hbm)
    targets = (last_ref.at[:, :ys], first_ref, links_x_ref, links_y_ref, raw_ref)
    copies = [
        pltpu.make_async_copy(source, target, arrived.at[i])
        for i, (source, target) in enumerate(zip(sources, targets))
    ]
    for copy in copies:
        copy.start()
    last_ref[:, ys:] = jnp.zeros((parts, colours) + last_ref.shape[2:], last_ref.dtype)
    write_maps(maps_ref, parts, colours, planes, ys, zs)
    write_maps(past_maps_ref, parts, colours, 1, ys, zs)
    copies[2].wait()
    last_ref[:, ys:, :, :, :ys] = links_x_ref[:, :, :, planes - 1]
    for copy in copies[:2] + copies[3:]:
        copy.wait()


def site_matrix(rows_and_masks, count):
    blocks = []
    for q in range(count):
        block = None
        for rows, mask in rows_and_masks:
            term = rows[q : q + 1] * mask
            block = term if block is None else block + term
        blocks.append(block.astype(jnp.bfloat16))
    return jnp.concatenate(blocks, axis=0)


def prepare_kernel(
    raw_ref, links_x_ref, links_y_ref, maps_ref, ends_ref, ahead_x_ref, back_x_ref, ahead_y_ref, back_y_ref
):
    parts, planes, ys, colours, zs, width = raw_ref.shape
    lanes = ahead_y_ref.shape[2]
    ahead_x, ahead_y, back_x, back_y = coefficients(
        links_x_ref[...].reshape(-1, ys), links_y_ref[...].reshape(-1, ys), maps_ref, planes
    )
    ahead_x_ref[...] = ahead_x
    back_x_ref[...] = back_x
    ahead_y_ref[...] = ahead_y
    back_y_ref[...] = back_y
    filler = jnp.zeros((8, width - 128), jnp.float32)
    spare = ends_ref.shape[1] - 2 * parts * colours * zs - 8
    for x in range(planes):
        pieces = [
            raw_ref[p, x, y].astype(jnp.float32).reshape(colours * zs, width) for y in (0, ys - 1) for p in range(parts)
        ]
        pieces.append(jnp.concatenate([back_y[x, :, lanes - 128 :], filler], axis=1))
        if spare:
            pieces.append(jnp.zeros((spare, width), jnp.float32))
        ends_ref[x] = jnp.concatenate(pieces, axis=0).astype(jnp.bfloat16)


def turn_kernel(raw_ref, rows_ref, turned_ref):
    planes, depth, width = rows_ref.shape
    for x in range(planes):
        rows_ref[place_of(x, planes)] = plane_rows(raw_ref.at[:, x], raw_ref.shape[2])
    turned_ref[...] = rows_ref[...].reshape(planes * depth, width).T


def move_plane(same, count, ahead, back, above, below):
    depth = same.shape[1]
    moved = dot(site_matrix([(ahead[:, :depth], same)], count), above)
    return (moved + dot(site_matrix([(back[:, :depth], same)], count), below)).astype(jnp.bfloat16)


def same_site(sites, depth):
    site, lane = iotas((sites, depth))
    return (lane % sites == site).astype(jnp.float32)


def set_right(right_ref, place, moved):
    depth, width = moved.shape
    half = depth // 2
    start = place * depth
    real, imag = moved[:half], moved[half:]
    right_ref[start : start + half, :width] = real
    right_ref[start : start + half, width:] = imag
    right_ref[start + half : start + depth, :width] = imag
    right_ref[start + half : start + depth, width:] = -real


def inner_kernel(
    sites, raw_ref, ahead_ref, back_ref, rows_ref, right_ref, turned_ref, matrix_ref, ahead_part_ref, back_part_ref
):
    planes, depth, width = rows_ref.shape
    for x in range(planes):
        rows_ref[place_of(x, planes)] = plane_rows(raw_ref.at[:, x], raw_ref.shape[2])
    same = same_site(sites, depth)
    for x in range(1, planes - 1):
        above = rows_ref[place_of(x + 1, planes)]
        below = rows_ref[place_of(x - 1, planes)]
        moved = move_plane(same, depth // sites, ahead_ref[x], back_ref[x - 1], above, below)
        set_right(right_ref, place_of(x, planes), moved)
    turned_ref[...] = rows_ref[...].reshape(planes * depth, width).T
    x, count = planes - 1, depth // sites
    matrix_ref[...] = site_matrix([(ahead_ref[x, :, :depth], same)], count)
    ahead_part_ref[...] = dot(site_matrix([(ahead_ref[0, :, :depth], same)], count), rows_ref[place_of(1, planes)])
    below = rows_ref[place_of(x - 1, planes)]
    back_part_ref[...] = dot(site_matrix([(back_ref[x - 1, :, :depth], same)], count), below)


def begin_first_kernel(own_ref, others_ref, right_ref, total_ref):
    inner = right_ref.shape[0]
    right = right_ref[...]
    total_ref[0] = dot(own_ref[:, :inner], right)
    for k in range(others_ref.shape[0]):
        total_ref[k + 1] = dot(others_ref[k, :, :inner], right)


def bits(axis):
    return range(lax.axis_size(axis).bit_length() - 1)


def steps():
    one = [("gx", bit) for bit in bits("gx")[:-1]]
    two = [("gy", bit) for bit in bits("gy")]
    both = min(len(one), len(two))
    pairs = [pair for ends in zip(one, two) for pair in (ends, ends[::-1])]
    return pairs + [(step, step) for step in one[both:] + two[both:]]


def my_bit(axis, bit):
    return lax.bitwise_and(lax.shift_right_logical(lax.axis_index(axis), bit), 1)


def my_side(step):
    even, odd = (my_bit(*way) for way in step)
    return jnp.where(my_bit("ma", 0) == 0, even, odd)


def half_of(kind):
    half = lax.bitwise_xor(my_bit("gx", bits("gx")[-1]), 1 - kind)
    return lax.bitwise_xor(half, lax.axis_index("ma"))


def share(total, keep_ref, send_ref, total_ref):
    blocks, rows, double = total_ref.shape
    parts, count, _, width = keep_ref.shape
    total_ref[...] = total.reshape(blocks, rows, double)
    odd_core = my_bit("ma", 0)
    across_y = lax.axis_size("gy")
    plan = steps()
    mine = my_side(plan[0])

    def at(side, index):
        owners = []
        for core in range(2):
            place = {"gx": 0, "gy": 0}
            for k, step in enumerate(plan):
                axis, bit = step[core]
                digit = side if k == 0 else index >> (len(plan) - 1 - k) & 1
                place[axis] += digit * (1 << bit)
            owners.append(place["gx"] * across_y + place["gy"])
        return jnp.where(odd_core == 0, owners[0], owners[1])

    for index in range(count):
        for ref, side in ((keep_ref, mine), (send_ref, 1 - mine)):
            block = total_ref[at(side, index)].astype(ref.dtype)
            for p in range(parts):
                ref[p, index] = block[:, p * width : (p + 1) * width]


def first_share(kind, own_ref, others_ref, begun_ref, right, keep_ref, send_ref, total_ref):
    half = half_of(kind)
    inner = own_ref.shape[1] - right.shape[0]
    left = jnp.where(half == 0, own_ref[:, inner:], others_ref[0, :, inner:])
    share(begun_ref[half] + dot(left, right), keep_ref, send_ref, total_ref)


def first_kernel(
    sites, high_ref, low_ref, matrix_ref, ahead_part_ref, back_part_ref, past_maps_ref, own_ref, others_ref, begun_ref,
    *refs,
):
    keep_ref, send_ref, right_ref, total_ref = refs
    depth = matrix_ref.shape[0]
    same = same_site(sites, depth)
    _, ys, colours, zs, _ = high_ref.shape
    links = low_ref[:, ys:, :, :, :ys].reshape(-1, ys)
    lanes = past_maps_ref.shape[1] // 2
    count = links.shape[0]
    spread = past_maps_ref[:ys, :lanes].astype(jnp.bfloat16)
    match = past_maps_ref[ys : ys + count, lanes:]
    start = past_maps_ref.shape[0] - 24
    choose = past_maps_ref[start : start + 16, :count].astype(jnp.bfloat16)
    past = dot(choose, (dot(links, spread) * match).astype(jnp.bfloat16))
    past = jnp.where(past_maps_ref[start + 16 : start + 17, :lanes] > 0.5, past[:8], past[8:])
    past = site_matrix([(past[:, :depth], same)], depth // sites)
    moved = ahead_part_ref[...] + dot(past, plane_rows(low_ref, ys))
    set_right(right_ref, 0, moved.astype(jnp.bfloat16))
    moved = dot(matrix_ref[...], plane_rows(high_ref, ys)) + back_part_ref[...]
    set_right(right_ref, 1, moved.astype(jnp.bfloat16))
    first_share(0, own_ref, others_ref, begun_ref, right_ref[...], keep_ref, send_ref, total_ref)


def first_own_kernel(own_ref, others_ref, begun_ref, right_ref, keep_ref, send_ref, total_ref):
    first_share(1, own_ref, others_ref, begun_ref, right_ref[...], keep_ref, send_ref, total_ref)


def begin_y_kernel(sites, zs, rows_ref, others_ref, ahead_ref, back_ref, part_ref):
    planes, depth, _ = rows_ref.shape
    site, lane = iotas((sites, depth))
    to_next = jnp.where(lane % sites == site + zs, -1.0, 0.0)
    to_last = jnp.where(lane % sites == site - zs, -1.0, 0.0)
    for x in range(planes):
        ahead, back = ahead_ref[x, :, :depth], back_ref[x, :, :depth]
        matrix = site_matrix([(ahead, to_next), (back, to_last)], depth // sites)
        place = place_of(x, planes)
        part_ref[0, place] = dot(matrix, rows_ref[place])
        for k in range(others_ref.shape[0]):
            part_ref[k + 1, place] = dot(matrix, others_ref[k, place])


def move_y_kernel(sites, zs, part_ref, near_ref, far_ref, ahead_ref, turned_ref, field_ref):
    groups, planes, depth, width = part_ref.shape
    row_size = depth // sites * zs
    tail = 128
    head = ahead_ref.shape[2] - tail
    site, lane = iotas((sites, tail))
    lane = lane + head
    upper = (lane >= depth) & (lane < depth + row_size)
    lower = (lane >= depth + row_size) & (lane < depth + 2 * row_size)
    to_next = jnp.where(upper & (site == sites - zs + lane % zs), -1.0, 0.0)
    to_last = jnp.where(lower & (site == lane % zs), -1.0, 0.0)
    above = jnp.zeros((depth - head, width), jnp.float32)
    below = jnp.zeros((tail - 2 * row_size - (depth - head), width), jnp.float32)
    for x in range(planes):
        near = near_ref[x].astype(jnp.float32)
        past = near[2 * row_size : 2 * row_size + 8, :tail]
        matrix = site_matrix([(ahead_ref[x, :, head:], to_next), (past, to_last)], depth // sites)
        place = place_of(x, planes)
        for k in range(groups):
            edge = near[: 2 * row_size] if k == 0 else far_ref[k - 1, x].astype(jnp.float32)
            column = jnp.concatenate([above, edge, below], axis=0).astype(jnp.bfloat16)
            field_ref[k, place] = (part_ref[k, place] + dot(matrix, column)).astype(jnp.bfloat16)
    for k in range(groups):
        turned_ref[k] = field_ref[k].reshape(planes * depth, width).T


def second_share(kind, lefts_ref, right_ref, edge_ref, keep_ref, send_ref, total_ref):
    half = half_of(kind)
    inner = right_ref.shape[0]
    total = dot(lefts_ref[half, :, :inner], right_ref[...]) + dot(lefts_ref[half, :, inner:], edge_ref[...])
    share(total, keep_ref, send_ref, total_ref)


def second_kernel(lefts_ref, right_ref, edge_ref, keep_ref, send_ref, total_ref):
    second_share(0, lefts_ref, right_ref, edge_ref, keep_ref, send_ref, total_ref)


def second_own_kernel(lefts_ref, right_ref, edge_ref, first_ref, keep_ref, send_ref, total_ref):
    parts = first_ref.shape[0]
    send_ref[:parts] = first_ref[...]
    second_share(1, lefts_ref, right_ref, edge_ref, keep_ref, send_ref.at[parts:], total_ref)


def exchange(block, step):
    axes = ("gx", "gy", "ma")
    sizes = [lax.axis_size(axis) for axis in axes]
    route = []
    for source in range(sizes[0] * sizes[1] * sizes[2]):
        where = [source // (sizes[1] * sizes[2]), source // sizes[2] % sizes[1], source % sizes[2]]
        axis, bit = step[where[2] % 2]
        where[axes.index(axis)] ^= 1 << bit
        route.append((source, (where[0] * sizes[1] + where[1]) * sizes[2] + where[2]))
    return lax.ppermute(block, axes, route)


def halve(sums, step, weight=0):
    parts = sum(kept.shape[0] for kept, _, _ in sums)
    count, rows, width = sums[0][0].shape[1:]
    dims = (parts, count // 2, rows, width)

    def merge(*refs):
        *refs, keep_ref, send_ref = refs
        mine = my_side(step)
        start = 0
        for k, (_, _, which) in enumerate(sums):
            kept_ref, came_ref = refs[2 * k : 2 * k + 2]
            came_ref = came_ref if which is None else came_ref.at[which]
            end = start + kept_ref.shape[0]
            for index in range(count // 2):
                low, high = (
                    kept_ref[:, at] + came_ref[:, at].astype(jnp.float32) for at in (index, index + count // 2)
                )
                keep_ref[start:end, index] = jnp.where(mine == 0, low, high)
                send_ref[start:end, index] = jnp.where(mine == 0, high, low).astype(send_ref.dtype)
            start = end

    operands = [a for kept, came, _ in sums for a in (kept, came)]
    keep, send = call(merge, (pltpu.VMEM(dims, jnp.float32), pltpu.VMEM(dims, jnp.bfloat16)), weight, operands)
    return keep, exchange(send, step)


def sum_kernel(kept_ref, came_ref, send_ref):
    send_ref[...] = (kept_ref[...] + came_ref[...].astype(jnp.float32)).astype(send_ref.dtype)


def cross_kernel(start, kept_ref, crossed_ref, out_ref):
    kept = kept_ref[start : start + out_ref.shape[0]]
    out_ref[...] = kept + crossed_ref[...].astype(jnp.float32)


def finish_kernel(came_ref, *refs):
    *kept_refs, out_ref = refs
    parts = out_ref.shape[1]
    for d, kept_ref in enumerate(kept_refs):
        out_ref[d] = kept_ref[:, 0] + came_ref[d * parts : (d + 1) * parts, 0].astype(jnp.float32)


def local(eigen_modes, links_first, links_second):
    f32, bf16 = jnp.float32, jnp.bfloat16
    parts, planes, ys, zs, colours, width = eigen_modes.shape
    sites = ys * zs
    depth = parts * colours * sites
    row_size = parts * colours * zs
    edge = -(-(2 * row_size + 8) // 16) * 16
    lanes = -(-(depth + 2 * row_size) // 128) * 128
    across_x, across_y, groups = (lax.axis_size(a) for a in ("gx", "gy", "ma"))
    rows = groups * width // (across_x * across_y)
    inner_depth = (planes - 2) * depth
    raw = eigen_modes.transpose(0, 1, 2, 4, 3, 5)

    def shape(*dims, dtype=bf16):
        return pltpu.VMEM(dims, dtype)

    field_shape = shape(planes, depth, width)
    turned_shape = shape(width, planes * depth)
    total_shape = shape(groups, width, parts * width, dtype=f32)
    link_shape = shape(planes, 8, lanes, dtype=f32)
    total = pltpu.VMEM((width // rows, rows, parts * width), f32)
    step_flops = 2 * planes * depth * depth * width
    project_flops = 2 * groups * width * planes * depth * parts * width

    raw_others = [shifted(raw, "ma", -step) for step in range(1, groups)]
    raw_links_x, raw_links_y = (a.transpose(0, 1, 2, 3, 5, 4) for a in (links_first, links_second))
    inputs = [raw, raw_links_x, raw_links_y]
    first_plane, last_plane, *inputs, past_maps = call(
        edges_kernel,
        (
            shape(parts, ys, colours, zs, width), shape(parts, ys + colours, colours, zs, width),
            *(shape(*a.shape) for a in inputs),
            shape(map_rows(parts, colours, planes, ys, zs)[-1], 2 * lanes, dtype=f32),
            shape(map_rows(parts, colours, 1, ys, zs)[-1], 2 * lanes, dtype=f32),
        ),
        0,
        inputs,
        [pltpu.SemaphoreType.DMA((5,))],
        [pltpu.HBM] * len(inputs),
    )
    low = shifted(last_plane, "gx", 1)
    high = shifted(first_plane, "gx", -1)
    ends, ahead_x, back_x, ahead_y, back_y = call(
        prepare_kernel,
        (shape(planes, edge, width), link_shape, link_shape, link_shape, link_shape),
        0,
        inputs,
    )
    near = shifted(ends, "gy", 1)
    if across_y != 2:
        ahead_row = lax.broadcasted_iota(jnp.int32, ends.shape, 1) < row_size
        near = jnp.where(ahead_row, shifted(ends, "gy", -1), near)

    plan = steps()
    top = ("gx", bits("gx")[-1])
    pieces = across_x * across_y // 4
    kept_shape = shape(parts, pieces, rows, width, dtype=f32)
    sent_shape = shape(parts, pieces, rows, width)

    def inner(*refs):
        inner_kernel(sites, *refs)

    def first(*refs):
        first_kernel(sites, *refs)

    def begin_y(*refs):
        begin_y_kernel(sites, zs, *refs)

    def move_y(*refs):
        move_y_kernel(sites, zs, *refs)

    field, right, own, matrix, ahead_part, back_part = call(
        inner,
        (
            field_shape, shape(inner_depth, parts * width), turned_shape, shape(depth, depth),
            shape(depth, width, dtype=f32), shape(depth, width, dtype=f32),
        ),
        2 * step_flops,
        [inputs[0], ahead_x, back_x],
    )
    turned = [call(turn_kernel, (field_shape, turned_shape), step_flops // 4, [r]) for r in raw_others]
    fields = jnp.stack([t[0] for t in turned])
    others = jnp.stack([t[1] for t in turned])
    begun_first = call(begin_first_kernel, total_shape, project_flops, [own, others, right])
    part_y = call(
        begin_y, shape(groups, planes, depth, width, dtype=f32), 2 * step_flops, [field, fields, ahead_y, back_y]
    )
    part_y, begun_first = lax.optimization_barrier((part_y, begun_first))
    kept_first, sent_first, right_edge = call(
        first,
        (kept_shape, sent_shape, shape(2 * depth, parts * width)),
        project_flops,
        [high, low, matrix, ahead_part, back_part, past_maps, own, others, begun_first],
        [total],
    )
    came_first = exchange(sent_first, plan[0])
    near, right_edge = lax.optimization_barrier((near, right_edge))
    near_rows = near[:, : 2 * row_size]
    far = jnp.stack([shifted(near_rows, "ma", -step) for step in range(1, groups)])
    lefts = call(
        move_y, shape(groups, width, planes * depth), 2 * step_flops,
        [part_y, near, far, ahead_y],
        [pltpu.VMEM((groups,) + field_shape.shape, bf16)],
    )
    kept_second, sent_second = call(
        second_kernel, (kept_shape, sent_shape), 8 * project_flops, [lefts, right, right_edge], [total]
    )
    came_second = exchange(sent_second, plan[0])
    right_edge, kept_second = lax.optimization_barrier((right_edge, kept_second))
    own_first, sent_own = call(
        first_own_kernel, (kept_shape, sent_shape), 0, [own, others, begun_first, right_edge], [total]
    )
    own_second, sent_own = call(
        second_own_kernel, (kept_shape, shape(2 * parts, pieces, rows, width)), 0,
        [lefts, right, right_edge, sent_own], [total],
    )
    crossing = [(kept_first, came_first), (kept_second, came_second)]
    after = own_second
    staying = None
    for step in plan[1:]:
        for d, (kept, came) in enumerate(crossing):
            came, after = lax.optimization_barrier((came, after))
            crossing[d] = halve([(kept, came, None)], step)
            after = crossing[d][0]
            if staying is None:
                sent_own, after = lax.optimization_barrier((sent_own, after))
                came_own = exchange(sent_own, plan[0])
                staying = [
                    (own_first, came_own, slice(0, parts)), (own_second, came_own, slice(parts, 2 * parts))
                ]
    crossed = []
    for kept, came in crossing:
        came, after = lax.optimization_barrier((came, after))
        after = call(sum_kernel, pltpu.VMEM(kept.shape, bf16), 8 * project_flops, [kept, came])
        crossed.append(exchange(after, (top, top)))
    for step in plan[1:]:
        kept, came, which = staying[0]
        came, after = lax.optimization_barrier((came, after))
        sums = [(kept, came, which)] + [(k, came, w) for k, _, w in staying[1:]]
        kept, came = halve(sums, step)
        staying, after = [(kept, came, None)], kept
    kept, came, _ = staying[0]
    totals = []
    for d, block in enumerate(crossed):

        def cross(*refs, start=d * parts):
            cross_kernel(start, *refs)

        block, after = lax.optimization_barrier((block, after))
        after = call(cross, shape(*block.shape, dtype=f32), 4 * project_flops, [kept, block])
        totals.append(after)
    came, after = lax.optimization_barrier((came, after))
    return call(
        finish_kernel, jax.ShapeDtypeStruct((2, parts, rows, width), f32), 0, [came, *totals]
    )


def solution(mesh):
    return jax.shard_map(
        local,
        mesh=mesh,
        in_specs=(
            P("cuts", "gx", "gy", None, None, "ma"),
            P("cuts", None, None, "gx", "gy", None),
            P("cuts", None, None, "gx", "gy", None),
        ),
        out_specs=P("cuts", None, ("gx", "gy"), "ma"),
        check_vma=False,
    )
```
